128 devices in a mesh: seq: 16 (over z, x_lo, core), dp: 8 (over x_hi, y).
Axes of the slice: x: 4 (x_hi: 2, x_lo: 2; x = x_hi * 2 + x_lo), y: 4, z: 4, core: 2. Of those that a mesh axis runs over, the one named last changes fastest.
Arguments:
- hidden_in: bfloat16 [8, 2048, 1024], P('dp', 'seq'), may hold values from -6 to 6
- out_cot: bfloat16 [8, 2048, 1024], P('dp', 'seq'), may hold values from -6 to 6
- in_weight: float32 [1024, 7168], P(('seq', 'dp')), may hold values from -0.1875 to 0.1875
- out_weight: float32 [5120, 1024], P(('seq', 'dp')), may hold values from -0.3125 to 0.3125
- vectors: float32 [13, 1024], P(None, ('seq', 'dp')), as said below
- in_first: float32 [1024, 7168], P(('seq', 'dp')), may hold values from -0.0017089844 to 0.0017089844
- in_second: float32 [1024, 7168], P(('seq', 'dp')), may hold values from 3.9694434e-08 to 6.3511095e-07
- out_first: float32 [5120, 1024], P(('seq', 'dp')), may hold values from -0.0017089844 to 0.0017089844
- out_second: float32 [5120, 1024], P(('seq', 'dp')), may hold values from 3.9694434e-08 to 6.3511095e-07
- vec_first: float32 [13, 1024], P(None, ('seq', 'dp')), may hold values from -0.0048828125 to 0.0048828125
- vec_second: float32 [13, 1024], P(None, ('seq', 'dp')), may hold values from 3.5724992e-07 to 5.7159987e-06
- lengths: int32 [8], P('dp'), may hold values from 1024 to 2048, as said below
- span_of: int32 [16, 2], replicated, may hold values from 0 to 31, as said below
Outputs:
- block_out: bfloat16 [8, 2048, 1024], P('dp', 'seq')
- input_grad: bfloat16 [8, 2048, 1024], P('dp', 'seq')
- grad_norm: float32 [], replicated
- new_in: float32 [1024, 7168], P(('seq', 'dp'))
- new_out: float32 [5120, 1024], P(('seq', 'dp'))
- new_vectors: float32 [13, 1024], P(None, ('seq', 'dp'))
- new_in_first: float32 [1024, 7168], P(('seq', 'dp'))
- new_out_first: float32 [5120, 1024], P(('seq', 'dp'))
- new_vec_first: float32 [13, 1024], P(None, ('seq', 'dp'))
- new_in_second: float32 [1024, 7168], P(('seq', 'dp'))
- new_out_second: float32 [5120, 1024], P(('seq', 'dp'))
- new_vec_second: float32 [13, 1024], P(None, ('seq', 'dp'))
- low_in: bfloat16 [1024, 7168], P(('seq', 'dp'))
- low_out: bfloat16 [5120, 1024], P(('seq', 'dp'))
- low_vectors: bfloat16 [13, 1024], P(None, ('seq', 'dp'))
The draws below stay inside these ranges and needn't reach their ends.
Inputs may be any that keep to these rules, and one draw needn't show every extreme that they name: `lengths`: one row, drawn from the seed, holds 2048 real tokens. `span_of`: row s holds c and 31 - c; the first entries over all s are a permutation. `vectors`: rows 0 and 2 are the norms' gains, rows 1 and 3 their biases, the rest biases as the steps name them.
All inputs are finite; a program needn't handle non-finite values.
Results may differ from the reference program's by a relative error of at most 0.014.
Values may be sent and summed in bfloat16 or wider, within the bound.
A program may use at most 256 MiB of HBM per device.

```python
import math
import jax
import jax.numpy as jnp
from jax import lax

D = 1024
FF = 4096
HEADS = 16
HEAD = 64
ROT = 16
TOK_DEV = 128
STEP = 5
ROW = 2048
GROUPS = 8
VEC_ROWS = 13
PARAMS = 12596224
N_SEQ = 16


def draw_vectors(key, part):
    key = jax.random.fold_in(key, 7)
    gain_key, rest_key = jax.random.split(key)
    ramp = 0.5 + jnp.arange(D, dtype=jnp.float32) / D
    gains = ramp[None, :] * jax.random.uniform(gain_key, (2, D), jnp.float32, 0.7, 1.3)
    others = 0.3 * jax.random.normal(rest_key, (VEC_ROWS - 2, D), jnp.float32)
    return jnp.concatenate([gains[0:1], others[0:1], gains[1:2], others[1:]], axis=0)


def draw_lengths(key, part):
    key = jax.random.fold_in(key, 11)
    len_key, full_key = jax.random.split(key)
    drawn = jax.random.randint(len_key, (GROUPS,), ROW // 2, ROW + 1)
    chosen = jax.random.randint(full_key, (), 0, GROUPS)
    return jnp.where(jnp.arange(GROUPS) == chosen, ROW, drawn).astype(jnp.int32)


def draw_span_of(key, part):
    key = jax.random.fold_in(key, 13)
    order = jax.random.permutation(key, N_SEQ).astype(jnp.int32)
    return jnp.stack([order, 2 * N_SEQ - 1 - order], axis=1).astype(jnp.int32)


def levels(key, shape, pieces, low, top_value):
    loudness = 1.0
    for dim, shards_of in pieces:
        draws = jax.random.uniform(jax.random.fold_in(jax.random.fold_in(key, 6), dim), (shards_of,), jnp.float32, low / len(pieces), top_value / len(pieces))
        loudness = loudness * jnp.repeat(jnp.exp(draws), shape[dim] // shards_of).reshape((-1,) + (1,) * (len(shape) - 1 - dim))
    return loudness


def centred(key, shape, spread, bound, pieces=(), kind=jnp.bfloat16):
    values = jax.random.normal(key, shape, jnp.float32) * spread
    if len(pieces) > 0:
        values = levels(key, shape, pieces, -0.22, 0.18) * values
    return jnp.clip(values, min=-bound, max=bound).astype(kind)


def setup_inputs(seed: int = 0) -> dict:
    streams_of = jax.random.split(jax.random.key(seed), 14)
    return {
        "hidden_in": centred(streams_of[0], (GROUPS, ROW, D), 1.0, 6.0, ((0, 8), (1, 16))),
        "out_cot": centred(streams_of[1], (GROUPS, ROW, D), 1.0, 6.0, ((0, 8), (1, 16))),
        "in_weight": centred(streams_of[2], (D, 3 * D + FF), D ** -0.5, 0.1875, ((0, 128),), jnp.float32),
        "out_weight": centred(streams_of[3], (D + FF, D), ((D + FF) // 16) ** -0.5, 0.3125, ((0, 128),), jnp.float32),
        "vectors": draw_vectors(jax.random.fold_in(streams_of[13], 71), 0),
        "in_first": centred(streams_of[5], (D, 3 * D + FF), (PARAMS ** -0.5), 0.0017089844, ((0, 128),), jnp.float32),
        "in_second": jnp.clip(jnp.exp(math.log(6.351109504976193e-07) - 2.7725887 * jax.random.uniform(streams_of[6], (D, 3 * D + FF), jnp.float32) ** levels(streams_of[6], (D, 3 * D + FF), ((0, 128),), -0.2, 0.2)), 3.969443440610121e-08, 6.351109504976193e-07),
        "out_first": centred(streams_of[7], (D + FF, D), (PARAMS ** -0.5), 0.0017089844, ((0, 128),), jnp.float32),
        "out_second": jnp.clip(jnp.exp(math.log(6.351109504976193e-07) - 2.7725887 * jax.random.uniform(streams_of[8], (D + FF, D), jnp.float32) ** levels(streams_of[8], (D + FF, D), ((0, 128),), -0.2, 0.2)), 3.969443440610121e-08, 6.351109504976193e-07),
        "vec_first": centred(streams_of[9], (VEC_ROWS, D), (3.0 * PARAMS ** -0.5), 0.0048828125, ((1, 128),), jnp.float32),
        "vec_second": jnp.clip(jnp.exp(math.log(5.715998668165412e-06) - 2.7725887 * jax.random.uniform(streams_of[10], (VEC_ROWS, D), jnp.float32) ** levels(streams_of[10], (VEC_ROWS, D), ((1, 128),), -0.2, 0.2)), 3.5724991676033824e-07, 5.715998668165412e-06),
        "lengths": draw_lengths(jax.random.fold_in(streams_of[13], 71), 0),
        "span_of": draw_span_of(jax.random.fold_in(streams_of[13], 71), 0),
    }


NORM_EPS = 1e-05
NEG_FILL = -1e+30
CLIP_NORM = 1.0
RATE_MATRIX = 0.02
RATE_VECTOR = 0.2
BETA_ONE = 0.5
BETA_TWO = 0.5
DECAY_RATE = 0.1
ADAM_EPS = 1e-08
THETA_BASE = 10000.0

@jax.custom_vjp
def low(v):
    return lax.optimization_barrier(v.astype(jnp.bfloat16)).astype(jnp.float32)

@jax.custom_vjp
def low_back(v):
    return v

def low_keep(v):
    return (low(v), None)

def low_pass(kept, grad):
    return (grad,)

def back_keep(v):
    return (v, None)

def back_low(kept, grad):
    return (low(grad),)
low.defvjp(low_keep, low_pass)
low_back.defvjp(back_keep, back_low)

def token_positions(span_of, tok_dev, shards):
    rows_all = jnp.arange(tok_dev * shards, dtype=jnp.int32)
    span_len = tok_dev // 2
    slot_ids = rows_all // tok_dev * 2 + rows_all % tok_dev // span_len
    table = span_of.reshape(-1)
    match = slot_ids[:, None] == jnp.arange(2 * shards, dtype=jnp.int32)[None, :]
    starts = lax.optimization_barrier(jnp.sum(jnp.where(match, table[None, :], 0), axis=1))
    return (starts * span_len + rows_all % span_len).astype(jnp.int32)

def rotary_tables(positions, rot_dims):
    half_dims = rot_dims // 2
    freqs = THETA_BASE ** (-2.0 * jnp.arange(half_dims, dtype=jnp.float32) / rot_dims)
    angles = positions.astype(jnp.float32)[:, None] * freqs[None, :]
    return (jnp.cos(angles), jnp.sin(angles))

def rotate(values, cosine, sine_table, rot_dims):
    half_dims = rot_dims // 2
    first_half = values[..., :half_dims]
    second_half = values[..., half_dims:rot_dims]
    cos_part = cosine[:, None, :]
    sin_part = sine_table[:, None, :]
    return jnp.concatenate([first_half * cos_part - second_half * sin_part, second_half * cos_part + first_half * sin_part, values[..., rot_dims:]], axis=-1)

def attention(query, keys, values, positions, length):
    block_rows = 512 if ROW % 512 == 0 else ROW
    key_valid = positions < length

    def one_block(inputs):
        query_blk, pos_blk = inputs
        scores = jnp.einsum('qhd,khd->hqk', query_blk, keys, precision=lax.Precision.HIGHEST) * HEAD ** (-0.5)
        scores = low_back(scores)
        allowed = (positions[None, :] <= pos_blk[:, None]) & key_valid[None, :]
        scores = jnp.where(allowed[None], scores, NEG_FILL)
        row_max = lax.optimization_barrier(jnp.max(scores, axis=-1, keepdims=True))
        exp_scores = jnp.exp(scores - row_max)
        probs = low(exp_scores / lax.optimization_barrier(jnp.sum(exp_scores, axis=-1, keepdims=True)))
        return jnp.einsum('hqk,khd->qhd', probs, values, precision=lax.Precision.HIGHEST)
    blocks = lax.map(jax.checkpoint(one_block), (query.reshape(-1, block_rows, HEADS, HEAD), positions.reshape(-1, block_rows)))
    return blocks.reshape(ROW, D)

def block_forward(x_rows, in_full, out_full, vec_full, positions, length):
    vec_used = low(vec_full)
    in_used = low(in_full)
    out_used = low(out_full)
    row_mean = lax.optimization_barrier(jnp.mean(x_rows, axis=-1, keepdims=True))
    centered = x_rows - row_mean
    inv_std = lax.rsqrt(lax.optimization_barrier(jnp.mean(centered * centered, axis=-1, keepdims=True)) + NORM_EPS)
    x_hat = centered * inv_std
    normed_a = low(x_hat * vec_used[0] + vec_used[1])
    normed_m = low(x_hat * vec_used[2] + vec_used[3])
    qkv_bias = jnp.concatenate([vec_used[4], vec_used[5], vec_used[6]])
    qkv = jnp.dot(normed_a, in_used[:, :3 * D], precision=lax.Precision.HIGHEST, preferred_element_type=jnp.float32) + qkv_bias
    qkv = low_back(qkv)
    pre = jnp.dot(normed_m, in_used[:, 3 * D:], precision=lax.Precision.HIGHEST, preferred_element_type=jnp.float32) + vec_used[9:].reshape(FF)
    pre = low_back(pre)
    cosine, sine_table = rotary_tables(positions, ROT)
    query = low(rotate(qkv[:, :D].reshape(ROW, HEADS, HEAD), cosine, sine_table, ROT))
    keys = low(rotate(qkv[:, D:2 * D].reshape(ROW, HEADS, HEAD), cosine, sine_table, ROT))
    values = low(qkv[:, 2 * D:3 * D].reshape(ROW, HEADS, HEAD))
    attended = low(low_back(attention(query, keys, values, positions, length)))
    activ = low(jax.nn.gelu(pre, approximate=False))
    joined = jnp.concatenate([attended, activ], axis=1)
    return x_rows + jnp.dot(joined, out_used, precision=lax.Precision.HIGHEST, preferred_element_type=jnp.float32) + vec_used[7] + vec_used[8]

def reference(hidden_in, out_cot, in_weight, out_weight, vectors, in_first, in_second, out_first, out_second, vec_first, vec_second, lengths, span_of):
    positions = token_positions(span_of, TOK_DEV, N_SEQ)

    def one_group(sums, inputs):
        rows_in, cot_in, length = inputs
        x_rows = rows_in.astype(jnp.float32)
        valid = (positions < length).astype(jnp.float32)

        def forward_fn(x_part, in_part, out_part, vec_part):
            return block_forward(x_part, in_part, out_part, vec_part, positions, length)
        result, backward_fn = jax.vjp(forward_fn, x_rows, in_weight, out_weight, vectors)
        grad_x, grad_in, grad_out, grad_vec = backward_fn(cot_in.astype(jnp.float32) * valid[:, None])
        sums = (sums[0] + grad_in, sums[1] + grad_out, sums[2] + grad_vec)
        return (sums, (result.astype(jnp.bfloat16), grad_x.astype(jnp.bfloat16)))
    zeros_init = (jnp.zeros_like(in_weight), jnp.zeros_like(out_weight), jnp.zeros_like(vectors))
    sums, outputs = lax.scan(one_group, zeros_init, (hidden_in, out_cot, lengths))
    block_out, input_grad = outputs
    grad_in, grad_out, grad_vec = sums
    squares = jnp.sum(grad_in * grad_in) + jnp.sum(grad_out * grad_out) + jnp.sum(grad_vec * grad_vec)
    grad_norm = jnp.sqrt(squares)
    factor = jnp.minimum(1.0, CLIP_NORM / grad_norm)

    def adam_step(weight, grad, first, second, rate, decay):
        clipped = grad * factor
        first_new = BETA_ONE * first + (1.0 - BETA_ONE) * clipped
        second_new = BETA_TWO * second + (1.0 - BETA_TWO) * clipped * clipped
        first_hat = first_new / (1.0 - BETA_ONE ** STEP)
        second_hat = second_new / (1.0 - BETA_TWO ** STEP)
        weight_new = weight * (1.0 - rate * decay) - rate * first_hat / (jnp.sqrt(second_hat) + ADAM_EPS)
        return (weight_new, first_new, second_new)
    new_in, new_in_first, new_in_second = adam_step(in_weight, grad_in, in_first, in_second, RATE_MATRIX, DECAY_RATE)
    new_out, new_out_first, new_out_second = adam_step(out_weight, grad_out, out_first, out_second, RATE_MATRIX, DECAY_RATE)
    new_vectors, new_vec_first, new_vec_second = adam_step(vectors, grad_vec, vec_first, vec_second, RATE_VECTOR, 0.0)
    return (block_out, input_grad, grad_norm, new_in, new_out, new_vectors, new_in_first, new_out_first, new_vec_first, new_in_second, new_out_second, new_vec_second, new_in.astype(jnp.bfloat16), new_out.astype(jnp.bfloat16), new_vectors.astype(jnp.bfloat16))
```

```python
import functools
import math

import jax
import jax.numpy as jnp
import numpy as np
from jax import lax
from jax.experimental import pallas as pl
from jax.experimental.pallas import tpu as pltpu
from jax.sharding import PartitionSpec as P

D = 1024
FF = 4096
HEADS = 16
HEAD = 64
ROT = 16
STEP = 5
SEQ = 16
DP = 8
TOK = 128
ROW = 2048
SPAN = 64

NORM_EPS = 1e-05
NEG_FILL = -1e30
CLIP_NORM = 1.0
RATE_MATRIX = 0.02
RATE_VECTOR = 0.2
BETA_ONE = 0.5
BETA_TWO = 0.5
DECAY_RATE = 0.1
ADAM_EPS = 1e-08
THETA_BASE = 10000.0

F32 = jnp.float32
BF16 = jnp.bfloat16
MESH = pl.DeviceIdType.MESH
VMEM_LIMIT = 60 * 1024 * 1024


def head_of(s):
    if s < 4:
        return 5 * s
    return 5 * ((s - 4) // 4) + 1 + (s - 4) % 4


def hidden_pieces(s):
    if s < 3:
        return [20 * s + 5 * r + 8 for r in range(4)]
    if s == 3:
        return [0, 1, 2, 3]
    return [5 * s - 16 + r for r in range(4)]


def column_pieces():
    rows = []
    for s in range(SEQ):
        h = head_of(s)
        rows.append([h, 16 + h, 32 + h] + [48 + w for w in hidden_pieces(s)])
    return np.array(rows, np.int32)


PIECES = column_pieces()


def head_index(s):
    return jnp.where(s < 4, 5 * s, 5 * ((s - 4) // 4) + 1 + (s - 4) % 4)


def hidden_index(s, r):
    return jnp.where(s < 3, 20 * s + 5 * r + 8, jnp.where(s == 3, r, 5 * s - 16 + r))


def remote(src, dst, send, recv, **where):
    return pltpu.make_async_remote_copy(
        src_ref=src, dst_ref=dst, send_sem=send, recv_sem=recv, device_id=where, device_id_type=MESH
    )


def enter(me, dm):
    barrier = pltpu.get_barrier_semaphore()

    @pl.loop(1, SEQ)
    def _(k):
        pl.semaphore_signal(
            barrier, inc=1, device_id={"seq": lax.rem(me + k, SEQ)}, device_id_type=MESH
        )

    @pl.loop(1, DP)
    def _(k):
        pl.semaphore_signal(
            barrier, inc=1, device_id={"dp": lax.rem(dm + k, DP)}, device_id_type=MESH
        )

    pl.semaphore_wait(barrier, SEQ + DP - 2)


def gather_kernel(
    xh_ref,
    cot_ref,
    win_ref,
    wout_ref,
    xh_all,
    cot_all,
    win_all,
    wout_all,
    swap_all,
    local_sem,
    a_send,
    a_recv,
    l_send,
    l_recv,
    o_send,
    o_recv,
    x_send,
    x_recv,
    f_send,
    c_send,
    c_recv,
    g_send,
    w_send,
    w_recv,
):
    me = lax.axis_index("seq")
    dm = lax.axis_index("dp")
    sib = me + 1 - 2 * lax.rem(me, 2)
    own = [
        pltpu.make_async_copy(win_ref.at[me], win_all.at[dm, me], local_sem.at[0]),
        pltpu.make_async_copy(xh_ref, xh_all.at[me], local_sem.at[1]),
        pltpu.make_async_copy(wout_ref, wout_all.at[pl.ds(dm * 5, 5)], local_sem.at[2]),
        pltpu.make_async_copy(cot_ref, cot_all.at[me], local_sem.at[3]),
    ]
    for c in own:
        c.start()
    enter(me, dm)

    def a_copy(k):
        to = lax.rem(me + k, SEQ)
        return remote(win_ref.at[to], win_all.at[dm, me], a_send.at[k], a_recv.at[me], seq=to)

    def a_wait(k):
        frm = lax.rem(me + k, SEQ)
        return remote(win_ref.at[0], win_all.at[dm, frm], a_send.at[k], a_recv.at[frm], seq=frm)

    def l_copy(k, frm):
        to = lax.rem(dm + k, DP)
        return remote(win_all.at[frm], win_all.at[frm], l_send.at[k], l_recv.at[frm], dp=to)

    def o_copy(k, frm):
        to = lax.rem(dm + k, DP)
        return remote(
            wout_ref, wout_all.at[pl.ds(frm * 5, 5)], o_send.at[k], o_recv.at[frm], dp=to
        )

    def row_sends(src, dst, send, recv):
        remote(src, dst.at[me], send.at[0], recv.at[me], seq=sib).start()

        @pl.loop(1, 8)
        def _(j):
            to = lax.rem(me + 2 * j, SEQ)
            remote(src, dst.at[me], send.at[j], recv.at[me], seq=to).start()

    def row_forwards(src, dst, recv, fsend):
        @pl.loop(1, 8)
        def _(j):
            frm = lax.rem(me + 2 * j, SEQ)
            remote(src, dst.at[frm], fsend.at[j], recv.at[frm], seq=sib).wait_recv()
            remote(dst.at[frm], dst.at[frm], fsend.at[j], recv.at[frm], seq=sib).start()

    def row_finish(src, dst, send, recv, fsend):
        @pl.loop(0, 8)
        def _(j):
            frm = lax.rem(sib + 2 * j, SEQ)
            remote(src, dst.at[frm], send.at[j], recv.at[frm], seq=sib).wait_recv()
            remote(src, dst.at[me], send.at[j], recv.at[me], seq=sib).wait_send()

        @pl.loop(1, 8)
        def _(j):
            frm = lax.rem(me + 2 * j, SEQ)
            remote(dst.at[frm], dst.at[frm], fsend.at[j], recv.at[frm], seq=sib).wait_send()

    @pl.loop(1, SEQ)
    def _(k):
        a_copy(k).start()

    row_sends(xh_ref, xh_all, x_send, x_recv)

    @pl.loop(1, DP)
    def _(k):
        o_copy(k, dm).start()

    own[0].wait()

    @pl.loop(1, SEQ)
    def _(k):
        a_wait(k).wait_recv()

    @pl.loop(1, DP)
    def _(k):
        l_copy(k, dm).start()

    row_sends(cot_ref, cot_all, c_send, c_recv)
    row_forwards(xh_ref, xh_all, x_recv, f_send)

    own[2].wait()

    @pl.loop(1, DP)
    def _(k):
        o_copy(k, lax.rem(dm + k, DP)).wait_recv()

    def swap_few(r):
        return remote(
            wout_all.at[pl.ds(8 + 8 * r, 8)],
            swap_all.at[0],
            w_send.at[r],
            w_recv.at[0],
            seq=4 + 4 * me + r,
        )

    def swap_many():
        return remote(
            wout_all.at[pl.ds(32, 8)],
            swap_all.at[lax.rem(me, 4)],
            w_send.at[0],
            w_recv.at[lax.rem(me, 4)],
            seq=(me - 4) // 4,
        )

    @pl.when(me < 3)
    def _():
        for r in range(4):
            swap_few(r).start()

    @pl.when(me > 3)
    def _():
        swap_many().start()

    row_forwards(cot_ref, cot_all, c_recv, g_send)
    row_finish(xh_ref, xh_all, x_send, x_recv, f_send)
    row_finish(cot_ref, cot_all, c_send, c_recv, g_send)

    @pl.when(me < 3)
    def _():
        for r in range(4):
            remote(
                wout_all.at[pl.ds(32, 8)], swap_all.at[r], w_send.at[r], w_recv.at[r], seq=me
            ).wait_recv()
            swap_few(r).wait_send()

    @pl.when(me > 3)
    def _():
        swap_many().wait_send()
        remote(
            wout_all.at[pl.ds(32, 8)], swap_all.at[0], w_send.at[0], w_recv.at[0], seq=me
        ).wait_recv()

    @pl.loop(1, DP)
    def _(k):
        l_copy(k, lax.rem(dm + k, DP)).wait_recv()
        l_copy(k, dm).wait_send()
        o_copy(k, dm).wait_send()

    @pl.loop(1, SEQ)
    def _(k):
        a_copy(k).wait_send()

    own[1].wait()
    own[3].wait()


def gather_call(xh, cot, win, wout):
    any_spec = pl.BlockSpec(memory_space=pl.ANY)
    dma = pltpu.SemaphoreType.DMA
    return pl.pallas_call(
        gather_kernel,
        out_shape=(
            jax.ShapeDtypeStruct((SEQ, TOK, D), BF16),
            jax.ShapeDtypeStruct((SEQ, TOK, D), BF16),
            jax.ShapeDtypeStruct((DP, SEQ, 16, 256), BF16),
            jax.ShapeDtypeStruct((40, 16, 512), BF16),
            jax.ShapeDtypeStruct((4, 8, 16, 512), BF16),
        ),
        in_specs=[any_spec] * 4,
        out_specs=[any_spec] * 5,
        scratch_shapes=[
            dma((4,)),
            dma((SEQ,)),
            dma((SEQ,)),
            dma((DP,)),
            dma((DP,)),
            dma((DP,)),
            dma((DP,)),
            dma((8,)),
            dma((SEQ,)),
            dma((8,)),
            dma((8,)),
            dma((SEQ,)),
            dma((8,)),
            dma((4,)),
            dma((4,)),
        ],
        compiler_params=pltpu.CompilerParams(collective_id=0, has_side_effects=True),
        name="gather_rows_weights",
    )(xh, cot, win, wout)


def dot(a, b):
    return jnp.dot(a, b, preferred_element_type=F32)


def dot_nt(a, b):
    return lax.dot_general(a, b, (((1,), (1,)), ((), ())), preferred_element_type=F32)


def lane_iota(shape):
    return lax.broadcasted_iota(jnp.int32, shape, len(shape) - 1)


CH = 512
NCH = ROW // CH


def core_kernel(
    span_ref,
    inv_ref,
    len_ref,
    xh_ref,
    cot_ref,
    win_ref,
    wout_ref,
    swap_ref,
    cos_ref,
    sin_ref,
    po_ref,
    hg_ref,
    gin_ref,
    goa_ref,
    gof_ref,
    vec_ref,
    xs,
    cs,
    wqr,
    wfr,
    wqp,
    wfp,
    woa,
    wof,
    qt,
    qn,
    kt,
    kn,
    vt,
    vn,
    dot_t,
    dot_n,
    ot,
    lse,
    delta,
    act,
    act_t,
    dact,
    mixf,
    mixf_t,
    mixq,
    mixq_t,
    att,
    att_t,
    dqt,
    dkn,
    dvn,
    vg,
):
    me = lax.axis_index("seq")
    head = head_index(me)

    def unpack(sb, carry):
        cq, cf = carry
        tiles = [win_ref[d, sb].astype(F32) for d in range(DP)]
        ff = jnp.concatenate([t[:8] for t in tiles], axis=0)
        qk = jnp.concatenate([t[8:] for t in tiles], axis=0)
        rows = pl.ds(pl.multiple_of(sb * 64, 64), 64)
        gain_a, bias_a, gain_m, bias_m = (qk[:, 192 + i : 193 + i] for i in range(4))
        wfr[rows] = ff.astype(BF16)
        wqr[rows] = qk.astype(BF16)
        wfp[rows] = (ff * gain_m).astype(BF16)
        wqp[rows] = jnp.where(lane_iota(qk.shape) < 192, qk * gain_a, 0.0).astype(BF16)
        return (
            cq + jnp.sum(qk * bias_a, axis=0, keepdims=True),
            cf + jnp.sum(ff * bias_m, axis=0, keepdims=True),
        )

    zero_row = jnp.zeros((1, 256), F32)
    cq, cf = lax.fori_loop(0, SEQ, unpack, (zero_row, zero_row))

    slab = jnp.transpose(wqr[:, 128:256].astype(F32))
    vec_ref[...] = slab[64:80]

    hid = []
    for r in range(4):
        w = hidden_index(me, r)
        rows = pl.ds(pl.multiple_of(lax.rem(w, 16) * 64, 64), 64)
        part = wqr[rows, 128:256].astype(F32)
        lane = 64 + 9 + w // 16
        hid.append(jnp.sum(jnp.where(lane_iota(part.shape) == lane, part, 0.0), axis=1, keepdims=True))
    hid = jnp.concatenate(hid, axis=0)
    cf = cf + jnp.transpose(jnp.broadcast_to(hid, (256, 128)))[0:1]

    head_rows = pl.ds(pl.multiple_of(head * 64, 64), 64)
    head_vecs = wqr[head_rows, 128:256].astype(F32)
    bq, bk, bv = (head_vecs[:, 68 + i : 69 + i] for i in range(3))

    def unit(ref, index, dst, at):
        u = ref[index].astype(F32)
        return jnp.concatenate([u[:8], u[8:]], axis=1)

    def put_units(src, base, dst, count):
        @pl.loop(0, count // 2)
        def _(i):
            pair = [src[base + 2 * i + j].astype(F32) for j in range(2)]
            pair = [jnp.concatenate([u[:8], u[8:]], axis=1) for u in pair]
            dst[pl.ds(pl.multiple_of(i * 16, 16), 16)] = jnp.concatenate(pair, axis=0).astype(BF16)

    def put_swap(dst, rs):
        for r in range(rs):
            for i in range(4):
                pair = [swap_ref[r, 2 * i + j].astype(F32) for j in range(2)]
                pair = [jnp.concatenate([u[:8], u[8:]], axis=1) for u in pair]
                dst[r * 64 + i * 16 : r * 64 + i * 16 + 16] = jnp.concatenate(pair, axis=0).astype(
                    BF16
                )

    @pl.when(me < 4)
    def _():
        put_units(wout_ref, 0, woa, 8)

    @pl.when(me < 3)
    def _():
        put_swap(wof, 4)

    @pl.when(me == 3)
    def _():
        put_units(wout_ref, 8, wof, 32)

    @pl.when(me > 3)
    def _():
        put_swap(woa, 1)
        put_units(wout_ref, 0, wof, 32)

    @pl.loop(0, 32)
    def _(i):
        rows = pl.ds(pl.multiple_of(i * 64, 64), 64)
        xs[rows] = xh_ref[inv_ref[i]]
        cs[rows] = cot_ref[inv_ref[i]]

    aug = jnp.where(lax.broadcasted_iota(jnp.int32, (64, CH), 0) == 0, 1.0, 0.0)
    zeros_aug = jnp.zeros((64, CH), F32)

    def rotate_t(u, cosine, sine, sign):
        first, second = u[0:8], u[8:16]
        return jnp.concatenate(
            [
                first * cosine - sign * (second * sine),
                second * cosine + sign * (first * sine),
                u[16:],
            ],
            axis=0,
        )

    @pl.loop(0, NCH)
    def _(i):
        start = pl.multiple_of(i * CH, CH)
        rows = pl.ds(start, CH)
        xh = xs[rows]
        qkv = jnp.transpose(dot(xh, wqp[...]) + cq)
        cosine, sine = cos_ref[:, rows], sin_ref[:, rows]
        q = rotate_t(qkv[0:64] + bq, cosine, sine, 1.0) * 0.125
        k = rotate_t(qkv[64:128] + bk, cosine, sine, 1.0)
        v = qkv[128:192] + bv
        q_full = jnp.concatenate([q, aug], axis=0)
        past = (start + lane_iota((64, CH))) >= len_ref[0]
        k_full = jnp.concatenate([k, jnp.where(past, NEG_FILL, 0.0) * aug], axis=0)
        v_full = jnp.concatenate([v, zeros_aug], axis=0)
        qt[:, rows] = q_full.astype(BF16)
        kt[:, rows] = k.astype(BF16)
        vt[:, rows] = v.astype(BF16)
        qn[rows] = jnp.transpose(q_full).astype(BF16)
        kn[rows] = jnp.transpose(k_full).astype(BF16)
        vn[rows] = jnp.transpose(v_full).astype(BF16)
        pre = dot(xh, wfp[...]) + cf
        cdf = 0.5 * (1.0 + lax.erf(pre * (1.0 / math.sqrt(2.0))))
        pdf = jnp.exp(-0.5 * pre * pre) * (1.0 / math.sqrt(2.0 * math.pi))
        activ = pre * cdf
        act[rows] = activ.astype(BF16)
        act_t[:, rows] = jnp.transpose(activ).astype(BF16)
        dact[rows] = cdf + pre * pdf

    causal = lax.broadcasted_iota(jnp.int32, (CH, CH), 0) <= lane_iota((CH, CH))

    def scores(kc, qi):
        s = dot(kn[kc * CH : (kc + 1) * CH], qt[:, qi * CH : (qi + 1) * CH])
        if kc == qi:
            s = jnp.where(causal, s, NEG_FILL)
        return s

    for qi in range(NCH):
        lanes = slice(qi * CH, (qi + 1) * CH)
        parts = [scores(kc, qi) for kc in range(qi + 1)]
        top = functools.reduce(jnp.maximum, [jnp.max(s, axis=0, keepdims=True) for s in parts])
        total = jnp.zeros((1, CH), F32)
        out = jnp.zeros((64, CH), F32)
        for kc, s in enumerate(parts):
            p = jnp.exp(s - top)
            total = total + jnp.sum(p, axis=0, keepdims=True)
            out = out + dot(vt[:, kc * CH : (kc + 1) * CH], p.astype(BF16))
        out = out / total
        ot[:, lanes] = out
        lse[:, lanes] = jnp.broadcast_to(top + jnp.log(total), (8, CH))
        att_t[:, lanes] = out.astype(BF16)
        att[lanes] = jnp.transpose(out).astype(BF16)

    @pl.loop(0, NCH)
    def _(i):
        rows = pl.ds(pl.multiple_of(i * CH, CH), CH)
        cot = cs[rows]
        ag = dot_nt(cot, woa[...]).astype(BF16).astype(F32)
        ag_t = jnp.transpose(ag)
        dot_n[rows] = ag.astype(BF16)
        dot_t[:, rows] = ag_t.astype(BF16)
        delta[:, rows] = jnp.broadcast_to(jnp.sum(ag_t * ot[:, rows], axis=0, keepdims=True), (8, CH))
        pg = dot_nt(cot, wof[...]) * dact[rows]
        mixf[rows] = pg.astype(BF16)
        mixf_t[:, rows] = jnp.transpose(pg).astype(BF16)

    for qi in range(NCH):
        lanes = slice(qi * CH, (qi + 1) * CH)
        dq = jnp.zeros((64, CH), F32)
        for kc in range(qi + 1):
            keys = slice(kc * CH, (kc + 1) * CH)
            p = jnp.exp(scores(kc, qi) - lse[0:1, lanes])
            dp = dot(vn[keys, 0:64], dot_t[:, lanes])
            ds = (p * (dp - delta[0:1, lanes])).astype(BF16)
            dv = dot(p.astype(BF16), dot_n[lanes])
            dk = dot(ds, qn[lanes, 0:64])
            dq = dq + dot(kt[:, keys], ds)
            if kc == qi:
                dvn[keys] = dv
                dkn[keys] = dk
            else:
                dvn[keys] += dv
                dkn[keys] += dk
        dqt[:, lanes] = dq * 0.125

    @pl.loop(0, NCH)
    def _(i):
        rows = pl.ds(pl.multiple_of(i * CH, CH), CH)
        cosine, sine = cos_ref[:, rows], sin_ref[:, rows]
        dq = rotate_t(dqt[:, rows], cosine, sine, -1.0)
        dk = rotate_t(jnp.transpose(dkn[rows]), cosine, sine, -1.0)
        dv = jnp.transpose(dvn[rows])
        full = jnp.concatenate([dq, dk, dv, zeros_aug], axis=0)
        mixq_t[:, rows] = full.astype(BF16)
        mixq[rows] = jnp.transpose(full).astype(BF16)

    @pl.loop(0, SEQ)
    def _(s):
        def both(ref):
            return jnp.concatenate(
                [
                    ref[pl.ds(pl.multiple_of(span_ref[2 * s + j] * SPAN, SPAN), SPAN)]
                    for j in range(2)
                ],
                axis=0,
            )

        po_ref[s] = (dot(both(att), woa[...]) + dot(both(act), wof[...])).astype(BF16)
        hg_ref[s] = (dot_nt(both(mixq), wqp[...]) + dot_nt(both(mixf), wfp[...])).astype(BF16)

    goa = dot(att_t[...], cs[...]).reshape(8, 8, D)
    goa_ref[...] = jnp.concatenate([goa[:, :, :512], goa[:, :, 512:]], axis=1).astype(BF16)

    @pl.loop(0, 4)
    def _(i):
        rows = pl.ds(pl.multiple_of(i * 64, 64), 64)
        gof = dot(act_t[rows], cs[...]).reshape(8, 8, D)
        gof_ref[pl.ds(i * 8, 8)] = jnp.concatenate(
            [gof[:, :, :512], gof[:, :, 512:]], axis=1
        ).astype(BF16)

    sums_q = jnp.sum(mixq[...].astype(F32), axis=0, keepdims=True)
    sums_f = jnp.sum(mixf[...].astype(F32), axis=0, keepdims=True)
    cols_q = jnp.sum(mixq_t[...].astype(F32), axis=1, keepdims=True)
    cols_f = jnp.sum(mixf_t[...].astype(F32), axis=1, keepdims=True)
    cot_own = jnp.sum(cot_ref[2 * me].astype(F32), axis=0, keepdims=True) + jnp.sum(
        cot_ref[2 * me + 1].astype(F32), axis=0, keepdims=True
    )
    cot_cols = jnp.transpose(jnp.broadcast_to(cot_own, (128, D)))
    lanes_d = lane_iota((D, 128))
    vg[...] = jnp.where((lanes_d == 71) | (lanes_d == 72), cot_cols, 0.0)
    lanes_h = lane_iota((64, 128))
    for i in range(3):
        vg[head_rows] += jnp.where(lanes_h == 68 + i, cols_q[64 * i : 64 * i + 64], 0.0)
    for r in range(4):
        w = hidden_index(me, r)
        rows = pl.ds(pl.multiple_of(lax.rem(w, 16) * 64, 64), 64)
        vg[rows] += jnp.where(lanes_h == 64 + 9 + w // 16, cols_f[64 * r : 64 * r + 64], 0.0)

    @pl.loop(0, 4)
    def _(i):
        rows = pl.ds(pl.multiple_of(i * 256, 256), 256)
        hq = jnp.transpose(dot(mixq_t[...], xs[:, rows]))
        hf = jnp.transpose(dot(mixf_t[...], xs[:, rows]))
        raw_q = wqr[rows].astype(F32)
        raw_f = wfr[rows].astype(F32)
        gain_a, bias_a, gain_m, bias_m = (raw_q[:, 192 + j : 193 + j] for j in range(4))
        gq = gain_a * hq + bias_a * sums_q
        gf = gain_m * hf + bias_m * sums_f
        extra = vg[rows]
        lanes = lane_iota((256, 128))
        for j, col in enumerate((raw_q * hq, raw_q * sums_q, raw_f * hf, raw_f * sums_f)):
            extra = extra + jnp.where(lanes == 64 + j, jnp.sum(col, axis=1, keepdims=True), 0.0)
        gq = jnp.concatenate([gq[:, :128], gq[:, 128:] + extra], axis=1)
        for j in range(4):
            part_f = gf[64 * j : 64 * j + 64].reshape(8, 8, 256)
            part_q = gq[64 * j : 64 * j + 64].reshape(8, 8, 256)
            gin_ref[:, 4 * i + j] = jnp.concatenate([part_f, part_q], axis=1).astype(BF16)


def core_call(span, inv, length, xh, cot, win, wout, swap):
    half = ROT // 2
    freqs = THETA_BASE ** (-2.0 * np.arange(half, dtype=np.float32) / ROT)
    angles = jnp.arange(ROW, dtype=F32)[None, :] * jnp.asarray(freqs, F32)[:, None]
    smem = pl.BlockSpec(memory_space=pltpu.SMEM)
    vmem = pl.BlockSpec(memory_space=pltpu.VMEM)
    sds = jax.ShapeDtypeStruct

    def buf(shape, dtype=BF16):
        return pltpu.VMEM(shape, dtype)

    return pl.pallas_call(
        core_kernel,
        out_shape=(
            sds((SEQ, TOK, D), BF16),
            sds((SEQ, TOK, D), BF16),
            sds((DP, SEQ, 16, 256), BF16),
            sds((8, 16, 512), BF16),
            sds((32, 16, 512), BF16),
            sds((16, D), F32),
        ),
        in_specs=[smem] * 3 + [vmem] * 7,
        out_specs=[vmem] * 6,
        scratch_shapes=[
            buf((ROW, D)),
            buf((ROW, D)),
            buf((D, 256)),
            buf((D, 256)),
            buf((D, 256)),
            buf((D, 256)),
            buf((64, D)),
            buf((256, D)),
            buf((128, ROW)),
            buf((ROW, 128)),
            buf((64, ROW)),
            buf((ROW, 128)),
            buf((64, ROW)),
            buf((ROW, 128)),
            buf((64, ROW)),
            buf((ROW, 64)),
            buf((64, ROW), F32),
            buf((8, ROW), F32),
            buf((8, ROW), F32),
            buf((ROW, 256)),
            buf((256, ROW)),
            buf((ROW, 256), F32),
            buf((ROW, 256)),
            buf((256, ROW)),
            buf((ROW, 256)),
            buf((256, ROW)),
            buf((ROW, 64)),
            buf((64, ROW)),
            buf((64, ROW), F32),
            buf((ROW, 64), F32),
            buf((ROW, 64), F32),
            buf((D, 128), F32),
        ],
        compiler_params=pltpu.CompilerParams(vmem_limit_bytes=VMEM_LIMIT),
        name="layer_of_one_row",
    )(
        span,
        inv,
        length,
        xh.reshape(32, 64, D),
        cot.reshape(32, 64, D),
        win,
        wout,
        swap,
        jnp.cos(angles),
        jnp.sin(angles),
    )


def scatter_kernel(
    po_ref,
    hg_ref,
    gin_ref,
    goa_ref,
    gof_ref,
    out_sum,
    grad_sum,
    win_sum,
    wout_sum,
    square_ref,
    po_sib,
    hg_sib,
    po_pair,
    hg_pair,
    po_got,
    hg_got,
    gin_got,
    own_out,
    out_got,
    win_part,
    tile_a,
    tile_b,
    got_a,
    got_b,
    local_sem,
    ps_send,
    ps_recv,
    pg_send,
    pg_recv,
    hs_send,
    hs_recv,
    hgs_send,
    hgs_recv,
    g_send,
    g_recv,
    w_send,
    w_recv,
    o_send,
    o_recv,
    a_send,
    a_recv,
    ta_send,
    ta_recv,
    tb_send,
    tb_recv,
):
    me = lax.axis_index("seq")
    dm = lax.axis_index("dp")
    core = lax.rem(me, 2)
    chip = me // 2
    sib = me + 1 - 2 * core
    enter(me, dm)

    def g_copy(k, to, frm):
        return remote(gin_ref.at[to], gin_got.at[frm], g_send.at[k], g_recv.at[frm], dp=to)

    @pl.loop(1, DP)
    def _(k):
        g_copy(k, lax.rem(dm + k, DP), dm).start()

    def swap_few(r):
        return remote(
            gof_ref.at[pl.ds(8 * r, 8)],
            own_out.at[pl.ds(32, 8)],
            w_send.at[r],
            w_recv.at[0],
            seq=4 + 4 * me + r,
        )

    def swap_many():
        return remote(
            goa_ref,
            own_out.at[pl.ds(8 + 8 * lax.rem(me, 4), 8)],
            w_send.at[0],
            w_recv.at[lax.rem(me, 4)],
            seq=(me - 4) // 4,
        )

    keep_a = pltpu.make_async_copy(goa_ref, own_out.at[pl.ds(0, 8)], local_sem.at[0])
    keep_f3 = pltpu.make_async_copy(gof_ref, own_out.at[pl.ds(8, 32)], local_sem.at[1])
    keep_f = pltpu.make_async_copy(gof_ref, own_out.at[pl.ds(0, 32)], local_sem.at[1])

    @pl.when(me < 3)
    def _():
        for r in range(4):
            swap_few(r).start()

    @pl.when(me < 4)
    def _():
        keep_a.start()

    @pl.when(me == 3)
    def _():
        keep_f3.start()

    @pl.when(me > 3)
    def _():
        swap_many().start()
        keep_f.start()

    def sib_copy(src, dst, send, recv, j):
        return remote(src.at[2 * j + 1 - core], dst.at[j], send.at[j], recv.at[j], seq=sib)

    def chip_copy(src, dst, send, recv, j, frm):
        return remote(src.at[j], dst.at[frm], send.at[j], recv.at[frm], seq=2 * j + core)

    for src, dst, send, recv in (
        (po_ref, po_sib, ps_send, ps_recv),
        (hg_ref, hg_sib, hs_send, hs_recv),
    ):

        @pl.loop(0, 8)
        def _(k, src=src, dst=dst, send=send, recv=recv):
            sib_copy(src, dst, send, recv, lax.rem(chip + 1 + k, 8)).start()

    sets = (
        (po_ref, po_sib, po_pair, po_got, ps_send, ps_recv, pg_send, pg_recv, out_sum),
        (hg_ref, hg_sib, hg_pair, hg_got, hs_send, hs_recv, hgs_send, hgs_recv, grad_sum),
    )
    for src, dst, pair, got, send, recv, send2, recv2, total in sets:

        @pl.loop(0, 8)
        def _(k, src=src, dst=dst, pair=pair, got=got, send=send, recv=recv, send2=send2, recv2=recv2):
            j = lax.rem(chip + 1 + k, 8)
            sib_copy(src, dst, send, recv, j).wait_recv()
            pair[j] = (src[2 * j + core].astype(F32) + dst[j].astype(F32)).astype(BF16)

            @pl.when(j != chip)
            def _():
                chip_copy(pair, got, send2, recv2, j, chip).start()

    @pl.loop(1, DP)
    def _(k):
        g_copy(k, dm, lax.rem(dm + k, DP)).wait_recv()

    @pl.loop(0, SEQ)
    def _(s):
        total = gin_ref[dm, s].astype(F32)
        for k in range(1, DP):
            total = total + gin_got[lax.rem(dm + k, DP), s].astype(F32)
        win_part[s] = total

    def a_copy(k, to, frm):
        return remote(win_part.at[to], win_sum.at[frm], a_send.at[k], a_recv.at[frm], seq=to)

    @pl.loop(1, SEQ)
    def _(k):
        a_copy(k, lax.rem(me + k, SEQ), me).start()

    win_sum[me] = win_part[me]

    @pl.when(me < 3)
    def _():
        for r in range(4):
            swap_few(r).wait_send()
            remote(
                goa_ref, own_out.at[pl.ds(8 + 8 * r, 8)], w_send.at[r], w_recv.at[r], seq=me
            ).wait_recv()

    @pl.when(me < 4)
    def _():
        keep_a.wait()

    @pl.when(me == 3)
    def _():
        keep_f3.wait()

    @pl.when(me > 3)
    def _():
        swap_many().wait_send()
        keep_f.wait()
        remote(
            goa_ref, own_out.at[pl.ds(32, 8)], w_send.at[0], w_recv.at[0], seq=me
        ).wait_recv()

    def o_copy(k, to, frm):
        return remote(
            own_out.at[pl.ds(5 * to, 5)], out_got.at[frm], o_send.at[k], o_recv.at[frm], dp=to
        )

    @pl.loop(1, DP)
    def _(k):
        o_copy(k, lax.rem(dm + k, DP), dm).start()

    @pl.loop(1, DP)
    def _(k):
        o_copy(k, dm, lax.rem(dm + k, DP)).wait_recv()

    total = own_out[pl.ds(5 * dm, 5)].astype(F32)
    for k in range(1, DP):
        total = total + out_got[lax.rem(dm + k, DP)].astype(F32)
    wout_sum[...] = total
    squares = jnp.sum(total * total, axis=0)
    squares = jnp.sum(squares, axis=0, keepdims=True)

    @pl.loop(1, SEQ)
    def _(k):
        a_copy(k, me, lax.rem(me + k, SEQ)).wait_recv()

    all_in = win_sum[...]
    weights = jnp.where(
        (lax.broadcasted_iota(jnp.int32, all_in.shape, 1) < 8) | (lane_iota(all_in.shape) < 192),
        all_in,
        0.0,
    )
    in_squares = jnp.sum(jnp.sum(weights * weights, axis=0), axis=0, keepdims=True)
    vec_total = jnp.sum(all_in, axis=0)[8:, 128:]
    vec_total = jnp.where(lane_iota(vec_total.shape) >= 64, vec_total, 0.0)
    vec_squares = jnp.sum(vec_total * vec_total, axis=0, keepdims=True)
    row = (
        in_squares[:, :128]
        + in_squares[:, 128:]
        + vec_squares
        + squares[:, :128]
        + squares[:, 128:256]
        + squares[:, 256:384]
        + squares[:, 384:]
    )
    tile_a[...] = jnp.broadcast_to(row, (8, 128))

    def ta_copy(k, to, frm):
        return remote(tile_a, got_a.at[frm], ta_send.at[k], ta_recv.at[frm], seq=to)

    def tb_copy(k, to, frm):
        return remote(tile_b, got_b.at[frm], tb_send.at[k], tb_recv.at[frm], dp=to)

    @pl.loop(1, SEQ)
    def _(k):
        ta_copy(k, lax.rem(me + k, SEQ), me).start()

    got_a[me] = tile_a[...]

    @pl.loop(1, SEQ)
    def _(k):
        ta_copy(k, me, lax.rem(me + k, SEQ)).wait_recv()

    tile_b[...] = jnp.sum(got_a[...], axis=0)

    @pl.loop(1, DP)
    def _(k):
        tb_copy(k, lax.rem(dm + k, DP), dm).start()

    got_b[dm] = tile_b[...]

    @pl.loop(1, DP)
    def _(k):
        tb_copy(k, dm, lax.rem(dm + k, DP)).wait_recv()

    everything = jnp.sum(got_b[...], axis=0)
    square_ref[...] = jnp.broadcast_to(jnp.sum(everything, axis=1, keepdims=True), (8, 128))

    for src, dst, pair, got, send, recv, send2, recv2, total in sets:

        @pl.loop(1, 8)
        def _(k, pair=pair, got=got, send2=send2, recv2=recv2):
            frm = lax.rem(chip + k, 8)
            chip_copy(pair, got, send2, recv2, chip, frm).wait_recv()

        value = pair[chip].astype(F32)
        for k in range(1, 8):
            value = value + got[lax.rem(chip + k, 8)].astype(F32)
        total[...] = value

        @pl.loop(0, 8)
        def _(k, src=src, dst=dst, pair=pair, got=got, send=send, recv=recv, send2=send2, recv2=recv2):
            j = lax.rem(chip + 1 + k, 8)
            sib_copy(src, dst, send, recv, j).wait_send()

            @pl.when(j != chip)
            def _():
                chip_copy(pair, got, send2, recv2, j, chip).wait_send()

    @pl.loop(1, DP)
    def _(k):
        g_copy(k, lax.rem(dm + k, DP), dm).wait_send()
        o_copy(k, lax.rem(dm + k, DP), dm).wait_send()
        tb_copy(k, lax.rem(dm + k, DP), dm).wait_send()

    @pl.loop(1, SEQ)
    def _(k):
        a_copy(k, lax.rem(me + k, SEQ), me).wait_send()
        ta_copy(k, lax.rem(me + k, SEQ), me).wait_send()


def scatter_call(po, hg, gin, goa, gof):
    vmem = pl.BlockSpec(memory_space=pltpu.VMEM)
    sds = jax.ShapeDtypeStruct
    dma = pltpu.SemaphoreType.DMA
    buf = pltpu.VMEM
    return pl.pallas_call(
        scatter_kernel,
        out_shape=(
            sds((TOK, D), F32),
            sds((TOK, D), F32),
            sds((SEQ, 16, 256), F32),
            sds((5, 16, 512), F32),
            sds((8, 128), F32),
        ),
        in_specs=[vmem] * 5,
        out_specs=[vmem] * 5,
        scratch_shapes=[
            buf((8, TOK, D), BF16),
            buf((8, TOK, D), BF16),
            buf((8, TOK, D), BF16),
            buf((8, TOK, D), BF16),
            buf((8, TOK, D), BF16),
            buf((8, TOK, D), BF16),
            buf((DP, SEQ, 16, 256), BF16),
            buf((40, 16, 512), BF16),
            buf((DP, 5, 16, 512), BF16),
            buf((SEQ, 16, 256), F32),
            buf((8, 128), F32),
            buf((8, 128), F32),
            buf((SEQ, 8, 128), F32),
            buf((DP, 8, 128), F32),
            dma((2,)),
            dma((8,)),
            dma((8,)),
            dma((8,)),
            dma((8,)),
            dma((8,)),
            dma((8,)),
            dma((8,)),
            dma((8,)),
            dma((DP,)),
            dma((DP,)),
            dma((4,)),
            dma((4,)),
            dma((DP,)),
            dma((DP,)),
            dma((SEQ,)),
            dma((SEQ,)),
            dma((SEQ,)),
            dma((SEQ,)),
            dma((DP,)),
            dma((DP,)),
        ],
        compiler_params=pltpu.CompilerParams(
            collective_id=1, has_side_effects=True, vmem_limit_bytes=VMEM_LIMIT
        ),
        name="scatter_sums",
    )(po, hg, gin, goa, gof)


def norm_back(scaled_grad, x_hat, inv_std):
    return inv_std * (
        scaled_grad
        - jnp.mean(scaled_grad, axis=-1, keepdims=True)
        - x_hat * jnp.mean(scaled_grad * x_hat, axis=-1, keepdims=True)
    )


def adam_step(weight, grad, first, second, factor, rate, decay):
    clipped = grad * factor
    first_new = BETA_ONE * first + (1.0 - BETA_ONE) * clipped
    second_new = BETA_TWO * second + (1.0 - BETA_TWO) * clipped * clipped
    first_hat = first_new / (1.0 - BETA_ONE**STEP)
    second_hat = second_new / (1.0 - BETA_TWO**STEP)
    weight_new = weight * (1.0 - rate * decay) - rate * first_hat / (
        jnp.sqrt(second_hat) + ADAM_EPS
    )
    return (weight_new, first_new, second_new)


def pack_in(in_weight, vectors):
    low = in_weight.astype(BF16).reshape(8, 112, 64)
    pieces = jnp.stack(
        [jnp.stack([low[:, int(p)] for p in PIECES[s]], axis=1) for s in range(SEQ)], axis=0
    )
    qkv = pieces[:, :, :3].reshape(SEQ, 8, 192)
    hidden = pieces[:, :, 3:].reshape(SEQ, 8, 256)
    vec = jnp.pad(vectors.astype(BF16).T, ((0, 0), (0, 64 - vectors.shape[0])))
    qkv = jnp.concatenate([qkv, jnp.broadcast_to(vec[None], (SEQ, 8, 64))], axis=2)
    return jnp.concatenate([hidden, qkv], axis=1)


def unpack_in(total):
    hidden = total[:, :8].reshape(SEQ, 8, 4, 64)
    qkv = total[:, 8:, :192].reshape(SEQ, 8, 3, 64)
    pieces = jnp.concatenate([qkv, hidden], axis=2)
    where = {int(PIECES[s, j]): (s, j) for s in range(SEQ) for j in range(7)}
    grad = jnp.stack([pieces[where[p][0], :, where[p][1]] for p in range(112)], axis=1)
    vec = jnp.sum(total[:, 8:, 192:205], axis=0).T
    return grad.reshape(8, 7 * D), vec


def body(
    hidden_in,
    out_cot,
    in_weight,
    out_weight,
    vectors,
    in_first,
    in_second,
    out_first,
    out_second,
    vec_first,
    vec_second,
    lengths,
    span_of,
):
    seq_index = lax.axis_index("seq")
    span = span_of.reshape(32)
    inv = jnp.sum(
        jnp.where(
            span[None, :] == jnp.arange(32, dtype=jnp.int32)[:, None],
            jnp.arange(32, dtype=jnp.int32)[None, :],
            0,
        ),
        axis=1,
    )
    mine = lax.dynamic_slice_in_dim(span_of, seq_index, 1, 0)[0]
    position = (mine[:, None] * SPAN + jnp.arange(SPAN, dtype=jnp.int32)[None, :]).reshape(TOK)
    valid = (position < lengths[0]).astype(F32)
    x_rows = hidden_in[0].astype(F32)
    row_mean = jnp.mean(x_rows, axis=-1, keepdims=True)
    centered = x_rows - row_mean
    inv_std = lax.rsqrt(jnp.mean(centered * centered, axis=-1, keepdims=True) + NORM_EPS)
    x_hat = centered * inv_std
    cot_low = (out_cot[0].astype(F32) * valid[:, None]).astype(BF16)
    win = pack_in(in_weight, vectors)
    wout = (
        out_weight.astype(BF16).reshape(5, 8, 2, 512).transpose(0, 2, 1, 3).reshape(5, 16, 512)
    )
    xh_all, cot_all, win_all, wout_all, swap_all = gather_call(
        x_hat.astype(BF16), cot_low, win, wout
    )
    po, hg, gin, goa, gof, vec_full = core_call(
        span, inv, lengths, xh_all, cot_all, win_all, wout_all, swap_all
    )
    out_sum, grad_sum, win_sum, wout_sum, squares = scatter_call(po, hg, gin, goa, gof)
    block_out = (x_rows + out_sum + (vec_full[7] + vec_full[8])).astype(BF16)
    input_grad = (cot_low.astype(F32) + norm_back(grad_sum, x_hat, inv_std)).astype(BF16)
    grad_in, grad_vec = unpack_in(win_sum)
    grad_out = wout_sum.reshape(5, 2, 8, 512).transpose(0, 2, 1, 3).reshape(40, D)
    grad_norm = jnp.sqrt(squares[0, 0])
    factor = jnp.minimum(1.0, CLIP_NORM / grad_norm)
    new_in, new_in_first, new_in_second = adam_step(
        in_weight, grad_in, in_first, in_second, factor, RATE_MATRIX, DECAY_RATE
    )
    new_out, new_out_first, new_out_second = adam_step(
        out_weight, grad_out, out_first, out_second, factor, RATE_MATRIX, DECAY_RATE
    )
    new_vectors, new_vec_first, new_vec_second = adam_step(
        vectors, grad_vec, vec_first, vec_second, factor, RATE_VECTOR, 0.0
    )
    return (
        block_out[None],
        input_grad[None],
        grad_norm,
        new_in,
        new_out,
        new_vectors,
        new_in_first,
        new_out_first,
        new_vec_first,
        new_in_second,
        new_out_second,
        new_vec_second,
        new_in.astype(BF16),
        new_out.astype(BF16),
        new_vectors.astype(BF16),
    )


def solution(mesh):
    tokens = P("dp", "seq", None)
    matrix = P(("seq", "dp"), None)
    vector = P(None, ("seq", "dp"))
    return jax.shard_map(
        body,
        mesh=mesh,
        in_specs=(
            tokens,
            tokens,
            matrix,
            matrix,
            vector,
            matrix,
            matrix,
            matrix,
            matrix,
            vector,
            vector,
            P("dp"),
            P(),
        ),
        out_specs=(tokens, tokens, P()) + (matrix, matrix, vector) * 4,
        check_vma=False,
    )
```

```python
import functools
import math

import jax
import jax.numpy as jnp
import numpy as np
from jax import lax
from jax.experimental import pallas as pl
from jax.experimental.pallas import tpu as pltpu
from jax.sharding import PartitionSpec as P

D = 1024
FF = 4096
HEADS = 16
HEAD = 64
ROT = 16
STEP = 5
SEQ = 16
DP = 8
TOK = 128
ROW = 2048
SPAN = 64
VEC_ROWS = 13

NORM_EPS = 1e-05
NEG_FILL = -1e30
CLIP_NORM = 1.0
RATE_MATRIX = 0.02
RATE_VECTOR = 0.2
BETA_ONE = 0.5
BETA_TWO = 0.5
DECAY_RATE = 0.1
ADAM_EPS = 1e-08
THETA_BASE = 10000.0

F32 = jnp.float32
BF16 = jnp.bfloat16
MESH = pl.DeviceIdType.MESH
VMEM_LIMIT = 60 * 1024 * 1024


def head_of(s):
    if s < 4:
        return 5 * s
    return 5 * ((s - 4) // 4) + 1 + (s - 4) % 4


def hidden_pieces(s):
    if s < 3:
        return [20 * s + 5 * r + 8 for r in range(4)]
    if s == 3:
        return [0, 1, 2, 3]
    return [5 * s - 16 + r for r in range(4)]


def column_pieces():
    rows = []
    for s in range(SEQ):
        h = head_of(s)
        rows.append([h, 16 + h, 32 + h] + [48 + w for w in hidden_pieces(s)])
    return np.array(rows, np.int32)


PIECES = column_pieces()


def head_index(s):
    late = (s + 12) // 16
    return (1 - late) * (5 * s) + late * (5 * ((s - 4) // 4) + 1 + lax.rem(s, 4))


def hidden_index(s, r):
    late, not_few = (s + 12) // 16, (s + 13) // 16
    return (
        (1 - not_few) * (20 * s + 5 * r + 8) + (not_few - late) * r + late * (5 * s - 16 + r)
    )


def remote(src, dst, send, recv, where):
    return pltpu.make_async_remote_copy(
        src_ref=src, dst_ref=dst, send_sem=send, recv_sem=recv, device_id=where, device_id_type=MESH
    )


def greet(me, dm):
    barrier = pltpu.get_barrier_semaphore()

    @pl.loop(1, SEQ)
    def _(k):
        pl.semaphore_signal(
            barrier, inc=1, device_id={"seq": lax.rem(me + k, SEQ)}, device_id_type=MESH
        )

    @pl.loop(1, DP)
    def _(k):
        pl.semaphore_signal(
            barrier, inc=1, device_id={"dp": lax.rem(dm + k, DP)}, device_id_type=MESH
        )


def await_greetings():
    pl.semaphore_wait(pltpu.get_barrier_semaphore(), SEQ + DP - 2)


class Tree:
    def __init__(self, axis, piece, me, turn, mate, sib, send, recv, over_mate):
        self.axis, self.piece, self.me, self.turn, self.mate, self.sib = (
            axis,
            piece,
            me,
            turn,
            mate,
            sib,
        )
        self.send, self.recv, self.over_mate = send, recv, over_mate
        self.started = []

    def put(self, slot, h, to):
        part = self.piece(slot, h)
        copy = remote(
            part, part, self.send.at[len(self.started)], self.recv.at[slot, h], {self.axis: to}
        )
        copy.start()
        self.started.append(copy)

    def hand(self, slot, h):
        if self.sib is not None:
            self.put(slot, h, self.sib)

    def got(self, slot, h):
        part = self.piece(slot, h)
        remote(
            part, part, self.send.at[0], self.recv.at[slot, h], {self.axis: self.mate}
        ).wait_recv()

    def own(self):
        for h in range(2):
            for to in (self.mate, self.turn(self.me, 1), self.turn(self.me, 3)):
                self.put(self.me, h, to)
        for h in range(2):
            self.hand(self.me, h)

    def of_mate(self):
        for h in range(2):
            self.got(self.mate, h)
            for k in (1, 3):
                self.put(self.mate, h, self.turn(self.me, k))
            self.hand(self.mate, h)

    def near(self, base):
        for h in range(2):
            for k in (3, 1):
                slot = self.turn(base, k)
                self.got(slot, h)
                if (k == 3) == (h == 0):
                    self.put(slot, h, self.turn(self.me, 4 - k))
                self.hand(slot, h)

    def near_of_me(self):
        self.near(self.me)

    def far_of_me(self):
        slot = self.turn(self.me, 2)
        for h in range(2):
            self.got(slot, h)
            if self.over_mate:
                self.put(slot, h, self.mate)
            self.hand(slot, h)

    def near_of_mate(self):
        if not self.over_mate:
            return self.near(self.mate)
        for h in range(2):
            for k in (3, 1):
                slot = self.turn(self.mate, k)
                self.got(slot, h)
                self.hand(slot, h)

    def far_of_mate(self):
        slot = self.turn(self.mate, 2)
        for h in range(2):
            self.got(slot, h)
            self.hand(slot, h)

    def handed(self, other_mate):
        for h in range(2):
            for slot in (self.sib, other_mate):
                for k in range(4):
                    self.got(self.turn(slot, k), h)

    def sent(self):
        for copy in self.started:
            copy.wait_send()


def dot(a, b):
    return jnp.dot(a, b, preferred_element_type=F32)


def dot_nt(a, b):
    return lax.dot_general(a, b, (((1,), (1,)), ((), ())), preferred_element_type=F32)


def lane_iota(shape):
    return lax.broadcasted_iota(jnp.int32, shape, len(shape) - 1)


def fold(u):
    return jnp.concatenate([u[:, : D // 2], u[:, D // 2 :]], axis=0)


def unfold(u):
    return jnp.concatenate([u[:8], u[8:]], axis=1)


CH = 512
NCH = ROW // CH


def layer_kernel(
    span_ref,
    inv_ref,
    len_ref,
    x_ref,
    cot_ref,
    w_in_ref,
    w_out_ref,
    vectors_ref,
    cos_ref,
    sin_ref,
    out_sum,
    grad_sum,
    win_sum,
    wout_sum,
    square_ref,
    vec_ref,
    xh_all,
    cot_all,
    win_own,
    win_all,
    wout_all,
    swap_all,
    small,
    xs,
    cs,
    wqr,
    wfr,
    wqp,
    wfp,
    woa,
    wof,
    qt,
    qn,
    kt,
    kn,
    vt,
    vn,
    dot_t,
    dot_n,
    ot,
    lse,
    delta,
    act,
    act_t,
    dact,
    mixf,
    mixf_t,
    mixq,
    mixq_t,
    att,
    att_t,
    dqt,
    dkn,
    dvn,
    vg,
    cot_cols,
    gin,
    goa_buf,
    gof_buf,
    po_sib,
    hg_sib,
    po_got,
    hg_got,
    gin_got,
    own_out,
    out_got,
    win_part,
    tile_a,
    tile_b,
    got_a,
    got_b,
    local_sem,
    a_send,
    a_recv,
    x_send,
    x_recv,
    c_send,
    c_recv,
    l_send,
    l_recv,
    o_send,
    o_recv,
    w_send,
    w_recv,
    ps_send,
    ps_recv,
    pg_send,
    pg_recv,
    hs_send,
    hs_recv,
    hgs_send,
    hgs_recv,
    g_send,
    g_recv,
    v_send,
    v_recv,
    go_send,
    go_recv,
    b_send,
    b_recv,
    ta_send,
    ta_recv,
    tb_send,
    tb_recv,
):
    me = lax.axis_index("seq")
    dm = lax.axis_index("dp")
    core = lax.rem(me, 2)
    chip = me // 2
    sib = me + 1 - 2 * core
    mate = me + 2 - 4 * lax.rem(chip, 2)
    sib_mate = mate + 1 - 2 * core
    dp_mate = lax.rem(dm + 4, DP)
    head = head_index(me)
    greet(me, dm)

    row = lax.broadcasted_iota(jnp.int32, (TOK, 1), 0)
    place = jnp.where(row < SPAN, span_ref[2 * me] * SPAN + row, span_ref[2 * me + 1] * SPAN + row - SPAN)
    x_rows = x_ref[...].astype(F32)
    centered = x_rows - jnp.mean(x_rows, axis=-1, keepdims=True)
    inv_std = lax.rsqrt(jnp.mean(centered * centered, axis=-1, keepdims=True) + NORM_EPS)
    xh_all[pl.ds(2 * me, 2)] = (centered * inv_std).astype(BF16).reshape(2, SPAN, D)

    small[...] = jnp.zeros((128, 128), F32)
    small[0:VEC_ROWS, 0:8] = vectors_ref[...]
    vec_t = jnp.transpose(small[...])[0:8, 0:64]
    for s in range(SEQ):
        take = [w_in_ref[:, 64 * int(p) : 64 * int(p) + 64] for p in PIECES[s]]
        qkv = jnp.concatenate(take[:3] + [vec_t], axis=1)
        win_own[s] = jnp.concatenate([jnp.concatenate(take[3:], axis=1), qkv], axis=0).astype(BF16)
    for u in range(5):
        wout_all[5 * dm + u] = fold(w_out_ref[8 * u : 8 * u + 8]).astype(BF16)
    cot_own = jnp.where(place < len_ref[0], cot_ref[...].astype(F32), 0.0)
    cot_all[pl.ds(2 * me, 2)] = cot_own.astype(BF16).reshape(2, SPAN, D)
    cot_sum = jnp.sum(cot_own, axis=0, keepdims=True)
    cot_cols[...] = jnp.transpose(jnp.broadcast_to(cot_sum, (128, D)))
    keep = pltpu.make_async_copy(win_own.at[me], win_all.at[dm, me], local_sem.at[0])
    keep.start()

    def seq_turn(s, k):
        return lax.rem(s + 4 * k, SEQ)

    def dp_turn(d, k):
        return d // 4 * 4 + lax.rem(d + k, 4)

    x_tree = Tree(
        "seq",
        lambda slot, h: xh_all.at[2 * slot + h],
        me,
        seq_turn,
        mate,
        sib,
        x_send,
        x_recv,
        True,
    )
    cot_tree = Tree(
        "seq",
        lambda slot, h: cot_all.at[2 * slot + h],
        me,
        seq_turn,
        mate,
        sib,
        c_send,
        c_recv,
        True,
    )
    in_tree = Tree(
        "dp",
        lambda slot, h: win_all.at[slot, pl.ds(8 * h, 8)],
        dm,
        dp_turn,
        dp_mate,
        None,
        l_send,
        l_recv,
        False,
    )
    out_tree = Tree(
        "dp",
        lambda slot, h: wout_all.at[pl.ds(5 * slot + 2 * h, 2 + h)],
        dm,
        dp_turn,
        dp_mate,
        None,
        o_send,
        o_recv,
        False,
    )

    def a_copy(k, to, frm):
        return remote(
            win_own.at[to], win_all.at[dm, frm], a_send.at[k], a_recv.at[frm], {"seq": to}
        )

    await_greetings()

    @pl.loop(1, SEQ)
    def _(k):
        a_copy(k, lax.rem(me + k, SEQ), me).start()

    x_tree.own()
    out_tree.own()
    keep.wait()

    @pl.loop(1, SEQ)
    def _(k):
        a_copy(k, me, lax.rem(me + k, SEQ)).wait_recv()

    in_tree.own()
    out_tree.of_mate()
    x_tree.of_mate()
    out_tree.near_of_me()
    in_tree.of_mate()
    x_tree.near_of_me()
    out_tree.near_of_mate()
    in_tree.near_of_me()
    x_tree.far_of_me()
    cot_tree.own()
    in_tree.near_of_mate()
    x_tree.near_of_mate()
    x_tree.far_of_mate()
    in_tree.far_of_me()
    in_tree.far_of_mate()
    out_tree.far_of_me()
    out_tree.far_of_mate()

    def swap_few(r):
        return remote(
            wout_all.at[pl.ds(8 + 8 * r, 8)],
            swap_all.at[0],
            w_send.at[r],
            w_recv.at[0],
            {"seq": 4 + 4 * me + r},
        )

    def swap_many():
        return remote(
            wout_all.at[pl.ds(32, 8)],
            swap_all.at[lax.rem(me, 4)],
            w_send.at[0],
            w_recv.at[lax.rem(me, 4)],
            {"seq": (me - 4) // 4},
        )

    @pl.when(me < 3)
    def _():
        for r in range(4):
            swap_few(r).start()

    @pl.when(me > 3)
    def _():
        swap_many().start()

    def unpack(sb, carry):
        cq, cf = carry
        tiles = [win_all[d, sb].astype(F32) for d in range(DP)]
        ff = jnp.concatenate([t[:8] for t in tiles], axis=0)
        qk = jnp.concatenate([t[8:] for t in tiles], axis=0)
        rows = pl.ds(pl.multiple_of(sb * 64, 64), 64)
        gain_a, bias_a, gain_m, bias_m = (qk[:, 192 + i : 193 + i] for i in range(4))
        wfr[rows] = ff.astype(BF16)
        wqr[rows] = qk.astype(BF16)
        wfp[rows] = (ff * gain_m).astype(BF16)
        wqp[rows] = jnp.where(lane_iota(qk.shape) < 192, qk * gain_a, 0.0).astype(BF16)
        return (
            cq + jnp.sum(qk * bias_a, axis=0, keepdims=True),
            cf + jnp.sum(ff * bias_m, axis=0, keepdims=True),
        )

    zero_row = jnp.zeros((1, 256), F32)
    cq, cf = lax.fori_loop(0, SEQ, unpack, (zero_row, zero_row))

    slab = jnp.transpose(wqr[:, 128:256].astype(F32))
    vec_ref[...] = slab[64:80]

    hid = []
    for r in range(4):
        w = hidden_index(me, r)
        rows = pl.ds(pl.multiple_of(lax.rem(w, 16) * 64, 64), 64)
        part = wqr[rows, 128:256].astype(F32)
        lane = 64 + 9 + w // 16
        hid.append(
            jnp.sum(jnp.where(lane_iota(part.shape) == lane, part, 0.0), axis=1, keepdims=True)
        )
    hid = jnp.concatenate(hid, axis=0)
    cf = cf + jnp.transpose(jnp.broadcast_to(hid, (256, 128)))[0:1]

    head_rows = pl.ds(pl.multiple_of(head * 64, 64), 64)
    head_vecs = wqr[head_rows, 128:256].astype(F32)
    bq, bk, bv = (head_vecs[:, 68 + i : 69 + i] for i in range(3))

    x_tree.handed(sib_mate)

    @pl.loop(0, 32)
    def _(i):
        rows = pl.ds(pl.multiple_of(i * SPAN, SPAN), SPAN)
        xs[rows] = xh_all[inv_ref[i]]

    cot_tree.of_mate()

    aug = jnp.where(lax.broadcasted_iota(jnp.int32, (64, CH), 0) == 0, 1.0, 0.0)
    zeros_aug = jnp.zeros((64, CH), F32)

    def rotate_t(u, cosine, sine, sign):
        first, second = u[0:8], u[8:16]
        return jnp.concatenate(
            [
                first * cosine - sign * (second * sine),
                second * cosine + sign * (first * sine),
                u[16:],
            ],
            axis=0,
        )

    @pl.loop(0, NCH)
    def _(i):
        start = pl.multiple_of(i * CH, CH)
        rows = pl.ds(start, CH)
        xh = xs[rows]
        qkv = jnp.transpose(dot(xh, wqp[...]) + cq)
        cosine, sine = cos_ref[:, rows], sin_ref[:, rows]
        q = rotate_t(qkv[0:64] + bq, cosine, sine, 1.0) * 0.125
        k = rotate_t(qkv[64:128] + bk, cosine, sine, 1.0)
        v = qkv[128:192] + bv
        q_full = jnp.concatenate([q, aug], axis=0)
        past = (start + lane_iota((64, CH))) >= len_ref[0]
        k_full = jnp.concatenate([k, jnp.where(past, NEG_FILL, 0.0) * aug], axis=0)
        v_full = jnp.concatenate([v, zeros_aug], axis=0)
        qt[:, rows] = q_full.astype(BF16)
        kt[:, rows] = k.astype(BF16)
        vt[:, rows] = v.astype(BF16)
        qn[rows] = jnp.transpose(q_full).astype(BF16)
        kn[rows] = jnp.transpose(k_full).astype(BF16)
        vn[rows] = jnp.transpose(v_full).astype(BF16)
        pre = dot(xh, wfp[...]) + cf
        cdf = 0.5 * (1.0 + lax.erf(pre * (1.0 / math.sqrt(2.0))))
        pdf = jnp.exp(-0.5 * pre * pre) * (1.0 / math.sqrt(2.0 * math.pi))
        activ = pre * cdf
        act[pl.ds(8 * i, 8)] = activ.astype(BF16).reshape(8, SPAN, 256)
        act_t[:, rows] = jnp.transpose(activ).astype(BF16)
        dact[rows] = cdf + pre * pdf

    cot_tree.near_of_me()
    causal = lax.broadcasted_iota(jnp.int32, (CH, CH), 0) <= lane_iota((CH, CH))

    def scores(kc, qi):
        s = dot(kn[kc * CH : (kc + 1) * CH], qt[:, qi * CH : (qi + 1) * CH])
        if kc == qi:
            s = jnp.where(causal, s, NEG_FILL)
        return s

    for qi in range(NCH):
        lanes = slice(qi * CH, (qi + 1) * CH)
        parts = [scores(kc, qi) for kc in range(qi + 1)]
        top = functools.reduce(jnp.maximum, [jnp.max(s, axis=0, keepdims=True) for s in parts])
        total = jnp.zeros((1, CH), F32)
        out = jnp.zeros((64, CH), F32)
        for kc, s in enumerate(parts):
            p = jnp.exp(s - top)
            total = total + jnp.sum(p, axis=0, keepdims=True)
            out = out + dot(vt[:, kc * CH : (kc + 1) * CH], p.astype(BF16))
        out = out / total
        ot[:, lanes] = out
        lse[:, lanes] = jnp.broadcast_to(top + jnp.log(total), (8, CH))
        att_t[:, lanes] = out.astype(BF16)
        att[8 * qi : 8 * qi + 8] = jnp.transpose(out).astype(BF16).reshape(8, SPAN, HEAD)
        if qi == 2:
            cot_tree.far_of_me()
            cot_tree.near_of_mate()
    cot_tree.far_of_mate()

    def put_units(src, base, dst, count):
        @pl.loop(0, count // 2)
        def _(i):
            pair = [unfold(src[base + 2 * i + j].astype(F32)) for j in range(2)]
            dst[pl.ds(pl.multiple_of(i * 16, 16), 16)] = jnp.concatenate(pair, axis=0).astype(BF16)

    def put_swap(dst, rs):
        for r in range(rs):
            for i in range(4):
                pair = [unfold(swap_all[r, 2 * i + j].astype(F32)) for j in range(2)]
                dst[r * 64 + i * 16 : r * 64 + i * 16 + 16] = jnp.concatenate(pair, axis=0).astype(
                    BF16
                )

    @pl.when(me < 4)
    def _():
        put_units(wout_all, 0, woa, 8)

    @pl.when(me < 3)
    def _():
        for r in range(4):
            remote(
                wout_all.at[pl.ds(32, 8)], swap_all.at[r], w_send.at[r], w_recv.at[r], {"seq": sib}
            ).wait_recv()
            swap_few(r).wait_send()
        put_swap(wof, 4)

    @pl.when(me == 3)
    def _():
        put_units(wout_all, 8, wof, 32)

    @pl.when(me > 3)
    def _():
        swap_many().wait_send()
        remote(
            wout_all.at[pl.ds(32, 8)], swap_all.at[0], w_send.at[0], w_recv.at[0], {"seq": sib}
        ).wait_recv()
        put_swap(woa, 1)
        put_units(wout_all, 0, wof, 32)

    def of_chip(ref, j):
        return jnp.concatenate([ref[span_ref[4 * j + i]] for i in range(4)], axis=0)

    def chip_sums(part, buf, sib_buf, got, s_send, s_recv, c_send, c_recv):
        def to_sib(j):
            return remote(
                buf.at[pl.ds(4 * j + 2 - 2 * core, 2)], sib_buf.at[j], s_send.at[j], s_recv.at[j], {"seq": sib}
            )

        def to_chip(j, frm):
            return remote(
                buf.at[pl.ds(4 * j + 2 * core, 2)],
                got.at[frm],
                c_send.at[j],
                c_recv.at[frm],
                {"seq": 2 * j + core},
            )

        def compute():
            @pl.loop(0, 8)
            def _(k):
                j = lax.rem(chip + 1 + k, 8)
                buf[pl.ds(4 * j, 4)] = part(j).astype(BF16).reshape(4, SPAN, D)
                to_sib(j).start()

        def send():
            @pl.loop(0, 8)
            def _(k):
                j = lax.rem(chip + 1 + k, 8)
                to_sib(j).wait_recv()
                mine = pl.ds(4 * j + 2 * core, 2)
                buf[mine] = (buf[mine].astype(F32) + sib_buf[j].astype(F32)).astype(BF16)

                @pl.when(k < 7)
                def _():
                    to_chip(j, chip).start()

        def finish(total):
            @pl.loop(1, 8)
            def _(k):
                to_chip(chip, lax.rem(chip + k, 8)).wait_recv()

            value = buf[pl.ds(2 * me, 2)].astype(F32)
            for k in range(1, 8):
                value = value + got[lax.rem(chip + k, 8)].astype(F32)
            total[...] = value.reshape(TOK, D)

            @pl.loop(0, 8)
            def _(k):
                j = lax.rem(chip + 1 + k, 8)
                to_sib(j).wait_send()

                @pl.when(k < 7)
                def _():
                    to_chip(j, chip).wait_send()

        return compute, send, finish

    def out_part(j):
        return dot(of_chip(att, j), woa[...]) + dot(of_chip(act, j), wof[...])

    def grad_part(j):
        return dot_nt(of_chip(mixq, j), wqp[...]) + dot_nt(of_chip(mixf, j), wfp[...])

    po_compute, po_send, po_finish = chip_sums(
        out_part, xh_all, po_sib, po_got, ps_send, ps_recv, pg_send, pg_recv
    )
    hg_compute, hg_send, hg_finish = chip_sums(
        grad_part, cot_all, hg_sib, hg_got, hs_send, hs_recv, hgs_send, hgs_recv
    )
    x_tree.sent()
    po_compute()
    cot_tree.handed(sib_mate)

    @pl.loop(0, 32)
    def _(i):
        rows = pl.ds(pl.multiple_of(i * SPAN, SPAN), SPAN)
        cs[rows] = cot_all[inv_ref[i]]

    po_send()

    @pl.loop(0, NCH)
    def _(i):
        rows = pl.ds(pl.multiple_of(i * CH, CH), CH)
        cot = cs[rows]
        ag = dot_nt(cot, woa[...]).astype(BF16).astype(F32)
        ag_t = jnp.transpose(ag)
        dot_n[rows] = ag.astype(BF16)
        dot_t[:, rows] = ag_t.astype(BF16)
        delta[:, rows] = jnp.broadcast_to(
            jnp.sum(ag_t * ot[:, rows], axis=0, keepdims=True), (8, CH)
        )
        pg = dot_nt(cot, wof[...]) * dact[rows]
        mixf[pl.ds(8 * i, 8)] = pg.astype(BF16).reshape(8, SPAN, 256)
        mixf_t[:, rows] = jnp.transpose(pg).astype(BF16)

    goa = dot(att_t[...], cs[...])
    for u in range(8):
        goa_buf[u] = fold(goa[8 * u : 8 * u + 8]).astype(BF16)

    @pl.loop(0, 4)
    def _(i):
        gof = dot(act_t[pl.ds(pl.multiple_of(i * 64, 64), 64)], cs[...])
        for u in range(8):
            gof_buf[8 * i + u] = fold(gof[8 * u : 8 * u + 8]).astype(BF16)

    def back_few(r):
        return remote(
            gof_buf.at[pl.ds(8 * r, 8)],
            own_out.at[pl.ds(32, 8)],
            v_send.at[r],
            v_recv.at[0],
            {"seq": 4 + 4 * me + r},
        )

    def back_many():
        return remote(
            goa_buf,
            own_out.at[pl.ds(8 + 8 * lax.rem(me, 4), 8)],
            v_send.at[0],
            v_recv.at[lax.rem(me, 4)],
            {"seq": (me - 4) // 4},
        )

    keep_a = pltpu.make_async_copy(goa_buf, own_out.at[pl.ds(0, 8)], local_sem.at[0])
    keep_f3 = pltpu.make_async_copy(gof_buf, own_out.at[pl.ds(8, 32)], local_sem.at[1])
    keep_f = pltpu.make_async_copy(gof_buf, own_out.at[pl.ds(0, 32)], local_sem.at[1])

    @pl.when(me < 3)
    def _():
        for r in range(4):
            back_few(r).start()

    @pl.when(me < 4)
    def _():
        keep_a.start()

    @pl.when(me == 3)
    def _():
        keep_f3.start()

    @pl.when(me > 3)
    def _():
        back_many().start()
        keep_f.start()

    for qi in range(NCH):
        lanes = slice(qi * CH, (qi + 1) * CH)
        dq = jnp.zeros((64, CH), F32)
        for kc in range(qi + 1):
            keys = slice(kc * CH, (kc + 1) * CH)
            p = jnp.exp(scores(kc, qi) - lse[0:1, lanes])
            dp = dot(vn[keys, 0:64], dot_t[:, lanes])
            ds = (p * (dp - delta[0:1, lanes])).astype(BF16)
            dv = dot(p.astype(BF16), dot_n[lanes])
            dk = dot(ds, qn[lanes, 0:64])
            dq = dq + dot(kt[:, keys], ds)
            if kc == qi:
                dvn[keys] = dv
                dkn[keys] = dk
            else:
                dvn[keys] += dv
                dkn[keys] += dk
        dqt[:, lanes] = dq * 0.125

    @pl.loop(0, NCH)
    def _(i):
        rows = pl.ds(pl.multiple_of(i * CH, CH), CH)
        cosine, sine = cos_ref[:, rows], sin_ref[:, rows]
        dq = rotate_t(dqt[:, rows], cosine, sine, -1.0)
        dk = rotate_t(jnp.transpose(dkn[rows]), cosine, sine, -1.0)
        dv = jnp.transpose(dvn[rows])
        full = jnp.concatenate([dq, dk, dv, zeros_aug], axis=0)
        mixq_t[:, rows] = full.astype(BF16)
        mixq[pl.ds(8 * i, 8)] = jnp.transpose(full).astype(BF16).reshape(8, SPAN, 256)

    @pl.when(me < 3)
    def _():
        for r in range(4):
            back_few(r).wait_send()
            remote(
                goa_buf, own_out.at[pl.ds(8 + 8 * r, 8)], v_send.at[r], v_recv.at[r], {"seq": sib}
            ).wait_recv()

    @pl.when(me < 4)
    def _():
        keep_a.wait()

    @pl.when(me == 3)
    def _():
        keep_f3.wait()

    @pl.when(me > 3)
    def _():
        back_many().wait_send()
        keep_f.wait()
        remote(
            goa_buf, own_out.at[pl.ds(32, 8)], v_send.at[0], v_recv.at[0], {"seq": sib}
        ).wait_recv()

    def go_copy(k, to, frm):
        return remote(
            own_out.at[pl.ds(5 * to, 5)],
            out_got.at[frm],
            go_send.at[k],
            go_recv.at[frm],
            {"dp": to},
        )

    @pl.loop(1, DP)
    def _(k):
        go_copy(k, lax.rem(dm + k, DP), dm).start()

    cot_tree.sent()
    hg_compute()

    sums_q = jnp.sum(mixq[...].reshape(ROW, 256).astype(F32), axis=0, keepdims=True)
    sums_f = jnp.sum(mixf[...].reshape(ROW, 256).astype(F32), axis=0, keepdims=True)
    cols_q = jnp.sum(mixq_t[...].astype(F32), axis=1, keepdims=True)
    cols_f = jnp.sum(mixf_t[...].astype(F32), axis=1, keepdims=True)
    lanes_d = lane_iota((D, 128))
    vg[...] = jnp.where((lanes_d == 71) | (lanes_d == 72), cot_cols[...], 0.0)
    lanes_h = lane_iota((64, 128))
    for i in range(3):
        vg[head_rows] += jnp.where(lanes_h == 68 + i, cols_q[64 * i : 64 * i + 64], 0.0)
    for r in range(4):
        w = hidden_index(me, r)
        rows = pl.ds(pl.multiple_of(lax.rem(w, 16) * 64, 64), 64)
        vg[rows] += jnp.where(lanes_h == 64 + 9 + w // 16, cols_f[64 * r : 64 * r + 64], 0.0)

    @pl.loop(0, 4)
    def _(i):
        rows = pl.ds(pl.multiple_of(i * 256, 256), 256)
        hq = jnp.transpose(dot(mixq_t[...], xs[:, rows]))
        hf = jnp.transpose(dot(mixf_t[...], xs[:, rows]))
        raw_q = wqr[rows].astype(F32)
        raw_f = wfr[rows].astype(F32)
        gain_a, bias_a, gain_m, bias_m = (raw_q[:, 192 + j : 193 + j] for j in range(4))
        gq = gain_a * hq + bias_a * sums_q
        gf = gain_m * hf + bias_m * sums_f
        extra = vg[rows]
        lanes = lane_iota((256, 128))
        for j, col in enumerate((raw_q * hq, raw_q * sums_q, raw_f * hf, raw_f * sums_f)):
            extra = extra + jnp.where(lanes == 64 + j, jnp.sum(col, axis=1, keepdims=True), 0.0)
        gq = jnp.concatenate([gq[:, :128], gq[:, 128:] + extra], axis=1)
        for j in range(4):
            part_f = gf[64 * j : 64 * j + 64].reshape(8, 8, 256)
            part_q = gq[64 * j : 64 * j + 64].reshape(8, 8, 256)
            gin[:, 4 * i + j] = jnp.concatenate([part_f, part_q], axis=1).astype(BF16)

    def g_copy(k, to, frm):
        return remote(gin.at[to], gin_got.at[frm], g_send.at[k], g_recv.at[frm], {"dp": to})

    @pl.loop(1, DP)
    def _(k):
        g_copy(k, lax.rem(dm + k, DP), dm).start()

    hg_send()

    @pl.loop(1, DP)
    def _(k):
        go_copy(k, dm, lax.rem(dm + k, DP)).wait_recv()

    total = own_out[pl.ds(5 * dm, 5)].astype(F32)
    for k in range(1, DP):
        total = total + out_got[lax.rem(dm + k, DP)].astype(F32)
    wout_sum[...] = total
    squares = jnp.sum(total * total, axis=0)
    squares = jnp.sum(squares, axis=0, keepdims=True)

    po_finish(out_sum)

    @pl.loop(1, DP)
    def _(k):
        g_copy(k, dm, lax.rem(dm + k, DP)).wait_recv()

    @pl.loop(0, SEQ)
    def _(s):
        total = gin[dm, s].astype(F32)
        for k in range(1, DP):
            total = total + gin_got[lax.rem(dm + k, DP), s].astype(F32)
        win_part[s] = total

    def b_copy(k, to, frm):
        return remote(win_part.at[to], win_sum.at[frm], b_send.at[k], b_recv.at[frm], {"seq": to})

    @pl.loop(1, SEQ)
    def _(k):
        b_copy(k, lax.rem(me + k, SEQ), me).start()

    win_sum[me] = win_part[me]

    @pl.loop(1, SEQ)
    def _(k):
        b_copy(k, me, lax.rem(me + k, SEQ)).wait_recv()

    all_in = win_sum[...]
    weights = jnp.where(
        (lax.broadcasted_iota(jnp.int32, all_in.shape, 1) < 8) | (lane_iota(all_in.shape) < 192),
        all_in,
        0.0,
    )
    in_squares = jnp.sum(jnp.sum(weights * weights, axis=0), axis=0, keepdims=True)
    vec_total = jnp.sum(all_in, axis=0)[8:, 128:]
    vec_total = jnp.where(lane_iota(vec_total.shape) >= 64, vec_total, 0.0)
    vec_squares = jnp.sum(vec_total * vec_total, axis=0, keepdims=True)
    row = (
        in_squares[:, :128]
        + in_squares[:, 128:]
        + vec_squares
        + squares[:, :128]
        + squares[:, 128:256]
        + squares[:, 256:384]
        + squares[:, 384:]
    )
    tile_a[...] = jnp.broadcast_to(row, (8, 128))

    def ta_copy(k, to, frm):
        return remote(tile_a, got_a.at[frm], ta_send.at[k], ta_recv.at[frm], {"seq": to})

    def tb_copy(k, to, frm):
        return remote(tile_b, got_b.at[frm], tb_send.at[k], tb_recv.at[frm], {"dp": to})

    @pl.loop(1, SEQ)
    def _(k):
        ta_copy(k, lax.rem(me + k, SEQ), me).start()

    got_a[me] = tile_a[...]

    @pl.loop(1, SEQ)
    def _(k):
        ta_copy(k, me, lax.rem(me + k, SEQ)).wait_recv()

    tile_b[...] = jnp.sum(got_a[...], axis=0)

    @pl.loop(1, DP)
    def _(k):
        tb_copy(k, lax.rem(dm + k, DP), dm).start()

    got_b[dm] = tile_b[...]

    @pl.loop(1, DP)
    def _(k):
        tb_copy(k, dm, lax.rem(dm + k, DP)).wait_recv()

    everything = jnp.sum(got_b[...], axis=0)
    square_ref[...] = jnp.broadcast_to(jnp.sum(everything, axis=1, keepdims=True), (8, 128))

    hg_finish(grad_sum)
    in_tree.sent()
    out_tree.sent()

    @pl.loop(1, DP)
    def _(k):
        to = lax.rem(dm + k, DP)
        g_copy(k, to, dm).wait_send()
        go_copy(k, to, dm).wait_send()
        tb_copy(k, to, dm).wait_send()

    @pl.loop(1, SEQ)
    def _(k):
        to = lax.rem(me + k, SEQ)
        a_copy(k, to, me).wait_send()
        b_copy(k, to, me).wait_send()
        ta_copy(k, to, me).wait_send()


def layer_call(span, inv, length, x, cot, w_in, w_out, vectors):
    freqs = np.float32(THETA_BASE) ** (-2.0 * np.arange(ROT // 2) / ROT)
    angles = np.arange(ROW, dtype=np.float32)[None, :] * freqs.astype(np.float32)[:, None]
    cosine, sine = np.cos(angles).astype(np.float32), np.sin(angles).astype(np.float32)
    smem = pl.BlockSpec(memory_space=pltpu.SMEM)
    vmem = pl.BlockSpec(memory_space=pltpu.VMEM)
    sds = jax.ShapeDtypeStruct
    dma = pltpu.SemaphoreType.DMA

    def buf(shape, dtype=BF16):
        return pltpu.VMEM(shape, dtype)

    return pl.pallas_call(
        layer_kernel,
        out_shape=(
            sds((TOK, D), F32),
            sds((TOK, D), F32),
            sds((SEQ, 16, 256), F32),
            sds((5, 16, 512), F32),
            sds((8, 128), F32),
            sds((16, D), F32),
        ),
        in_specs=[smem] * 3 + [vmem] * 7,
        out_specs=[vmem] * 6,
        scratch_shapes=[
            buf((32, SPAN, D)),
            buf((32, SPAN, D)),
            buf((SEQ, 16, 256)),
            buf((DP, SEQ, 16, 256)),
            buf((40, 16, 512)),
            buf((4, 8, 16, 512)),
            buf((128, 128), F32),
            buf((ROW, D)),
            buf((ROW, D)),
            buf((D, 256)),
            buf((D, 256)),
            buf((D, 256)),
            buf((D, 256)),
            buf((64, D)),
            buf((256, D)),
            buf((128, ROW)),
            buf((ROW, 128)),
            buf((64, ROW)),
            buf((ROW, 128)),
            buf((64, ROW)),
            buf((ROW, 128)),
            buf((64, ROW)),
            buf((ROW, 64)),
            buf((64, ROW), F32),
            buf((8, ROW), F32),
            buf((8, ROW), F32),
            buf((32, SPAN, 256)),
            buf((256, ROW)),
            buf((ROW, 256), F32),
            buf((32, SPAN, 256)),
            buf((256, ROW)),
            buf((32, SPAN, 256)),
            buf((256, ROW)),
            buf((32, SPAN, HEAD)),
            buf((64, ROW)),
            buf((64, ROW), F32),
            buf((ROW, 64), F32),
            buf((ROW, 64), F32),
            buf((D, 128), F32),
            buf((D, 128), F32),
            buf((DP, SEQ, 16, 256)),
            buf((8, 16, 512)),
            buf((32, 16, 512)),
            buf((8, 2, SPAN, D)),
            buf((8, 2, SPAN, D)),
            buf((8, 2, SPAN, D)),
            buf((8, 2, SPAN, D)),
            buf((DP, SEQ, 16, 256)),
            buf((40, 16, 512)),
            buf((DP, 5, 16, 512)),
            buf((SEQ, 16, 256), F32),
            buf((8, 128), F32),
            buf((8, 128), F32),
            buf((SEQ, 8, 128), F32),
            buf((DP, 8, 128), F32),
            dma((2,)),
            dma((SEQ,)),
            dma((SEQ,)),
            dma((32,)),
            dma((SEQ, 2)),
            dma((32,)),
            dma((SEQ, 2)),
            dma((16,)),
            dma((DP, 2)),
            dma((16,)),
            dma((DP, 2)),
            dma((4,)),
            dma((4,)),
            dma((8,)),
            dma((8,)),
            dma((8,)),
            dma((8,)),
            dma((8,)),
            dma((8,)),
            dma((8,)),
            dma((8,)),
            dma((DP,)),
            dma((DP,)),
            dma((4,)),
            dma((4,)),
            dma((DP,)),
            dma((DP,)),
            dma((SEQ,)),
            dma((SEQ,)),
            dma((SEQ,)),
            dma((SEQ,)),
            dma((DP,)),
            dma((DP,)),
        ],
        compiler_params=pltpu.CompilerParams(
            collective_id=0, has_side_effects=True, vmem_limit_bytes=VMEM_LIMIT
        ),
        name="layer_of_one_row",
    )(span, inv, length, x, cot, w_in, w_out, vectors, jnp.asarray(cosine), jnp.asarray(sine))


def adam(weight, grad, first, second, factor, rate, decay):
    clipped = grad * factor
    first_new = BETA_ONE * first + (1.0 - BETA_ONE) * clipped
    second_new = BETA_TWO * second + (1.0 - BETA_TWO) * clipped * clipped
    first_hat = first_new / (1.0 - BETA_ONE**STEP)
    second_hat = second_new / (1.0 - BETA_TWO**STEP)
    weight_new = weight * (1.0 - rate * decay) - rate * first_hat / (
        jnp.sqrt(second_hat) + ADAM_EPS
    )
    return (weight_new, first_new, second_new)


def update_kernel(
    span_ref,
    len_ref,
    x_ref,
    cot_ref,
    out_sum,
    grad_sum,
    vec_ref,
    win_sum,
    wout_sum,
    square_ref,
    w_in,
    w_out,
    vectors,
    in_first,
    out_first,
    vec_first,
    in_second,
    out_second,
    vec_second,
    block_out,
    input_grad,
    norm_ref,
    new_in,
    new_out,
    new_vec,
    new_in_first,
    new_out_first,
    new_vec_first,
    new_in_second,
    new_out_second,
    new_vec_second,
    low_in,
    low_out,
    low_vec,
    grad_in,
    small,
):
    me = lax.axis_index("seq")
    x_rows = x_ref[...].astype(F32)
    block_out[...] = (x_rows + out_sum[...] + (vec_ref[7:8] + vec_ref[8:9])).astype(BF16)
    centered = x_rows - jnp.mean(x_rows, axis=-1, keepdims=True)
    inv_std = lax.rsqrt(jnp.mean(centered * centered, axis=-1, keepdims=True) + NORM_EPS)
    x_hat = centered * inv_std
    row = lax.broadcasted_iota(jnp.int32, (TOK, 1), 0)
    place = jnp.where(row < SPAN, span_ref[2 * me] * SPAN + row, span_ref[2 * me + 1] * SPAN + row - SPAN)
    cot = jnp.where(place < len_ref[0], cot_ref[...].astype(F32), 0.0)
    grad = grad_sum[...]
    back = (
        grad
        - jnp.mean(grad, axis=-1, keepdims=True)
        - x_hat * jnp.mean(grad * x_hat, axis=-1, keepdims=True)
    )
    input_grad[...] = (cot + inv_std * back).astype(BF16)

    norm = jnp.sqrt(square_ref[...])
    norm_ref[...] = norm
    factor = jnp.minimum(1.0, CLIP_NORM / norm)[0:1, 0:1]

    for s in range(SEQ):
        for j, p in enumerate(PIECES[s]):
            p = int(p)
            if j < 3:
                piece = win_sum[s, 8:16, 64 * j : 64 * j + 64]
            else:
                piece = win_sum[s, 0:8, 64 * (j - 3) : 64 * (j - 3) + 64]
            grad_in[:, 64 * p : 64 * p + 64] = piece
    new, first, second = adam(
        w_in[...], grad_in[...], in_first[...], in_second[...], factor, RATE_MATRIX, DECAY_RATE
    )
    new_in[...] = new
    new_in_first[...] = first
    new_in_second[...] = second
    low_in[...] = new.astype(BF16)

    grad_out = jnp.concatenate([unfold(wout_sum[u]) for u in range(5)], axis=0)
    new, first, second = adam(
        w_out[...], grad_out, out_first[...], out_second[...], factor, RATE_MATRIX, DECAY_RATE
    )
    new_out[...] = new
    new_out_first[...] = first
    new_out_second[...] = second
    low_out[...] = new.astype(BF16)

    small[...] = jnp.zeros((128, 128), F32)
    small[0:8, :] = jnp.sum(win_sum[:, 8:16, 128:256], axis=0)
    grad_vec = jnp.transpose(small[...])[64 : 64 + VEC_ROWS, 0:8]
    new, first, second = adam(
        vectors[...], grad_vec, vec_first[...], vec_second[...], factor, RATE_VECTOR, 0.0
    )
    new_vec[...] = new
    new_vec_first[...] = first
    new_vec_second[...] = second
    low_vec[...] = new.astype(BF16)


def update_call(*args):
    smem = pl.BlockSpec(memory_space=pltpu.SMEM)
    vmem = pl.BlockSpec(memory_space=pltpu.VMEM)
    sds = jax.ShapeDtypeStruct
    matrices = ((8, 7 * D), (40, D), (VEC_ROWS, 8))
    return pl.pallas_call(
        update_kernel,
        out_shape=(sds((TOK, D), BF16), sds((TOK, D), BF16), sds((8, 128), F32))
        + tuple(sds(m, F32) for m in matrices * 3)
        + tuple(sds(m, BF16) for m in matrices),
        in_specs=[smem] * 2 + [vmem] * (len(args) - 2),
        out_specs=[vmem] * 15,
        scratch_shapes=[pltpu.VMEM((8, 7 * D), F32), pltpu.VMEM((128, 128), F32)],
        compiler_params=pltpu.CompilerParams(vmem_limit_bytes=32 * 1024 * 1024),
        name="clipped_update",
    )(*args)


def body(
    hidden_in,
    out_cot,
    in_weight,
    out_weight,
    vectors,
    in_first,
    in_second,
    out_first,
    out_second,
    vec_first,
    vec_second,
    lengths,
    span_of,
):
    span = span_of.reshape(32)
    blocks = jnp.arange(32, dtype=jnp.int32)
    inv = jnp.sum(jnp.where(span[None, :] == blocks[:, None], blocks[None, :], 0), axis=1)
    out_sum, grad_sum, win_sum, wout_sum, squares, vec_full = layer_call(
        span, inv, lengths, hidden_in[0], out_cot[0], in_weight, out_weight, vectors
    )
    outs = update_call(
        span,
        lengths,
        hidden_in[0],
        out_cot[0],
        out_sum,
        grad_sum,
        vec_full,
        win_sum,
        wout_sum,
        squares,
        in_weight,
        out_weight,
        vectors,
        in_first,
        out_first,
        vec_first,
        in_second,
        out_second,
        vec_second,
    )
    return (outs[0][None], outs[1][None], outs[2][0, 0]) + tuple(outs[3:])


def solution(mesh):
    tokens = P("dp", "seq", None)
    matrix = P(("seq", "dp"), None)
    vector = P(None, ("seq", "dp"))
    return jax.shard_map(
        body,
        mesh=mesh,
        in_specs=(
            tokens,
            tokens,
            matrix,
            matrix,
            vector,
            matrix,
            matrix,
            matrix,
            matrix,
            vector,
            vector,
            P("dp"),
            P(),
        ),
        out_specs=(tokens, tokens, P()) + (matrix, matrix, vector) * 4,
        check_vma=False,
    )
```

```python
import functools
import math

import jax
import jax.numpy as jnp
import numpy as np
from jax import lax
from jax.experimental import pallas as pl
from jax.experimental.pallas import tpu as pltpu
from jax.sharding import PartitionSpec as P

D = 1024
FF = 4096
HEADS = 16
HEAD = 64
ROT = 16
STEP = 5
SEQ = 16
DP = 8
TOK = 128
ROW = 2048
SPAN = 64
VEC_ROWS = 13

NORM_EPS = 1e-05
NEG_FILL = -1e30
CLIP_NORM = 1.0
RATE_MATRIX = 0.02
RATE_VECTOR = 0.2
BETA_ONE = 0.5
BETA_TWO = 0.5
DECAY_RATE = 0.1
ADAM_EPS = 1e-08
THETA_BASE = 10000.0

F32 = jnp.float32
BF16 = jnp.bfloat16
MESH = pl.DeviceIdType.MESH
VMEM_LIMIT = 60 * 1024 * 1024
UPDATE_LIMIT = 60 * 1024 * 1024


def head_of(s):
    if s < 4:
        return 5 * s
    return 5 * ((s - 4) // 4) + 1 + (s - 4) % 4


def hidden_pieces(s):
    if s < 3:
        return [20 * s + 5 * r + 8 for r in range(4)]
    if s == 3:
        return [0, 1, 2, 3]
    return [5 * s - 16 + r for r in range(4)]


def column_pieces():
    rows = []
    for s in range(SEQ):
        h = head_of(s)
        rows.append([h, 16 + h, 32 + h] + [48 + w for w in hidden_pieces(s)])
    return np.array(rows, np.int32)


PIECES = column_pieces()


def head_index(s):
    late = (s + 12) // 16
    return (1 - late) * (5 * s) + late * (5 * ((s - 4) // 4) + 1 + lax.rem(s, 4))


def hidden_index(s, r):
    late, not_few = (s + 12) // 16, (s + 13) // 16
    return (
        (1 - not_few) * (20 * s + 5 * r + 8) + (not_few - late) * r + late * (5 * s - 16 + r)
    )


def remote(src, dst, send, recv, where):
    return pltpu.make_async_remote_copy(
        src_ref=src, dst_ref=dst, send_sem=send, recv_sem=recv, device_id=where, device_id_type=MESH
    )


def greet(me, dm):
    barrier = pltpu.get_barrier_semaphore()

    @pl.loop(1, SEQ)
    def _(k):
        pl.semaphore_signal(
            barrier, inc=1, device_id={"seq": lax.rem(me + k, SEQ)}, device_id_type=MESH
        )

    @pl.loop(1, DP)
    def _(k):
        pl.semaphore_signal(
            barrier, inc=1, device_id={"dp": lax.rem(dm + k, DP)}, device_id_type=MESH
        )


def await_greetings():
    pl.semaphore_wait(pltpu.get_barrier_semaphore(), SEQ + DP - 2)


class Tree:
    def __init__(self, axis, piece, me, turn, mate, sib, send, recv, over_mate):
        self.axis, self.piece, self.me, self.turn, self.mate, self.sib = (
            axis,
            piece,
            me,
            turn,
            mate,
            sib,
        )
        self.send, self.recv, self.over_mate = send, recv, over_mate
        self.started = []

    def put(self, slot, h, to):
        part = self.piece(slot, h)
        copy = remote(
            part, part, self.send.at[len(self.started)], self.recv.at[slot, h], {self.axis: to}
        )
        copy.start()
        self.started.append(copy)

    def hand(self, slot, h):
        if self.sib is not None:
            self.put(slot, h, self.sib)

    def got(self, slot, h):
        part = self.piece(slot, h)
        remote(
            part, part, self.send.at[0], self.recv.at[slot, h], {self.axis: self.mate}
        ).wait_recv()

    def own_to_ring(self):
        for h in range(2):
            for k in (1, 3):
                self.put(self.me, h, self.turn(self.me, k))

    def own_to_mate(self):
        for h in range(2):
            self.put(self.me, h, self.mate)
        for h in range(2):
            self.hand(self.me, h)

    def of_mate(self):
        for h in range(2):
            self.got(self.mate, h)
            for k in (1, 3):
                self.put(self.mate, h, self.turn(self.me, k))
            self.hand(self.mate, h)

    def near(self, base):
        for h in range(2):
            for k in (3, 1):
                slot = self.turn(base, k)
                self.got(slot, h)
                if (k == 3) == (h == 0):
                    self.put(slot, h, self.turn(self.me, 4 - k))
                self.hand(slot, h)

    def near_of_me(self):
        self.near(self.me)

    def far_of_me(self):
        slot = self.turn(self.me, 2)
        for h in range(2):
            self.got(slot, h)
            if self.over_mate:
                self.put(slot, h, self.mate)
            self.hand(slot, h)

    def near_of_mate(self):
        if not self.over_mate:
            return self.near(self.mate)
        for h in range(2):
            for k in (3, 1):
                slot = self.turn(self.mate, k)
                self.got(slot, h)
                self.hand(slot, h)

    def far_of_mate(self):
        slot = self.turn(self.mate, 2)
        for h in range(2):
            self.got(slot, h)
            self.hand(slot, h)

    def handed(self, other_mate):
        for h in range(2):
            for slot in (self.sib, other_mate):
                for k in range(4):
                    self.got(self.turn(slot, k), h)

    def sent(self):
        for copy in self.started:
            copy.wait_send()


class SumTree:
    def __init__(self, axis, piece, land, me, turn, mate, send, recv):
        self.axis, self.piece, self.land, self.me, self.turn, self.mate = (
            axis,
            piece,
            land,
            me,
            turn,
            mate,
        )
        self.send, self.recv = send, recv
        self.started = []

    def put(self, slot, kind, h, to):
        copy = remote(
            self.piece(slot, h),
            self.land(kind, h),
            self.send.at[len(self.started)],
            self.recv.at[kind, h],
            {self.axis: to},
        )
        copy.start()
        self.started.append(copy)

    def got(self, kind, h):
        part = self.land(kind, h)
        remote(
            part, part, self.send.at[0], self.recv.at[kind, h], {self.axis: self.mate}
        ).wait_recv()
        return part[...].astype(F32)

    def add(self, slot, h, *kinds):
        part = self.piece(slot, h)
        total = part[...].astype(F32)
        for kind in kinds:
            total = total + self.got(kind, h)
        part[...] = total.astype(BF16)

    def far_of_mate(self):
        for h in range(2):
            self.put(self.turn(self.mate, 2), 0, h, self.mate)

    def near_of_mate(self, k):
        for h in range(2):
            self.put(self.turn(self.mate, k), 2 if k == 1 else 1, h, self.turn(self.me, k))

    def near_early(self, k):
        h = 0 if k == 1 else 1
        self.put(self.turn(self.me, k), 5 if k == 1 else 4, h, self.turn(self.me, k))

    def far_of_me(self):
        slot = self.turn(self.me, 2)
        for h in range(2):
            self.add(slot, h, 0)
            self.put(slot, 3, h, self.turn(self.me, 3 - 2 * h))

    def near_late(self):
        for h in range(2):
            k = 3 - 2 * h
            slot = self.turn(self.me, k)
            self.add(slot, h, 3)
            self.put(slot, 4 + h, h, self.turn(self.me, k))

    def of_mate(self):
        for h in range(2):
            self.add(self.mate, h, 1, 2)
            self.put(self.mate, 6, h, self.mate)

    def begin(self):
        self.far_of_mate()
        for k in (1, 3):
            self.near_of_mate(k)
        for k in (1, 3):
            self.near_early(k)

    def total(self, h):
        value = self.piece(self.me, h)[...].astype(F32)
        for kind in (4, 5, 6):
            value = value + self.got(kind, h)
        return value

    def sent(self):
        for copy in self.started:
            copy.wait_send()


def dot(a, b):
    return jnp.dot(a, b, preferred_element_type=F32)


def dot_nt(a, b):
    return lax.dot_general(a, b, (((1,), (1,)), ((), ())), preferred_element_type=F32)


def lane_iota(shape):
    return lax.broadcasted_iota(jnp.int32, shape, len(shape) - 1)


def fold(u):
    return jnp.concatenate([u[:, : D // 2], u[:, D // 2 :]], axis=0)


def unfold(u):
    return jnp.concatenate([u[:8], u[8:]], axis=1)


CH = 512
NCH = ROW // CH


def layer_kernel(
    span_ref,
    len_ref,
    x_ref,
    cot_ref,
    w_in_ref,
    w_out_ref,
    vectors_ref,
    cos_ref,
    sin_ref,
    out_sum,
    grad_sum,
    f_sum,
    q_sum,
    wout_sum,
    square_ref,
    vec_ref,
    vec_grad,
    inv_ref,
    xh_all,
    cot_all,
    win_own,
    win_all,
    wout_all,
    swap_all,
    small,
    xs,
    cs,
    wr,
    wp,
    wo,
    qt,
    qn,
    kt,
    kn,
    vt,
    vn,
    dot_t,
    dot_n,
    ot,
    lse,
    delta,
    joined,
    joined_t,
    dact,
    mixed,
    mixed_t,
    dqt,
    dkn,
    dvn,
    vg,
    goa_buf,
    gof_buf,
    own_out,
    gf,
    gq,
    po_sib,
    hg_sib,
    po_land,
    hg_land,
    gf_land,
    gq_got,
    vt_part,
    vt_seq,
    vt_own,
    vt_dp,
    go_land,
    f_part,
    q_part,
    tile_b,
    got_b,
    local_sem,
    a_send,
    a_recv,
    x_send,
    x_recv,
    c_send,
    c_recv,
    l_send,
    l_recv,
    o_send,
    o_recv,
    w_send,
    w_recv,
    ps_send,
    ps_recv,
    p_send,
    p_recv,
    hs_send,
    hs_recv,
    h_send,
    h_recv,
    gf_send,
    gf_recv,
    gq_send,
    gq_recv,
    go_send,
    go_recv,
    v_send,
    v_recv,
    bf_send,
    bf_recv,
    bq_send,
    bq_recv,
    vs_send,
    vs_recv,
    vd_send,
    vd_recv,
    tb_send,
    tb_recv,
):
    me = lax.axis_index("seq")
    dm = lax.axis_index("dp")
    core = lax.rem(me, 2)
    chip = me // 2
    sib = me + 1 - 2 * core
    mate = me + 2 - 4 * lax.rem(chip, 2)
    sib_mate = mate + 1 - 2 * core
    dp_mate = lax.rem(dm + 4, DP)
    head = head_index(me)
    greet(me, dm)

    row = lax.broadcasted_iota(jnp.int32, (TOK, 1), 0)
    place = jnp.where(row < SPAN, span_ref[0, me] * SPAN + row, span_ref[1, me] * SPAN + row - SPAN)
    x_rows = x_ref[...].astype(F32)
    centered = x_rows - jnp.mean(x_rows, axis=-1, keepdims=True)
    inv_std = lax.rsqrt(jnp.mean(centered * centered, axis=-1, keepdims=True) + NORM_EPS)
    xh_all[pl.ds(2 * me, 2)] = (centered * inv_std).astype(BF16).reshape(2, SPAN, D)

    small[...] = jnp.zeros((128, 128), F32)
    small[0:8, 0:VEC_ROWS] = vectors_ref[...]
    vec_t = small[0:8, 0:64]
    for s in range(SEQ):
        take = [w_in_ref[:, 64 * int(p) : 64 * int(p) + 64] for p in PIECES[s]]
        qkv = jnp.concatenate(take[:3] + [vec_t], axis=1)
        win_own[s] = jnp.concatenate([jnp.concatenate(take[3:], axis=1), qkv], axis=0).astype(BF16)
    for u in range(5):
        wout_all[5 * dm + u] = fold(w_out_ref[8 * u : 8 * u + 8]).astype(BF16)
    cot_own = jnp.where(place < len_ref[0], cot_ref[...].astype(F32), 0.0)
    cot_all[pl.ds(2 * me, 2)] = cot_own.astype(BF16).reshape(2, SPAN, D)
    cot_sum = jnp.sum(cot_own, axis=0, keepdims=True)
    vg[...] = jnp.transpose(jnp.broadcast_to(cot_sum, (128, D)))
    keep = pltpu.make_async_copy(win_own.at[me], win_all.at[dm, me], local_sem.at[0])
    keep.start()

    @pl.loop(0, 32)
    def _(i):
        slot = jnp.int32(0)
        for s in range(SEQ):
            for j in range(2):
                slot = jnp.maximum(slot, jnp.where(span_ref[j, s] == i, 2 * s + j, 0))
        inv_ref[i] = slot

    def seq_turn(s, k):
        return lax.rem(s + 4 * k, SEQ)

    def dp_turn(d, k):
        return d // 4 * 4 + lax.rem(d + k, 4)

    x_tree = Tree(
        "seq",
        lambda slot, h: xh_all.at[2 * slot + h],
        me,
        seq_turn,
        mate,
        sib,
        x_send,
        x_recv,
        True,
    )
    cot_tree = Tree(
        "seq",
        lambda slot, h: cot_all.at[2 * slot + h],
        me,
        seq_turn,
        mate,
        sib,
        c_send,
        c_recv,
        True,
    )
    in_tree = Tree(
        "dp",
        lambda slot, h: win_all.at[slot, pl.ds(8 * h, 8)],
        dm,
        dp_turn,
        dp_mate,
        None,
        l_send,
        l_recv,
        False,
    )
    out_tree = Tree(
        "dp",
        lambda slot, h: wout_all.at[pl.ds(5 * slot + 2 * h, 2 + h)],
        dm,
        dp_turn,
        dp_mate,
        None,
        o_send,
        o_recv,
        False,
    )

    def a_copy(k, to, frm):
        return remote(
            win_own.at[to], win_all.at[dm, frm], a_send.at[k], a_recv.at[frm], {"seq": to}
        )

    await_greetings()

    @pl.loop(1, SEQ)
    def _(k):
        a_copy(k, lax.rem(me + k, SEQ), me).start()

    x_tree.own_to_mate()
    x_tree.own_to_ring()
    out_tree.own_to_mate()
    out_tree.own_to_ring()
    keep.wait()

    @pl.loop(1, SEQ)
    def _(k):
        a_copy(k, me, lax.rem(me + k, SEQ)).wait_recv()

    in_tree.own_to_mate()
    in_tree.own_to_ring()
    x_tree.near_of_me()
    x_tree.of_mate()
    out_tree.of_mate()
    out_tree.near_of_me()
    x_tree.far_of_me()
    cot_tree.own_to_ring()
    cot_tree.own_to_mate()
    in_tree.of_mate()
    in_tree.near_of_me()
    out_tree.near_of_mate()
    in_tree.near_of_mate()
    x_tree.near_of_mate()
    in_tree.far_of_me()
    in_tree.far_of_mate()
    out_tree.far_of_me()
    out_tree.far_of_mate()

    def swap_few(r):
        return remote(
            wout_all.at[pl.ds(8 + 8 * r, 8)],
            swap_all.at[0],
            w_send.at[r],
            w_recv.at[0],
            {"seq": 4 + 4 * me + r},
        )

    def swap_many():
        return remote(
            wout_all.at[pl.ds(32, 8)],
            swap_all.at[lax.rem(me, 4)],
            w_send.at[0],
            w_recv.at[lax.rem(me, 4)],
            {"seq": (me - 4) // 4},
        )

    @pl.when(me < 3)
    def _():
        for r in range(4):
            swap_few(r).start()

    @pl.when(me > 3)
    def _():
        swap_many().start()

    def unpack(sb, carry):
        cq, cf = carry
        tiles = [win_all[d, sb].astype(F32) for d in range(DP)]
        ff = jnp.concatenate([t[:8] for t in tiles], axis=0)
        qk = jnp.concatenate([t[8:] for t in tiles], axis=0)
        rows = pl.ds(pl.multiple_of(sb * 64, 64), 64)
        gain_a, bias_a, gain_m, bias_m = (qk[:, 192 + i : 193 + i] for i in range(4))
        wr[rows] = jnp.concatenate([ff, qk], axis=1).astype(BF16)
        folded = jnp.where(lane_iota(qk.shape) < 192, qk * gain_a, 0.0)
        wp[rows] = jnp.concatenate([ff * gain_m, folded], axis=1).astype(BF16)
        return (
            cq + jnp.sum(qk * bias_a, axis=0, keepdims=True),
            cf + jnp.sum(ff * bias_m, axis=0, keepdims=True),
        )

    zero_row = jnp.zeros((1, 256), F32)
    cq, cf = lax.fori_loop(0, SEQ, unpack, (zero_row, zero_row))

    slab = jnp.transpose(wr[:, 384:512].astype(F32))
    vec_ref[...] = slab[64:80]

    hid = []
    for r in range(4):
        w = hidden_index(me, r)
        rows = pl.ds(pl.multiple_of(lax.rem(w, 16) * 64, 64), 64)
        part = wr[rows, 384:512].astype(F32)
        lane = 64 + 9 + w // 16
        hid.append(
            jnp.sum(jnp.where(lane_iota(part.shape) == lane, part, 0.0), axis=1, keepdims=True)
        )
    hid = jnp.concatenate(hid, axis=0)
    cf = cf + jnp.transpose(jnp.broadcast_to(hid, (256, 128)))[0:1]

    head_rows = pl.ds(pl.multiple_of(head * 64, 64), 64)
    head_vecs = wr[head_rows, 384:512].astype(F32)
    bq, bk, bv = (head_vecs[:, 68 + i : 69 + i] for i in range(3))

    x_tree.far_of_mate()
    x_tree.handed(sib_mate)

    @pl.loop(0, 32)
    def _(i):
        rows = pl.ds(pl.multiple_of(i * SPAN, SPAN), SPAN)
        xs[rows] = xh_all[inv_ref[i]]

    cot_tree.of_mate()

    aug = jnp.where(lax.broadcasted_iota(jnp.int32, (64, CH), 0) == 0, 1.0, 0.0)
    zeros_aug = jnp.zeros((64, CH), F32)

    def rotate_t(u, cosine, sine, sign):
        first, second = u[0:8], u[8:16]
        return jnp.concatenate(
            [
                first * cosine - sign * (second * sine),
                second * cosine + sign * (first * sine),
                u[16:],
            ],
            axis=0,
        )

    @pl.loop(0, NCH)
    def _(i):
        start = pl.multiple_of(i * CH, CH)
        rows = pl.ds(start, CH)
        xh = xs[rows]
        first = dot(xh, wp[...])
        qkv = jnp.transpose(first[:, 256:] + cq)
        cosine, sine = cos_ref[:, rows], sin_ref[:, rows]
        q = rotate_t(qkv[0:64] + bq, cosine, sine, 1.0) * 0.125
        k = rotate_t(qkv[64:128] + bk, cosine, sine, 1.0)
        v = qkv[128:192] + bv
        q_full = jnp.concatenate([q, aug], axis=0)
        past = (start + lane_iota((64, CH))) >= len_ref[0]
        k_full = jnp.concatenate([k, jnp.where(past, NEG_FILL, 0.0) * aug], axis=0)
        v_full = jnp.concatenate([v, zeros_aug], axis=0)
        qt[:, rows] = q_full.astype(BF16)
        kt[:, rows] = k.astype(BF16)
        vt[:, rows] = v.astype(BF16)
        qn[rows] = jnp.transpose(q_full).astype(BF16)
        kn[rows] = jnp.transpose(k_full).astype(BF16)
        vn[rows] = jnp.transpose(v_full).astype(BF16)
        pre = first[:, :256] + cf
        cdf = 0.5 * (1.0 + lax.erf(pre * (1.0 / math.sqrt(2.0))))
        pdf = jnp.exp(-0.5 * pre * pre) * (1.0 / math.sqrt(2.0 * math.pi))
        activ = pre * cdf
        joined[pl.ds(8 * i, 8), :, 0:256] = activ.astype(BF16).reshape(8, SPAN, 256)
        joined_t[0:256, rows] = jnp.transpose(activ).astype(BF16)
        dact[rows] = cdf + pre * pdf

    cot_tree.near_of_me()
    causal = lax.broadcasted_iota(jnp.int32, (CH, CH), 0) <= lane_iota((CH, CH))

    def scores(kc, qi):
        s = dot(kn[kc * CH : (kc + 1) * CH], qt[:, qi * CH : (qi + 1) * CH])
        if kc == qi:
            s = jnp.where(causal, s, NEG_FILL)
        return s

    for qi in range(NCH):
        lanes = slice(qi * CH, (qi + 1) * CH)
        parts = [scores(kc, qi) for kc in range(qi + 1)]
        top = functools.reduce(jnp.maximum, [jnp.max(s, axis=0, keepdims=True) for s in parts])
        total = jnp.zeros((1, CH), F32)
        out = jnp.zeros((64, CH), F32)
        for kc, s in enumerate(parts):
            p = jnp.exp(s - top)
            total = total + jnp.sum(p, axis=0, keepdims=True)
            out = out + dot(vt[:, kc * CH : (kc + 1) * CH], p.astype(BF16))
        out = out / total
        ot[:, lanes] = out
        lse[:, lanes] = jnp.broadcast_to(top + jnp.log(total), (8, CH))
        joined_t[256:320, lanes] = out.astype(BF16)
        joined[8 * qi : 8 * qi + 8, :, 256:320] = jnp.transpose(out).astype(BF16).reshape(8, SPAN, HEAD)
        if qi == 2:
            cot_tree.far_of_me()
            cot_tree.near_of_mate()
    def put_units(base, at, count):
        @pl.loop(0, count // 2)
        def _(i):
            pair = [unfold(wout_all[base + 2 * i + j].astype(F32)) for j in range(2)]
            rows = pl.ds(pl.multiple_of(at + i * 16, 16), 16)
            wo[rows] = jnp.concatenate(pair, axis=0).astype(BF16)

    def put_swap(base, rs):
        for r in range(rs):
            for i in range(4):
                pair = [unfold(swap_all[r, 2 * i + j].astype(F32)) for j in range(2)]
                at = base + r * 64 + i * 16
                wo[at : at + 16] = jnp.concatenate(pair, axis=0).astype(BF16)

    @pl.when(me < 4)
    def _():
        put_units(0, 256, 8)

    @pl.when(me < 3)
    def _():
        for r in range(4):
            remote(
                wout_all.at[pl.ds(32, 8)], swap_all.at[r], w_send.at[r], w_recv.at[r], {"seq": sib}
            ).wait_recv()
            swap_few(r).wait_send()
        put_swap(0, 4)

    @pl.when(me == 3)
    def _():
        put_units(8, 0, 32)

    @pl.when(me > 3)
    def _():
        swap_many().wait_send()
        remote(
            wout_all.at[pl.ds(32, 8)], swap_all.at[0], w_send.at[0], w_recv.at[0], {"seq": sib}
        ).wait_recv()
        put_swap(256, 1)
        put_units(0, 0, 32)

    def of_chip(ref, j):
        return jnp.concatenate([ref[span_ref[i % 2, 2 * j + i // 2]] for i in range(4)], axis=0)

    order = [(mate, 2), (mate, 1), (mate, 3), (me, 2), (me, 3), (me, 1), (mate, 0), (me, 0)]

    class ChipSums:
        def __init__(self, part, buf, sib_buf, land, s_send, s_recv, send, recv):
            self.part, self.buf, self.sib_buf = part, buf, sib_buf
            self.s_send, self.s_recv = s_send, s_recv
            self.tree = SumTree(
                "seq",
                lambda slot, h: buf.at[2 * slot + h],
                lambda kind, h: land.at[kind, h],
                me,
                seq_turn,
                mate,
                send,
                recv,
            )

        def to_sib(self, j):
            return remote(
                self.buf.at[pl.ds(4 * j + 2 - 2 * core, 2)],
                self.sib_buf.at[j],
                self.s_send.at[j],
                self.s_recv.at[j],
                {"seq": sib},
            )

        def compute(self, n):
            j = seq_turn(*order[n]) // 2
            self.buf[pl.ds(4 * j, 4)] = self.part(j).astype(BF16).reshape(4, SPAN, D)
            self.to_sib(j).start()

        def pair(self, n):
            j = seq_turn(*order[n]) // 2
            self.to_sib(j).wait_recv()
            mine = pl.ds(4 * j + 2 * core, 2)
            self.buf[mine] = (self.buf[mine].astype(F32) + self.sib_buf[j].astype(F32)).astype(BF16)
            if n == 0:
                self.tree.far_of_mate()
            elif n < 3:
                self.tree.near_of_mate(order[n][1])
            elif n in (4, 5):
                self.tree.near_early(order[n][1])

        def begin(self):
            for n in range(8):
                self.compute(n)
                if n > 2:
                    self.pair(n - 3)
            for n in range(5, 8):
                self.pair(n)

        def finish(self, total):
            for h in range(2):
                total[SPAN * h : SPAN * (h + 1)] = self.tree.total(h)
            self.tree.sent()
            for n in range(8):
                self.to_sib(seq_turn(*order[n]) // 2).wait_send()

    po = ChipSums(
        lambda j: dot(of_chip(joined, j), wo[...]),
        xh_all,
        po_sib,
        po_land,
        ps_send,
        ps_recv,
        p_send,
        p_recv,
    )
    hg = ChipSums(
        lambda j: dot_nt(of_chip(mixed, j), wp[...]),
        cot_all,
        hg_sib,
        hg_land,
        hs_send,
        hs_recv,
        h_send,
        h_recv,
    )
    x_tree.sent()
    po.begin()
    cot_tree.far_of_mate()
    cot_tree.handed(sib_mate)

    @pl.loop(0, 32)
    def _(i):
        rows = pl.ds(pl.multiple_of(i * SPAN, SPAN), SPAN)
        cs[rows] = cot_all[inv_ref[i]]

    @pl.loop(0, NCH)
    def _(i):
        rows = pl.ds(pl.multiple_of(i * CH, CH), CH)
        cot = cs[rows]
        back = dot_nt(cot, wo[...])
        ag = back[:, 256:].astype(BF16).astype(F32)
        ag_t = jnp.transpose(ag)
        dot_n[rows] = ag.astype(BF16)
        dot_t[:, rows] = ag_t.astype(BF16)
        delta[:, rows] = jnp.broadcast_to(
            jnp.sum(ag_t * ot[:, rows], axis=0, keepdims=True), (8, CH)
        )
        pg = back[:, :256] * dact[rows]
        mixed[pl.ds(8 * i, 8), :, 0:256] = pg.astype(BF16).reshape(8, SPAN, 256)
        mixed_t[0:256, rows] = jnp.transpose(pg).astype(BF16)

    @pl.loop(0, 2)
    def _(i):
        left = dot(joined_t[...], cs[:, pl.ds(pl.multiple_of(i * 256, 256), 256)])
        right = dot(joined_t[...], cs[:, pl.ds(pl.multiple_of(i * 256 + 512, 256), 256)])
        units = jnp.concatenate([left.reshape(40, 8, 256), right.reshape(40, 8, 256)], axis=1)
        lanes = pl.ds(pl.multiple_of(i * 256, 256), 256)
        gof_buf[:, :, lanes] = units[:32].astype(BF16)
        goa_buf[:, :, lanes] = units[32:].astype(BF16)

    def back_few(r):
        return remote(
            gof_buf.at[pl.ds(8 * r, 8)],
            own_out.at[pl.ds(32, 8)],
            v_send.at[r],
            v_recv.at[0],
            {"seq": 4 + 4 * me + r},
        )

    def back_many():
        return remote(
            goa_buf,
            own_out.at[pl.ds(8 + 8 * lax.rem(me, 4), 8)],
            v_send.at[0],
            v_recv.at[lax.rem(me, 4)],
            {"seq": (me - 4) // 4},
        )

    keep_a = pltpu.make_async_copy(goa_buf, own_out.at[pl.ds(0, 8)], local_sem.at[0])
    keep_f3 = pltpu.make_async_copy(gof_buf, own_out.at[pl.ds(8, 32)], local_sem.at[1])
    keep_f = pltpu.make_async_copy(gof_buf, own_out.at[pl.ds(0, 32)], local_sem.at[1])

    @pl.when(me < 3)
    def _():
        for r in range(4):
            back_few(r).start()

    @pl.when(me < 4)
    def _():
        keep_a.start()

    @pl.when(me == 3)
    def _():
        keep_f3.start()

    @pl.when(me > 3)
    def _():
        back_many().start()
        keep_f.start()

    def grads_by_owner(dst, base, columns):
        sums = jnp.sum(
            mixed[:, :, base : base + 256].reshape(ROW, 256).astype(F32), axis=0, keepdims=True
        )

        @pl.loop(0, 4)
        def _(i):
            rows = pl.ds(pl.multiple_of(i * 256, 256), 256)
            h = jnp.transpose(dot(mixed_t[base : base + 256], xs[:, rows]))
            raw = wr[rows, base : base + 256].astype(F32)
            vecs = wr[rows, 384:512].astype(F32)
            gain, bias = (vecs[:, columns + 64 + j : columns + 65 + j] for j in range(2))
            grad = gain * h + bias * sums
            lanes = lane_iota((256, 128))
            extra = vg[rows]
            for j, col in enumerate((raw * h, raw * sums)):
                extra = extra + jnp.where(
                    lanes == 64 + columns + j, jnp.sum(col, axis=1, keepdims=True), 0.0
                )
            vg[rows] = extra
            for j in range(2):
                pair = [
                    grad[128 * j + 64 * t : 128 * j + 64 * t + 64].reshape(8, 8, 256)
                    for t in range(2)
                ]
                dst[:, 2 * i + j] = jnp.concatenate(pair, axis=1).astype(BF16)

    def owner_tree(dst, land, send, recv):
        return SumTree(
            "dp",
            lambda slot, h: dst.at[slot, pl.ds(4 * h, 4)],
            lambda kind, h: land.at[kind, pl.ds(4 * h, 4)],
            dm,
            dp_turn,
            dp_mate,
            send,
            recv,
        )

    gf_tree = owner_tree(gf, gf_land, gf_send, gf_recv)
    go_tree = SumTree(
        "dp",
        lambda slot, h: own_out.at[pl.ds(5 * slot + 2 * h, 2 + h)],
        lambda kind, h: go_land.at[kind, pl.ds(2 * h, 2 + h)],
        dm,
        dp_turn,
        dp_mate,
        go_send,
        go_recv,
    )
    lanes_d = lane_iota((D, 128))
    vg[...] = jnp.where((lanes_d == 71) | (lanes_d == 72), vg[...], 0.0)
    lanes_h = lane_iota((64, 128))
    cols_f = jnp.sum(mixed_t[0:256].astype(F32), axis=1, keepdims=True)
    for r in range(4):
        w = hidden_index(me, r)
        rows = pl.ds(pl.multiple_of(lax.rem(w, 16) * 64, 64), 64)
        vg[rows] += jnp.where(lanes_h == 64 + 9 + w // 16, cols_f[64 * r : 64 * r + 64], 0.0)
    grads_by_owner(gf, 0, 2)
    gf_tree.begin()
    po.tree.far_of_me()
    po.tree.of_mate()

    def back_arrived():
        @pl.when(me < 3)
        def _():
            for r in range(4):
                back_few(r).wait_send()
                remote(
                    goa_buf,
                    own_out.at[pl.ds(8 + 8 * r, 8)],
                    v_send.at[r],
                    v_recv.at[r],
                    {"seq": sib},
                ).wait_recv()

        @pl.when(me < 4)
        def _():
            keep_a.wait()

        @pl.when(me == 3)
        def _():
            keep_f3.wait()

        @pl.when(me > 3)
        def _():
            back_many().wait_send()
            keep_f.wait()
            remote(
                goa_buf, own_out.at[pl.ds(32, 8)], v_send.at[0], v_recv.at[0], {"seq": sib}
            ).wait_recv()

    for qi in reversed(range(NCH)):
        lanes = slice(qi * CH, (qi + 1) * CH)
        dq = jnp.zeros((64, CH), F32)
        for kc in range(qi + 1):
            keys = slice(kc * CH, (kc + 1) * CH)
            p = jnp.exp(scores(kc, qi) - lse[0:1, lanes])
            dp = dot(vn[keys, 0:64], dot_t[:, lanes])
            ds = (p * (dp - delta[0:1, lanes])).astype(BF16)
            dv = dot(p.astype(BF16), dot_n[lanes])
            dk = dot(ds, qn[lanes, 0:64])
            dq = dq + dot(kt[:, keys], ds)
            if qi == NCH - 1:
                dvn[keys] = dv
                dkn[keys] = dk
            else:
                dvn[keys] += dv
                dkn[keys] += dk
        dqt[:, lanes] = dq * 0.125
        if qi == 2:
            back_arrived()
            go_tree.begin()

    @pl.loop(0, NCH)
    def _(i):
        rows = pl.ds(pl.multiple_of(i * CH, CH), CH)
        cosine, sine = cos_ref[:, rows], sin_ref[:, rows]
        dq = rotate_t(dqt[:, rows], cosine, sine, -1.0)
        dk = rotate_t(jnp.transpose(dkn[rows]), cosine, sine, -1.0)
        dv = jnp.transpose(dvn[rows])
        full = jnp.concatenate([dq, dk, dv, zeros_aug], axis=0)
        mixed_t[256:512, rows] = full.astype(BF16)
        mixed[pl.ds(8 * i, 8), :, 256:512] = jnp.transpose(full).astype(BF16).reshape(8, SPAN, 256)

    cols_q = jnp.sum(mixed_t[256:448].astype(F32), axis=1, keepdims=True)
    for i in range(3):
        vg[head_rows] += jnp.where(lanes_h == 68 + i, cols_q[64 * i : 64 * i + 64], 0.0)
    po.tree.near_late()
    gf_tree.far_of_me()
    gf_tree.of_mate()
    grads_by_owner(gq, 256, 0)

    def gq_copy(k, to, frm):
        return remote(gq.at[to], gq_got.at[frm], gq_send.at[k], gq_recv.at[frm], {"dp": to})

    @pl.loop(1, DP)
    def _(k):
        gq_copy(k, lax.rem(dm + k, DP), dm).start()

    slab = jnp.transpose(vg[...])
    for p in range(8):
        vt_part[p] = slab[64:80, 128 * p : 128 * p + 128]

    def vs_copy(k, to, frm):
        return remote(
            vt_part.at[to // 2], vt_seq.at[frm], vs_send.at[k], vs_recv.at[frm], {"seq": to}
        )

    def vd_copy(k, to, frm):
        return remote(vt_own, vt_dp.at[frm], vd_send.at[k], vd_recv.at[frm], {"dp": to})

    @pl.loop(1, SEQ)
    def _(k):
        vs_copy(k, lax.rem(me + k, SEQ), me).start()

    vt_seq[me] = vt_part[chip]
    gf_tree.near_late()
    cot_tree.sent()
    hg.begin()
    go_tree.far_of_me()
    go_tree.of_mate()
    hg.tree.far_of_me()
    hg.tree.of_mate()

    @pl.loop(1, SEQ)
    def _(k):
        vs_copy(k, me, lax.rem(me + k, SEQ)).wait_recv()

    vt_own[...] = jnp.sum(vt_seq[...], axis=0)

    @pl.loop(1, DP)
    def _(k):
        vd_copy(k, lax.rem(dm + k, DP), dm).start()

    vt_dp[dm] = vt_own[...]
    go_tree.near_late()

    def to_owner(part, total, send, recv, k, to, frm):
        return remote(part.at[to], total.at[frm], send.at[k], recv.at[frm], {"seq": to})

    def own_sums(part, total, send, recv):
        @pl.loop(1, SEQ)
        def _(k):
            to_owner(part, total, send, recv, k, lax.rem(me + k, SEQ), me).start()

        total[me] = part[me]

    def own_arrived(part, total, send, recv):
        @pl.loop(1, SEQ)
        def _(k):
            to_owner(part, total, send, recv, k, me, lax.rem(me + k, SEQ)).wait_recv()

    def squares_of(value):
        return jnp.sum(jnp.sum(value * value, axis=0), axis=0, keepdims=True)

    for h in range(2):
        f_part[8 * h : 8 * h + 8] = gf_tree.total(h).reshape(8, 8, 256)
    own_sums(f_part, f_sum, bf_send, bf_recv)
    squares = squares_of(f_part[...])

    @pl.loop(1, DP)
    def _(k):
        gq_copy(k, dm, lax.rem(dm + k, DP)).wait_recv()

    total = gq[dm].astype(F32)
    for k in range(1, DP):
        total = total + gq_got[lax.rem(dm + k, DP)].astype(F32)
    total = total.reshape(SEQ, 8, 256)
    squares = squares + squares_of(total)
    for h in range(2):
        out_total = go_tree.total(h)
        wout_sum[2 * h : 2 * h + 2 + h] = out_total
        out_squares = squares_of(out_total)
        squares = squares + out_squares[:, :256] + out_squares[:, 256:]

    @pl.loop(1, DP)
    def _(k):
        vd_copy(k, dm, lax.rem(dm + k, DP)).wait_recv()

    vec_total = jnp.sum(vt_dp[...], axis=0)
    first = lax.rem(me, 2) * 64 + dm * 8
    lanes = lane_iota(vec_total.shape)
    vec_mine = jnp.where((lanes >= first) & (lanes < first + 8), vec_total, 0.0)
    vec_squares = jnp.sum(vec_mine * vec_mine, axis=0, keepdims=True)
    small[...] = jnp.zeros((128, 128), F32)
    small[0:16] = vec_total
    small[...] = jnp.transpose(small[...])
    vec_grad[...] = small[pl.ds(pl.multiple_of(first, 8), 8)]
    row = squares[:, :128] + squares[:, 128:] + vec_squares
    mine = jnp.sum(row, axis=1, keepdims=True)
    q_part[...] = jnp.where(lane_iota(total.shape) < 192, total, mine[None])
    own_sums(q_part, q_sum, bq_send, bq_recv)
    hg.tree.near_late()
    po.finish(out_sum)
    own_arrived(q_part, q_sum, bq_send, bq_recv)
    tile_b[...] = jnp.sum(q_sum[:, :, 128:256], axis=0)

    def tb_copy(k, to, frm):
        return remote(tile_b, got_b.at[frm], tb_send.at[k], tb_recv.at[frm], {"dp": to})

    @pl.loop(1, DP)
    def _(k):
        tb_copy(k, lax.rem(dm + k, DP), dm).start()

    got_b[dm] = tile_b[...]

    @pl.loop(1, DP)
    def _(k):
        tb_copy(k, dm, lax.rem(dm + k, DP)).wait_recv()

    everything = jnp.sum(got_b[...], axis=0)
    square_ref[...] = jnp.broadcast_to(everything[:, 127:128], (8, 128))
    own_arrived(f_part, f_sum, bf_send, bf_recv)

    hg.finish(grad_sum)
    for tree in (in_tree, out_tree, gf_tree, go_tree):
        tree.sent()

    @pl.loop(1, DP)
    def _(k):
        to = lax.rem(dm + k, DP)
        tb_copy(k, to, dm).wait_send()
        gq_copy(k, to, dm).wait_send()
        vd_copy(k, to, dm).wait_send()

    @pl.loop(1, SEQ)
    def _(k):
        to = lax.rem(me + k, SEQ)
        a_copy(k, to, me).wait_send()
        vs_copy(k, to, me).wait_send()
        to_owner(f_part, f_sum, bf_send, bf_recv, k, to, me).wait_send()
        to_owner(q_part, q_sum, bq_send, bq_recv, k, to, me).wait_send()


def layer_call(span, length, x, cot, w_in, w_out, vectors):
    freqs = np.float32(THETA_BASE) ** (-2.0 * np.arange(ROT // 2) / ROT)
    angles = np.arange(ROW, dtype=np.float32)[None, :] * freqs.astype(np.float32)[:, None]
    cosine, sine = np.cos(angles).astype(np.float32), np.sin(angles).astype(np.float32)
    smem = pl.BlockSpec(memory_space=pltpu.SMEM)
    vmem = pl.BlockSpec(memory_space=pltpu.VMEM)
    sds = jax.ShapeDtypeStruct
    dma = pltpu.SemaphoreType.DMA

    def buf(shape, dtype=BF16):
        return pltpu.VMEM(shape, dtype)

    return pl.pallas_call(
        layer_kernel,
        out_shape=(
            sds((TOK, D), F32),
            sds((TOK, D), F32),
            sds((SEQ, 8, 256), F32),
            sds((SEQ, 8, 256), F32),
            sds((5, 16, 512), F32),
            sds((8, 128), F32),
            sds((16, D), F32),
            sds((8, 128), F32),
        ),
        in_specs=[smem] * 2 + [vmem] * 7,
        out_specs=[vmem] * 8,
        scratch_shapes=[
            pltpu.SMEM((32,), jnp.int32),
            buf((32, SPAN, D)),
            buf((32, SPAN, D)),
            buf((SEQ, 16, 256)),
            buf((DP, SEQ, 16, 256)),
            buf((40, 16, 512)),
            buf((4, 8, 16, 512)),
            buf((128, 128), F32),
            buf((ROW, D)),
            buf((ROW, D)),
            buf((D, 512)),
            buf((D, 512)),
            buf((320, D)),
            buf((128, ROW)),
            buf((ROW, 128)),
            buf((64, ROW)),
            buf((ROW, 128)),
            buf((64, ROW)),
            buf((ROW, 128)),
            buf((64, ROW)),
            buf((ROW, 64)),
            buf((64, ROW), F32),
            buf((8, ROW), F32),
            buf((8, ROW), F32),
            buf((32, SPAN, 320)),
            buf((320, ROW)),
            buf((ROW, 256), F32),
            buf((32, SPAN, 512)),
            buf((512, ROW)),
            buf((64, ROW), F32),
            buf((ROW, 64), F32),
            buf((ROW, 64), F32),
            buf((D, 128), F32),
            buf((8, 16, 512)),
            buf((32, 16, 512)),
            buf((40, 16, 512)),
            buf((DP, 8, 16, 256)),
            buf((DP, 8, 16, 256)),
            buf((8, 2, SPAN, D)),
            buf((8, 2, SPAN, D)),
            buf((7, 2, SPAN, D)),
            buf((7, 2, SPAN, D)),
            buf((7, 8, 16, 256)),
            buf((DP, 8, 16, 256)),
            buf((8, 16, 128), F32),
            buf((SEQ, 16, 128), F32),
            buf((16, 128), F32),
            buf((DP, 16, 128), F32),
            buf((7, 5, 16, 512)),
            buf((SEQ, 8, 256), F32),
            buf((SEQ, 8, 256), F32),
            buf((8, 128), F32),
            buf((DP, 8, 128), F32),
            dma((2,)),
            dma((SEQ,)),
            dma((SEQ,)),
            dma((32,)),
            dma((SEQ, 2)),
            dma((32,)),
            dma((SEQ, 2)),
            dma((16,)),
            dma((DP, 2)),
            dma((16,)),
            dma((DP, 2)),
            dma((4,)),
            dma((4,)),
            dma((8,)),
            dma((8,)),
            dma((16,)),
            dma((7, 2)),
            dma((8,)),
            dma((8,)),
            dma((16,)),
            dma((7, 2)),
            dma((16,)),
            dma((7, 2)),
            dma((DP,)),
            dma((DP,)),
            dma((16,)),
            dma((7, 2)),
            dma((4,)),
            dma((4,)),
            dma((SEQ,)),
            dma((SEQ,)),
            dma((SEQ,)),
            dma((SEQ,)),
            dma((SEQ,)),
            dma((SEQ,)),
            dma((DP,)),
            dma((DP,)),
            dma((DP,)),
            dma((DP,)),
        ],
        compiler_params=pltpu.CompilerParams(
            collective_id=0, has_side_effects=True, vmem_limit_bytes=VMEM_LIMIT
        ),
        name="layer_of_one_row",
    )(span, length, x, cot, w_in, w_out, vectors, jnp.asarray(cosine), jnp.asarray(sine))


def adam(weight, grad, first, second, factor, rate, decay):
    clipped = grad * factor
    first_new = BETA_ONE * first + (1.0 - BETA_ONE) * clipped
    second_new = BETA_TWO * second + (1.0 - BETA_TWO) * clipped * clipped
    first_hat = first_new / (1.0 - BETA_ONE**STEP)
    second_hat = second_new / (1.0 - BETA_TWO**STEP)
    weight_new = weight * (1.0 - rate * decay) - rate * first_hat / (
        jnp.sqrt(second_hat) + ADAM_EPS
    )
    return (weight_new, first_new, second_new, weight_new.astype(BF16))


UPDATE_IN = (
    ("square", (8, 128), F32),
    ("f_sum", (SEQ, 8, 256), F32),
    ("q_sum", (SEQ, 8, 256), F32),
    ("w_in", (8, 7 * D), F32),
    ("in_first", (8, 7 * D), F32),
    ("in_second", (8, 7 * D), F32),
    ("wout_sum", (5, 16, 512), F32),
    ("w_out", (40, D), F32),
    ("out_first", (40, D), F32),
    ("out_second", (40, D), F32),
    ("vectors", (8, VEC_ROWS), F32),
    ("vec_first", (8, VEC_ROWS), F32),
    ("vec_second", (8, VEC_ROWS), F32),
    ("x", (TOK, D), BF16),
    ("cot", (TOK, D), BF16),
    ("grad_sum", (TOK, D), F32),
    ("out_sum", (TOK, D), F32),
    ("vec", (16, D), F32),
    ("vec_grad", (8, 128), F32),
)
UPDATE_OUT = (
    ((TOK, D), BF16),
    ((TOK, D), BF16),
    ((8, 128), F32),
    ((8, 7 * D), F32),
    ((40, D), F32),
    ((8, VEC_ROWS), F32),
    ((8, 7 * D), F32),
    ((40, D), F32),
    ((8, VEC_ROWS), F32),
    ((8, 7 * D), F32),
    ((40, D), F32),
    ((8, VEC_ROWS), F32),
    ((8, 7 * D), BF16),
    ((40, D), BF16),
    ((8, VEC_ROWS), BF16),
)


def update_kernel(span_ref, len_ref, *refs):
    ins, refs = refs[: len(UPDATE_IN)], refs[len(UPDATE_IN) :]
    outs, refs = refs[: len(UPDATE_OUT)], refs[len(UPDATE_OUT) :]
    in_bufs, refs = refs[: len(UPDATE_IN)], refs[len(UPDATE_IN) :]
    out_bufs, (in_sem, out_sem, grad_in) = refs[: len(UPDATE_OUT)], refs[len(UPDATE_OUT) :]
    me = lax.axis_index("seq")
    loads = [
        pltpu.make_async_copy(a, b, in_sem.at[i]) for i, (a, b) in enumerate(zip(ins, in_bufs))
    ]
    stores = [
        pltpu.make_async_copy(b, a, out_sem.at[i]) for i, (a, b) in enumerate(zip(outs, out_bufs))
    ]
    for load in loads:
        load.start()
    names = [name for name, _, _ in UPDATE_IN]

    def take(name):
        i = names.index(name)
        loads[i].wait()
        return in_bufs[i]

    def give(i, value):
        out_bufs[i][...] = value
        stores[i].start()

    norm = jnp.sqrt(take("square")[...])
    give(2, norm)
    factor = jnp.minimum(1.0, CLIP_NORM / norm)[0:1, 0:1]

    f_sum, q_sum = take("f_sum"), take("q_sum")
    for s in range(SEQ):
        for j, p in enumerate(PIECES[s]):
            p = int(p)
            piece = (
                q_sum[s, :, 64 * j : 64 * j + 64]
                if j < 3
                else f_sum[s, :, 64 * (j - 3) : 64 * (j - 3) + 64]
            )
            grad_in[:, 64 * p : 64 * p + 64] = piece

    def matrix(at, grad, weight, first, second, rate, decay):
        values = adam(
            take(weight)[...], grad, take(first)[...], take(second)[...], factor, rate, decay
        )
        for k, value in enumerate(values):
            give(at + 3 * k, value)

    matrix(3, grad_in[...], "w_in", "in_first", "in_second", RATE_MATRIX, DECAY_RATE)
    sums = take("wout_sum")
    grad_out = jnp.concatenate([unfold(sums[u]) for u in range(5)], axis=0)
    matrix(4, grad_out, "w_out", "out_first", "out_second", RATE_MATRIX, DECAY_RATE)
    grad_vec = take("vec_grad")[:, 0:VEC_ROWS]
    matrix(5, grad_vec, "vectors", "vec_first", "vec_second", RATE_VECTOR, 0.0)

    x_rows = take("x")[...].astype(F32)
    centered = x_rows - jnp.mean(x_rows, axis=-1, keepdims=True)
    inv_std = lax.rsqrt(jnp.mean(centered * centered, axis=-1, keepdims=True) + NORM_EPS)
    x_hat = centered * inv_std
    row = lax.broadcasted_iota(jnp.int32, (TOK, 1), 0)
    place = jnp.where(row < SPAN, span_ref[0, me] * SPAN + row, span_ref[1, me] * SPAN + row - SPAN)
    cot = jnp.where(place < len_ref[0], take("cot")[...].astype(F32), 0.0)
    grad = take("grad_sum")[...]
    back = (
        grad
        - jnp.mean(grad, axis=-1, keepdims=True)
        - x_hat * jnp.mean(grad * x_hat, axis=-1, keepdims=True)
    )
    give(1, (cot + inv_std * back).astype(BF16))
    out, vec = take("out_sum")[...], take("vec")
    give(0, (x_rows + out + (vec[7:8] + vec[8:9])).astype(BF16))
    for store in stores:
        store.wait()


def update_call(span, length, *args):
    smem = pl.BlockSpec(memory_space=pltpu.SMEM)
    anywhere = pl.BlockSpec(memory_space=pl.ANY)
    dma = pltpu.SemaphoreType.DMA
    return pl.pallas_call(
        update_kernel,
        out_shape=tuple(jax.ShapeDtypeStruct(shape, kind) for shape, kind in UPDATE_OUT),
        in_specs=[smem] * 2 + [anywhere] * len(UPDATE_IN),
        out_specs=[anywhere] * len(UPDATE_OUT),
        scratch_shapes=[pltpu.VMEM(shape, kind) for _, shape, kind in UPDATE_IN]
        + [pltpu.VMEM(shape, kind) for shape, kind in UPDATE_OUT]
        + [dma((len(UPDATE_IN),)), dma((len(UPDATE_OUT),)), pltpu.VMEM((8, 7 * D), F32)],
        compiler_params=pltpu.CompilerParams(vmem_limit_bytes=UPDATE_LIMIT),
        name="clipped_update",
    )(span, length, *args)


def body(
    hidden_in,
    out_cot,
    in_weight,
    out_weight,
    vectors,
    in_first,
    in_second,
    out_first,
    out_second,
    vec_first,
    vec_second,
    lengths,
    span_of,
):
    span = span_of.T
    out_sum, grad_sum, f_sum, q_sum, wout_sum, squares, vec_full, vec_grad = layer_call(
        span, lengths, hidden_in[0], out_cot[0], in_weight, out_weight, vectors.T
    )
    outs = update_call(
        span,
        lengths,
        squares,
        f_sum,
        q_sum,
        in_weight,
        in_first,
        in_second,
        wout_sum,
        out_weight,
        out_first,
        out_second,
        vectors.T,
        vec_first.T,
        vec_second.T,
        hidden_in[0],
        out_cot[0],
        grad_sum,
        out_sum,
        vec_full,
        vec_grad,
    )
    block_out, input_grad, norm = outs[:3]
    rest = [out.T if i % 3 == 2 else out for i, out in enumerate(outs[3:])]
    return (block_out[None], input_grad[None], norm[0, 0], *rest)


def solution(mesh):
    tokens = P("dp", "seq", None)
    matrix = P(("seq", "dp"), None)
    vector = P(None, ("seq", "dp"))
    return jax.shard_map(
        body,
        mesh=mesh,
        in_specs=(
            tokens,
            tokens,
            matrix,
            matrix,
            vector,
            matrix,
            matrix,
            matrix,
            matrix,
            vector,
            vector,
            P("dp"),
            P(),
        ),
        out_specs=(tokens, tokens, P()) + (matrix, matrix, vector) * 4,
        check_vma=False,
    )
```

```python
import functools
import math

import jax
import jax.numpy as jnp
import numpy as np
from jax import lax
from jax.experimental import pallas as pl
from jax.experimental.pallas import tpu as pltpu
from jax.sharding import PartitionSpec as P

D = 1024
FF = 4096
HEADS = 16
HEAD = 64
ROT = 16
STEP = 5
SEQ = 16
DP = 8
TOK = 128
ROW = 2048
SPAN = 64
VEC_ROWS = 13

NORM_EPS = 1e-05
NEG_FILL = -1e30
CLIP_NORM = 1.0
RATE_MATRIX = 0.02
RATE_VECTOR = 0.2
BETA_ONE = 0.5
BETA_TWO = 0.5
DECAY_RATE = 0.1
ADAM_EPS = 1e-08
THETA_BASE = 10000.0

F32 = jnp.float32
BF16 = jnp.bfloat16
MESH = pl.DeviceIdType.MESH
VMEM_LIMIT = 60 * 1024 * 1024
UPDATE_LIMIT = 60 * 1024 * 1024


def head_of(s):
    if s < 4:
        return 5 * s
    return 5 * ((s - 4) // 4) + 1 + (s - 4) % 4


def hidden_pieces(s):
    if s < 3:
        return [20 * s + 5 * r + 8 for r in range(4)]
    if s == 3:
        return [0, 1, 2, 3]
    return [5 * s - 16 + r for r in range(4)]


def column_pieces():
    rows = []
    for s in range(SEQ):
        h = head_of(s)
        rows.append([h, 16 + h, 32 + h] + [48 + w for w in hidden_pieces(s)])
    return np.array(rows, np.int32)


PIECES = column_pieces()


def head_index(s):
    late = (s + 12) // 16
    return (1 - late) * (5 * s) + late * (5 * ((s - 4) // 4) + 1 + lax.rem(s, 4))


def hidden_index(s, r):
    late, not_few = (s + 12) // 16, (s + 13) // 16
    return (
        (1 - not_few) * (20 * s + 5 * r + 8) + (not_few - late) * r + late * (5 * s - 16 + r)
    )


def remote(src, dst, send, recv, where):
    return pltpu.make_async_remote_copy(
        src_ref=src, dst_ref=dst, send_sem=send, recv_sem=recv, device_id=where, device_id_type=MESH
    )


def greet(me, dm):
    barrier = pltpu.get_barrier_semaphore()

    @pl.loop(1, SEQ)
    def _(k):
        pl.semaphore_signal(
            barrier, inc=1, device_id={"seq": lax.rem(me + k, SEQ)}, device_id_type=MESH
        )

    @pl.loop(1, DP)
    def _(k):
        pl.semaphore_signal(
            barrier, inc=1, device_id={"dp": lax.rem(dm + k, DP)}, device_id_type=MESH
        )


def await_greetings(me, dm):
    barrier = pltpu.get_barrier_semaphore()

    def wait_if(condition, more):
        @pl.when(condition)
        def _():
            pl.semaphore_wait(barrier, SEQ + DP - 2 + more)

    @pl.when(me < 3)
    def _():
        wait_if(dm == 0, 0)
        wait_if(dm == 1, 2)
        wait_if(dm > 1, 5)

    @pl.when(me == 3)
    def _():
        pl.semaphore_wait(barrier, SEQ + DP - 2)

    @pl.when(me > 3)
    def _():
        wait_if(dm < 6, 0)
        wait_if(dm == 6, 3)
        wait_if(dm == 7, 5)


def all_sent(ref, sem):
    remote(ref, ref, sem, sem, {"seq": 0}).wait_send()


def all_here(ref, sem):
    pltpu.make_async_copy(ref, ref, sem).wait()


class Tree:
    def __init__(self, axis, piece, me, turn, mate, send, recv, over_mate, sib=None, given=None):
        self.axis, self.piece, self.me, self.turn, self.mate = (axis, piece, me, turn, mate)
        self.send, self.recv, self.over_mate = send, recv, over_mate
        self.sib, self.given = sib, given
        self.per = 1 if sib is None else 2

    def put(self, slot, h, to):
        part = self.piece(slot, h)
        remote(part, part, self.send, self.arrival(slot, h), {self.axis: to}).start()

    def hand(self, slot, h):
        if self.sib is not None:
            part = self.piece(slot, h)
            remote(part, part, self.send, self.given, {self.axis: self.sib}).start()

    def arrival(self, slot, h):
        return self.recv.at[slot // self.per, h]

    def got(self, slot, h):
        part = self.piece(slot, h)
        remote(
            part, part, self.send, self.arrival(slot, h), {self.axis: self.mate}
        ).wait_recv()

    def own_to_ring(self):
        for h in range(2):
            for k in (1, 3):
                self.put(self.me, h, self.turn(self.me, k))

    def own_to_mate(self):
        for h in range(2):
            self.put(self.me, h, self.mate)
        for h in range(2):
            self.hand(self.me, h)

    def of_mate(self):
        for h in range(2):
            self.got(self.mate, h)
            for k in (1, 3):
                self.put(self.mate, h, self.turn(self.me, k))
            self.hand(self.mate, h)

    def near(self, base):
        for h in range(2):
            for k in (3, 1):
                slot = self.turn(base, k)
                self.got(slot, h)
                if (k == 3) == (h == 0):
                    self.put(slot, h, self.turn(self.me, 4 - k))
                self.hand(slot, h)

    def near_of_me(self):
        self.near(self.me)

    def far_of_me(self):
        slot = self.turn(self.me, 2)
        for h in range(2):
            self.got(slot, h)
            if self.over_mate:
                self.put(slot, h, self.mate)
            self.hand(slot, h)

    def near_of_mate(self):
        if not self.over_mate:
            return self.near(self.mate)
        for h in range(2):
            for k in (3, 1):
                slot = self.turn(self.mate, k)
                self.got(slot, h)
                self.hand(slot, h)

    def far_of_mate(self):
        slot = self.turn(self.mate, 2)
        for h in range(2):
            self.got(slot, h)
            self.hand(slot, h)


class SumTree:
    def __init__(self, axis, piece, land, me, turn, mate, send, recv):
        self.axis, self.piece, self.land, self.me, self.turn, self.mate = (
            axis,
            piece,
            land,
            me,
            turn,
            mate,
        )
        self.send, self.recv = send, recv

    def put(self, slot, kind, h, to):
        copy = remote(
            self.piece(slot, h),
            self.land(kind, h),
            self.send,
            self.recv.at[kind, h],
            {self.axis: to},
        )
        copy.start()

    def got(self, kind, h):
        part = self.land(kind, h)
        remote(part, part, self.send, self.recv.at[kind, h], {self.axis: self.mate}).wait_recv()
        return part[...].astype(F32)

    def add(self, slot, h, *kinds):
        part = self.piece(slot, h)
        total = part[...].astype(F32)
        for kind in kinds:
            total = total + self.got(kind, h)
        part[...] = total.astype(BF16)

    def far_of_mate(self):
        for h in range(2):
            self.put(self.turn(self.mate, 2), 0, h, self.mate)

    def near_of_mate(self, k):
        for h in range(2):
            self.put(self.turn(self.mate, k), 2 if k == 1 else 1, h, self.turn(self.me, k))

    def near_early(self, k):
        h = 0 if k == 1 else 1
        self.put(self.turn(self.me, k), 5 if k == 1 else 4, h, self.turn(self.me, k))

    def far_of_me(self):
        slot = self.turn(self.me, 2)
        for h in range(2):
            self.add(slot, h, 0)
            self.put(slot, 3, h, self.turn(self.me, 3 - 2 * h))

    def near_late(self):
        for h in range(2):
            k = 3 - 2 * h
            slot = self.turn(self.me, k)
            self.add(slot, h, 3)
            self.put(slot, 4 + h, h, self.turn(self.me, k))

    def of_mate(self):
        for h in range(2):
            self.add(self.mate, h, 1, 2)
            self.put(self.mate, 6, h, self.mate)

    def begin(self):
        self.far_of_mate()
        for k in (1, 3):
            self.near_of_mate(k)
        for k in (1, 3):
            self.near_early(k)

    def total(self, h):
        value = self.piece(self.me, h)[...].astype(F32)
        for kind in (4, 5, 6):
            value = value + self.got(kind, h)
        return value


class ColumnSums:
    def __init__(self, axis, piece, landing, me, turn, mate, send, recv):
        self.axis, self.piece, self.me, self.turn, self.mate = (axis, piece, me, turn, mate)
        self.land = lambda i: landing.at[i]
        self.lands = lambda i, n: landing.at[pl.ds(i, n)]
        self.send, self.recv = send, recv

    def copy(self, k, of_mate):
        to = self.turn(self.me, k)
        return remote(
            self.piece(self.turn(self.mate, k) if of_mate else to),
            self.land(4 * of_mate + 4 - k),
            self.send,
            self.recv.at[1 + of_mate],
            {self.axis: to},
        )

    def last(self):
        return remote(
            self.piece(self.mate),
            self.land(0),
            self.send,
            self.recv.at[0],
            {self.axis: self.mate},
        )

    def start(self):
        for of_mate in (1, 0):
            for k in (1, 3, 2):
                self.copy(k, of_mate).start()

    def summed(self, slot, of_mate):
        total = self.piece(slot)[...].astype(F32)
        all_here(self.lands(4 * of_mate + 1, 3), self.recv.at[1 + of_mate])
        for k in (1, 3, 2):
            total = total + self.land(4 * of_mate + 4 - k)[...].astype(F32)
        return total

    def middle(self):
        self.piece(self.mate)[...] = self.summed(self.mate, 1).astype(BF16)
        self.last().start()

    def total(self):
        value = self.summed(self.me, 0)
        self.last().wait_recv()
        return value + self.land(0)[...].astype(F32)

    def sent(self):
        all_sent(self.lands(0, 7), self.send)


def dot(a, b):
    return jnp.dot(a, b, preferred_element_type=F32)


def dot_nt(a, b):
    return lax.dot_general(a, b, (((1,), (1,)), ((), ())), preferred_element_type=F32)


def lane_iota(shape):
    return lax.broadcasted_iota(jnp.int32, shape, len(shape) - 1)


def fold(u):
    return jnp.concatenate([u[:, : D // 2], u[:, D // 2 :]], axis=0)


def unfold(u):
    return jnp.concatenate([u[:8], u[8:]], axis=1)


CH = 512
NCH = ROW // CH


def layer_kernel(
    span_ref,
    len_ref,
    x_any,
    cot_any,
    w_in_any,
    w_out_any,
    vectors_any,
    cos_any,
    sin_any,
    block_out_any,
    input_grad_any,
    f_sum_any,
    q_sum_any,
    wout_sum_any,
    square_any,
    vec_grad_any,
    x_ref,
    cot_ref,
    w_in_ref,
    w_out_ref,
    vectors_ref,
    cos_ref,
    sin_ref,
    block_out,
    input_grad,
    f_sum,
    q_sum,
    wout_sum,
    square_ref,
    vec_grad,
    load_sem,
    store_sem,
    inv_ref,
    xh_all,
    cot_all,
    win_own,
    win_all,
    wout_all,
    wout_own,
    small,
    vec_ref,
    xs,
    cs,
    wr,
    wp,
    wo,
    qt,
    qn,
    kt,
    kn,
    vt,
    vn,
    dot_t,
    dot_n,
    ot,
    lse,
    delta,
    joined,
    joined_t,
    dact,
    mixed,
    mixed_t,
    dqt,
    dkn,
    dvn,
    vg,
    go_buf,
    out_part,
    gf,
    gq,
    po_sib,
    hg_sib,
    po_land,
    hg_land,
    gf_land,
    gq_land,
    vt_part,
    vt_seq,
    vt_own,
    vt_dp,
    go_land,
    f_part,
    q_part,
    tile_a,
    tile_b,
    got_a,
    got_b,
    local_sem,
    a_send,
    a_recv,
    x_send,
    x_recv,
    x_given,
    c_send,
    c_recv,
    c_given,
    l_send,
    l_recv,
    o_send,
    o_recv,
    w_send,
    w_recv,
    ps_send,
    ps_recv,
    p_send,
    p_recv,
    hs_send,
    hs_recv,
    h_send,
    h_recv,
    gf_send,
    gf_recv,
    gq_send,
    gq_recv,
    go_send,
    go_recv,
    v_send,
    v_recv,
    bf_send,
    bf_recv,
    bq_send,
    bq_recv,
    ta_send,
    ta_recv,
    vs_send,
    vs_recv,
    vd_send,
    vd_recv,
    tb_send,
    tb_recv,
):
    me = lax.axis_index("seq")
    dm = lax.axis_index("dp")
    core = lax.rem(me, 2)
    chip = me // 2
    sib = me + 1 - 2 * core
    mate = me + 2 - 4 * lax.rem(chip, 2)
    dp_mate = lax.rem(dm + 4, DP)
    head = head_index(me)
    loads = [
        pltpu.make_async_copy(a, b, load_sem.at[i])
        for i, (a, b) in enumerate(
            (
                (x_any, x_ref),
                (w_in_any, w_in_ref),
                (vectors_any, vectors_ref),
                (cot_any, cot_ref),
                (w_out_any, w_out_ref),
                (cos_any, cos_ref),
                (sin_any, sin_ref),
            )
        )
    ]
    block_store, grad_store, f_store, q_store, wout_store, square_store, vec_store = stores = [
        pltpu.make_async_copy(a, b, store_sem.at[i])
        for i, (a, b) in enumerate(
            (
                (block_out, block_out_any),
                (input_grad, input_grad_any),
                (f_sum, f_sum_any),
                (q_sum, q_sum_any),
                (wout_sum, wout_sum_any),
                (square_ref, square_any),
                (vec_grad, vec_grad_any),
            )
        )
    ]
    def trades(step):
        for u in range(5):
            i = 5 * dm + u

            @pl.when(me < 3)
            def _(u=u, i=i):
                @pl.when(i >= 8)
                def _():
                    k = lax.rem(i, 8)
                    step(u, 4 * me + 3 + i // 8, (32 + k) // 5, 32 + k)

            @pl.when(me > 3)
            def _(u=u, i=i):
                @pl.when(i >= 32)
                def _():
                    slot = 8 + 8 * lax.rem(me, 4) + i - 32
                    step(u, (me - 4) // 4, slot // 5, slot)

    def kept(step):
        for u in range(5):
            i = 5 * dm + u

            @pl.when(me < 3)
            def _(u=u, i=i):
                @pl.when(i < 8)
                def _():
                    step(u)

            @pl.when(me == 3)
            def _(u=u):
                step(u)

            @pl.when(me > 3)
            def _(u=u, i=i):
                @pl.when(i < 32)
                def _():
                    step(u)

    barrier = pltpu.get_barrier_semaphore()
    trades(
        lambda u, s, d, slot: pl.semaphore_signal(
            barrier, inc=1, device_id={"seq": s, "dp": d}, device_id_type=MESH
        )
    )
    greet(me, dm)
    for load in loads:
        load.start()

    row = lax.broadcasted_iota(jnp.int32, (TOK, 1), 0)
    place = jnp.where(row < SPAN, span_ref[0, me] * SPAN + row, span_ref[1, me] * SPAN + row - SPAN)
    def own_rows():
        x_rows = x_ref[...].astype(F32)
        centered = x_rows - jnp.mean(x_rows, axis=-1, keepdims=True)
        inv_std = lax.rsqrt(jnp.mean(centered * centered, axis=-1, keepdims=True) + NORM_EPS)
        return x_rows, centered * inv_std, inv_std

    def own_cot():
        return jnp.where(place < len_ref[0], cot_ref[...].astype(F32), 0.0)

    loads[0].wait()
    xh_all[pl.ds(2 * me, 2)] = own_rows()[1].astype(BF16).reshape(2, SPAN, D)

    loads[1].wait()
    loads[2].wait()
    small[...] = jnp.zeros((128, 128), F32)
    small[0:8, 0:VEC_ROWS] = vectors_ref[...]
    vec_t = small[0:8, 0:64]
    for s in range(SEQ):
        take = [w_in_ref[:, 64 * int(p) : 64 * int(p) + 64] for p in PIECES[s]]
        qkv = jnp.concatenate(take[:3] + [vec_t], axis=1)
        win_own[s] = jnp.concatenate([jnp.concatenate(take[3:], axis=1), qkv], axis=0).astype(BF16)
    loads[4].wait()
    for u in range(5):
        wout_own[u] = fold(w_out_ref[8 * u : 8 * u + 8]).astype(BF16)

    def keep_unit(u):
        wout_all[5 * dm + u] = wout_own[u]

    kept(keep_unit)
    loads[3].wait()
    cot_own = own_cot()
    cot_all[pl.ds(2 * me, 2)] = cot_own.astype(BF16).reshape(2, SPAN, D)
    cot_sum = jnp.sum(cot_own, axis=0, keepdims=True)
    vg[...] = jnp.transpose(jnp.broadcast_to(cot_sum, (128, D)))
    keep = pltpu.make_async_copy(win_own.at[me], win_all.at[dm, me], local_sem.at[0])
    keep.start()

    @pl.loop(0, 32)
    def _(i):
        slot = jnp.int32(0)
        for s in range(SEQ):
            for j in range(2):
                slot = jnp.maximum(slot, jnp.where(span_ref[j, s] == i, 2 * s + j, 0))
        inv_ref[i] = slot

    def seq_turn(s, k):
        return lax.rem(s + 4 * k, SEQ)

    def dp_turn(d, k):
        return d // 4 * 4 + lax.rem(d + k, 4)

    x_tree = Tree(
        "seq",
        lambda slot, h: xh_all.at[2 * slot + h],
        me,
        seq_turn,
        mate,
        x_send.at[0],
        x_recv,
        True,
        sib,
        x_given.at[0],
    )
    cot_tree = Tree(
        "seq",
        lambda slot, h: cot_all.at[2 * slot + h],
        me,
        seq_turn,
        mate,
        c_send.at[0],
        c_recv,
        True,
        sib,
        c_given.at[0],
    )
    in_tree = Tree(
        "dp",
        lambda slot, h: win_all.at[slot, pl.ds(8 * h, 8)],
        dm,
        dp_turn,
        dp_mate,
        l_send.at[0],
        l_recv,
        False,
    )
    out_tree = Tree(
        "dp",
        lambda slot, h: wout_all.at[pl.ds(5 * slot + 2 * h, 2 + h)],
        dm,
        dp_turn,
        dp_mate,
        o_send.at[0],
        o_recv,
        False,
    )

    def a_copy(k, to, frm):
        return remote(
            win_own.at[to], win_all.at[dm, frm], a_send.at[0], a_recv.at[0], {"seq": to}
        )

    await_greetings(me, dm)

    @pl.loop(1, SEQ)
    def _(k):
        a_copy(k, lax.rem(me + k, SEQ), me).start()

    def trade_out(u, s, d, slot):
        return remote(
            wout_own.at[u],
            wout_all.at[slot],
            w_send.at[u],
            w_recv.at[lax.rem(slot, 5)],
            {"seq": s, "dp": d},
        )

    def trade_in(u):
        return remote(
            wout_own.at[u], wout_all.at[5 * dm + u], w_send.at[u], w_recv.at[u], {"seq": sib}
        )

    trades(lambda u, s, d, slot: trade_out(u, s, d, slot).start())
    x_tree.own_to_mate()
    x_tree.own_to_ring()
    keep.wait()

    all_here(win_own.at[pl.ds(0, SEQ - 1)], a_recv.at[0])

    in_tree.own_to_mate()
    in_tree.own_to_ring()
    trades(lambda u, s, d, slot: trade_in(u).wait_recv())
    out_tree.own_to_mate()
    out_tree.own_to_ring()
    x_tree.near_of_me()
    x_tree.of_mate()
    in_tree.near_of_me()
    in_tree.of_mate()
    out_tree.near_of_me()
    out_tree.of_mate()
    x_tree.far_of_me()
    in_tree.far_of_me()
    cot_tree.own_to_ring()

    def unpack(column):
        def step(sb, carry):
            cq, cf = carry
            tiles = [win_all[4 * column + y, sb].astype(F32) for y in range(4)]
            ff = jnp.concatenate([t[:8] for t in tiles], axis=0)
            qk = jnp.concatenate([t[8:] for t in tiles], axis=0)
            rows = pl.ds(pl.multiple_of(sb * 64 + 32 * column, 32), 32)
            gain_a, bias_a, gain_m, bias_m = (qk[:, 192 + i : 193 + i] for i in range(4))
            wr[rows] = jnp.concatenate([ff, qk], axis=1).astype(BF16)
            folded = jnp.where(lane_iota(qk.shape) < 192, qk * gain_a, 0.0)
            wp[rows] = jnp.concatenate([ff * gain_m, folded], axis=1).astype(BF16)
            return (
                cq + jnp.sum(qk * bias_a, axis=0, keepdims=True),
                cf + jnp.sum(ff * bias_m, axis=0, keepdims=True),
            )

        return step

    zero_row = jnp.zeros((1, 256), F32)
    sums = lax.fori_loop(0, SEQ, unpack(dm // 4), (zero_row, zero_row))
    x_tree.near_of_mate()
    cot_tree.own_to_mate()
    in_tree.near_of_mate()
    in_tree.far_of_mate()
    cot_tree.near_of_me()
    cq, cf = lax.fori_loop(0, SEQ, unpack(dp_mate // 4), sums)

    slab = jnp.transpose(wr[:, 384:512].astype(F32))
    vec_ref[...] = slab[64:80]
    loads[5].wait()
    loads[6].wait()

    hid = []
    for r in range(4):
        w = hidden_index(me, r)
        rows = pl.ds(pl.multiple_of(lax.rem(w, 16) * 64, 64), 64)
        part = wr[rows, 384:512].astype(F32)
        lane = 64 + 9 + w // 16
        hid.append(
            jnp.sum(jnp.where(lane_iota(part.shape) == lane, part, 0.0), axis=1, keepdims=True)
        )
    hid = jnp.concatenate(hid, axis=0)
    cf = cf + jnp.transpose(jnp.broadcast_to(hid, (256, 128)))[0:1]

    head_rows = pl.ds(pl.multiple_of(head * 64, 64), 64)
    head_vecs = wr[head_rows, 384:512].astype(F32)
    bq, bk, bv = (head_vecs[:, 68 + i : 69 + i] for i in range(3))

    x_tree.far_of_mate()
    all_here(xh_all.at[pl.ds(0, 16)], x_given.at[0])

    @pl.loop(0, 32)
    def _(i):
        rows = pl.ds(pl.multiple_of(i * SPAN, SPAN), SPAN)
        xs[rows] = xh_all[inv_ref[i]]

    out_tree.near_of_mate()
    out_tree.far_of_me()

    aug = jnp.where(lax.broadcasted_iota(jnp.int32, (64, CH), 0) == 0, 1.0, 0.0)
    zeros_aug = jnp.zeros((64, CH), F32)

    def rotate_t(u, cosine, sine, sign):
        first, second = u[0:8], u[8:16]
        return jnp.concatenate(
            [
                first * cosine - sign * (second * sine),
                second * cosine + sign * (first * sine),
                u[16:],
            ],
            axis=0,
        )

    def project(i):
        start = pl.multiple_of(i * CH, CH)
        rows = pl.ds(start, CH)
        xh = xs[rows]
        first = dot(xh, wp[...])
        qkv = jnp.transpose(first[:, 256:] + cq)
        cosine, sine = cos_ref[:, rows], sin_ref[:, rows]
        q = rotate_t(qkv[0:64] + bq, cosine, sine, 1.0) * 0.125
        k = rotate_t(qkv[64:128] + bk, cosine, sine, 1.0)
        v = qkv[128:192] + bv
        q_full = jnp.concatenate([q, aug], axis=0)
        past = (start + lane_iota((64, CH))) >= len_ref[0]
        k_full = jnp.concatenate([k, jnp.where(past, NEG_FILL, 0.0) * aug], axis=0)
        v_full = jnp.concatenate([v, zeros_aug], axis=0)
        qt[:, rows] = q_full.astype(BF16)
        kt[:, rows] = k.astype(BF16)
        vt[:, rows] = v.astype(BF16)
        qn[rows] = jnp.transpose(q_full).astype(BF16)
        kn[rows] = jnp.transpose(k_full).astype(BF16)
        vn[rows] = jnp.transpose(v_full).astype(BF16)
        pre = first[:, :256] + cf
        cdf = 0.5 * (1.0 + lax.erf(pre * (1.0 / math.sqrt(2.0))))
        pdf = jnp.exp(-0.5 * pre * pre) * (1.0 / math.sqrt(2.0 * math.pi))
        activ = pre * cdf
        joined[pl.ds(8 * i, 8), :, 0:256] = activ.astype(BF16).reshape(8, SPAN, 256)
        joined_t[0:256, rows] = jnp.transpose(activ).astype(BF16)
        dact[rows] = cdf + pre * pdf

    pl.loop(0, 2)(project)
    cot_tree.of_mate()
    cot_tree.far_of_me()
    pl.loop(2, NCH)(project)
    out_tree.far_of_mate()
    causal = lax.broadcasted_iota(jnp.int32, (CH, CH), 0) <= lane_iota((CH, CH))

    def scores(kc, qi):
        s = dot(kn[kc * CH : (kc + 1) * CH], qt[:, qi * CH : (qi + 1) * CH])
        if kc == qi:
            s = jnp.where(causal, s, NEG_FILL)
        return s

    for qi in range(NCH):
        lanes = slice(qi * CH, (qi + 1) * CH)
        parts = [scores(kc, qi) for kc in range(qi + 1)]
        top = functools.reduce(jnp.maximum, [jnp.max(s, axis=0, keepdims=True) for s in parts])
        total = jnp.zeros((1, CH), F32)
        out = jnp.zeros((64, CH), F32)
        for kc, s in enumerate(parts):
            p = jnp.exp(s - top)
            total = total + jnp.sum(p, axis=0, keepdims=True)
            out = out + dot(vt[:, kc * CH : (kc + 1) * CH], p.astype(BF16))
        out = out / total
        ot[:, lanes] = out
        lse[:, lanes] = jnp.broadcast_to(top + jnp.log(total), (8, CH))
        joined_t[256:320, lanes] = out.astype(BF16)
        joined[8 * qi : 8 * qi + 8, :, 256:320] = jnp.transpose(out).astype(BF16).reshape(8, SPAN, HEAD)
    def put_units(base, at, count):
        @pl.loop(0, count // 2)
        def _(i):
            pair = [unfold(wout_all[base + 2 * i + j].astype(F32)) for j in range(2)]
            rows = pl.ds(pl.multiple_of(at + i * 16, 16), 16)
            wo[rows] = jnp.concatenate(pair, axis=0).astype(BF16)

    late = (me + 12) // 16
    put_units(8 * (1 - late), 0, 32)
    put_units(32 * late, 256, 8)

    def of_chip(ref, j):
        return jnp.concatenate([ref[span_ref[i % 2, 2 * j + i // 2]] for i in range(4)], axis=0)

    order = [(mate, 2), (mate, 1), (mate, 3), (me, 2), (me, 3), (me, 1), (mate, 0), (me, 0)]

    class ChipSums:
        def __init__(self, part, buf, sib_buf, land, s_send, s_recv, send, recv):
            self.part, self.buf, self.sib_buf, self.land = part, buf, sib_buf, land
            self.s_send, self.s_recv = s_send, s_recv
            self.tree = SumTree(
                "seq",
                lambda slot, h: buf.at[2 * slot + h],
                lambda kind, h: land.at[kind, h],
                me,
                seq_turn,
                mate,
                send,
                recv,
            )

        def to_sib(self, j):
            return remote(
                self.buf.at[pl.ds(4 * j + 2 - 2 * core, 2)],
                self.sib_buf.at[j],
                self.s_send,
                self.s_recv.at[j],
                {"seq": sib},
            )

        def compute(self, n):
            j = seq_turn(*order[n]) // 2
            self.buf[pl.ds(4 * j, 4)] = self.part(j).astype(BF16).reshape(4, SPAN, D)
            self.to_sib(j).start()

        def pair(self, n):
            j = seq_turn(*order[n]) // 2
            self.to_sib(j).wait_recv()
            mine = pl.ds(4 * j + 2 * core, 2)
            self.buf[mine] = (self.buf[mine].astype(F32) + self.sib_buf[j].astype(F32)).astype(BF16)
            if n == 0:
                self.tree.far_of_mate()
            elif n < 3:
                self.tree.near_of_mate(order[n][1])
            elif n in (4, 5):
                self.tree.near_early(order[n][1])

        def begin(self, between=()):
            for n in range(8):
                self.compute(n)
                for at, step in between:
                    if at == n:
                        step()
                if n > 2:
                    self.pair(n - 3)
            for n in range(5, 8):
                self.pair(n)

        def total(self):
            return jnp.concatenate([self.tree.total(h) for h in range(2)], axis=0)

        def sent(self):
            all_sent(self.land, self.tree.send)
            all_sent(self.sib_buf, self.s_send)

    po = ChipSums(
        lambda j: dot(of_chip(joined, j), wo[...]),
        xh_all,
        po_sib,
        po_land,
        ps_send.at[0],
        ps_recv,
        p_send.at[0],
        p_recv,
    )
    hg = ChipSums(
        lambda j: dot_nt(of_chip(mixed, j), wp[...]),
        cot_all,
        hg_sib,
        hg_land,
        hs_send.at[0],
        hs_recv,
        h_send.at[0],
        h_recv,
    )
    all_sent(xh_all.at[pl.ds(0, 30)], x_send.at[0])
    po.begin()
    cot_tree.near_of_mate()
    cot_tree.far_of_mate()
    all_here(cot_all.at[pl.ds(0, 16)], c_given.at[0])

    @pl.loop(0, 32)
    def _(i):
        rows = pl.ds(pl.multiple_of(i * SPAN, SPAN), SPAN)
        cs[rows] = cot_all[inv_ref[i]]

    @pl.loop(0, NCH)
    def _(i):
        rows = pl.ds(pl.multiple_of(i * CH, CH), CH)
        cot = cs[rows]
        back = dot_nt(cot, wo[...])
        ag = back[:, 256:].astype(BF16).astype(F32)
        ag_t = jnp.transpose(ag)
        dot_n[rows] = ag.astype(BF16)
        dot_t[:, rows] = ag_t.astype(BF16)
        delta[:, rows] = jnp.broadcast_to(
            jnp.sum(ag_t * ot[:, rows], axis=0, keepdims=True), (8, CH)
        )
        pg = back[:, :256] * dact[rows]
        mixed[pl.ds(8 * i, 8), :, 0:256] = pg.astype(BF16).reshape(8, SPAN, 256)
        mixed_t[0:256, rows] = jnp.transpose(pg).astype(BF16)

    @pl.loop(0, 2)
    def _(i):
        left = dot(joined_t[...], cs[:, pl.ds(pl.multiple_of(i * 256, 256), 256)])
        right = dot(joined_t[...], cs[:, pl.ds(pl.multiple_of(i * 256 + 512, 256), 256)])
        units = jnp.concatenate([left.reshape(40, 8, 256), right.reshape(40, 8, 256)], axis=1)
        lanes = pl.ds(pl.multiple_of(i * 256, 256), 256)
        go_buf[pl.ds(8 * (1 - late), 32), :, lanes] = units[:32].astype(BF16)
        go_buf[pl.ds(32 * late, 8), :, lanes] = units[32:].astype(BF16)

    def grads_by_owner(dst, base, columns):
        sums = jnp.sum(
            mixed[:, :, base : base + 256].reshape(ROW, 256).astype(F32), axis=0, keepdims=True
        )

        @pl.loop(0, 4)
        def _(i):
            rows = pl.ds(pl.multiple_of(i * 256, 256), 256)
            h = jnp.transpose(dot(mixed_t[base : base + 256], xs[:, rows]))
            raw = wr[rows, base : base + 256].astype(F32)
            vecs = wr[rows, 384:512].astype(F32)
            gain, bias = (vecs[:, columns + 64 + j : columns + 65 + j] for j in range(2))
            grad = gain * h + bias * sums
            lanes = lane_iota((256, 128))
            extra = vg[rows]
            for j, col in enumerate((raw * h, raw * sums)):
                extra = extra + jnp.where(
                    lanes == 64 + columns + j, jnp.sum(col, axis=1, keepdims=True), 0.0
                )
            vg[rows] = extra
            for j in range(2):
                pair = [
                    grad[128 * j + 64 * t : 128 * j + 64 * t + 64].reshape(8, 8, 256)
                    for t in range(2)
                ]
                dst[:, 2 * i + j] = jnp.concatenate(pair, axis=1).astype(BF16)

    def owner_sums(dst, land, send, recv):
        return ColumnSums(
            "dp",
            lambda slot: dst.at[slot],
            land,
            dm,
            dp_turn,
            dp_mate,
            send.at[0],
            recv,
        )

    gf_sums = owner_sums(gf, gf_land, gf_send, gf_recv)
    gq_sums = owner_sums(gq, gq_land, gq_send, gq_recv)
    go_sums = ColumnSums(
        "dp",
        lambda slot: go_buf.at[pl.ds(5 * slot, 5)],
        go_land,
        dm,
        dp_turn,
        dp_mate,
        go_send.at[0],
        go_recv,
    )
    lanes_d = lane_iota((D, 128))
    vg[...] = jnp.where((lanes_d == 71) | (lanes_d == 72), vg[...], 0.0)
    lanes_h = lane_iota((64, 128))
    cols_f = jnp.sum(mixed_t[0:256].astype(F32), axis=1, keepdims=True)
    for r in range(4):
        w = hidden_index(me, r)
        rows = pl.ds(pl.multiple_of(lax.rem(w, 16) * 64, 64), 64)
        vg[rows] += jnp.where(lanes_h == 64 + 9 + w // 16, cols_f[64 * r : 64 * r + 64], 0.0)
    grads_by_owner(gf, 0, 2)
    gf_sums.start()
    po.tree.far_of_me()
    po.tree.of_mate()

    go_sums.start()

    for qi in reversed(range(NCH)):
        lanes = slice(qi * CH, (qi + 1) * CH)
        dq = jnp.zeros((64, CH), F32)
        for kc in range(qi + 1):
            keys = slice(kc * CH, (kc + 1) * CH)
            p = jnp.exp(scores(kc, qi) - lse[0:1, lanes])
            dp = dot(vn[keys, 0:64], dot_t[:, lanes])
            ds = (p * (dp - delta[0:1, lanes])).astype(BF16)
            dv = dot(p.astype(BF16), dot_n[lanes])
            dk = dot(ds, qn[lanes, 0:64])
            dq = dq + dot(kt[:, keys], ds)
            if qi == NCH - 1:
                dvn[keys] = dv
                dkn[keys] = dk
            else:
                dvn[keys] += dv
                dkn[keys] += dk
        dqt[:, lanes] = dq * 0.125

    @pl.loop(0, NCH)
    def _(i):
        rows = pl.ds(pl.multiple_of(i * CH, CH), CH)
        cosine, sine = cos_ref[:, rows], sin_ref[:, rows]
        dq = rotate_t(dqt[:, rows], cosine, sine, -1.0)
        dk = rotate_t(jnp.transpose(dkn[rows]), cosine, sine, -1.0)
        dv = jnp.transpose(dvn[rows])
        full = jnp.concatenate([dq, dk, dv, zeros_aug], axis=0)
        mixed_t[256:512, rows] = full.astype(BF16)
        mixed[pl.ds(8 * i, 8), :, 256:512] = jnp.transpose(full).astype(BF16).reshape(8, SPAN, 256)

    cols_q = jnp.sum(mixed_t[256:448].astype(F32), axis=1, keepdims=True)
    for i in range(3):
        vg[head_rows] += jnp.where(lanes_h == 68 + i, cols_q[64 * i : 64 * i + 64], 0.0)
    po.tree.near_late()
    gf_sums.middle()
    grads_by_owner(gq, 256, 0)
    gq_sums.start()

    slab = jnp.transpose(vg[...])
    for p in range(8):
        vt_part[p] = slab[64:80, 128 * p : 128 * p + 128]

    def vs_copy(k, to, frm):
        return remote(
            vt_part.at[to // 2], vt_seq.at[frm], vs_send.at[0], vs_recv.at[0], {"seq": to}
        )

    def vd_copy(k, to, frm):
        return remote(vt_own, vt_dp.at[frm], vd_send.at[0], vd_recv.at[0], {"dp": to})

    @pl.loop(1, SEQ)
    def _(k):
        vs_copy(k, lax.rem(me + k, SEQ), me).start()

    vt_seq[me] = vt_part[chip]
    all_sent(cot_all.at[pl.ds(0, 30)], c_send.at[0])

    def vectors_on():
        all_here(vt_seq.at[pl.ds(0, SEQ - 1)], vs_recv.at[0])
        vt_own[...] = jnp.sum(vt_seq[...], axis=0)

        @pl.loop(1, DP)
        def _(k):
            vd_copy(k, lax.rem(dm + k, DP), dm).start()

        vt_dp[dm] = vt_own[...]

    def to_owner(part, total, send, recv, k, to, frm):
        return remote(part.at[to], total.at[frm], send.at[0], recv.at[0], {"seq": to})

    def own_sums(part, total, send, recv):
        @pl.loop(1, SEQ)
        def _(k):
            to_owner(part, total, send, recv, k, lax.rem(me + k, SEQ), me).start()

        total[me] = part[me]

    def own_arrived(part, total, send, recv):
        all_here(total.at[pl.ds(0, SEQ - 1)], recv.at[0])

    def squares_of(value):
        return jnp.sum(jnp.sum(value * value, axis=0), axis=0, keepdims=True)

    def hidden_on():
        f_part[...] = gf_sums.total().reshape(SEQ, 8, 256)
        own_sums(f_part, f_sum, bf_send, bf_recv)

    hg.begin(((5, hidden_on), (6, go_sums.middle), (7, vectors_on)))
    gq_sums.middle()
    hg.tree.far_of_me()
    out_total = go_sums.total()
    out_part[...] = out_total

    def back_out(u, s, d, slot):
        at = lax.rem(slot, 5)
        return remote(
            out_part.at[u], wout_sum.at[at], v_send.at[u], v_recv.at[at], {"seq": s, "dp": d}
        )

    def back_in(u):
        return remote(out_part.at[u], wout_sum.at[u], v_send.at[u], v_recv.at[u], {"seq": sib})

    def keep_total(u):
        wout_sum[u] = out_part[u]

    trades(lambda u, s, d, slot: back_out(u, s, d, slot).start())
    kept(keep_total)
    out_squares = squares_of(out_total)
    squares = squares_of(f_part[...]) + out_squares[:, :256] + out_squares[:, 256:]

    all_here(vt_dp.at[pl.ds(0, DP - 1)], vd_recv.at[0])
    vec_total = jnp.sum(vt_dp[...], axis=0)
    first = lax.rem(me, 2) * 64 + dm * 8
    lanes = lane_iota(vec_total.shape)
    vec_mine = jnp.where((lanes >= first) & (lanes < first + 8), vec_total, 0.0)
    vec_squares = jnp.sum(vec_mine * vec_mine, axis=0, keepdims=True)
    small[...] = jnp.zeros((128, 128), F32)
    small[0:16] = vec_total
    small[...] = jnp.transpose(small[...])
    vec_grad[...] = small[pl.ds(pl.multiple_of(first, 8), 8)]
    vec_store.start()
    total = gq_sums.total().reshape(SEQ, 8, 256)
    squares = squares + squares_of(total)
    row = squares[:, :128] + squares[:, 128:] + vec_squares
    mine = jnp.sum(row, axis=1, keepdims=True)
    tile_a[...] = jnp.broadcast_to(mine, (8, 128))

    def ta_copy(k, to, frm):
        return remote(tile_a, got_a.at[frm], ta_send.at[0], ta_recv.at[0], {"seq": to})

    @pl.loop(1, SEQ)
    def _(k):
        ta_copy(k, lax.rem(me + k, SEQ), me).start()

    got_a[me] = tile_a[...]
    q_part[...] = total
    own_sums(q_part, q_sum, bq_send, bq_recv)
    hg.tree.of_mate()
    hg.tree.near_late()
    all_here(got_a.at[pl.ds(0, SEQ - 1)], ta_recv.at[0])
    tile_b[...] = jnp.sum(got_a[...], axis=0)

    def tb_copy(k, to, frm):
        return remote(tile_b, got_b.at[frm], tb_send.at[0], tb_recv.at[0], {"dp": to})

    @pl.loop(1, DP)
    def _(k):
        tb_copy(k, lax.rem(dm + k, DP), dm).start()

    got_b[dm] = tile_b[...]
    own_arrived(f_part, f_sum, bf_send, bf_recv)
    f_store.start()
    x_rows, x_hat, inv_std = own_rows()
    cot_own = own_cot()
    block_out[...] = (x_rows + po.total() + (vec_ref[7:8] + vec_ref[8:9])).astype(BF16)
    block_store.start()
    own_arrived(q_part, q_sum, bq_send, bq_recv)
    q_store.start()
    trades(lambda u, s, d, slot: back_in(u).wait_recv())
    wout_store.start()

    all_here(got_b.at[pl.ds(0, DP - 1)], tb_recv.at[0])
    everything = jnp.sum(got_b[...], axis=0)
    square_ref[...] = jnp.broadcast_to(everything[:, 0:1], (8, 128))
    square_store.start()
    grad = hg.total()
    back = (
        grad
        - jnp.mean(grad, axis=-1, keepdims=True)
        - x_hat * jnp.mean(grad * x_hat, axis=-1, keepdims=True)
    )
    input_grad[...] = (cot_own + inv_std * back).astype(BF16)
    grad_store.start()
    po.sent()
    hg.sent()
    trades(lambda u, s, d, slot: trade_out(u, s, d, slot).wait_send())
    trades(lambda u, s, d, slot: back_out(u, s, d, slot).wait_send())
    for sums in (gf_sums, gq_sums, go_sums):
        sums.sent()
    all_sent(win_all.at[pl.ds(0, 7)], l_send.at[0])
    all_sent(wout_all.at[pl.ds(0, 35)], o_send.at[0])
    all_sent(win_own.at[pl.ds(0, SEQ - 1)], a_send.at[0])
    all_sent(vt_seq.at[pl.ds(0, SEQ - 1)], vs_send.at[0])
    all_sent(vt_dp.at[pl.ds(0, DP - 1)], vd_send.at[0])
    all_sent(got_a.at[pl.ds(0, SEQ - 1)], ta_send.at[0])
    all_sent(got_b.at[pl.ds(0, DP - 1)], tb_send.at[0])
    all_sent(f_part.at[pl.ds(0, SEQ - 1)], bf_send.at[0])
    all_sent(q_part.at[pl.ds(0, SEQ - 1)], bq_send.at[0])
    for store in stores:
        store.wait()


def layer_call(span, length, x, cot, w_in, w_out, vectors):
    freqs = np.float32(THETA_BASE) ** (-2.0 * np.arange(ROT // 2) / ROT)
    angles = np.arange(ROW, dtype=np.float32)[None, :] * freqs.astype(np.float32)[:, None]
    cosine, sine = np.cos(angles).astype(np.float32), np.sin(angles).astype(np.float32)
    smem = pl.BlockSpec(memory_space=pltpu.SMEM)
    anywhere = pl.BlockSpec(memory_space=pl.ANY)
    sds = jax.ShapeDtypeStruct
    dma = pltpu.SemaphoreType.DMA

    def buf(shape, dtype=BF16):
        return pltpu.VMEM(shape, dtype)

    return pl.pallas_call(
        layer_kernel,
        out_shape=(
            sds((TOK, D), BF16),
            sds((TOK, D), BF16),
            sds((SEQ, 8, 256), F32),
            sds((SEQ, 8, 256), F32),
            sds((5, 16, 512), F32),
            sds((8, 128), F32),
            sds((8, 128), F32),
        ),
        in_specs=[smem] * 2 + [anywhere] * 7,
        out_specs=[anywhere] * 7,
        scratch_shapes=[
            buf((TOK, D)),
            buf((TOK, D)),
            buf((8, 7 * D), F32),
            buf((40, D), F32),
            buf((8, VEC_ROWS), F32),
            buf((8, ROW), F32),
            buf((8, ROW), F32),
            buf((TOK, D)),
            buf((TOK, D)),
            buf((SEQ, 8, 256), F32),
            buf((SEQ, 8, 256), F32),
            buf((5, 16, 512), F32),
            buf((8, 128), F32),
            buf((8, 128), F32),
            dma((7,)),
            dma((7,)),
            pltpu.SMEM((32,), jnp.int32),
            buf((32, SPAN, D)),
            buf((32, SPAN, D)),
            buf((SEQ, 16, 256)),
            buf((DP, SEQ, 16, 256)),
            buf((40, 16, 512)),
            buf((5, 16, 512)),
            buf((128, 128), F32),
            buf((16, D), F32),
            buf((ROW, D)),
            buf((ROW, D)),
            buf((D, 512)),
            buf((D, 512)),
            buf((320, D)),
            buf((128, ROW)),
            buf((ROW, 128)),
            buf((64, ROW)),
            buf((ROW, 128)),
            buf((64, ROW)),
            buf((ROW, 128)),
            buf((64, ROW)),
            buf((ROW, 64)),
            buf((64, ROW), F32),
            buf((8, ROW), F32),
            buf((8, ROW), F32),
            buf((32, SPAN, 320)),
            buf((320, ROW)),
            buf((ROW, 256), F32),
            buf((32, SPAN, 512)),
            buf((512, ROW)),
            buf((64, ROW), F32),
            buf((ROW, 64), F32),
            buf((ROW, 64), F32),
            buf((D, 128), F32),
            buf((40, 16, 512)),
            buf((5, 16, 512), F32),
            buf((DP, 8, 16, 256)),
            buf((DP, 8, 16, 256)),
            buf((8, 2, SPAN, D)),
            buf((8, 2, SPAN, D)),
            buf((7, 2, SPAN, D)),
            buf((7, 2, SPAN, D)),
            buf((8, 8, 16, 256)),
            buf((8, 8, 16, 256)),
            buf((8, 16, 128), F32),
            buf((SEQ, 16, 128), F32),
            buf((16, 128), F32),
            buf((DP, 16, 128), F32),
            buf((8, 5, 16, 512)),
            buf((SEQ, 8, 256), F32),
            buf((SEQ, 8, 256), F32),
            buf((8, 128), F32),
            buf((8, 128), F32),
            buf((SEQ, 8, 128), F32),
            buf((DP, 8, 128), F32),
            dma((1,)),
            dma((1,)),
            dma((1,)),
            dma((1,)),
            dma((8, 2)),
            dma((1,)),
            dma((1,)),
            dma((8, 2)),
            dma((1,)),
            dma((1,)),
            dma((DP, 2)),
            dma((1,)),
            dma((DP, 2)),
            dma((5,)),
            dma((5,)),
            dma((1,)),
            dma((8,)),
            dma((1,)),
            dma((7, 2)),
            dma((1,)),
            dma((8,)),
            dma((1,)),
            dma((7, 2)),
            dma((1,)),
            dma((3,)),
            dma((1,)),
            dma((3,)),
            dma((1,)),
            dma((3,)),
            dma((5,)),
            dma((5,)),
            dma((1,)),
            dma((1,)),
            dma((1,)),
            dma((1,)),
            dma((1,)),
            dma((1,)),
            dma((1,)),
            dma((1,)),
            dma((1,)),
            dma((1,)),
            dma((1,)),
            dma((1,)),
        ],
        compiler_params=pltpu.CompilerParams(
            collective_id=0, has_side_effects=True, vmem_limit_bytes=VMEM_LIMIT
        ),
        name="layer_of_one_row",
    )(span, length, x, cot, w_in, w_out, vectors, jnp.asarray(cosine), jnp.asarray(sine))


def adam(weight, grad, first, second, factor, rate, decay):
    clipped = grad * factor
    first_new = BETA_ONE * first + (1.0 - BETA_ONE) * clipped
    second_new = BETA_TWO * second + (1.0 - BETA_TWO) * clipped * clipped
    first_hat = first_new / (1.0 - BETA_ONE**STEP)
    second_hat = second_new / (1.0 - BETA_TWO**STEP)
    weight_new = weight * (1.0 - rate * decay) - rate * first_hat / (
        jnp.sqrt(second_hat) + ADAM_EPS
    )
    return (weight_new, first_new, second_new, weight_new.astype(BF16))


UPDATE_IN = (
    ("block_out", (TOK, D), BF16),
    ("input_grad", (TOK, D), BF16),
    ("square", (8, 128), F32),
    ("f_sum", (SEQ, 8, 256), F32),
    ("q_sum", (SEQ, 8, 256), F32),
    ("w_in", (8, 7 * D), F32),
    ("in_first", (8, 7 * D), F32),
    ("in_second", (8, 7 * D), F32),
    ("wout_sum", (5, 16, 512), F32),
    ("w_out", (40, D), F32),
    ("out_first", (40, D), F32),
    ("out_second", (40, D), F32),
    ("vectors", (8, VEC_ROWS), F32),
    ("vec_first", (8, VEC_ROWS), F32),
    ("vec_second", (8, VEC_ROWS), F32),
    ("vec_grad", (8, 128), F32),
)
UPDATE_OUT = (
    ((TOK, D), BF16),
    ((TOK, D), BF16),
    ((8, 7 * D), F32),
    ((40, D), F32),
    ((8, VEC_ROWS), F32),
    ((8, 7 * D), F32),
    ((40, D), F32),
    ((8, VEC_ROWS), F32),
    ((8, 7 * D), F32),
    ((40, D), F32),
    ((8, VEC_ROWS), F32),
    ((8, 7 * D), BF16),
    ((40, D), BF16),
    ((8, VEC_ROWS), BF16),
)


def update_kernel(*refs):
    ins, refs = refs[: len(UPDATE_IN)], refs[len(UPDATE_IN) :]
    norm_ref, refs = refs[0], refs[1:]
    outs, refs = refs[: len(UPDATE_OUT)], refs[len(UPDATE_OUT) :]
    in_bufs, refs = refs[: len(UPDATE_IN)], refs[len(UPDATE_IN) :]
    out_bufs, (in_sem, out_sem, grad_in) = refs[: len(UPDATE_OUT)], refs[len(UPDATE_OUT) :]
    loads = [
        pltpu.make_async_copy(a, b, in_sem.at[i]) for i, (a, b) in enumerate(zip(ins, in_bufs))
    ]
    stores = [
        pltpu.make_async_copy(in_bufs[i] if i < 2 else b, a, out_sem.at[i])
        for i, (a, b) in enumerate(zip(outs, out_bufs))
    ]
    order = list(range(2, len(loads))) + [0, 1]
    for i in order:
        loads[i].start()
    names = [name for name, _, _ in UPDATE_IN]

    def take(name):
        i = names.index(name)
        loads[i].wait()
        return in_bufs[i]

    def give(i, value):
        out_bufs[i][...] = value
        stores[i].start()

    norm = jnp.sqrt(take("square")[...])
    norm_ref[0, 0] = norm[0, 0]
    factor = jnp.minimum(1.0, CLIP_NORM / norm)[0:1, 0:1]

    for i in range(2):
        loads[i].wait()
        stores[i].start()
    f_sum, q_sum = take("f_sum"), take("q_sum")
    for s in range(SEQ):
        for j, p in enumerate(PIECES[s]):
            p = int(p)
            piece = (
                q_sum[s, :, 64 * j : 64 * j + 64]
                if j < 3
                else f_sum[s, :, 64 * (j - 3) : 64 * (j - 3) + 64]
            )
            grad_in[:, 64 * p : 64 * p + 64] = piece

    def matrix(at, grad, weight, first, second, rate, decay):
        values = adam(
            take(weight)[...], grad, take(first)[...], take(second)[...], factor, rate, decay
        )
        for k, value in enumerate(values):
            give(at + 3 * k, value)

    matrix(2, grad_in[...], "w_in", "in_first", "in_second", RATE_MATRIX, DECAY_RATE)
    sums = take("wout_sum")
    grad_out = jnp.concatenate([unfold(sums[u]) for u in range(5)], axis=0)
    matrix(3, grad_out, "w_out", "out_first", "out_second", RATE_MATRIX, DECAY_RATE)
    grad_vec = take("vec_grad")[:, 0:VEC_ROWS]
    matrix(4, grad_vec, "vectors", "vec_first", "vec_second", RATE_VECTOR, 0.0)

    for store in stores:
        store.wait()


def update_call(*args):
    anywhere = pl.BlockSpec(memory_space=pl.ANY)
    dma = pltpu.SemaphoreType.DMA
    sds = jax.ShapeDtypeStruct
    return pl.pallas_call(
        update_kernel,
        out_shape=(sds((1, 1), F32),) + tuple(sds(shape, kind) for shape, kind in UPDATE_OUT),
        in_specs=[anywhere] * len(UPDATE_IN),
        out_specs=[pl.BlockSpec(memory_space=pltpu.SMEM)] + [anywhere] * len(UPDATE_OUT),
        scratch_shapes=[pltpu.VMEM(shape, kind) for _, shape, kind in UPDATE_IN]
        + [pltpu.VMEM(shape, kind) for shape, kind in UPDATE_OUT]
        + [dma((len(UPDATE_IN),)), dma((len(UPDATE_OUT),)), pltpu.VMEM((8, 7 * D), F32)],
        compiler_params=pltpu.CompilerParams(vmem_limit_bytes=UPDATE_LIMIT),
        name="clipped_update",
    )(*args)


def body(
    hidden_in,
    out_cot,
    in_weight,
    out_weight,
    vectors,
    in_first,
    in_second,
    out_first,
    out_second,
    vec_first,
    vec_second,
    lengths,
    span_of,
):
    block_out, input_grad, f_sum, q_sum, wout_sum, squares, vec_grad = layer_call(
        span_of.T, lengths, hidden_in[0], out_cot[0], in_weight, out_weight, vectors.T
    )
    norm, block_out, input_grad, *rest = update_call(
        block_out,
        input_grad,
        squares,
        f_sum,
        q_sum,
        in_weight,
        in_first,
        in_second,
        wout_sum,
        out_weight,
        out_first,
        out_second,
        vectors.T,
        vec_first.T,
        vec_second.T,
        vec_grad,
    )
    rest = [out.T if i % 3 == 2 else out for i, out in enumerate(rest)]
    return (block_out[None], input_grad[None], norm.reshape(()), *rest)


def solution(mesh):
    tokens = P("dp", "seq", None)
    matrix = P(("seq", "dp"), None)
    vector = P(None, ("seq", "dp"))
    return jax.shard_map(
        body,
        mesh=mesh,
        in_specs=(
            tokens,
            tokens,
            matrix,
            matrix,
            vector,
            matrix,
            matrix,
            matrix,
            matrix,
            vector,
            vector,
            P("dp"),
            P(),
        ),
        out_specs=(tokens, tokens, P()) + (matrix, matrix, vector) * 4,
        check_vma=False,
    )
```

```python
import functools
import math

import jax
import jax.numpy as jnp
import numpy as np
from jax import lax
from jax.experimental import pallas as pl
from jax.experimental.pallas import tpu as pltpu
from jax.sharding import PartitionSpec as P

D = 1024
FF = 4096
HEADS = 16
HEAD = 64
ROT = 16
STEP = 5
SEQ = 16
DP = 8
TOK = 128
ROW = 2048
SPAN = 64
VEC_ROWS = 13

NORM_EPS = 1e-05
NEG_FILL = -1e30
CLIP_NORM = 1.0
RATE_MATRIX = 0.02
RATE_VECTOR = 0.2
BETA_ONE = 0.5
BETA_TWO = 0.5
DECAY_RATE = 0.1
ADAM_EPS = 1e-08
THETA_BASE = 10000.0

F32 = jnp.float32
BF16 = jnp.bfloat16
MESH = pl.DeviceIdType.MESH
VMEM_LIMIT = 60 * 1024 * 1024
UPDATE_LIMIT = 60 * 1024 * 1024


def head_of(s):
    if s < 4:
        return 5 * s
    return 5 * ((s - 4) // 4) + 1 + (s - 4) % 4


def hidden_pieces(s):
    if s < 3:
        return [20 * s + 5 * r + 8 for r in range(4)]
    if s == 3:
        return [0, 1, 2, 3]
    return [5 * s - 16 + r for r in range(4)]


def column_pieces():
    rows = []
    for s in range(SEQ):
        h = head_of(s)
        rows.append([h, 16 + h, 32 + h] + [48 + w for w in hidden_pieces(s)])
    return np.array(rows, np.int32)


PIECES = column_pieces()


def head_index(s):
    late = (s + 12) // 16
    return (1 - late) * (5 * s) + late * (5 * ((s - 4) // 4) + 1 + lax.rem(s, 4))


def hidden_index(s, r):
    late, not_few = (s + 12) // 16, (s + 13) // 16
    return (
        (1 - not_few) * (20 * s + 5 * r + 8) + (not_few - late) * r + late * (5 * s - 16 + r)
    )


def remote(src, dst, send, recv, where):
    return pltpu.make_async_remote_copy(
        src_ref=src, dst_ref=dst, send_sem=send, recv_sem=recv, device_id=where, device_id_type=MESH
    )


def greet(me, dm):
    barrier = pltpu.get_barrier_semaphore()

    @pl.loop(1, SEQ)
    def _(k):
        pl.semaphore_signal(
            barrier, inc=1, device_id={"seq": lax.rem(me + k, SEQ)}, device_id_type=MESH
        )

    @pl.loop(1, DP)
    def _(k):
        pl.semaphore_signal(
            barrier, inc=1, device_id={"dp": lax.rem(dm + k, DP)}, device_id_type=MESH
        )


def await_greetings():
    pl.semaphore_wait(pltpu.get_barrier_semaphore(), SEQ + DP - 2)


def all_sent(ref, sem):
    remote(ref, ref, sem, sem, {"seq": 0}).wait_send()


def all_here(ref, sem):
    pltpu.make_async_copy(ref, ref, sem).wait()


class Tree:
    def __init__(self, axis, piece, me, turn, mate, send, recv, over_mate, sib=None, given=None):
        self.axis, self.piece, self.me, self.turn, self.mate = (axis, piece, me, turn, mate)
        self.send, self.recv, self.over_mate = send, recv, over_mate
        self.sib, self.given = sib, given
        self.per = 1 if sib is None else 2

    def put(self, slot, h, to):
        part = self.piece(slot, h)
        remote(part, part, self.send, self.arrival(slot, h), {self.axis: to}).start()

    def hand(self, slot, h):
        if self.sib is not None:
            part = self.piece(slot, h)
            remote(part, part, self.send, self.given, {self.axis: self.sib}).start()

    def arrival(self, slot, h):
        return self.recv.at[slot // self.per, h]

    def got(self, slot, h):
        part = self.piece(slot, h)
        remote(
            part, part, self.send, self.arrival(slot, h), {self.axis: self.mate}
        ).wait_recv()

    def own_to_ring(self):
        for h in range(2):
            for k in (1, 3):
                self.put(self.me, h, self.turn(self.me, k))

    def own_to_mate(self):
        for h in range(2):
            self.put(self.me, h, self.mate)
        for h in range(2):
            self.hand(self.me, h)

    def of_mate(self):
        for h in range(2):
            self.got(self.mate, h)
            for k in (1, 3):
                self.put(self.mate, h, self.turn(self.me, k))
            self.hand(self.mate, h)

    def near(self, base):
        for h in range(2):
            for k in (3, 1):
                slot = self.turn(base, k)
                self.got(slot, h)
                if (k == 3) == (h == 0):
                    self.put(slot, h, self.turn(self.me, 4 - k))
                self.hand(slot, h)

    def near_of_me(self):
        self.near(self.me)

    def far_of_me(self):
        slot = self.turn(self.me, 2)
        for h in range(2):
            self.got(slot, h)
            if self.over_mate:
                self.put(slot, h, self.mate)
            self.hand(slot, h)

    def near_of_mate(self):
        if not self.over_mate:
            return self.near(self.mate)
        for h in range(2):
            for k in (3, 1):
                slot = self.turn(self.mate, k)
                self.got(slot, h)
                self.hand(slot, h)

    def far_of_mate(self):
        slot = self.turn(self.mate, 2)
        for h in range(2):
            self.got(slot, h)
            self.hand(slot, h)


class SumTree:
    def __init__(self, axis, piece, land, me, turn, mate, send, recv):
        self.axis, self.piece, self.land, self.me, self.turn, self.mate = (
            axis,
            piece,
            land,
            me,
            turn,
            mate,
        )
        self.send, self.recv = send, recv

    def put(self, slot, kind, h, to):
        copy = remote(
            self.piece(slot, h),
            self.land(kind, h),
            self.send,
            self.recv.at[kind, h],
            {self.axis: to},
        )
        copy.start()

    def got(self, kind, h):
        part = self.land(kind, h)
        remote(part, part, self.send, self.recv.at[kind, h], {self.axis: self.mate}).wait_recv()
        return part[...].astype(F32)

    def add(self, slot, h, *kinds):
        part = self.piece(slot, h)
        total = part[...].astype(F32)
        for kind in kinds:
            total = total + self.got(kind, h)
        part[...] = total.astype(BF16)

    def far_of_mate(self):
        for h in range(2):
            self.put(self.turn(self.mate, 2), 0, h, self.mate)

    def near_of_mate(self, k):
        for h in range(2):
            self.put(self.turn(self.mate, k), 2 if k == 1 else 1, h, self.turn(self.me, k))

    def near_early(self, k):
        h = 0 if k == 1 else 1
        self.put(self.turn(self.me, k), 5 if k == 1 else 4, h, self.turn(self.me, k))

    def far_of_me(self):
        slot = self.turn(self.me, 2)
        for h in range(2):
            self.add(slot, h, 0)
            self.put(slot, 3, h, self.turn(self.me, 3 - 2 * h))

    def near_late(self):
        for h in range(2):
            k = 3 - 2 * h
            slot = self.turn(self.me, k)
            self.add(slot, h, 3)
            self.put(slot, 4 + h, h, self.turn(self.me, k))

    def of_mate(self):
        for h in range(2):
            self.add(self.mate, h, 1, 2)
            self.put(self.mate, 6, h, self.mate)

    def begin(self):
        self.far_of_mate()
        for k in (1, 3):
            self.near_of_mate(k)
        for k in (1, 3):
            self.near_early(k)

    def total(self, h):
        value = self.piece(self.me, h)[...].astype(F32)
        for kind in (4, 5, 6):
            value = value + self.got(kind, h)
        return value


class ColumnSums:
    def __init__(self, axis, piece, landing, me, turn, mate, send, recv):
        self.axis, self.piece, self.me, self.turn, self.mate = (axis, piece, me, turn, mate)
        self.land = lambda i: landing.at[i]
        self.lands = lambda i, n: landing.at[pl.ds(i, n)]
        self.send, self.recv = send, recv

    def copy(self, k, of_mate):
        to = self.turn(self.me, k)
        return remote(
            self.piece(self.turn(self.mate, k) if of_mate else to),
            self.land(4 * of_mate + 4 - k),
            self.send,
            self.recv.at[1 + of_mate],
            {self.axis: to},
        )

    def last(self):
        return remote(
            self.piece(self.mate),
            self.land(0),
            self.send,
            self.recv.at[0],
            {self.axis: self.mate},
        )

    def start(self):
        for of_mate in (1, 0):
            for k in (1, 3, 2):
                self.copy(k, of_mate).start()

    def summed(self, slot, of_mate):
        total = self.piece(slot)[...].astype(F32)
        all_here(self.lands(4 * of_mate + 1, 3), self.recv.at[1 + of_mate])
        for k in (1, 3, 2):
            total = total + self.land(4 * of_mate + 4 - k)[...].astype(F32)
        return total

    def middle(self):
        self.piece(self.mate)[...] = self.summed(self.mate, 1).astype(BF16)
        self.last().start()

    def total(self):
        value = self.summed(self.me, 0)
        self.last().wait_recv()
        return value + self.land(0)[...].astype(F32)

    def sent(self):
        all_sent(self.lands(0, 7), self.send)


def dot(a, b):
    return jnp.dot(a, b, preferred_element_type=F32)


def dot_nt(a, b):
    return lax.dot_general(a, b, (((1,), (1,)), ((), ())), preferred_element_type=F32)


def lane_iota(shape):
    return lax.broadcasted_iota(jnp.int32, shape, len(shape) - 1)


def fold(u):
    return jnp.concatenate([u[:, : D // 2], u[:, D // 2 :]], axis=0)


def unfold(u):
    return jnp.concatenate([u[:8], u[8:]], axis=1)


CH = 512
NCH = ROW // CH


def layer_kernel(
    span_ref,
    len_ref,
    x_any,
    cot_any,
    w_in_any,
    w_out_any,
    vectors_any,
    cos_any,
    sin_any,
    block_out_any,
    input_grad_any,
    f_sum_any,
    q_sum_any,
    wout_sum_any,
    square_any,
    vec_grad_any,
    x_ref,
    cot_ref,
    w_in_ref,
    w_out_ref,
    vectors_ref,
    cos_ref,
    sin_ref,
    block_out,
    input_grad,
    f_sum,
    q_sum,
    wout_sum,
    square_ref,
    vec_grad,
    load_sem,
    store_sem,
    inv_ref,
    xh_all,
    cot_all,
    win_own,
    win_all,
    wout_all,
    wout_own,
    w_relay,
    v_relay,
    small,
    vec_ref,
    xs,
    cs,
    wr,
    wp,
    wo,
    qt,
    qn,
    kt,
    kn,
    vt,
    vn,
    dot_t,
    dot_n,
    ot,
    lse,
    delta,
    joined,
    joined_t,
    dact,
    mixed,
    mixed_t,
    dqt,
    dkn,
    dvn,
    vg,
    go_buf,
    out_part,
    gf,
    gq,
    po_sib,
    hg_sib,
    po_land,
    hg_land,
    gf_land,
    gq_land,
    go_land,
    f_part,
    q_part,
    tile_a,
    tile_b,
    got_a,
    got_b,
    local_sem,
    a_send,
    a_recv,
    x_send,
    x_recv,
    x_given,
    c_send,
    c_recv,
    c_given,
    l_send,
    l_recv,
    o_send,
    o_recv,
    w_send,
    w_recv,
    ps_send,
    ps_recv,
    p_send,
    p_recv,
    hs_send,
    hs_recv,
    h_send,
    h_recv,
    gf_send,
    gf_recv,
    gq_send,
    gq_recv,
    go_send,
    go_recv,
    v_send,
    v_recv,
    bf_send,
    bf_recv,
    bq_send,
    bq_recv,
    ta_send,
    ta_recv,
    tb_send,
    tb_recv,
):
    me = lax.axis_index("seq")
    dm = lax.axis_index("dp")
    core = lax.rem(me, 2)
    chip = me // 2
    sib = me + 1 - 2 * core
    mate = me + 2 - 4 * lax.rem(chip, 2)
    dp_mate = lax.rem(dm + 4, DP)
    head = head_index(me)
    loads = [
        pltpu.make_async_copy(a, b, load_sem.at[i])
        for i, (a, b) in enumerate(
            (
                (x_any, x_ref),
                (w_in_any, w_in_ref),
                (vectors_any, vectors_ref),
                (cot_any, cot_ref),
                (w_out_any, w_out_ref),
                (cos_any, cos_ref),
                (sin_any, sin_ref),
            )
        )
    ]
    block_store, grad_store, f_store, q_store, wout_store, square_store, vec_store = stores = [
        pltpu.make_async_copy(a, b, store_sem.at[i])
        for i, (a, b) in enumerate(
            (
                (block_out, block_out_any),
                (input_grad, input_grad_any),
                (f_sum, f_sum_any),
                (q_sum, q_sum_any),
                (wout_sum, wout_sum_any),
                (square_ref, square_any),
                (vec_grad, vec_grad_any),
            )
        )
    ]
    def units_of(step):
        for u in range(5):
            i = 5 * dm + u

            @pl.when(me < 3)
            def _(u=u, i=i):
                @pl.when(i >= 8)
                def _():
                    step.few(u, i)

            @pl.when(me > 3)
            def _(u=u, i=i):
                r = lax.rem(me, 4)

                @pl.when(i >= 32)
                def _():
                    @pl.when(r < 3)
                    def _():
                        step.many(u, i, 8 + 8 * r + i - 32)

                    @pl.when(r == 3)
                    def _():
                        step.straight(u, i)

                @pl.when((i >= 8 + 8 * r) & (i < 16 + 8 * r) & (r < 3))
                def _():
                    step.between(u, i, 32 + lax.rem(i, 8))

    class Trade:
        def __init__(self, src, dst, relay, base, send, recv):
            self.src, self.dst, self.relay, self.base = src, dst, relay, base
            self.send, self.recv = send, recv

        def place(self, u):
            return self.dst.at[self.base + u]

        def few_out(self, u, i):
            to = 4 * me + 3 + i // 8
            last = i >= 32

            @pl.when(last)
            def _():
                remote(
                    self.src.at[u], self.place(u), self.send.at[0, u], self.recv.at[0, u], {"seq": to}
                ).start()

            @pl.when(jnp.logical_not(last))
            def _():
                remote(
                    self.src.at[u],
                    self.relay.at[0, u],
                    self.send.at[0, u],
                    self.recv.at[1, u],
                    {"seq": to},
                ).start()

        def many_out(self, u, i, far):
            at = lax.rem(far, 5)
            return remote(
                self.src.at[u],
                self.relay.at[1, at],
                self.send.at[0, u],
                self.recv.at[2, at],
                {"dp": far // 5},
            )

        def straight_out(self, u):
            return remote(
                self.src.at[u],
                self.place(u),
                self.send.at[0, u],
                self.recv.at[0, u],
                {"seq": (me - 4) // 4},
            )

        def on_to_few(self, u):
            return remote(
                self.relay.at[1, u],
                self.place(u),
                self.send.at[1, u],
                self.recv.at[0, u],
                {"seq": (me - 4) // 4},
            )

        def on_to_many(self, u, far):
            at = lax.rem(far, 5)
            base = self.base - 5 * dm + far - at if self.whole else self.base
            return remote(
                self.relay.at[0, u],
                self.dst.at[base + at],
                self.send.at[2, u],
                self.recv.at[0, at],
                {"dp": far // 5},
            )

        def arrived(self, ref, sem):
            remote(ref, ref, self.send.at[0, 0], sem, {"seq": sib}).wait_recv()

        def begin(self):
            class Step:
                few = staticmethod(self.few_out)
                many = staticmethod(lambda u, i, far: self.many_out(u, i, far).start())
                straight = staticmethod(lambda u, i: self.straight_out(u).start())
                between = staticmethod(lambda u, i, far: None)

            units_of(Step)

        def relay_on(self):
            def between(u, i, far):
                self.arrived(self.relay.at[0, u], self.recv.at[1, u])
                self.on_to_many(u, far).start()
                self.arrived(self.relay.at[1, u], self.recv.at[2, u])
                self.on_to_few(u).start()

            class Step:
                few = staticmethod(lambda u, i: None)
                many = staticmethod(lambda u, i, far: None)
                straight = staticmethod(lambda u, i: None)

            Step.between = staticmethod(between)
            units_of(Step)

        def end(self):
            class Step:
                few = staticmethod(lambda u, i: self.arrived(self.place(u), self.recv.at[0, u]))
                many = staticmethod(
                    lambda u, i, far: self.arrived(self.place(u), self.recv.at[0, u])
                )
                straight = staticmethod(lambda u, i: self.arrived(self.place(u), self.recv.at[0, u]))
                between = staticmethod(lambda u, i, far: None)

            units_of(Step)

        def sent(self):
            def done(k, u):
                remote(
                    self.src.at[u], self.src.at[u], self.send.at[k, u], self.recv.at[0, u], {"seq": sib}
                ).wait_send()

            def between(u, i, far):
                done(1, u)
                done(2, u)

            class Step:
                few = staticmethod(lambda u, i: done(0, u))
                many = staticmethod(lambda u, i, far: done(0, u))
                straight = staticmethod(lambda u, i: done(0, u))

            Step.between = staticmethod(between)
            units_of(Step)

    def kept(step):
        for u in range(5):
            i = 5 * dm + u

            @pl.when(me < 3)
            def _(u=u, i=i):
                @pl.when(i < 8)
                def _():
                    step(u)

            @pl.when(me == 3)
            def _(u=u):
                step(u)

            @pl.when(me > 3)
            def _(u=u, i=i):
                @pl.when(i < 32)
                def _():
                    step(u)

    greet(me, dm)
    for load in loads:
        load.start()

    row = lax.broadcasted_iota(jnp.int32, (TOK, 1), 0)
    place = jnp.where(row < SPAN, span_ref[0, me] * SPAN + row, span_ref[1, me] * SPAN + row - SPAN)
    def own_rows():
        x_rows = x_ref[...].astype(F32)
        centered = x_rows - jnp.mean(x_rows, axis=-1, keepdims=True)
        inv_std = lax.rsqrt(jnp.mean(centered * centered, axis=-1, keepdims=True) + NORM_EPS)
        return x_rows, centered * inv_std, inv_std

    def own_cot():
        return jnp.where(place < len_ref[0], cot_ref[...].astype(F32), 0.0)

    loads[0].wait()
    xh_all[pl.ds(2 * me, 2)] = own_rows()[1].astype(BF16).reshape(2, SPAN, D)

    loads[1].wait()
    loads[2].wait()
    small[...] = jnp.zeros((128, 128), F32)
    small[0:8, 0:VEC_ROWS] = vectors_ref[...]
    vec_t = small[0:8, 0:64]
    for s in range(SEQ):
        take = [w_in_ref[:, 64 * int(p) : 64 * int(p) + 64] for p in PIECES[s]]
        qkv = jnp.concatenate(take[:3] + [vec_t], axis=1)
        win_own[s] = jnp.concatenate([jnp.concatenate(take[3:], axis=1), qkv], axis=0).astype(BF16)
    loads[4].wait()
    for u in range(5):
        wout_own[u] = fold(w_out_ref[8 * u : 8 * u + 8]).astype(BF16)

    def keep_unit(u):
        wout_all[5 * dm + u] = wout_own[u]

    kept(keep_unit)
    loads[3].wait()
    cot_own = own_cot()
    cot_all[pl.ds(2 * me, 2)] = cot_own.astype(BF16).reshape(2, SPAN, D)
    cot_sum = jnp.sum(cot_own, axis=0, keepdims=True)
    vg[...] = jnp.transpose(jnp.broadcast_to(cot_sum, (128, D)))
    keep = pltpu.make_async_copy(win_own.at[me], win_all.at[dm, me], local_sem.at[0])
    keep.start()

    @pl.loop(0, 32)
    def _(i):
        slot = jnp.int32(0)
        for s in range(SEQ):
            for j in range(2):
                slot = jnp.maximum(slot, jnp.where(span_ref[j, s] == i, 2 * s + j, 0))
        inv_ref[i] = slot

    def seq_turn(s, k):
        return lax.rem(s + 4 * k, SEQ)

    def dp_turn(d, k):
        return d // 4 * 4 + lax.rem(d + k, 4)

    x_tree = Tree(
        "seq",
        lambda slot, h: xh_all.at[2 * slot + h],
        me,
        seq_turn,
        mate,
        x_send.at[0],
        x_recv,
        True,
        sib,
        x_given.at[0],
    )
    cot_tree = Tree(
        "seq",
        lambda slot, h: cot_all.at[2 * slot + h],
        me,
        seq_turn,
        mate,
        c_send.at[0],
        c_recv,
        True,
        sib,
        c_given.at[0],
    )
    in_tree = Tree(
        "dp",
        lambda slot, h: win_all.at[slot, pl.ds(8 * h, 8)],
        dm,
        dp_turn,
        dp_mate,
        l_send.at[0],
        l_recv,
        False,
    )
    out_tree = Tree(
        "dp",
        lambda slot, h: wout_all.at[pl.ds(5 * slot + 2 * h, 2 + h)],
        dm,
        dp_turn,
        dp_mate,
        o_send.at[0],
        o_recv,
        False,
    )

    def a_copy(k, to, frm):
        return remote(
            win_own.at[to], win_all.at[dm, frm], a_send.at[0], a_recv.at[0], {"seq": to}
        )

    await_greetings()

    @pl.loop(1, SEQ)
    def _(k):
        a_copy(k, lax.rem(me + k, SEQ), me).start()

    out_trade = Trade(wout_own, wout_all, w_relay, 5 * dm, w_send, w_recv)
    out_trade.whole = True
    x_tree.own_to_mate()
    x_tree.own_to_ring()
    keep.wait()

    all_here(win_own.at[pl.ds(0, SEQ - 1)], a_recv.at[0])

    in_tree.own_to_mate()
    in_tree.own_to_ring()
    out_trade.begin()
    x_tree.near_of_me()
    x_tree.of_mate()
    in_tree.near_of_me()
    in_tree.of_mate()
    x_tree.far_of_me()
    out_trade.relay_on()
    in_tree.far_of_me()
    cot_tree.own_to_ring()

    def unpack(column):
        def step(sb, carry):
            cq, cf = carry
            tiles = [win_all[4 * column + y, sb].astype(F32) for y in range(4)]
            ff = jnp.concatenate([t[:8] for t in tiles], axis=0)
            qk = jnp.concatenate([t[8:] for t in tiles], axis=0)
            rows = pl.ds(pl.multiple_of(sb * 64 + 32 * column, 32), 32)
            gain_a, bias_a, gain_m, bias_m = (qk[:, 192 + i : 193 + i] for i in range(4))
            wr[rows] = jnp.concatenate([ff, qk], axis=1).astype(BF16)
            folded = jnp.where(lane_iota(qk.shape) < 192, qk * gain_a, 0.0)
            wp[rows] = jnp.concatenate([ff * gain_m, folded], axis=1).astype(BF16)
            return (
                cq + jnp.sum(qk * bias_a, axis=0, keepdims=True),
                cf + jnp.sum(ff * bias_m, axis=0, keepdims=True),
            )

        return step

    zero_row = jnp.zeros((1, 256), F32)
    sums = lax.fori_loop(0, SEQ, unpack(dm // 4), (zero_row, zero_row))
    in_tree.near_of_mate()
    x_tree.near_of_mate()
    out_trade.end()
    out_tree.own_to_mate()
    out_tree.own_to_ring()
    cot_tree.own_to_mate()
    in_tree.far_of_mate()
    x_tree.far_of_mate()
    cq, cf = lax.fori_loop(0, SEQ, unpack(dp_mate // 4), sums)

    slab = jnp.transpose(wr[:, 384:512].astype(F32))
    vec_ref[...] = slab[64:80]
    loads[5].wait()
    loads[6].wait()

    hid = []
    for r in range(4):
        w = hidden_index(me, r)
        rows = pl.ds(pl.multiple_of(lax.rem(w, 16) * 64, 64), 64)
        part = wr[rows, 384:512].astype(F32)
        lane = 64 + 9 + w // 16
        hid.append(
            jnp.sum(jnp.where(lane_iota(part.shape) == lane, part, 0.0), axis=1, keepdims=True)
        )
    hid = jnp.concatenate(hid, axis=0)
    cf = cf + jnp.transpose(jnp.broadcast_to(hid, (256, 128)))[0:1]

    head_rows = pl.ds(pl.multiple_of(head * 64, 64), 64)
    head_vecs = wr[head_rows, 384:512].astype(F32)
    bq, bk, bv = (head_vecs[:, 68 + i : 69 + i] for i in range(3))

    all_here(xh_all.at[pl.ds(0, 16)], x_given.at[0])

    @pl.loop(0, 32)
    def _(i):
        rows = pl.ds(pl.multiple_of(i * SPAN, SPAN), SPAN)
        xs[rows] = xh_all[inv_ref[i]]


    aug = jnp.where(lax.broadcasted_iota(jnp.int32, (64, CH), 0) == 0, 1.0, 0.0)
    zeros_aug = jnp.zeros((64, CH), F32)

    def rotate_t(u, cosine, sine, sign):
        first, second = u[0:8], u[8:16]
        return jnp.concatenate(
            [
                first * cosine - sign * (second * sine),
                second * cosine + sign * (first * sine),
                u[16:],
            ],
            axis=0,
        )

    def project(i):
        start = pl.multiple_of(i * CH, CH)
        rows = pl.ds(start, CH)
        xh = xs[rows]
        first = dot(xh, wp[...])
        qkv = jnp.transpose(first[:, 256:] + cq)
        cosine, sine = cos_ref[:, rows], sin_ref[:, rows]
        q = rotate_t(qkv[0:64] + bq, cosine, sine, 1.0) * 0.125
        k = rotate_t(qkv[64:128] + bk, cosine, sine, 1.0)
        v = qkv[128:192] + bv
        q_full = jnp.concatenate([q, aug], axis=0)
        past = (start + lane_iota((64, CH))) >= len_ref[0]
        k_full = jnp.concatenate([k, jnp.where(past, NEG_FILL, 0.0) * aug], axis=0)
        v_full = jnp.concatenate([v, zeros_aug], axis=0)
        qt[:, rows] = q_full.astype(BF16)
        kt[:, rows] = k.astype(BF16)
        vt[:, rows] = v.astype(BF16)
        qn[rows] = jnp.transpose(q_full).astype(BF16)
        kn[rows] = jnp.transpose(k_full).astype(BF16)
        vn[rows] = jnp.transpose(v_full).astype(BF16)
        pre = first[:, :256] + cf
        cdf = 0.5 * (1.0 + lax.erf(pre * (1.0 / math.sqrt(2.0))))
        pdf = jnp.exp(-0.5 * pre * pre) * (1.0 / math.sqrt(2.0 * math.pi))
        activ = pre * cdf
        joined[pl.ds(8 * i, 8), :, 0:256] = activ.astype(BF16).reshape(8, SPAN, 256)
        joined_t[0:256, rows] = jnp.transpose(activ).astype(BF16)
        dact[rows] = cdf + pre * pdf

    project(0)
    cot_tree.near_of_me()
    out_tree.near_of_me()
    out_tree.of_mate()
    project(1)
    project(2)
    cot_tree.of_mate()
    project(3)
    cot_tree.far_of_me()
    out_tree.near_of_mate()
    out_tree.far_of_me()
    causal = lax.broadcasted_iota(jnp.int32, (CH, CH), 0) <= lane_iota((CH, CH))

    def scores(kc, qi):
        s = dot(kn[kc * CH : (kc + 1) * CH], qt[:, qi * CH : (qi + 1) * CH])
        if kc == qi:
            s = jnp.where(causal, s, NEG_FILL)
        return s

    for qi in range(NCH):
        lanes = slice(qi * CH, (qi + 1) * CH)
        parts = [scores(kc, qi) for kc in range(qi + 1)]
        top = functools.reduce(jnp.maximum, [jnp.max(s, axis=0, keepdims=True) for s in parts])
        total = jnp.zeros((1, CH), F32)
        out = jnp.zeros((64, CH), F32)
        for kc, s in enumerate(parts):
            p = jnp.exp(s - top)
            total = total + jnp.sum(p, axis=0, keepdims=True)
            out = out + dot(vt[:, kc * CH : (kc + 1) * CH], p.astype(BF16))
        out = out / total
        ot[:, lanes] = out
        lse[:, lanes] = jnp.broadcast_to(top + jnp.log(total), (8, CH))
        joined_t[256:320, lanes] = out.astype(BF16)
        joined[8 * qi : 8 * qi + 8, :, 256:320] = jnp.transpose(out).astype(BF16).reshape(8, SPAN, HEAD)
    out_tree.far_of_mate()

    def put_units(base, at, count):
        @pl.loop(0, count // 2)
        def _(i):
            pair = [unfold(wout_all[base + 2 * i + j].astype(F32)) for j in range(2)]
            rows = pl.ds(pl.multiple_of(at + i * 16, 16), 16)
            wo[rows] = jnp.concatenate(pair, axis=0).astype(BF16)

    late = (me + 12) // 16
    put_units(8 * (1 - late), 0, 32)
    put_units(32 * late, 256, 8)

    def of_chips(ref, chips):
        return jnp.concatenate(
            [ref[span_ref[i % 2, 2 * j + i // 2]] for j in chips for i in range(4)], axis=0
        )

    order = [(mate, 2), (mate, 1), (mate, 3), (me, 2), (me, 3), (me, 1), (mate, 0), (me, 0)]

    class ChipSums:
        def __init__(self, part, buf, sib_buf, land, s_send, s_recv, send, recv):
            self.part, self.buf, self.sib_buf, self.land = part, buf, sib_buf, land
            self.s_send, self.s_recv = s_send, s_recv
            self.tree = SumTree(
                "seq",
                lambda slot, h: buf.at[2 * slot + h],
                lambda kind, h: land.at[kind, h],
                me,
                seq_turn,
                mate,
                send,
                recv,
            )

        def to_sib(self, j):
            return remote(
                self.buf.at[pl.ds(4 * j + 2 - 2 * core, 2)],
                self.sib_buf.at[j],
                self.s_send,
                self.s_recv.at[j],
                {"seq": sib},
            )

        def compute(self, n):
            chips = [seq_turn(*order[m]) // 2 for m in (n, n + 1)]
            value = self.part(chips).astype(BF16).reshape(8, SPAN, D)
            for m, j in enumerate(chips):
                self.buf[pl.ds(4 * j, 4)] = value[4 * m : 4 * m + 4]
                self.to_sib(j).start()

        def pair(self, n):
            j = seq_turn(*order[n]) // 2
            self.to_sib(j).wait_recv()
            mine = pl.ds(4 * j + 2 * core, 2)
            self.buf[mine] = (self.buf[mine].astype(F32) + self.sib_buf[j].astype(F32)).astype(BF16)
            if n == 0:
                self.tree.far_of_mate()
            elif n < 3:
                self.tree.near_of_mate(order[n][1])
            elif n in (4, 5):
                self.tree.near_early(order[n][1])

        def begin(self, between=()):
            for n in range(8):
                if n % 2 == 0:
                    self.compute(n)
                for at, step in between:
                    if at == n:
                        step()
                if n > 2:
                    self.pair(n - 3)
            self.pair(5)

        def of_mate(self):
            self.pair(6)
            self.tree.of_mate()
            self.pair(7)

        def total(self):
            return jnp.concatenate([self.tree.total(h) for h in range(2)], axis=0)

        def sent(self):
            all_sent(self.land, self.tree.send)
            all_sent(self.sib_buf, self.s_send)

    po = ChipSums(
        lambda chips: dot(of_chips(joined, chips), wo[...]),
        xh_all,
        po_sib,
        po_land,
        ps_send.at[0],
        ps_recv,
        p_send.at[0],
        p_recv,
    )
    hg = ChipSums(
        lambda chips: dot_nt(of_chips(mixed, chips), wp[...]),
        cot_all,
        hg_sib,
        hg_land,
        hs_send.at[0],
        hs_recv,
        h_send.at[0],
        h_recv,
    )
    all_sent(xh_all.at[pl.ds(0, 30)], x_send.at[0])
    po.begin(((4, cot_tree.near_of_mate), (5, cot_tree.far_of_mate)))
    all_here(cot_all.at[pl.ds(0, 16)], c_given.at[0])

    @pl.loop(0, 32)
    def _(i):
        rows = pl.ds(pl.multiple_of(i * SPAN, SPAN), SPAN)
        cs[rows] = cot_all[inv_ref[i]]

    @pl.loop(0, NCH, unroll=True)
    def _(i):
        rows = pl.ds(pl.multiple_of(i * CH, CH), CH)
        cot = cs[rows]
        back = dot_nt(cot, wo[...])
        ag = back[:, 256:].astype(BF16).astype(F32)
        ag_t = jnp.transpose(ag)
        dot_n[rows] = ag.astype(BF16)
        dot_t[:, rows] = ag_t.astype(BF16)
        delta[:, rows] = jnp.broadcast_to(
            jnp.sum(ag_t * ot[:, rows], axis=0, keepdims=True), (8, CH)
        )
        pg = back[:, :256] * dact[rows]
        mixed[pl.ds(8 * i, 8), :, 0:256] = pg.astype(BF16).reshape(8, SPAN, 256)
        mixed_t[0:256, rows] = jnp.transpose(pg).astype(BF16)

    po.tree.far_of_me()

    @pl.loop(0, 2, unroll=True)
    def _(i):
        left = dot(joined_t[...], cs[:, pl.ds(pl.multiple_of(i * 256, 256), 256)])
        right = dot(joined_t[...], cs[:, pl.ds(pl.multiple_of(i * 256 + 512, 256), 256)])
        units = jnp.concatenate([left.reshape(40, 8, 256), right.reshape(40, 8, 256)], axis=1)
        lanes = pl.ds(pl.multiple_of(i * 256, 256), 256)
        go_buf[pl.ds(8 * (1 - late), 32), :, lanes] = units[:32].astype(BF16)
        go_buf[pl.ds(32 * late, 8), :, lanes] = units[32:].astype(BF16)

    def grads_by_owner(dst, base, columns):
        sums = jnp.sum(
            mixed[:, :, base : base + 256].reshape(ROW, 256).astype(F32), axis=0, keepdims=True
        )

        @pl.loop(0, 4, unroll=True)
        def _(i):
            rows = pl.ds(pl.multiple_of(i * 256, 256), 256)
            h = jnp.transpose(dot(mixed_t[base : base + 256], xs[:, rows]))
            raw = wr[rows, base : base + 256].astype(F32)
            vecs = wr[rows, 384:512].astype(F32)
            gain, bias = (vecs[:, columns + 64 + j : columns + 65 + j] for j in range(2))
            grad = gain * h + bias * sums
            lanes = lane_iota((256, 128))
            extra = vg[rows]
            for j, col in enumerate((raw * h, raw * sums)):
                extra = extra + jnp.where(
                    lanes == 64 + columns + j, jnp.sum(col, axis=1, keepdims=True), 0.0
                )
            if base:
                grad = jnp.concatenate([grad[:, :128], grad[:, 128:] + extra], axis=1)
            else:
                vg[rows] = extra
            for j in range(2):
                pair = [
                    grad[128 * j + 64 * t : 128 * j + 64 * t + 64].reshape(8, 8, 256)
                    for t in range(2)
                ]
                dst[:, 2 * i + j] = jnp.concatenate(pair, axis=1).astype(BF16)

    def owner_sums(dst, land, send, recv):
        return ColumnSums(
            "dp",
            lambda slot: dst.at[slot],
            land,
            dm,
            dp_turn,
            dp_mate,
            send.at[0],
            recv,
        )

    gf_sums = owner_sums(gf, gf_land, gf_send, gf_recv)
    gq_sums = owner_sums(gq, gq_land, gq_send, gq_recv)
    go_sums = ColumnSums(
        "dp",
        lambda slot: go_buf.at[pl.ds(5 * slot, 5)],
        go_land,
        dm,
        dp_turn,
        dp_mate,
        go_send.at[0],
        go_recv,
    )
    lanes_d = lane_iota((D, 128))
    vg[...] = jnp.where((lanes_d == 71) | (lanes_d == 72), vg[...], 0.0)
    lanes_h = lane_iota((64, 128))
    cols_f = jnp.sum(mixed_t[0:256].astype(F32), axis=1, keepdims=True)
    for r in range(4):
        w = hidden_index(me, r)
        rows = pl.ds(pl.multiple_of(lax.rem(w, 16) * 64, 64), 64)
        vg[rows] += jnp.where(lanes_h == 64 + 9 + w // 16, cols_f[64 * r : 64 * r + 64], 0.0)
    grads_by_owner(gf, 0, 2)
    gf_sums.start()
    po.of_mate()

    go_sums.start()

    for qi in reversed(range(NCH)):
        lanes = slice(qi * CH, (qi + 1) * CH)
        dq = jnp.zeros((64, CH), F32)
        for kc in range(qi + 1):
            keys = slice(kc * CH, (kc + 1) * CH)
            p = jnp.exp(scores(kc, qi) - lse[0:1, lanes])
            dp = dot(vn[keys, 0:64], dot_t[:, lanes])
            ds = (p * (dp - delta[0:1, lanes])).astype(BF16)
            dv = dot(p.astype(BF16), dot_n[lanes])
            dk = dot(ds, qn[lanes, 0:64])
            dq = dq + dot(kt[:, keys], ds)
            if qi == NCH - 1:
                dvn[keys] = dv
                dkn[keys] = dk
            else:
                dvn[keys] += dv
                dkn[keys] += dk
        dqt[:, lanes] = dq * 0.125
        if qi == 2:
            po.tree.near_late()
        if qi == 1:
            gf_sums.middle()

    @pl.loop(0, NCH, unroll=True)
    def _(i):
        rows = pl.ds(pl.multiple_of(i * CH, CH), CH)
        cosine, sine = cos_ref[:, rows], sin_ref[:, rows]
        dq = rotate_t(dqt[:, rows], cosine, sine, -1.0)
        dk = rotate_t(jnp.transpose(dkn[rows]), cosine, sine, -1.0)
        dv = jnp.transpose(dvn[rows])
        full = jnp.concatenate([dq, dk, dv, zeros_aug], axis=0)
        mixed_t[256:512, rows] = full.astype(BF16)
        mixed[pl.ds(8 * i, 8), :, 256:512] = jnp.transpose(full).astype(BF16).reshape(8, SPAN, 256)

    cols_q = jnp.sum(mixed_t[256:448].astype(F32), axis=1, keepdims=True)
    for i in range(3):
        vg[head_rows] += jnp.where(lanes_h == 68 + i, cols_q[64 * i : 64 * i + 64], 0.0)
    grads_by_owner(gq, 256, 0)
    gq_sums.start()

    all_sent(cot_all.at[pl.ds(0, 30)], c_send.at[0])

    def to_owner(part, total, send, recv, k, to, frm):
        return remote(part.at[to], total.at[frm], send.at[0], recv.at[0], {"seq": to})

    def own_sums(part, total, send, recv):
        @pl.loop(1, SEQ)
        def _(k):
            to_owner(part, total, send, recv, k, lax.rem(me + k, SEQ), me).start()

        total[me] = part[me]

    def own_arrived(part, total, send, recv):
        all_here(total.at[pl.ds(0, SEQ - 1)], recv.at[0])

    def squares_of(value):
        return jnp.sum(jnp.sum(value * value, axis=0), axis=0, keepdims=True)

    def hidden_on():
        f_part[...] = gf_sums.total().reshape(SEQ, 8, 256)
        own_sums(f_part, f_sum, bf_send, bf_recv)

    hg.begin(((1, hidden_on), (2, go_sums.middle)))
    gq_sums.middle()
    out_total = go_sums.total()
    out_part[...] = out_total

    out_back = Trade(out_part, wout_sum, v_relay, 0, v_send, v_recv)
    out_back.whole = False

    def keep_total(u):
        wout_sum[u] = out_part[u]

    out_back.begin()
    kept(keep_total)
    out_squares = squares_of(out_total)
    squares = squares_of(f_part[...]) + out_squares[:, :256] + out_squares[:, 256:]

    hg.tree.far_of_me()
    total = gq_sums.total().reshape(SEQ, 8, 256)
    weights = jnp.where(lane_iota(total.shape) < 192, total, 0.0)
    squares = squares + squares_of(weights)
    tile_a[0:8] = jnp.broadcast_to(squares[:, :128] + squares[:, 128:], (8, 128))
    tile_a[8:24] = jnp.transpose(total[:, :, 128:].reshape(128, 128))[64:80]

    def ta_copy(k, to, frm):
        return remote(tile_a, got_a.at[frm], ta_send.at[0], ta_recv.at[0], {"seq": to})

    @pl.loop(1, SEQ)
    def _(k):
        ta_copy(k, lax.rem(me + k, SEQ), me).start()

    got_a[me] = tile_a[...]
    q_part[...] = total
    own_sums(q_part, q_sum, bq_send, bq_recv)
    out_back.relay_on()
    hg.of_mate()
    hg.tree.near_late()
    all_here(got_a.at[pl.ds(0, SEQ - 1)], ta_recv.at[0])
    sums = jnp.sum(got_a[...], axis=0)
    vec_total = sums[8:24]
    row = sums[0:1] + jnp.sum(vec_total * vec_total, axis=0, keepdims=True)
    tile_b[...] = jnp.broadcast_to(jnp.sum(row, axis=1, keepdims=True), (8, 128))

    def tb_copy(k, to, frm):
        return remote(tile_b, got_b.at[frm], tb_send.at[0], tb_recv.at[0], {"dp": to})

    @pl.loop(1, DP)
    def _(k):
        tb_copy(k, lax.rem(dm + k, DP), dm).start()

    got_b[dm] = tile_b[...]
    small[...] = jnp.zeros((128, 128), F32)
    small[0:16] = vec_total
    small[...] = jnp.transpose(small[...])
    vec_grad[...] = small[pl.ds(pl.multiple_of(8 * me, 8), 8)]
    vec_store.start()
    own_arrived(f_part, f_sum, bf_send, bf_recv)
    f_store.start()
    x_rows, x_hat, inv_std = own_rows()
    cot_own = own_cot()
    block_out[...] = (x_rows + po.total() + (vec_ref[7:8] + vec_ref[8:9])).astype(BF16)
    block_store.start()
    own_arrived(q_part, q_sum, bq_send, bq_recv)
    q_store.start()
    out_back.end()
    wout_store.start()

    all_here(got_b.at[pl.ds(0, DP - 1)], tb_recv.at[0])
    everything = jnp.sum(got_b[...], axis=0)
    square_ref[...] = jnp.broadcast_to(everything[:, 0:1], (8, 128))
    square_store.start()
    grad = hg.total()
    back = (
        grad
        - jnp.mean(grad, axis=-1, keepdims=True)
        - x_hat * jnp.mean(grad * x_hat, axis=-1, keepdims=True)
    )
    input_grad[...] = (cot_own + inv_std * back).astype(BF16)
    grad_store.start()
    po.sent()
    hg.sent()
    out_trade.sent()
    out_back.sent()
    for sums in (gf_sums, gq_sums, go_sums):
        sums.sent()
    all_sent(win_all.at[pl.ds(0, 7)], l_send.at[0])
    all_sent(wout_all.at[pl.ds(0, 35)], o_send.at[0])
    all_sent(win_own.at[pl.ds(0, SEQ - 1)], a_send.at[0])
    all_sent(got_a.at[pl.ds(0, SEQ - 1)], ta_send.at[0])
    all_sent(got_b.at[pl.ds(0, DP - 1)], tb_send.at[0])
    all_sent(f_part.at[pl.ds(0, SEQ - 1)], bf_send.at[0])
    all_sent(q_part.at[pl.ds(0, SEQ - 1)], bq_send.at[0])
    for store in stores:
        store.wait()


def layer_call(span, length, x, cot, w_in, w_out, vectors):
    freqs = np.float32(THETA_BASE) ** (-2.0 * np.arange(ROT // 2) / ROT)
    angles = np.arange(ROW, dtype=np.float32)[None, :] * freqs.astype(np.float32)[:, None]
    cosine, sine = np.cos(angles).astype(np.float32), np.sin(angles).astype(np.float32)
    smem = pl.BlockSpec(memory_space=pltpu.SMEM)
    anywhere = pl.BlockSpec(memory_space=pl.ANY)
    sds = jax.ShapeDtypeStruct
    dma = pltpu.SemaphoreType.DMA

    def buf(shape, dtype=BF16):
        return pltpu.VMEM(shape, dtype)

    return pl.pallas_call(
        layer_kernel,
        out_shape=(
            sds((TOK, D), BF16),
            sds((TOK, D), BF16),
            sds((SEQ, 8, 256), F32),
            sds((SEQ, 8, 256), F32),
            sds((5, 16, 512), F32),
            sds((8, 128), F32),
            sds((8, 128), F32),
        ),
        in_specs=[smem] * 2 + [anywhere] * 7,
        out_specs=[anywhere] * 7,
        scratch_shapes=[
            buf((TOK, D)),
            buf((TOK, D)),
            buf((8, 7 * D), F32),
            buf((40, D), F32),
            buf((8, VEC_ROWS), F32),
            buf((8, ROW), F32),
            buf((8, ROW), F32),
            buf((TOK, D)),
            buf((TOK, D)),
            buf((SEQ, 8, 256), F32),
            buf((SEQ, 8, 256), F32),
            buf((5, 16, 512), F32),
            buf((8, 128), F32),
            buf((8, 128), F32),
            dma((7,)),
            dma((7,)),
            pltpu.SMEM((32,), jnp.int32),
            buf((32, SPAN, D)),
            buf((32, SPAN, D)),
            buf((SEQ, 16, 256)),
            buf((DP, SEQ, 16, 256)),
            buf((40, 16, 512)),
            buf((5, 16, 512)),
            buf((2, 5, 16, 512)),
            buf((2, 5, 16, 512), F32),
            buf((128, 128), F32),
            buf((16, D), F32),
            buf((ROW, D)),
            buf((ROW, D)),
            buf((D, 512)),
            buf((D, 512)),
            buf((320, D)),
            buf((128, ROW)),
            buf((ROW, 128)),
            buf((64, ROW)),
            buf((ROW, 128)),
            buf((64, ROW)),
            buf((ROW, 128)),
            buf((64, ROW)),
            buf((ROW, 64)),
            buf((64, ROW), F32),
            buf((8, ROW), F32),
            buf((8, ROW), F32),
            buf((32, SPAN, 320)),
            buf((320, ROW)),
            buf((ROW, 256), F32),
            buf((32, SPAN, 512)),
            buf((512, ROW)),
            buf((64, ROW), F32),
            buf((ROW, 64), F32),
            buf((ROW, 64), F32),
            buf((D, 128), F32),
            buf((40, 16, 512)),
            buf((5, 16, 512), F32),
            buf((DP, 8, 16, 256)),
            buf((DP, 8, 16, 256)),
            buf((8, 2, SPAN, D)),
            buf((8, 2, SPAN, D)),
            buf((7, 2, SPAN, D)),
            buf((7, 2, SPAN, D)),
            buf((8, 8, 16, 256)),
            buf((8, 8, 16, 256)),
            buf((8, 5, 16, 512)),
            buf((SEQ, 8, 256), F32),
            buf((SEQ, 8, 256), F32),
            buf((24, 128), F32),
            buf((8, 128), F32),
            buf((SEQ, 24, 128), F32),
            buf((DP, 8, 128), F32),
            dma((1,)),
            dma((1,)),
            dma((1,)),
            dma((1,)),
            dma((8, 2)),
            dma((1,)),
            dma((1,)),
            dma((8, 2)),
            dma((1,)),
            dma((1,)),
            dma((DP, 2)),
            dma((1,)),
            dma((DP, 2)),
            dma((3, 5)),
            dma((3, 5)),
            dma((1,)),
            dma((8,)),
            dma((1,)),
            dma((7, 2)),
            dma((1,)),
            dma((8,)),
            dma((1,)),
            dma((7, 2)),
            dma((1,)),
            dma((3,)),
            dma((1,)),
            dma((3,)),
            dma((1,)),
            dma((3,)),
            dma((3, 5)),
            dma((3, 5)),
            dma((1,)),
            dma((1,)),
            dma((1,)),
            dma((1,)),
            dma((1,)),
            dma((1,)),
            dma((1,)),
            dma((1,)),
        ],
        compiler_params=pltpu.CompilerParams(
            collective_id=0, has_side_effects=True, vmem_limit_bytes=VMEM_LIMIT
        ),
        name="layer_of_one_row",
    )(span, length, x, cot, w_in, w_out, vectors, jnp.asarray(cosine), jnp.asarray(sine))


def adam(weight, grad, first, second, factor, rate, decay):
    clipped = grad * factor
    first_new = BETA_ONE * first + (1.0 - BETA_ONE) * clipped
    second_new = BETA_TWO * second + (1.0 - BETA_TWO) * clipped * clipped
    first_hat = first_new / (1.0 - BETA_ONE**STEP)
    second_hat = second_new / (1.0 - BETA_TWO**STEP)
    weight_new = weight * (1.0 - rate * decay) - rate * first_hat / (
        jnp.sqrt(second_hat) + ADAM_EPS
    )
    return (weight_new, first_new, second_new, weight_new.astype(BF16))


UPDATE_IN = (
    ("block_out", (TOK, D), BF16),
    ("input_grad", (TOK, D), BF16),
    ("square", (8, 128), F32),
    ("f_sum", (SEQ, 8, 256), F32),
    ("q_sum", (SEQ, 8, 256), F32),
    ("w_in", (8, 7 * D), F32),
    ("in_first", (8, 7 * D), F32),
    ("in_second", (8, 7 * D), F32),
    ("wout_sum", (5, 16, 512), F32),
    ("w_out", (40, D), F32),
    ("out_first", (40, D), F32),
    ("out_second", (40, D), F32),
    ("vectors", (8, VEC_ROWS), F32),
    ("vec_first", (8, VEC_ROWS), F32),
    ("vec_second", (8, VEC_ROWS), F32),
    ("vec_grad", (8, 128), F32),
)
UPDATE_OUT = (
    ((TOK, D), BF16),
    ((TOK, D), BF16),
    ((8, 7 * D), F32),
    ((40, D), F32),
    ((8, VEC_ROWS), F32),
    ((8, 7 * D), F32),
    ((40, D), F32),
    ((8, VEC_ROWS), F32),
    ((8, 7 * D), F32),
    ((40, D), F32),
    ((8, VEC_ROWS), F32),
    ((8, 7 * D), BF16),
    ((40, D), BF16),
    ((8, VEC_ROWS), BF16),
)


def update_kernel(*refs):
    ins, refs = refs[: len(UPDATE_IN)], refs[len(UPDATE_IN) :]
    norm_ref, refs = refs[0], refs[1:]
    outs, refs = refs[: len(UPDATE_OUT)], refs[len(UPDATE_OUT) :]
    in_bufs, refs = refs[: len(UPDATE_IN)], refs[len(UPDATE_IN) :]
    out_bufs, (in_sem, out_sem, grad_in) = refs[: len(UPDATE_OUT)], refs[len(UPDATE_OUT) :]
    loads = [
        pltpu.make_async_copy(a, b, in_sem.at[i]) for i, (a, b) in enumerate(zip(ins, in_bufs))
    ]
    stores = [
        pltpu.make_async_copy(in_bufs[i] if i < 2 else b, a, out_sem.at[i])
        for i, (a, b) in enumerate(zip(outs, out_bufs))
    ]
    order = list(range(2, len(loads))) + [0, 1]
    for i in order:
        loads[i].start()
    names = [name for name, _, _ in UPDATE_IN]

    def take(name):
        i = names.index(name)
        loads[i].wait()
        return in_bufs[i]

    def give(i, value):
        out_bufs[i][...] = value
        stores[i].start()

    norm = jnp.sqrt(take("square")[...])
    norm_ref[0, 0] = norm[0, 0]
    factor = jnp.minimum(1.0, CLIP_NORM / norm)[0:1, 0:1]

    for i in range(2):
        loads[i].wait()
        stores[i].start()
    f_sum, q_sum = take("f_sum"), take("q_sum")
    for s in range(SEQ):
        for j, p in enumerate(PIECES[s]):
            p = int(p)
            piece = (
                q_sum[s, :, 64 * j : 64 * j + 64]
                if j < 3
                else f_sum[s, :, 64 * (j - 3) : 64 * (j - 3) + 64]
            )
            grad_in[:, 64 * p : 64 * p + 64] = piece

    def matrix(at, grad, weight, first, second, rate, decay):
        values = adam(
            take(weight)[...], grad, take(first)[...], take(second)[...], factor, rate, decay
        )
        for k, value in enumerate(values):
            give(at + 3 * k, value)

    matrix(2, grad_in[...], "w_in", "in_first", "in_second", RATE_MATRIX, DECAY_RATE)
    sums = take("wout_sum")
    grad_out = jnp.concatenate([unfold(sums[u]) for u in range(5)], axis=0)
    matrix(3, grad_out, "w_out", "out_first", "out_second", RATE_MATRIX, DECAY_RATE)
    grad_vec = take("vec_grad")[:, 0:VEC_ROWS]
    matrix(4, grad_vec, "vectors", "vec_first", "vec_second", RATE_VECTOR, 0.0)

    for store in stores:
        store.wait()


def update_call(*args):
    anywhere = pl.BlockSpec(memory_space=pl.ANY)
    dma = pltpu.SemaphoreType.DMA
    sds = jax.ShapeDtypeStruct
    return pl.pallas_call(
        update_kernel,
        out_shape=(sds((1, 1), F32),) + tuple(sds(shape, kind) for shape, kind in UPDATE_OUT),
        in_specs=[anywhere] * len(UPDATE_IN),
        out_specs=[pl.BlockSpec(memory_space=pltpu.SMEM)] + [anywhere] * len(UPDATE_OUT),
        scratch_shapes=[pltpu.VMEM(shape, kind) for _, shape, kind in UPDATE_IN]
        + [pltpu.VMEM(shape, kind) for shape, kind in UPDATE_OUT]
        + [dma((len(UPDATE_IN),)), dma((len(UPDATE_OUT),)), pltpu.VMEM((8, 7 * D), F32)],
        compiler_params=pltpu.CompilerParams(vmem_limit_bytes=UPDATE_LIMIT),
        name="clipped_update",
    )(*args)


def body(
    hidden_in,
    out_cot,
    in_weight,
    out_weight,
    vectors,
    in_first,
    in_second,
    out_first,
    out_second,
    vec_first,
    vec_second,
    lengths,
    span_of,
):
    block_out, input_grad, f_sum, q_sum, wout_sum, squares, vec_grad = layer_call(
        span_of.T, lengths, hidden_in[0], out_cot[0], in_weight, out_weight, vectors.T
    )
    norm, block_out, input_grad, *rest = update_call(
        block_out,
        input_grad,
        squares,
        f_sum,
        q_sum,
        in_weight,
        in_first,
        in_second,
        wout_sum,
        out_weight,
        out_first,
        out_second,
        vectors.T,
        vec_first.T,
        vec_second.T,
        vec_grad,
    )
    rest = [out.T if i % 3 == 2 else out for i, out in enumerate(rest)]
    return (block_out[None], input_grad[None], norm.reshape(()), *rest)


def solution(mesh):
    tokens = P("dp", "seq", None)
    matrix = P(("seq", "dp"), None)
    vector = P(None, ("seq", "dp"))
    return jax.shard_map(
        body,
        mesh=mesh,
        in_specs=(
            tokens,
            tokens,
            matrix,
            matrix,
            vector,
            matrix,
            matrix,
            matrix,
            matrix,
            vector,
            vector,
            P("dp"),
            P(),
        ),
        out_specs=(tokens, tokens, P()) + (matrix, matrix, vector) * 4,
        check_vma=False,
    )
```

```python
import functools
import math

import jax
import jax.numpy as jnp
import numpy as np
from jax import lax
from jax.experimental import pallas as pl
from jax.experimental.pallas import tpu as pltpu
from jax.sharding import PartitionSpec as P

D = 1024
FF = 4096
HEADS = 16
HEAD = 64
ROT = 16
STEP = 5
SEQ = 16
DP = 8
TOK = 128
ROW = 2048
SPAN = 64
VEC_ROWS = 13

NORM_EPS = 1e-05
NEG_FILL = -1e30
CLIP_NORM = 1.0
RATE_MATRIX = 0.02
RATE_VECTOR = 0.2
BETA_ONE = 0.5
BETA_TWO = 0.5
DECAY_RATE = 0.1
ADAM_EPS = 1e-08
THETA_BASE = 10000.0

F32 = jnp.float32
BF16 = jnp.bfloat16
MESH = pl.DeviceIdType.MESH
VMEM_LIMIT = 60 * 1024 * 1024
UPDATE_LIMIT = 60 * 1024 * 1024


def head_of(s):
    if s < 4:
        return 5 * s
    return 5 * ((s - 4) // 4) + 1 + (s - 4) % 4


def hidden_pieces(s):
    if s < 3:
        return [20 * s + 5 * r + 8 for r in range(4)]
    if s == 3:
        return [0, 1, 2, 3]
    return [5 * s - 16 + r for r in range(4)]


def column_pieces():
    rows = []
    for s in range(SEQ):
        h = head_of(s)
        rows.append([h, 16 + h, 32 + h] + [48 + w for w in hidden_pieces(s)])
    return np.array(rows, np.int32)


PIECES = column_pieces()


def head_index(s):
    late = (s + 12) // 16
    return (1 - late) * (5 * s) + late * (5 * ((s - 4) // 4) + 1 + lax.rem(s, 4))


def hidden_index(s, r):
    late, not_few = (s + 12) // 16, (s + 13) // 16
    return (
        (1 - not_few) * (20 * s + 5 * r + 8) + (not_few - late) * r + late * (5 * s - 16 + r)
    )


def remote(src, dst, send, recv, where):
    return pltpu.make_async_remote_copy(
        src_ref=src, dst_ref=dst, send_sem=send, recv_sem=recv, device_id=where, device_id_type=MESH
    )


def greet(me, dm):
    barrier = pltpu.get_barrier_semaphore()

    @pl.loop(1, SEQ)
    def _(k):
        pl.semaphore_signal(
            barrier, inc=1, device_id={"seq": lax.rem(me + k, SEQ)}, device_id_type=MESH
        )

    @pl.loop(1, DP)
    def _(k):
        pl.semaphore_signal(
            barrier, inc=1, device_id={"dp": lax.rem(dm + k, DP)}, device_id_type=MESH
        )


def await_greetings():
    pl.semaphore_wait(pltpu.get_barrier_semaphore(), SEQ + DP - 2)


def all_sent(ref, sem):
    remote(ref, ref, sem, sem, {"seq": 0}).wait_send()


def all_here(ref, sem):
    pltpu.make_async_copy(ref, ref, sem).wait()


class Tree:
    def __init__(self, axis, piece, me, turn, mate, send, recv, over_mate, sib=None, given=None):
        self.axis, self.piece, self.me, self.turn, self.mate = (axis, piece, me, turn, mate)
        self.send, self.recv, self.over_mate = send, recv, over_mate
        self.sib, self.given = sib, given
        self.per = 1 if sib is None else 2

    def put(self, slot, h, to):
        part = self.piece(slot, h)
        remote(part, part, self.send, self.arrival(slot, h), {self.axis: to}).start()

    def hand(self, slot, h):
        if self.sib is not None:
            part = self.piece(slot, h)
            remote(part, part, self.send, self.given, {self.axis: self.sib}).start()

    def arrival(self, slot, h):
        return self.recv.at[slot // self.per, h]

    def got(self, slot, h):
        part = self.piece(slot, h)
        remote(
            part, part, self.send, self.arrival(slot, h), {self.axis: self.mate}
        ).wait_recv()

    def own_to_ring(self):
        for h, k in ((0, 1), (1, 3), (1, 1), (0, 3)):
            self.put(self.me, h, self.turn(self.me, k))

    def own_to_mate(self):
        for h in range(2):
            self.put(self.me, h, self.mate)
        for h in range(2):
            self.hand(self.me, h)

    def of_mate(self, halves=(0, 1)):
        for h in halves:
            self.got(self.mate, h)
            for k in (1, 3):
                self.put(self.mate, h, self.turn(self.me, k))
            self.hand(self.mate, h)

    def near_first(self, base):
        for h, k in ((0, 3), (1, 1)):
            slot = self.turn(base, k)
            self.got(slot, h)
            self.put(slot, h, self.turn(self.me, 4 - k))
            self.hand(slot, h)

    def near_rest(self, base):
        for h, k in ((1, 3), (0, 1)):
            slot = self.turn(base, k)
            self.got(slot, h)
            self.hand(slot, h)

    def near(self, base):
        self.near_first(base)
        self.near_rest(base)

    def near_of_me(self):
        self.near(self.me)

    def far_of_me(self):
        slot = self.turn(self.me, 2)
        for h in range(2):
            self.got(slot, h)
            if self.over_mate:
                self.put(slot, h, self.mate)
            self.hand(slot, h)

    def near_of_mate(self):
        if not self.over_mate:
            return self.near(self.mate)
        for h in range(2):
            for k in (3, 1):
                slot = self.turn(self.mate, k)
                self.got(slot, h)
                self.hand(slot, h)

    def far_of_mate(self):
        slot = self.turn(self.mate, 2)
        for h in range(2):
            self.got(slot, h)
            self.hand(slot, h)


class SumTree:
    def __init__(self, axis, piece, landing, me, turn, mate, send, recv):
        self.axis, self.piece, self.me, self.turn, self.mate = (axis, piece, me, turn, mate)
        self.landing, self.send, self.recv = landing, send, recv

    def land(self, kind, h):
        return self.landing.at[kind, h]

    def arrival(self, kind, h):
        return self.recv.at[(h, 2, 2, 3 + h, 5, 5, 5)[kind]]

    def put(self, slot, kind, h, to):
        copy = remote(
            self.piece(slot, h),
            self.land(kind, h),
            self.send,
            self.arrival(kind, h),
            {self.axis: to},
        )
        copy.start()

    def add(self, slot, h, *kinds):
        part = self.piece(slot, h)
        total = part[...].astype(F32)
        for kind in kinds:
            total = total + self.land(kind, h)[...].astype(F32)
        part[...] = total.astype(BF16)

    def far_of_mate(self):
        for h in range(2):
            self.put(self.turn(self.mate, 2), 0, h, self.mate)

    def near_of_mate(self, k):
        for h in range(2):
            self.put(self.turn(self.mate, k), 2 if k == 1 else 1, h, self.turn(self.me, k))

    def near_early(self, k):
        h = 0 if k == 1 else 1
        self.put(self.turn(self.me, k), 5 if k == 1 else 4, h, self.turn(self.me, k))

    def far_of_me(self):
        slot = self.turn(self.me, 2)
        for h in range(2):
            all_here(self.land(0, h), self.arrival(0, h))
            self.add(slot, h, 0)
            self.put(slot, 3, h, self.turn(self.me, 3 - 2 * h))

    def near_late(self):
        for h in range(2):
            k = 3 - 2 * h
            slot = self.turn(self.me, k)
            all_here(self.land(3, h), self.arrival(3, h))
            self.add(slot, h, 3)
            self.put(slot, 4 + h, h, self.turn(self.me, k))

    def of_mate(self):
        all_here(self.landing.at[pl.ds(1, 2)], self.arrival(1, 0))
        for h in range(2):
            self.add(self.mate, h, 1, 2)
            self.put(self.mate, 6, h, self.mate)

    def begin(self):
        self.far_of_mate()
        for k in (1, 3):
            self.near_of_mate(k)
        for k in (1, 3):
            self.near_early(k)

    def total(self):
        all_here(self.landing.at[pl.ds(4, 3)], self.arrival(4, 0))
        parts = []
        for h in range(2):
            value = self.piece(self.me, h)[...].astype(F32)
            for kind in (4, 5, 6):
                value = value + self.land(kind, h)[...].astype(F32)
            parts.append(value)
        return jnp.concatenate(parts, axis=0)


class ColumnSums:
    def __init__(self, axis, piece, landing, me, turn, mate, send, recv):
        self.axis, self.piece, self.me, self.turn, self.mate = (axis, piece, me, turn, mate)
        self.land = lambda i: landing.at[i]
        self.lands = lambda i, n: landing.at[pl.ds(i, n)]
        self.send, self.recv = send, recv

    def copy(self, k, of_mate):
        to = self.turn(self.me, k)
        return remote(
            self.piece(self.turn(self.mate, k) if of_mate else to),
            self.land(4 * of_mate + 4 - k),
            self.send,
            self.recv.at[1 + of_mate],
            {self.axis: to},
        )

    def last(self):
        return remote(
            self.piece(self.mate),
            self.land(0),
            self.send,
            self.recv.at[0],
            {self.axis: self.mate},
        )

    def start(self):
        for of_mate in (1, 0):
            for k in (1, 3, 2):
                self.copy(k, of_mate).start()

    def summed(self, slot, of_mate):
        total = self.piece(slot)[...].astype(F32)
        all_here(self.lands(4 * of_mate + 1, 3), self.recv.at[1 + of_mate])
        for k in (1, 3, 2):
            total = total + self.land(4 * of_mate + 4 - k)[...].astype(F32)
        return total

    def middle(self):
        self.piece(self.mate)[...] = self.summed(self.mate, 1).astype(BF16)
        self.last().start()

    def total(self):
        value = self.summed(self.me, 0)
        self.last().wait_recv()
        return value + self.land(0)[...].astype(F32)

    def sent(self):
        all_sent(self.lands(0, 7), self.send)


def dot(a, b):
    return jnp.dot(a, b, preferred_element_type=F32)


def dot_nt(a, b):
    return lax.dot_general(a, b, (((1,), (1,)), ((), ())), preferred_element_type=F32)


def lane_iota(shape):
    return lax.broadcasted_iota(jnp.int32, shape, len(shape) - 1)


def fold(u):
    return jnp.concatenate([u[:, : D // 2], u[:, D // 2 :]], axis=0)


def unfold(u):
    return jnp.concatenate([u[:8], u[8:]], axis=1)


CH = 512
NCH = ROW // CH


def layer_kernel(
    span_ref,
    len_ref,
    x_any,
    cot_any,
    w_in_any,
    w_out_any,
    vectors_any,
    cos_any,
    sin_any,
    block_out_any,
    input_grad_any,
    grad_in_any,
    grad_out_any,
    square_any,
    vec_grad_any,
    x_ref,
    cot_ref,
    w_in_ref,
    w_out_ref,
    vectors_ref,
    cos_ref,
    sin_ref,
    block_out,
    input_grad,
    grad_in,
    grad_out,
    f_sum,
    q_sum,
    wout_sum,
    square_ref,
    vec_grad,
    load_sem,
    store_sem,
    inv_ref,
    xh_all,
    cot_all,
    win_own,
    win_all,
    wout_all,
    wout_own,
    w_relay,
    v_relay,
    small,
    vec_ref,
    xs,
    cs,
    wr,
    wp,
    wo,
    qt,
    qn,
    kt,
    kn,
    vt,
    vn,
    dot_t,
    dot_n,
    ot,
    lse,
    delta,
    joined,
    joined_t,
    dact,
    mixed,
    mixed_t,
    dqt,
    dkn,
    dvn,
    vg,
    go_buf,
    out_part,
    gf,
    gq,
    po_sib,
    hg_sib,
    po_land,
    hg_land,
    gf_land,
    gq_land,
    go_land,
    f_part,
    q_part,
    tile_a,
    tile_b,
    got_a,
    got_b,
    local_sem,
    a_send,
    a_recv,
    x_send,
    x_recv,
    x_given,
    c_send,
    c_recv,
    c_given,
    l_send,
    l_recv,
    o_send,
    o_recv,
    w_send,
    w_recv,
    ps_send,
    ps_recv,
    p_send,
    p_recv,
    hs_send,
    hs_recv,
    h_send,
    h_recv,
    gf_send,
    gf_recv,
    gq_send,
    gq_recv,
    go_send,
    go_recv,
    v_send,
    v_recv,
    bf_send,
    bf_recv,
    bq_send,
    bq_recv,
    ta_send,
    ta_recv,
    tb_send,
    tb_recv,
):
    me = lax.axis_index("seq")
    dm = lax.axis_index("dp")
    core = lax.rem(me, 2)
    chip = me // 2
    sib = me + 1 - 2 * core
    mate = me + 2 - 4 * lax.rem(chip, 2)
    dp_mate = lax.rem(dm + 4, DP)
    head = head_index(me)
    loads = [
        pltpu.make_async_copy(a, b, load_sem.at[i])
        for i, (a, b) in enumerate(
            (
                (x_any, x_ref),
                (w_in_any, w_in_ref),
                (vectors_any, vectors_ref),
                (cot_any, cot_ref),
                (w_out_any, w_out_ref),
                (cos_any, cos_ref),
                (sin_any, sin_ref),
            )
        )
    ]
    block_store, grad_store, in_store, out_store, square_store, vec_store = stores = [
        pltpu.make_async_copy(a, b, store_sem.at[i])
        for i, (a, b) in enumerate(
            (
                (block_out, block_out_any),
                (input_grad, input_grad_any),
                (grad_in, grad_in_any),
                (grad_out, grad_out_any),
                (square_ref, square_any),
                (vec_grad, vec_grad_any),
            )
        )
    ]
    def units_of(step):
        for u in range(5):
            i = 5 * dm + u

            @pl.when(me < 3)
            def _(u=u, i=i):
                @pl.when(i >= 8)
                def _():
                    step.few(u, i)

            @pl.when(me > 3)
            def _(u=u, i=i):
                r = lax.rem(me, 4)

                @pl.when(i >= 32)
                def _():
                    @pl.when(r < 3)
                    def _():
                        step.many(u, i, 8 + 8 * r + i - 32)

                    @pl.when(r == 3)
                    def _():
                        step.straight(u, i)

                @pl.when((i >= 8 + 8 * r) & (i < 16 + 8 * r) & (r < 3))
                def _():
                    step.between(u, i, 32 + lax.rem(i, 8))

    class Trade:
        def __init__(self, src, dst, relay, base, send, recv):
            self.src, self.dst, self.relay, self.base = src, dst, relay, base
            self.send, self.recv = send, recv

        def place(self, u):
            return self.dst.at[self.base + u]

        def few_out(self, u, i):
            to = 4 * me + 3 + i // 8
            last = i >= 32

            @pl.when(last)
            def _():
                remote(
                    self.src.at[u], self.place(u), self.send.at[0, u], self.recv.at[0, u], {"seq": to}
                ).start()

            @pl.when(jnp.logical_not(last))
            def _():
                remote(
                    self.src.at[u],
                    self.relay.at[0, u],
                    self.send.at[0, u],
                    self.recv.at[0, u],
                    {"seq": to},
                ).start()

        def many_out(self, u, i, far):
            at = lax.rem(far, 5)
            return remote(
                self.src.at[u],
                self.relay.at[1, at],
                self.send.at[0, u],
                self.recv.at[1, at],
                {"dp": far // 5},
            )

        def straight_out(self, u):
            return remote(
                self.src.at[u],
                self.place(u),
                self.send.at[0, u],
                self.recv.at[0, u],
                {"seq": (me - 4) // 4},
            )

        def on_to_few(self, u):
            return remote(
                self.relay.at[1, u],
                self.place(u),
                self.send.at[1, u],
                self.recv.at[0, u],
                {"seq": (me - 4) // 4},
            )

        def on_to_many(self, u, far):
            at = lax.rem(far, 5)
            base = self.base - 5 * dm + far - at if self.whole else self.base
            return remote(
                self.relay.at[0, u],
                self.dst.at[base + at],
                self.send.at[0, u],
                self.recv.at[0, at],
                {"dp": far // 5},
            )

        def arrived(self, ref, sem):
            remote(ref, ref, self.send.at[0, 0], sem, {"seq": sib}).wait_recv()

        def begin(self):
            class Step:
                few = staticmethod(self.few_out)
                many = staticmethod(lambda u, i, far: self.many_out(u, i, far).start())
                straight = staticmethod(lambda u, i: self.straight_out(u).start())
                between = staticmethod(lambda u, i, far: None)

            units_of(Step)

        def relay_on(self):
            def between(u, i, far):
                self.arrived(self.relay.at[0, u], self.recv.at[0, u])
                self.on_to_many(u, far).start()
                self.arrived(self.relay.at[1, u], self.recv.at[1, u])
                self.on_to_few(u).start()

            class Step:
                few = staticmethod(lambda u, i: None)
                many = staticmethod(lambda u, i, far: None)
                straight = staticmethod(lambda u, i: None)

            Step.between = staticmethod(between)
            units_of(Step)

        def end(self):
            class Step:
                few = staticmethod(lambda u, i: self.arrived(self.place(u), self.recv.at[0, u]))
                many = staticmethod(
                    lambda u, i, far: self.arrived(self.place(u), self.recv.at[0, u])
                )
                straight = staticmethod(lambda u, i: self.arrived(self.place(u), self.recv.at[0, u]))
                between = staticmethod(lambda u, i, far: None)

            units_of(Step)

        def sent(self):
            def done(k, u):
                remote(
                    self.src.at[u], self.src.at[u], self.send.at[k, u], self.recv.at[0, u], {"seq": sib}
                ).wait_send()

            def between(u, i, far):
                done(1, u)
                done(0, u)

            class Step:
                few = staticmethod(lambda u, i: done(0, u))
                many = staticmethod(lambda u, i, far: done(0, u))
                straight = staticmethod(lambda u, i: done(0, u))

            Step.between = staticmethod(between)
            units_of(Step)

    def kept(step):
        for u in range(5):
            i = 5 * dm + u

            @pl.when(me < 3)
            def _(u=u, i=i):
                @pl.when(i < 8)
                def _():
                    step(u)

            @pl.when(me == 3)
            def _(u=u):
                step(u)

            @pl.when(me > 3)
            def _(u=u, i=i):
                @pl.when(i < 32)
                def _():
                    step(u)

    greet(me, dm)
    for load in loads:
        load.start()

    row = lax.broadcasted_iota(jnp.int32, (TOK, 1), 0)
    place = jnp.where(row < SPAN, span_ref[0, me] * SPAN + row, span_ref[1, me] * SPAN + row - SPAN)
    def own_rows():
        x_rows = x_ref[...].astype(F32)
        centered = x_rows - jnp.mean(x_rows, axis=-1, keepdims=True)
        inv_std = lax.rsqrt(jnp.mean(centered * centered, axis=-1, keepdims=True) + NORM_EPS)
        return x_rows, centered * inv_std, inv_std

    def own_cot():
        return jnp.where(place < len_ref[0], cot_ref[...].astype(F32), 0.0)

    loads[0].wait()
    xh_all[pl.ds(2 * me, 2)] = own_rows()[1].astype(BF16).reshape(2, SPAN, D)

    loads[1].wait()
    loads[2].wait()
    small[...] = jnp.zeros((128, 128), F32)
    small[0:8, 0:VEC_ROWS] = vectors_ref[...]
    vec_t = small[0:8, 0:64]
    for s in range(SEQ):
        take = [w_in_ref[:, 64 * int(p) : 64 * int(p) + 64] for p in PIECES[s]]
        qkv = jnp.concatenate(take[:3] + [vec_t], axis=1)
        win_own[s] = jnp.concatenate([jnp.concatenate(take[3:], axis=1), qkv], axis=0).astype(BF16)
    loads[4].wait()
    for u in range(5):
        wout_own[u] = fold(w_out_ref[8 * u : 8 * u + 8]).astype(BF16)

    def keep_unit(u):
        wout_all[5 * dm + u] = wout_own[u]

    kept(keep_unit)
    loads[3].wait()
    cot_own = own_cot()
    cot_all[pl.ds(2 * me, 2)] = cot_own.astype(BF16).reshape(2, SPAN, D)
    cot_sum = jnp.sum(cot_own, axis=0, keepdims=True)
    vg[...] = jnp.transpose(jnp.broadcast_to(cot_sum, (128, D)))
    keep = pltpu.make_async_copy(win_own.at[me], win_all.at[dm, me], local_sem.at[0])
    keep.start()

    @pl.loop(0, 32)
    def _(i):
        slot = jnp.int32(0)
        for s in range(SEQ):
            for j in range(2):
                slot = jnp.maximum(slot, jnp.where(span_ref[j, s] == i, 2 * s + j, 0))
        inv_ref[i] = slot

    def seq_turn(s, k):
        return lax.rem(s + 4 * k, SEQ)

    def dp_turn(d, k):
        return d // 4 * 4 + lax.rem(d + k, 4)

    x_tree = Tree(
        "seq",
        lambda slot, h: xh_all.at[2 * slot + h],
        me,
        seq_turn,
        mate,
        x_send.at[0],
        x_recv,
        True,
        sib,
        x_given.at[0],
    )
    cot_tree = Tree(
        "seq",
        lambda slot, h: cot_all.at[2 * slot + h],
        me,
        seq_turn,
        mate,
        c_send.at[0],
        c_recv,
        True,
        sib,
        c_given.at[0],
    )
    in_tree = Tree(
        "dp",
        lambda slot, h: win_all.at[slot, pl.ds(8 * h, 8)],
        dm,
        dp_turn,
        dp_mate,
        l_send.at[0],
        l_recv,
        False,
    )
    out_tree = Tree(
        "dp",
        lambda slot, h: wout_all.at[pl.ds(5 * slot + 2 * h, 2 + h)],
        dm,
        dp_turn,
        dp_mate,
        o_send.at[0],
        o_recv,
        False,
    )

    def a_copy(k, to, frm):
        return remote(
            win_own.at[to], win_all.at[dm, frm], a_send.at[0], a_recv.at[0], {"seq": to}
        )

    await_greetings()

    @pl.loop(1, SEQ)
    def _(k):
        a_copy(k, lax.rem(me + k, SEQ), me).start()

    out_trade = Trade(wout_own, wout_all, w_relay, 5 * dm, w_send, w_recv)
    out_trade.whole = True
    out_trade.begin()
    x_tree.own_to_mate()
    x_tree.own_to_ring()
    keep.wait()

    all_here(win_own.at[pl.ds(0, SEQ - 1)], a_recv.at[0])

    in_tree.own_to_mate()
    in_tree.own_to_ring()
    out_trade.relay_on()
    x_tree.near_first(me)
    x_tree.of_mate((0,))
    in_tree.near_first(dm)
    x_tree.near_rest(me)
    x_tree.of_mate((1,))
    in_tree.near_rest(dm)
    in_tree.of_mate()
    x_tree.far_of_me()
    in_tree.far_of_me()
    cot_tree.own_to_ring()

    def unpack(column):
        def step(sb, carry):
            cq, cf = carry
            tiles = [win_all[4 * column + y, sb].astype(F32) for y in range(4)]
            ff = jnp.concatenate([t[:8] for t in tiles], axis=0)
            qk = jnp.concatenate([t[8:] for t in tiles], axis=0)
            rows = pl.ds(pl.multiple_of(sb * 64 + 32 * column, 32), 32)
            gain_a, bias_a, gain_m, bias_m = (qk[:, 192 + i : 193 + i] for i in range(4))
            wr[rows] = jnp.concatenate([ff, qk], axis=1).astype(BF16)
            folded = jnp.where(lane_iota(qk.shape) < 192, qk * gain_a, 0.0)
            wp[rows] = jnp.concatenate([ff * gain_m, folded], axis=1).astype(BF16)
            return (
                cq + jnp.sum(qk * bias_a, axis=0, keepdims=True),
                cf + jnp.sum(ff * bias_m, axis=0, keepdims=True),
            )

        return step

    zero_row = jnp.zeros((1, 256), F32)
    sums = lax.fori_loop(0, SEQ, unpack(dm // 4), (zero_row, zero_row))
    in_tree.near_of_mate()
    x_tree.near_of_mate()
    out_trade.end()
    out_tree.own_to_mate()
    out_tree.own_to_ring()
    cot_tree.own_to_mate()
    in_tree.far_of_mate()
    x_tree.far_of_mate()
    cq, cf = lax.fori_loop(0, SEQ, unpack(dp_mate // 4), sums)

    slab = jnp.transpose(wr[:, 384:512].astype(F32))
    vec_ref[...] = slab[64:80]
    loads[5].wait()
    loads[6].wait()

    hid = []
    for r in range(4):
        w = hidden_index(me, r)
        rows = pl.ds(pl.multiple_of(lax.rem(w, 16) * 64, 64), 64)
        part = wr[rows, 384:512].astype(F32)
        lane = 64 + 9 + w // 16
        hid.append(
            jnp.sum(jnp.where(lane_iota(part.shape) == lane, part, 0.0), axis=1, keepdims=True)
        )
    hid = jnp.concatenate(hid, axis=0)
    cf = cf + jnp.transpose(jnp.broadcast_to(hid, (256, 128)))[0:1]

    head_rows = pl.ds(pl.multiple_of(head * 64, 64), 64)
    head_vecs = wr[head_rows, 384:512].astype(F32)
    bq, bk, bv = (head_vecs[:, 68 + i : 69 + i] for i in range(3))

    all_here(xh_all.at[pl.ds(0, 16)], x_given.at[0])

    aug = jnp.where(lax.broadcasted_iota(jnp.int32, (64, CH), 0) == 0, 1.0, 0.0)
    zeros_aug = jnp.zeros((64, CH), F32)

    def rotate_t(u, cosine, sine, sign):
        first, second = u[0:8], u[8:16]
        return jnp.concatenate(
            [
                first * cosine - sign * (second * sine),
                second * cosine + sign * (first * sine),
                u[16:],
            ],
            axis=0,
        )

    def project(i):
        start = pl.multiple_of(i * CH, CH)
        rows = pl.ds(start, CH)
        xh = jnp.concatenate([xh_all[inv_ref[8 * i + k]] for k in range(8)], axis=0)
        xs[rows] = xh
        first = dot(xh, wp[...])
        qkv = jnp.transpose(first[:, 256:] + cq)
        cosine, sine = cos_ref[:, rows], sin_ref[:, rows]
        q = rotate_t(qkv[0:64] + bq, cosine, sine, 1.0) * 0.125
        k = rotate_t(qkv[64:128] + bk, cosine, sine, 1.0)
        v = qkv[128:192] + bv
        q_full = jnp.concatenate([q, aug], axis=0)
        past = (start + lane_iota((64, CH))) >= len_ref[0]
        k_full = jnp.concatenate([k, jnp.where(past, NEG_FILL, 0.0) * aug], axis=0)
        v_full = jnp.concatenate([v, zeros_aug], axis=0)
        qt[:, rows] = q_full.astype(BF16)
        kt[:, rows] = k.astype(BF16)
        vt[:, rows] = v.astype(BF16)
        qn[rows] = jnp.transpose(q_full).astype(BF16)
        kn[rows] = jnp.transpose(k_full).astype(BF16)
        vn[rows] = jnp.transpose(v_full).astype(BF16)
        pre = first[:, :256] + cf
        cdf = 0.5 * (1.0 + lax.erf(pre * (1.0 / math.sqrt(2.0))))
        pdf = jnp.exp(-0.5 * pre * pre) * (1.0 / math.sqrt(2.0 * math.pi))
        activ = pre * cdf
        joined[pl.ds(8 * i, 8), :, 0:256] = activ.astype(BF16).reshape(8, SPAN, 256)
        joined_t[0:256, rows] = jnp.transpose(activ).astype(BF16)
        dact[rows] = cdf + pre * pdf

    project(0)
    cot_tree.near_of_me()
    out_tree.near_of_me()
    out_tree.of_mate()
    project(1)
    project(2)
    cot_tree.of_mate()
    project(3)
    cot_tree.far_of_me()
    out_tree.near_of_mate()
    out_tree.far_of_me()
    half = CH // 2

    def tiles(qi):
        below = [(kc * CH, CH, qi * CH, CH) for kc in range(qi)]
        return below + [(qi * CH, half, qi * CH, CH), (qi * CH + half, half, qi * CH + half, half)]

    def scores(k0, keys, q0, queries):
        s = dot(kn[k0 : k0 + keys], qt[:, q0 : q0 + queries])
        if k0 >= q0:
            shape = (keys, queries)
            seen = lax.broadcasted_iota(jnp.int32, shape, 0) <= lane_iota(shape)
            s = jnp.where(seen, s, NEG_FILL)
        return s

    def spread(value, queries, fill):
        if queries == CH:
            return value
        return jnp.concatenate([jnp.full_like(value, fill), value], axis=1)

    for qi in range(NCH):
        lanes = slice(qi * CH, (qi + 1) * CH)
        parts = [(t, scores(*t)) for t in tiles(qi)]
        tops = [spread(jnp.max(s, axis=0, keepdims=True), t[3], NEG_FILL) for t, s in parts]
        top = functools.reduce(jnp.maximum, tops)
        total = jnp.zeros((1, CH), F32)
        out = jnp.zeros((64, CH), F32)
        for (k0, keys, _, queries), s in parts:
            p = jnp.exp(s - top[:, CH - queries :])
            total = total + spread(jnp.sum(p, axis=0, keepdims=True), queries, 0.0)
            out = out + spread(dot(vt[:, k0 : k0 + keys], p.astype(BF16)), queries, 0.0)
        out = out / total
        ot[:, lanes] = out
        lse[:, lanes] = jnp.broadcast_to(top + jnp.log(total), (8, CH))
        joined_t[256:320, lanes] = out.astype(BF16)
        joined[8 * qi : 8 * qi + 8, :, 256:320] = (
            jnp.transpose(out).astype(BF16).reshape(8, SPAN, HEAD)
        )
    out_tree.far_of_mate()

    def put_units(base, at, count):
        @pl.loop(0, count // 2)
        def _(i):
            pair = [unfold(wout_all[base + 2 * i + j].astype(F32)) for j in range(2)]
            rows = pl.ds(pl.multiple_of(at + i * 16, 16), 16)
            wo[rows] = jnp.concatenate(pair, axis=0).astype(BF16)

    late = (me + 12) // 16
    put_units(8 * (1 - late), 0, 32)
    put_units(32 * late, 256, 8)

    def of_chips(ref, chips):
        return jnp.concatenate(
            [ref[span_ref[i % 2, 2 * j + i // 2]] for j in chips for i in range(4)], axis=0
        )

    order = [(mate, 2), (mate, 1), (mate, 3), (me, 2), (me, 3), (me, 1), (mate, 0), (me, 0)]

    class ChipSums:
        def __init__(self, part, buf, sib_buf, land, s_send, s_recv, send, recv):
            self.part, self.buf, self.sib_buf, self.land = part, buf, sib_buf, land
            self.s_send, self.s_recv = s_send, s_recv
            self.tree = SumTree(
                "seq",
                lambda slot, h: buf.at[2 * slot + h],
                land,
                me,
                seq_turn,
                mate,
                send,
                recv,
            )

        def to_sib(self, j):
            return remote(
                self.buf.at[pl.ds(4 * j + 2 - 2 * core, 2)],
                self.sib_buf.at[j],
                self.s_send,
                self.s_recv.at[j],
                {"seq": sib},
            )

        def compute(self, n):
            chips = [seq_turn(*order[m]) // 2 for m in (n, n + 1)]
            value = self.part(chips).astype(BF16).reshape(8, SPAN, D)
            for m, j in enumerate(chips):
                self.buf[pl.ds(4 * j, 4)] = value[4 * m : 4 * m + 4]
                self.to_sib(j).start()

        def pair(self, n):
            j = seq_turn(*order[n]) // 2
            self.to_sib(j).wait_recv()
            mine = pl.ds(4 * j + 2 * core, 2)
            self.buf[mine] = (self.buf[mine].astype(F32) + self.sib_buf[j].astype(F32)).astype(BF16)
            if n == 0:
                self.tree.far_of_mate()
            elif n < 3:
                self.tree.near_of_mate(order[n][1])
            elif n in (4, 5):
                self.tree.near_early(order[n][1])

        def begin(self, between=()):
            for n in range(8):
                if n % 2 == 0:
                    self.compute(n)
                for at, step in between:
                    if at == n:
                        step()
                if n > 2:
                    self.pair(n - 3)
            self.pair(5)

        def of_mate(self):
            self.pair(6)
            self.tree.of_mate()
            self.pair(7)

        def total(self):
            return self.tree.total()

        def sent(self):
            all_sent(self.land, self.tree.send)
            all_sent(self.sib_buf, self.s_send)

    po = ChipSums(
        lambda chips: dot(of_chips(joined, chips), wo[...]),
        xh_all,
        po_sib,
        po_land,
        ps_send.at[0],
        ps_recv,
        p_send.at[0],
        p_recv,
    )
    hg = ChipSums(
        lambda chips: dot_nt(of_chips(mixed, chips), wp[...]),
        cot_all,
        hg_sib,
        hg_land,
        hs_send.at[0],
        hs_recv,
        h_send.at[0],
        h_recv,
    )
    all_sent(xh_all.at[pl.ds(0, 30)], x_send.at[0])
    po.begin(((2, cot_tree.near_of_mate), (4, cot_tree.far_of_mate)))
    all_here(cot_all.at[pl.ds(0, 16)], c_given.at[0])

    @pl.loop(0, NCH, unroll=True)
    def _(i):
        rows = pl.ds(pl.multiple_of(i * CH, CH), CH)
        cot = jnp.concatenate([cot_all[inv_ref[8 * i + k]] for k in range(8)], axis=0)
        cs[rows] = cot
        back = dot_nt(cot, wo[...])
        ag = back[:, 256:].astype(BF16).astype(F32)
        ag_t = jnp.transpose(ag)
        dot_n[rows] = ag.astype(BF16)
        dot_t[:, rows] = ag_t.astype(BF16)
        delta[:, rows] = jnp.broadcast_to(
            jnp.sum(ag_t * ot[:, rows], axis=0, keepdims=True), (8, CH)
        )
        pg = back[:, :256] * dact[rows]
        mixed[pl.ds(8 * i, 8), :, 0:256] = pg.astype(BF16).reshape(8, SPAN, 256)
        mixed_t[0:256, rows] = jnp.transpose(pg).astype(BF16)

    @pl.loop(0, 2, unroll=True)
    def _(i):
        left = dot(joined_t[...], cs[:, pl.ds(pl.multiple_of(i * 256, 256), 256)])
        right = dot(joined_t[...], cs[:, pl.ds(pl.multiple_of(i * 256 + 512, 256), 256)])
        units = jnp.concatenate([left.reshape(40, 8, 256), right.reshape(40, 8, 256)], axis=1)
        lanes = pl.ds(pl.multiple_of(i * 256, 256), 256)
        go_buf[pl.ds(8 * (1 - late), 32), :, lanes] = units[:32].astype(BF16)
        go_buf[pl.ds(32 * late, 8), :, lanes] = units[32:].astype(BF16)

    def grads_by_owner(dst, base, columns):
        sums = jnp.sum(
            mixed[:, :, base : base + 256].reshape(ROW, 256).astype(F32), axis=0, keepdims=True
        )

        @pl.loop(0, 4, unroll=True)
        def _(i):
            rows = pl.ds(pl.multiple_of(i * 256, 256), 256)
            h = jnp.transpose(dot(mixed_t[base : base + 256], xs[:, rows]))
            raw = wr[rows, base : base + 256].astype(F32)
            vecs = wr[rows, 384:512].astype(F32)
            gain, bias = (vecs[:, columns + 64 + j : columns + 65 + j] for j in range(2))
            grad = gain * h + bias * sums
            lanes = lane_iota((256, 128))
            extra = vg[rows]
            for j, col in enumerate((raw * h, raw * sums)):
                extra = extra + jnp.where(
                    lanes == 64 + columns + j, jnp.sum(col, axis=1, keepdims=True), 0.0
                )
            if base:
                grad = jnp.concatenate([grad[:, :128], grad[:, 128:] + extra], axis=1)
            else:
                vg[rows] = extra
            for j in range(2):
                pair = [
                    grad[128 * j + 64 * t : 128 * j + 64 * t + 64].reshape(8, 8, 256)
                    for t in range(2)
                ]
                dst[:, 2 * i + j] = jnp.concatenate(pair, axis=1).astype(BF16)

    def owner_sums(dst, land, send, recv):
        return ColumnSums(
            "dp",
            lambda slot: dst.at[slot],
            land,
            dm,
            dp_turn,
            dp_mate,
            send.at[0],
            recv,
        )

    gf_sums = owner_sums(gf, gf_land, gf_send, gf_recv)
    gq_sums = owner_sums(gq, gq_land, gq_send, gq_recv)
    go_sums = ColumnSums(
        "dp",
        lambda slot: go_buf.at[pl.ds(5 * slot, 5)],
        go_land,
        dm,
        dp_turn,
        dp_mate,
        go_send.at[0],
        go_recv,
    )
    lanes_d = lane_iota((D, 128))
    vg[...] = jnp.where((lanes_d == 71) | (lanes_d == 72), vg[...], 0.0)
    lanes_h = lane_iota((64, 128))
    cols_f = jnp.sum(mixed_t[0:256].astype(F32), axis=1, keepdims=True)
    for r in range(4):
        w = hidden_index(me, r)
        rows = pl.ds(pl.multiple_of(lax.rem(w, 16) * 64, 64), 64)
        vg[rows] += jnp.where(lanes_h == 64 + 9 + w // 16, cols_f[64 * r : 64 * r + 64], 0.0)
    grads_by_owner(gf, 0, 2)
    gf_sums.start()
    po.of_mate()

    go_sums.start()
    po.tree.far_of_me()

    for qi in reversed(range(NCH)):
        lanes = slice(qi * CH, (qi + 1) * CH)
        dq = jnp.zeros((64, CH), F32)
        for k0, keys, q0, queries in tiles(qi):
            at, cols = slice(k0, k0 + keys), slice(q0, q0 + queries)
            p = jnp.exp(scores(k0, keys, q0, queries) - lse[0:1, cols])
            dp = dot(vn[at, 0:64], dot_t[:, cols])
            ds = (p * (dp - delta[0:1, cols])).astype(BF16)
            dv = dot(p.astype(BF16), dot_n[cols])
            dk = dot(ds, qn[cols, 0:64])
            dq = dq + spread(dot(kt[:, at], ds), queries, 0.0)
            if qi == NCH - 1:
                dvn[at] = dv
                dkn[at] = dk
            else:
                dvn[at] += dv
                dkn[at] += dk
        dqt[:, lanes] = dq * 0.125
        if qi == 1:
            po.tree.near_late()
        if qi == 0:
            gf_sums.middle()

    @pl.loop(0, NCH, unroll=True)
    def _(i):
        rows = pl.ds(pl.multiple_of(i * CH, CH), CH)
        cosine, sine = cos_ref[:, rows], sin_ref[:, rows]
        dq = rotate_t(dqt[:, rows], cosine, sine, -1.0)
        dk = rotate_t(jnp.transpose(dkn[rows]), cosine, sine, -1.0)
        dv = jnp.transpose(dvn[rows])
        full = jnp.concatenate([dq, dk, dv, zeros_aug], axis=0)
        mixed_t[256:512, rows] = full.astype(BF16)
        mixed[pl.ds(8 * i, 8), :, 256:512] = jnp.transpose(full).astype(BF16).reshape(8, SPAN, 256)

    cols_q = jnp.sum(mixed_t[256:448].astype(F32), axis=1, keepdims=True)
    for i in range(3):
        vg[head_rows] += jnp.where(lanes_h == 68 + i, cols_q[64 * i : 64 * i + 64], 0.0)
    grads_by_owner(gq, 256, 0)
    gq_sums.start()

    all_sent(cot_all.at[pl.ds(0, 30)], c_send.at[0])

    def to_owner(part, total, send, recv, k, to, frm):
        return remote(part.at[to], total.at[frm], send.at[0], recv.at[0], {"seq": to})

    def own_sums(part, total, send, recv):
        @pl.loop(1, SEQ)
        def _(k):
            to_owner(part, total, send, recv, k, lax.rem(me + k, SEQ), me).start()

        total[me] = part[me]

    def own_arrived(part, total, send, recv):
        all_here(total.at[pl.ds(0, SEQ - 1)], recv.at[0])

    def squares_of(value):
        return jnp.sum(jnp.sum(value * value, axis=0), axis=0, keepdims=True)

    def hidden_on():
        f_part[...] = gf_sums.total().reshape(SEQ, 8, 256)
        own_sums(f_part, f_sum, bf_send, bf_recv)

    hg.begin(((2, go_sums.middle), (4, hidden_on)))
    gq_sums.middle()
    out_total = go_sums.total()
    out_part[...] = out_total

    out_back = Trade(out_part, wout_sum, v_relay, 0, v_send, v_recv)
    out_back.whole = False

    def keep_total(u):
        wout_sum[u] = out_part[u]

    out_back.begin()
    kept(keep_total)
    out_squares = squares_of(out_total)
    squares = squares_of(f_part[...]) + out_squares[:, :256] + out_squares[:, 256:]

    hg.tree.far_of_me()
    total = gq_sums.total().reshape(SEQ, 8, 256)
    weights = jnp.where(lane_iota(total.shape) < 192, total, 0.0)
    squares = squares + squares_of(weights)
    tile_a[...] = jnp.transpose(total[:, :, 128:].reshape(128, 128))[64:80]
    tile_a[15:16] = squares[:, :128] + squares[:, 128:]

    def ta_copy(k, to, frm):
        return remote(tile_a, got_a.at[frm], ta_send.at[0], ta_recv.at[0], {"seq": to})

    @pl.loop(1, SEQ)
    def _(k):
        ta_copy(k, lax.rem(me + k, SEQ), me).start()

    got_a[me] = tile_a[...]
    q_part[...] = total
    own_sums(q_part, q_sum, bq_send, bq_recv)
    hg.of_mate()
    hg.tree.near_late()
    out_back.relay_on()
    all_here(got_a.at[pl.ds(0, SEQ - 1)], ta_recv.at[0])
    sums = jnp.sum(got_a[...], axis=0)
    vec_total = jnp.where(lax.broadcasted_iota(jnp.int32, sums.shape, 0) < VEC_ROWS, sums, 0.0)
    row = sums[15:16] + jnp.sum(vec_total * vec_total, axis=0, keepdims=True)
    tile_b[...] = jnp.broadcast_to(jnp.sum(row, axis=1, keepdims=True), (8, 128))

    def tb_copy(k, to, frm):
        return remote(tile_b, got_b.at[frm], tb_send.at[0], tb_recv.at[0], {"dp": to})

    @pl.loop(1, DP)
    def _(k):
        tb_copy(k, lax.rem(dm + k, DP), dm).start()

    got_b[dm] = tile_b[...]
    small[...] = jnp.zeros((128, 128), F32)
    small[0:16] = vec_total
    small[...] = jnp.transpose(small[...])
    vec_grad[...] = small[pl.ds(pl.multiple_of(8 * me, 8), 8)]
    vec_store.start()
    own_arrived(f_part, f_sum, bf_send, bf_recv)
    x_rows, x_hat, inv_std = own_rows()
    cot_own = own_cot()
    block_out[...] = (x_rows + po.total() + (vec_ref[7:8] + vec_ref[8:9])).astype(BF16)
    block_store.start()
    own_arrived(q_part, q_sum, bq_send, bq_recv)
    for s in range(SEQ):
        for j, p in enumerate(PIECES[s]):
            at = 64 * int(p)
            if j < 3:
                grad_in[:, at : at + 64] = q_sum[s, :, 64 * j : 64 * j + 64]
            else:
                grad_in[:, at : at + 64] = f_sum[s, :, 64 * j - 192 : 64 * j - 128]
    in_store.start()
    out_back.end()
    for u in range(5):
        grad_out[8 * u : 8 * u + 8] = unfold(wout_sum[u])
    out_store.start()

    all_here(got_b.at[pl.ds(0, DP - 1)], tb_recv.at[0])
    everything = jnp.sum(got_b[...], axis=0)
    square_ref[...] = jnp.broadcast_to(everything[:, 0:1], (8, 128))
    square_store.start()
    grad = hg.total()
    back = (
        grad
        - jnp.mean(grad, axis=-1, keepdims=True)
        - x_hat * jnp.mean(grad * x_hat, axis=-1, keepdims=True)
    )
    input_grad[...] = (cot_own + inv_std * back).astype(BF16)
    grad_store.start()
    po.sent()
    hg.sent()
    out_trade.sent()
    out_back.sent()
    for sums in (gf_sums, gq_sums, go_sums):
        sums.sent()
    all_sent(win_all.at[pl.ds(0, 7)], l_send.at[0])
    all_sent(wout_all.at[pl.ds(0, 35)], o_send.at[0])
    all_sent(win_own.at[pl.ds(0, SEQ - 1)], a_send.at[0])
    all_sent(got_a.at[pl.ds(0, SEQ - 1)], ta_send.at[0])
    all_sent(got_b.at[pl.ds(0, DP - 1)], tb_send.at[0])
    all_sent(f_part.at[pl.ds(0, SEQ - 1)], bf_send.at[0])
    all_sent(q_part.at[pl.ds(0, SEQ - 1)], bq_send.at[0])
    for store in stores:
        store.wait()


def layer_call(span, length, x, cot, w_in, w_out, vectors):
    freqs = np.float32(THETA_BASE) ** (-2.0 * np.arange(ROT // 2) / ROT)
    angles = np.arange(ROW, dtype=np.float32)[None, :] * freqs.astype(np.float32)[:, None]
    cosine, sine = np.cos(angles).astype(np.float32), np.sin(angles).astype(np.float32)
    smem = pl.BlockSpec(memory_space=pltpu.SMEM)
    anywhere = pl.BlockSpec(memory_space=pl.ANY)
    sds = jax.ShapeDtypeStruct
    dma = pltpu.SemaphoreType.DMA

    def buf(shape, dtype=BF16):
        return pltpu.VMEM(shape, dtype)

    return pl.pallas_call(
        layer_kernel,
        out_shape=(
            sds((TOK, D), BF16),
            sds((TOK, D), BF16),
            sds((8, 7 * D), F32),
            sds((40, D), F32),
            sds((8, 128), F32),
            sds((8, 128), F32),
        ),
        in_specs=[smem] * 2 + [anywhere] * 7,
        out_specs=[anywhere] * 6,
        scratch_shapes=[
            buf((TOK, D)),
            buf((TOK, D)),
            buf((8, 7 * D), F32),
            buf((40, D), F32),
            buf((8, VEC_ROWS), F32),
            buf((8, ROW), F32),
            buf((8, ROW), F32),
            buf((TOK, D)),
            buf((TOK, D)),
            buf((8, 7 * D), F32),
            buf((40, D), F32),
            buf((SEQ, 8, 256), F32),
            buf((SEQ, 8, 256), F32),
            buf((5, 16, 512), F32),
            buf((8, 128), F32),
            buf((8, 128), F32),
            dma((7,)),
            dma((6,)),
            pltpu.SMEM((32,), jnp.int32),
            buf((32, SPAN, D)),
            buf((32, SPAN, D)),
            buf((SEQ, 16, 256)),
            buf((DP, SEQ, 16, 256)),
            buf((40, 16, 512)),
            buf((5, 16, 512)),
            buf((2, 5, 16, 512)),
            buf((2, 5, 16, 512), F32),
            buf((128, 128), F32),
            buf((16, D), F32),
            buf((ROW, D)),
            buf((ROW, D)),
            buf((D, 512)),
            buf((D, 512)),
            buf((320, D)),
            buf((128, ROW)),
            buf((ROW, 128)),
            buf((64, ROW)),
            buf((ROW, 128)),
            buf((64, ROW)),
            buf((ROW, 128)),
            buf((64, ROW)),
            buf((ROW, 64)),
            buf((64, ROW), F32),
            buf((8, ROW), F32),
            buf((8, ROW), F32),
            buf((32, SPAN, 320)),
            buf((320, ROW)),
            buf((ROW, 256), F32),
            buf((32, SPAN, 512)),
            buf((512, ROW)),
            buf((64, ROW), F32),
            buf((ROW, 64), F32),
            buf((ROW, 64), F32),
            buf((D, 128), F32),
            buf((40, 16, 512)),
            buf((5, 16, 512), F32),
            buf((DP, 8, 16, 256)),
            buf((DP, 8, 16, 256)),
            buf((8, 2, SPAN, D)),
            buf((8, 2, SPAN, D)),
            buf((7, 2, SPAN, D)),
            buf((7, 2, SPAN, D)),
            buf((8, 8, 16, 256)),
            buf((8, 8, 16, 256)),
            buf((8, 5, 16, 512)),
            buf((SEQ, 8, 256), F32),
            buf((SEQ, 8, 256), F32),
            buf((16, 128), F32),
            buf((8, 128), F32),
            buf((SEQ, 16, 128), F32),
            buf((DP, 8, 128), F32),
            dma((1,)),
            dma((1,)),
            dma((1,)),
            dma((1,)),
            dma((8, 2)),
            dma((1,)),
            dma((1,)),
            dma((8, 2)),
            dma((1,)),
            dma((1,)),
            dma((DP, 2)),
            dma((1,)),
            dma((DP, 2)),
            dma((2, 5)),
            dma((2, 5)),
            dma((1,)),
            dma((8,)),
            dma((1,)),
            dma((6,)),
            dma((1,)),
            dma((8,)),
            dma((1,)),
            dma((6,)),
            dma((1,)),
            dma((3,)),
            dma((1,)),
            dma((3,)),
            dma((1,)),
            dma((3,)),
            dma((2, 5)),
            dma((2, 5)),
            dma((1,)),
            dma((1,)),
            dma((1,)),
            dma((1,)),
            dma((1,)),
            dma((1,)),
            dma((1,)),
            dma((1,)),
        ],
        compiler_params=pltpu.CompilerParams(
            collective_id=0, has_side_effects=True, vmem_limit_bytes=VMEM_LIMIT
        ),
        name="layer_of_one_row",
    )(span, length, x, cot, w_in, w_out, vectors, jnp.asarray(cosine), jnp.asarray(sine))


def adam(weight, grad, first, second, factor, rate, decay):
    clipped = grad * factor
    first_new = BETA_ONE * first + (1.0 - BETA_ONE) * clipped
    second_new = BETA_TWO * second + (1.0 - BETA_TWO) * clipped * clipped
    first_hat = first_new / (1.0 - BETA_ONE**STEP)
    second_hat = second_new / (1.0 - BETA_TWO**STEP)
    weight_new = weight * (1.0 - rate * decay) - rate * first_hat / (
        jnp.sqrt(second_hat) + ADAM_EPS
    )
    return (weight_new, first_new, second_new, weight_new.astype(BF16))


UPDATE_IN = (
    ("block_out", (TOK, D), BF16),
    ("input_grad", (TOK, D), BF16),
    ("square", (8, 128), F32),
    ("grad_in", (8, 7 * D), F32),
    ("w_in", (8, 7 * D), F32),
    ("in_first", (8, 7 * D), F32),
    ("in_second", (8, 7 * D), F32),
    ("grad_out", (40, D), F32),
    ("w_out", (40, D), F32),
    ("out_first", (40, D), F32),
    ("out_second", (40, D), F32),
    ("vectors", (8, VEC_ROWS), F32),
    ("vec_first", (8, VEC_ROWS), F32),
    ("vec_second", (8, VEC_ROWS), F32),
    ("vec_grad", (8, 128), F32),
)
UPDATE_OUT = (
    ((TOK, D), BF16),
    ((TOK, D), BF16),
    ((8, 7 * D), F32),
    ((40, D), F32),
    ((8, VEC_ROWS), F32),
    ((8, 7 * D), F32),
    ((40, D), F32),
    ((8, VEC_ROWS), F32),
    ((8, 7 * D), F32),
    ((40, D), F32),
    ((8, VEC_ROWS), F32),
    ((8, 7 * D), BF16),
    ((40, D), BF16),
    ((8, VEC_ROWS), BF16),
)


def update_kernel(*refs):
    ins, refs = refs[: len(UPDATE_IN)], refs[len(UPDATE_IN) :]
    norm_ref, refs = refs[0], refs[1:]
    outs, refs = refs[: len(UPDATE_OUT)], refs[len(UPDATE_OUT) :]
    in_bufs, refs = refs[: len(UPDATE_IN)], refs[len(UPDATE_IN) :]
    out_bufs, (in_sem, out_sem) = refs[: len(UPDATE_OUT)], refs[len(UPDATE_OUT) :]
    loads = [
        pltpu.make_async_copy(a, b, in_sem.at[i]) for i, (a, b) in enumerate(zip(ins, in_bufs))
    ]
    stores = [
        pltpu.make_async_copy(in_bufs[i] if i < 2 else b, a, out_sem.at[i])
        for i, (a, b) in enumerate(zip(outs, out_bufs))
    ]
    order = list(range(2, len(loads))) + [0, 1]
    for i in order:
        loads[i].start()
    names = [name for name, _, _ in UPDATE_IN]

    def take(name):
        i = names.index(name)
        loads[i].wait()
        return in_bufs[i]

    def give(i, value):
        out_bufs[i][...] = value
        stores[i].start()

    norm = jnp.sqrt(take("square")[...])
    norm_ref[0, 0] = norm[0, 0]
    factor = jnp.minimum(1.0, CLIP_NORM / norm)[0:1, 0:1]

    for i in range(2):
        loads[i].wait()
        stores[i].start()

    def matrix(at, grad, weight, first, second, rate, decay):
        values = adam(
            take(weight)[...], grad, take(first)[...], take(second)[...], factor, rate, decay
        )
        for k, value in enumerate(values):
            give(at + 3 * k, value)

    matrix(2, take("grad_in")[...], "w_in", "in_first", "in_second", RATE_MATRIX, DECAY_RATE)
    matrix(3, take("grad_out")[...], "w_out", "out_first", "out_second", RATE_MATRIX, DECAY_RATE)
    grad_vec = take("vec_grad")[:, 0:VEC_ROWS]
    matrix(4, grad_vec, "vectors", "vec_first", "vec_second", RATE_VECTOR, 0.0)

    for store in stores:
        store.wait()


def update_call(*args):
    anywhere = pl.BlockSpec(memory_space=pl.ANY)
    dma = pltpu.SemaphoreType.DMA
    sds = jax.ShapeDtypeStruct
    return pl.pallas_call(
        update_kernel,
        out_shape=(sds((1, 1), F32),) + tuple(sds(shape, kind) for shape, kind in UPDATE_OUT),
        in_specs=[anywhere] * len(UPDATE_IN),
        out_specs=[pl.BlockSpec(memory_space=pltpu.SMEM)] + [anywhere] * len(UPDATE_OUT),
        scratch_shapes=[pltpu.VMEM(shape, kind) for _, shape, kind in UPDATE_IN]
        + [pltpu.VMEM(shape, kind) for shape, kind in UPDATE_OUT]
        + [dma((len(UPDATE_IN),)), dma((len(UPDATE_OUT),))],
        compiler_params=pltpu.CompilerParams(vmem_limit_bytes=UPDATE_LIMIT),
        name="clipped_update",
    )(*args)


def body(
    hidden_in,
    out_cot,
    in_weight,
    out_weight,
    vectors,
    in_first,
    in_second,
    out_first,
    out_second,
    vec_first,
    vec_second,
    lengths,
    span_of,
):
    block_out, input_grad, grad_in, grad_out, squares, vec_grad = layer_call(
        span_of.T, lengths, hidden_in[0], out_cot[0], in_weight, out_weight, vectors.T
    )
    norm, block_out, input_grad, *rest = update_call(
        block_out,
        input_grad,
        squares,
        grad_in,
        in_weight,
        in_first,
        in_second,
        grad_out,
        out_weight,
        out_first,
        out_second,
        vectors.T,
        vec_first.T,
        vec_second.T,
        vec_grad,
    )
    rest = [out.T if i % 3 == 2 else out for i, out in enumerate(rest)]
    return (block_out[None], input_grad[None], norm.reshape(()), *rest)


def solution(mesh):
    tokens = P("dp", "seq", None)
    matrix = P(("seq", "dp"), None)
    vector = P(None, ("seq", "dp"))
    return jax.shard_map(
        body,
        mesh=mesh,
        in_specs=(
            tokens,
            tokens,
            matrix,
            matrix,
            vector,
            matrix,
            matrix,
            matrix,
            matrix,
            vector,
            vector,
            P("dp"),
            P(),
        ),
        out_specs=(tokens, tokens, P()) + (matrix, matrix, vector) * 4,
        check_vma=False,
    )
```

```python
import functools
import math

import jax
import jax.numpy as jnp
import numpy as np
from jax import lax
from jax.experimental import pallas as pl
from jax.experimental.pallas import tpu as pltpu
from jax.sharding import PartitionSpec as P

D = 1024
FF = 4096
HEADS = 16
HEAD = 64
ROT = 16
STEP = 5
SEQ = 16
DP = 8
TOK = 128
ROW = 2048
SPAN = 64
VEC_ROWS = 13

NORM_EPS = 1e-05
NEG_FILL = -1e30
CLIP_NORM = 1.0
RATE_MATRIX = 0.02
RATE_VECTOR = 0.2
BETA_ONE = 0.5
BETA_TWO = 0.5
DECAY_RATE = 0.1
ADAM_EPS = 1e-08
THETA_BASE = 10000.0

F32 = jnp.float32
BF16 = jnp.bfloat16
MESH = pl.DeviceIdType.MESH
VMEM_LIMIT = 60 * 1024 * 1024
UPDATE_LIMIT = 60 * 1024 * 1024


def head_of(s):
    if s < 4:
        return 5 * s
    return 5 * ((s - 4) // 4) + 1 + (s - 4) % 4


def hidden_pieces(s):
    if s < 3:
        return [20 * s + 5 * r + 8 for r in range(4)]
    if s == 3:
        return [0, 1, 2, 3]
    return [5 * s - 16 + r for r in range(4)]


def column_pieces():
    rows = []
    for s in range(SEQ):
        h = head_of(s)
        rows.append([h, 16 + h, 32 + h] + [48 + w for w in hidden_pieces(s)])
    return np.array(rows, np.int32)


PIECES = column_pieces()


def head_index(s):
    late = (s + 12) // 16
    return (1 - late) * (5 * s) + late * (5 * ((s - 4) // 4) + 1 + lax.rem(s, 4))


def hidden_index(s, r):
    late, not_few = (s + 12) // 16, (s + 13) // 16
    return (
        (1 - not_few) * (20 * s + 5 * r + 8) + (not_few - late) * r + late * (5 * s - 16 + r)
    )


def remote(src, dst, send, recv, where):
    return pltpu.make_async_remote_copy(
        src_ref=src, dst_ref=dst, send_sem=send, recv_sem=recv, device_id=where, device_id_type=MESH
    )


def greet(me, dm):
    barrier = pltpu.get_barrier_semaphore()

    @pl.loop(1, SEQ)
    def _(k):
        pl.semaphore_signal(
            barrier, inc=1, device_id={"seq": lax.rem(me + k, SEQ)}, device_id_type=MESH
        )

    @pl.loop(1, DP)
    def _(k):
        pl.semaphore_signal(
            barrier, inc=1, device_id={"dp": lax.rem(dm + k, DP)}, device_id_type=MESH
        )


def await_greetings():
    pl.semaphore_wait(pltpu.get_barrier_semaphore(), SEQ + DP - 2)


def all_sent(ref, sem):
    remote(ref, ref, sem, sem, {"seq": 0}).wait_send()


def all_here(ref, sem):
    pltpu.make_async_copy(ref, ref, sem).wait()


class Tree:
    def __init__(self, axis, piece, me, turn, mate, send, recv, over_mate, sib=None, given=None):
        self.axis, self.piece, self.me, self.turn, self.mate = (axis, piece, me, turn, mate)
        self.send, self.recv, self.over_mate = send, recv, over_mate
        self.sib, self.given = sib, given
        self.per = 1 if sib is None else 2

    def put(self, slot, h, to):
        part = self.piece(slot, h)
        remote(part, part, self.send, self.arrival(slot, h), {self.axis: to}).start()

    def hand(self, slot, h):
        if self.sib is not None:
            part = self.piece(slot, h)
            remote(part, part, self.send, self.given, {self.axis: self.sib}).start()

    def arrival(self, slot, h):
        return self.recv.at[slot // self.per, h]

    def got(self, slot, h):
        part = self.piece(slot, h)
        remote(
            part, part, self.send, self.arrival(slot, h), {self.axis: self.mate}
        ).wait_recv()

    def own_to_ring(self):
        for h, k in ((0, 1), (1, 3), (1, 1), (0, 3)):
            self.put(self.me, h, self.turn(self.me, k))

    def own_to_mate(self):
        for h in range(2):
            self.put(self.me, h, self.mate)
        for h in range(2):
            self.hand(self.me, h)

    def of_mate(self, halves=(0, 1)):
        for h in halves:
            self.got(self.mate, h)
            for k in (1, 3):
                self.put(self.mate, h, self.turn(self.me, k))
            self.hand(self.mate, h)

    def near_first(self, base):
        for h, k in ((0, 3), (1, 1)):
            slot = self.turn(base, k)
            self.got(slot, h)
            self.put(slot, h, self.turn(self.me, 4 - k))
            self.hand(slot, h)

    def near_rest(self, base):
        for h, k in ((1, 3), (0, 1)):
            slot = self.turn(base, k)
            self.got(slot, h)
            self.hand(slot, h)

    def near(self, base):
        self.near_first(base)
        self.near_rest(base)

    def near_of_me(self):
        self.near(self.me)

    def far_of_me(self):
        slot = self.turn(self.me, 2)
        for h in range(2):
            self.got(slot, h)
            if self.over_mate:
                self.put(slot, h, self.mate)
            self.hand(slot, h)

    def near_of_mate(self):
        if not self.over_mate:
            return self.near(self.mate)
        for h in range(2):
            for k in (3, 1):
                slot = self.turn(self.mate, k)
                self.got(slot, h)
                self.hand(slot, h)

    def far_of_mate(self):
        slot = self.turn(self.mate, 2)
        for h in range(2):
            self.got(slot, h)
            self.hand(slot, h)


class SumTree:
    def __init__(self, axis, piece, landing, me, turn, mate, send, recv):
        self.axis, self.piece, self.me, self.turn, self.mate = (axis, piece, me, turn, mate)
        self.landing, self.send, self.recv = landing, send, recv

    def land(self, kind, h):
        return self.landing.at[kind, h]

    def arrival(self, kind, h):
        return self.recv.at[(h, 2, 2, 3 + h, 5, 5, 5)[kind]]

    def put(self, slot, kind, h, to):
        copy = remote(
            self.piece(slot, h),
            self.land(kind, h),
            self.send,
            self.arrival(kind, h),
            {self.axis: to},
        )
        copy.start()

    def add(self, slot, h, *kinds):
        part = self.piece(slot, h)
        total = part[...].astype(F32)
        for kind in kinds:
            total = total + self.land(kind, h)[...].astype(F32)
        part[...] = total.astype(BF16)

    def far_of_mate(self):
        for h in range(2):
            self.put(self.turn(self.mate, 2), 0, h, self.mate)

    def near_of_mate(self, k):
        for h in range(2):
            self.put(self.turn(self.mate, k), 2 if k == 1 else 1, h, self.turn(self.me, k))

    def near_early(self, k):
        h = 0 if k == 1 else 1
        self.put(self.turn(self.me, k), 5 if k == 1 else 4, h, self.turn(self.me, k))

    def far_of_me(self):
        slot = self.turn(self.me, 2)
        for h in range(2):
            all_here(self.land(0, h), self.arrival(0, h))
            self.add(slot, h, 0)
            self.put(slot, 3, h, self.turn(self.me, 3 - 2 * h))

    def near_late(self):
        for h in range(2):
            k = 3 - 2 * h
            slot = self.turn(self.me, k)
            all_here(self.land(3, h), self.arrival(3, h))
            self.add(slot, h, 3)
            self.put(slot, 4 + h, h, self.turn(self.me, k))

    def of_mate(self):
        all_here(self.landing.at[pl.ds(1, 2)], self.arrival(1, 0))
        for h in range(2):
            self.add(self.mate, h, 1, 2)
            self.put(self.mate, 6, h, self.mate)

    def begin(self):
        self.far_of_mate()
        for k in (1, 3):
            self.near_of_mate(k)
        for k in (1, 3):
            self.near_early(k)

    def total(self):
        all_here(self.landing.at[pl.ds(4, 3)], self.arrival(4, 0))
        parts = []
        for h in range(2):
            value = self.piece(self.me, h)[...].astype(F32)
            for kind in (4, 5, 6):
                value = value + self.land(kind, h)[...].astype(F32)
            parts.append(value)
        return jnp.concatenate(parts, axis=0)


class ColumnSums:
    def __init__(self, axis, piece, landing, me, turn, mate, send, recv):
        self.axis, self.piece, self.me, self.turn, self.mate = (axis, piece, me, turn, mate)
        self.land = lambda i: landing.at[i]
        self.lands = lambda i, n: landing.at[pl.ds(i, n)]
        self.send, self.recv = send, recv

    def copy(self, k, of_mate):
        to = self.turn(self.me, k)
        return remote(
            self.piece(self.turn(self.mate, k) if of_mate else to),
            self.land(4 * of_mate + 4 - k),
            self.send,
            self.recv.at[1 + of_mate],
            {self.axis: to},
        )

    def last(self):
        return remote(
            self.piece(self.mate),
            self.land(0),
            self.send,
            self.recv.at[0],
            {self.axis: self.mate},
        )

    def start(self):
        for of_mate in (1, 0):
            for k in (1, 3, 2):
                self.copy(k, of_mate).start()

    def summed(self, slot, of_mate):
        total = self.piece(slot)[...].astype(F32)
        all_here(self.lands(4 * of_mate + 1, 3), self.recv.at[1 + of_mate])
        for k in (1, 3, 2):
            total = total + self.land(4 * of_mate + 4 - k)[...].astype(F32)
        return total

    def middle(self):
        self.piece(self.mate)[...] = self.summed(self.mate, 1).astype(BF16)
        self.last().start()

    def total(self):
        value = self.summed(self.me, 0)
        self.last().wait_recv()
        return value + self.land(0)[...].astype(F32)

    def sent(self):
        all_sent(self.lands(0, 7), self.send)


def dot(a, b):
    return jnp.dot(a, b, preferred_element_type=F32)


def dot_nt(a, b):
    return lax.dot_general(a, b, (((1,), (1,)), ((), ())), preferred_element_type=F32)


def lane_iota(shape):
    return lax.broadcasted_iota(jnp.int32, shape, len(shape) - 1)


def fold(u):
    return jnp.concatenate([u[:, : D // 2], u[:, D // 2 :]], axis=0)


def unfold(u):
    return jnp.concatenate([u[:8], u[8:]], axis=1)


CH = 512
NCH = ROW // CH


def layer_kernel(
    span_ref,
    len_ref,
    x_any,
    cot_any,
    w_in_any,
    w_out_any,
    vectors_any,
    cos_any,
    sin_any,
    block_out_any,
    input_grad_any,
    grad_in_any,
    grad_out_any,
    square_any,
    vec_grad_any,
    x_ref,
    cot_ref,
    w_in_ref,
    w_out_ref,
    vectors_ref,
    cos_ref,
    sin_ref,
    block_out,
    input_grad,
    grad_in,
    grad_out,
    f_sum,
    q_sum,
    wout_sum,
    square_ref,
    vec_grad,
    load_sem,
    store_sem,
    inv_ref,
    xh_all,
    cot_all,
    win_own,
    win_all,
    wout_all,
    wout_own,
    w_relay,
    v_relay,
    small,
    vec_ref,
    xs,
    cs,
    wr,
    wp,
    wo,
    qt,
    qn,
    kt,
    kn,
    vt,
    vn,
    dot_t,
    dot_n,
    ot,
    scale,
    exps,
    delta,
    joined,
    joined_t,
    dact,
    mixed,
    mixed_t,
    dqt,
    dkn,
    dvn,
    vg,
    go_buf,
    out_part,
    gf,
    gq,
    po_sib,
    hg_sib,
    po_land,
    hg_land,
    gf_land,
    gq_land,
    go_land,
    f_part,
    q_part,
    tile_a,
    tile_b,
    got_a,
    got_b,
    local_sem,
    a_send,
    a_recv,
    x_send,
    x_recv,
    x_given,
    c_send,
    c_recv,
    c_given,
    l_send,
    l_recv,
    o_send,
    o_recv,
    w_send,
    w_recv,
    ps_send,
    ps_recv,
    p_send,
    p_recv,
    hs_send,
    hs_recv,
    h_send,
    h_recv,
    gf_send,
    gf_recv,
    gq_send,
    gq_recv,
    go_send,
    go_recv,
    v_send,
    v_recv,
    bf_send,
    bf_recv,
    bq_send,
    bq_recv,
    ta_send,
    ta_recv,
    tb_send,
    tb_recv,
):
    me = lax.axis_index("seq")
    dm = lax.axis_index("dp")
    core = lax.rem(me, 2)
    chip = me // 2
    sib = me + 1 - 2 * core
    mate = me + 2 - 4 * lax.rem(chip, 2)
    dp_mate = lax.rem(dm + 4, DP)
    head = head_index(me)
    loads = [
        pltpu.make_async_copy(a, b, load_sem.at[i])
        for i, (a, b) in enumerate(
            (
                (x_any, x_ref),
                (w_in_any, w_in_ref),
                (vectors_any, vectors_ref),
                (cot_any, cot_ref),
                (w_out_any, w_out_ref),
                (cos_any, cos_ref),
                (sin_any, sin_ref),
            )
        )
    ]
    block_store, grad_store, in_store, out_store, square_store, vec_store = stores = [
        pltpu.make_async_copy(a, b, store_sem.at[i])
        for i, (a, b) in enumerate(
            (
                (block_out, block_out_any),
                (input_grad, input_grad_any),
                (grad_in, grad_in_any),
                (grad_out, grad_out_any),
                (square_ref, square_any),
                (vec_grad, vec_grad_any),
            )
        )
    ]
    def units_of(step):
        for u in range(5):
            i = 5 * dm + u

            @pl.when(me < 3)
            def _(u=u, i=i):
                @pl.when(i >= 8)
                def _():
                    step.few(u, i)

            @pl.when(me > 3)
            def _(u=u, i=i):
                r = lax.rem(me, 4)

                @pl.when(i >= 32)
                def _():
                    @pl.when(r < 3)
                    def _():
                        step.many(u, i, 8 + 8 * r + i - 32)

                    @pl.when(r == 3)
                    def _():
                        step.straight(u, i)

                @pl.when((i >= 8 + 8 * r) & (i < 16 + 8 * r) & (r < 3))
                def _():
                    step.between(u, i, 32 + lax.rem(i, 8))

    class Trade:
        def __init__(self, src, dst, relay, base, send, recv):
            self.src, self.dst, self.relay, self.base = src, dst, relay, base
            self.send, self.recv = send, recv

        def place(self, u):
            return self.dst.at[self.base + u]

        def few_out(self, u, i):
            to = 4 * me + 3 + i // 8
            last = i >= 32

            @pl.when(last)
            def _():
                remote(
                    self.src.at[u], self.place(u), self.send.at[0, u], self.recv.at[0, u], {"seq": to}
                ).start()

            @pl.when(jnp.logical_not(last))
            def _():
                remote(
                    self.src.at[u],
                    self.relay.at[0, u],
                    self.send.at[0, u],
                    self.recv.at[0, u],
                    {"seq": to},
                ).start()

        def many_out(self, u, i, far):
            at = lax.rem(far, 5)
            return remote(
                self.src.at[u],
                self.relay.at[1, at],
                self.send.at[0, u],
                self.recv.at[1, at],
                {"dp": far // 5},
            )

        def straight_out(self, u):
            return remote(
                self.src.at[u],
                self.place(u),
                self.send.at[0, u],
                self.recv.at[0, u],
                {"seq": (me - 4) // 4},
            )

        def on_to_few(self, u):
            return remote(
                self.relay.at[1, u],
                self.place(u),
                self.send.at[1, u],
                self.recv.at[0, u],
                {"seq": (me - 4) // 4},
            )

        def on_to_many(self, u, far):
            at = lax.rem(far, 5)
            base = self.base - 5 * dm + far - at if self.whole else self.base
            return remote(
                self.relay.at[0, u],
                self.dst.at[base + at],
                self.send.at[0, u],
                self.recv.at[0, at],
                {"dp": far // 5},
            )

        def arrived(self, ref, sem):
            remote(ref, ref, self.send.at[0, 0], sem, {"seq": sib}).wait_recv()

        def begin(self):
            class Step:
                few = staticmethod(self.few_out)
                many = staticmethod(lambda u, i, far: self.many_out(u, i, far).start())
                straight = staticmethod(lambda u, i: self.straight_out(u).start())
                between = staticmethod(lambda u, i, far: None)

            units_of(Step)

        def relay_on(self):
            def between(u, i, far):
                self.arrived(self.relay.at[0, u], self.recv.at[0, u])
                self.on_to_many(u, far).start()
                self.arrived(self.relay.at[1, u], self.recv.at[1, u])
                self.on_to_few(u).start()

            class Step:
                few = staticmethod(lambda u, i: None)
                many = staticmethod(lambda u, i, far: None)
                straight = staticmethod(lambda u, i: None)

            Step.between = staticmethod(between)
            units_of(Step)

        def end(self):
            class Step:
                few = staticmethod(lambda u, i: self.arrived(self.place(u), self.recv.at[0, u]))
                many = staticmethod(
                    lambda u, i, far: self.arrived(self.place(u), self.recv.at[0, u])
                )
                straight = staticmethod(lambda u, i: self.arrived(self.place(u), self.recv.at[0, u]))
                between = staticmethod(lambda u, i, far: None)

            units_of(Step)

        def sent(self):
            def done(k, u):
                remote(
                    self.src.at[u], self.src.at[u], self.send.at[k, u], self.recv.at[0, u], {"seq": sib}
                ).wait_send()

            def between(u, i, far):
                done(1, u)
                done(0, u)

            class Step:
                few = staticmethod(lambda u, i: done(0, u))
                many = staticmethod(lambda u, i, far: done(0, u))
                straight = staticmethod(lambda u, i: done(0, u))

            Step.between = staticmethod(between)
            units_of(Step)

    def kept(step):
        for u in range(5):
            i = 5 * dm + u

            @pl.when(me < 3)
            def _(u=u, i=i):
                @pl.when(i < 8)
                def _():
                    step(u)

            @pl.when(me == 3)
            def _(u=u):
                step(u)

            @pl.when(me > 3)
            def _(u=u, i=i):
                @pl.when(i < 32)
                def _():
                    step(u)

    greet(me, dm)
    for load in loads:
        load.start()

    row = lax.broadcasted_iota(jnp.int32, (TOK, 1), 0)
    place = jnp.where(row < SPAN, span_ref[0, me] * SPAN + row, span_ref[1, me] * SPAN + row - SPAN)
    def own_rows():
        x_rows = x_ref[...].astype(F32)
        centered = x_rows - jnp.mean(x_rows, axis=-1, keepdims=True)
        inv_std = lax.rsqrt(jnp.mean(centered * centered, axis=-1, keepdims=True) + NORM_EPS)
        return x_rows, centered * inv_std, inv_std

    def own_cot():
        return jnp.where(place < len_ref[0], cot_ref[...].astype(F32), 0.0)

    loads[0].wait()
    xh_all[pl.ds(2 * me, 2)] = own_rows()[1].astype(BF16).reshape(2, SPAN, D)

    loads[1].wait()
    loads[2].wait()
    small[...] = jnp.zeros((128, 128), F32)
    small[0:8, 0:VEC_ROWS] = vectors_ref[...]
    vec_t = small[0:8, 0:64]
    for s in range(SEQ):
        take = [w_in_ref[:, 64 * int(p) : 64 * int(p) + 64] for p in PIECES[s]]
        qkv = jnp.concatenate(take[:3] + [vec_t], axis=1)
        win_own[s] = jnp.concatenate([jnp.concatenate(take[3:], axis=1), qkv], axis=0).astype(BF16)
    loads[4].wait()
    for u in range(5):
        wout_own[u] = fold(w_out_ref[8 * u : 8 * u + 8]).astype(BF16)

    def keep_unit(u):
        wout_all[5 * dm + u] = wout_own[u]

    kept(keep_unit)
    loads[3].wait()
    cot_own = own_cot()
    cot_all[pl.ds(2 * me, 2)] = cot_own.astype(BF16).reshape(2, SPAN, D)
    cot_sum = jnp.sum(cot_own, axis=0, keepdims=True)
    vg[...] = jnp.transpose(jnp.broadcast_to(cot_sum, (128, D)))
    keep = pltpu.make_async_copy(win_own.at[me], win_all.at[dm, me], local_sem.at[0])
    keep.start()

    @pl.loop(0, 32)
    def _(i):
        slot = jnp.int32(0)
        for s in range(SEQ):
            for j in range(2):
                slot = jnp.maximum(slot, jnp.where(span_ref[j, s] == i, 2 * s + j, 0))
        inv_ref[i] = slot

    def seq_turn(s, k):
        return lax.rem(s + 4 * k, SEQ)

    def dp_turn(d, k):
        return d // 4 * 4 + lax.rem(d + k, 4)

    x_tree = Tree(
        "seq",
        lambda slot, h: xh_all.at[2 * slot + h],
        me,
        seq_turn,
        mate,
        x_send.at[0],
        x_recv,
        True,
        sib,
        x_given.at[0],
    )
    cot_tree = Tree(
        "seq",
        lambda slot, h: cot_all.at[2 * slot + h],
        me,
        seq_turn,
        mate,
        c_send.at[0],
        c_recv,
        True,
        sib,
        c_given.at[0],
    )
    in_tree = Tree(
        "dp",
        lambda slot, h: win_all.at[slot, pl.ds(8 * h, 8)],
        dm,
        dp_turn,
        dp_mate,
        l_send.at[0],
        l_recv,
        False,
    )
    out_tree = Tree(
        "dp",
        lambda slot, h: wout_all.at[pl.ds(5 * slot + 2 * h, 2 + h)],
        dm,
        dp_turn,
        dp_mate,
        o_send.at[0],
        o_recv,
        False,
    )

    def a_copy(k, to, frm):
        return remote(
            win_own.at[to], win_all.at[dm, frm], a_send.at[0], a_recv.at[0], {"seq": to}
        )

    await_greetings()

    @pl.loop(1, SEQ)
    def _(k):
        a_copy(k, lax.rem(me + k, SEQ), me).start()

    out_trade = Trade(wout_own, wout_all, w_relay, 5 * dm, w_send, w_recv)
    out_trade.whole = True
    out_trade.begin()
    x_tree.own_to_mate()
    x_tree.own_to_ring()
    keep.wait()

    all_here(win_own.at[pl.ds(0, SEQ - 1)], a_recv.at[0])

    in_tree.own_to_mate()
    in_tree.own_to_ring()
    out_trade.relay_on()
    x_tree.near_first(me)
    x_tree.of_mate((0,))
    in_tree.near_first(dm)
    x_tree.near_rest(me)
    x_tree.of_mate((1,))
    in_tree.near_rest(dm)
    in_tree.of_mate()
    x_tree.far_of_me()
    in_tree.far_of_me()
    cot_tree.own_to_ring()

    def unpack(column):
        def step(sb, carry):
            cq, cf = carry
            tiles = [win_all[4 * column + y, sb].astype(F32) for y in range(4)]
            ff = jnp.concatenate([t[:8] for t in tiles], axis=0)
            qk = jnp.concatenate([t[8:] for t in tiles], axis=0)
            rows = pl.ds(pl.multiple_of(sb * 64 + 32 * column, 32), 32)
            gain_a, bias_a, gain_m, bias_m = (qk[:, 192 + i : 193 + i] for i in range(4))
            wr[rows] = jnp.concatenate([ff, qk], axis=1).astype(BF16)
            folded = jnp.where(lane_iota(qk.shape) < 192, qk * gain_a, 0.0)
            wp[rows] = jnp.concatenate([ff * gain_m, folded], axis=1).astype(BF16)
            return (
                cq + jnp.sum(qk * bias_a, axis=0, keepdims=True),
                cf + jnp.sum(ff * bias_m, axis=0, keepdims=True),
            )

        return step

    zero_row = jnp.zeros((1, 256), F32)
    sums = (zero_row, zero_row)
    for sb in range(SEQ):
        sums = unpack(dm // 4)(sb, sums)
    in_tree.near_of_mate()
    x_tree.near_of_mate()
    out_trade.end()
    out_tree.own_to_mate()
    out_tree.own_to_ring()
    cot_tree.own_to_mate()
    in_tree.far_of_mate()
    x_tree.far_of_mate()
    for sb in range(SEQ):
        sums = unpack(dp_mate // 4)(sb, sums)
    cq, cf = sums

    slab = jnp.transpose(wr[:, 384:512].astype(F32))
    vec_ref[...] = slab[64:80]
    loads[5].wait()
    loads[6].wait()

    hid = []
    for r in range(4):
        w = hidden_index(me, r)
        rows = pl.ds(pl.multiple_of(lax.rem(w, 16) * 64, 64), 64)
        part = wr[rows, 384:512].astype(F32)
        lane = 64 + 9 + w // 16
        hid.append(
            jnp.sum(jnp.where(lane_iota(part.shape) == lane, part, 0.0), axis=1, keepdims=True)
        )
    hid = jnp.concatenate(hid, axis=0)
    cf = cf + jnp.transpose(jnp.broadcast_to(hid, (256, 128)))[0:1]

    head_rows = pl.ds(pl.multiple_of(head * 64, 64), 64)
    head_vecs = wr[head_rows, 384:512].astype(F32)
    bq, bk, bv = (head_vecs[:, 68 + i : 69 + i] for i in range(3))

    all_here(xh_all.at[pl.ds(0, 16)], x_given.at[0])

    aug = jnp.where(lax.broadcasted_iota(jnp.int32, (64, CH), 0) == 0, 1.0, 0.0)
    zeros_aug = jnp.zeros((64, CH), F32)

    def rotate_t(u, cosine, sine, sign):
        first, second = u[0:8], u[8:16]
        return jnp.concatenate(
            [
                first * cosine - sign * (second * sine),
                second * cosine + sign * (first * sine),
                u[16:],
            ],
            axis=0,
        )

    def project(i):
        start = pl.multiple_of(i * CH, CH)
        rows = pl.ds(start, CH)
        xh = jnp.concatenate([xh_all[inv_ref[8 * i + k]] for k in range(8)], axis=0)
        xs[rows] = xh
        first = dot(xh, wp[...])
        qkv = jnp.transpose(first[:, 256:] + cq)
        cosine, sine = cos_ref[:, rows], sin_ref[:, rows]
        q = rotate_t(qkv[0:64] + bq, cosine, sine, 1.0) * 0.125
        k = rotate_t(qkv[64:128] + bk, cosine, sine, 1.0)
        v = qkv[128:192] + bv
        q_full = jnp.concatenate([q, aug], axis=0)
        past = (start + lane_iota((64, CH))) >= len_ref[0]
        k_full = jnp.concatenate([k, jnp.where(past, NEG_FILL, 0.0) * aug], axis=0)
        v_full = jnp.concatenate([v, zeros_aug], axis=0)
        qt[:, rows] = q_full.astype(BF16)
        kt[:, rows] = k.astype(BF16)
        vt[:, rows] = v.astype(BF16)
        qn[rows] = jnp.transpose(q_full).astype(BF16)
        kn[rows] = jnp.transpose(k_full).astype(BF16)
        vn[rows] = jnp.transpose(v_full).astype(BF16)
        pre = first[:, :256] + cf
        cdf = 0.5 * (1.0 + lax.erf(pre * (1.0 / math.sqrt(2.0))))
        pdf = jnp.exp(-0.5 * pre * pre) * (1.0 / math.sqrt(2.0 * math.pi))
        activ = pre * cdf
        joined[pl.ds(8 * i, 8), :, 0:256] = activ.astype(BF16).reshape(8, SPAN, 256)
        joined_t[0:256, rows] = jnp.transpose(activ).astype(BF16)
        dact[rows] = cdf + pre * pdf

    project(0)
    cot_tree.near_of_me()
    out_tree.near_of_me()
    out_tree.of_mate()
    project(1)
    project(2)
    cot_tree.of_mate()
    project(3)
    cot_tree.far_of_me()
    out_tree.near_of_mate()
    out_tree.far_of_me()
    half = CH // 2

    def tiles(qi):
        below = [(kc * CH, CH, qi * CH, CH) for kc in range(qi)]
        return below + [(qi * CH, half, qi * CH, CH), (qi * CH + half, half, qi * CH + half, half)]

    def scores(k0, keys, q0, queries):
        s = dot(kn[k0 : k0 + keys], qt[:, q0 : q0 + queries])
        if k0 >= q0:
            shape = (keys, queries)
            seen = lax.broadcasted_iota(jnp.int32, shape, 0) <= lane_iota(shape)
            s = jnp.where(seen, s, NEG_FILL)
        return s

    def held(k0, keys, q0, queries):
        qi, kc = q0 // CH, k0 // CH
        rows, cols = slice(k0 % CH, k0 % CH + keys), slice(q0 % CH, q0 % CH + queries)
        return exps.at[qi * (qi + 1) // 2 + kc, rows, cols]

    def spread(value, queries, fill):
        if queries == CH:
            return value
        return jnp.concatenate([jnp.full_like(value, fill), value], axis=1)

    for qi in range(NCH):
        lanes = slice(qi * CH, (qi + 1) * CH)
        parts = [(t, scores(*t)) for t in tiles(qi)]
        tops = [spread(jnp.max(s, axis=0, keepdims=True), t[3], NEG_FILL) for t, s in parts]
        top = functools.reduce(jnp.maximum, tops)
        total = jnp.zeros((1, CH), F32)
        out = jnp.zeros((64, CH), F32)
        for (k0, keys, q0, queries), s in parts:
            p = jnp.exp(s - top[:, CH - queries :])
            total = total + spread(jnp.sum(p, axis=0, keepdims=True), queries, 0.0)
            p = p.astype(BF16)
            held(k0, keys, q0, queries)[...] = p
            out = out + spread(dot(vt[:, k0 : k0 + keys], p), queries, 0.0)
        one_over = 1.0 / total
        out = out * one_over
        ot[:, lanes] = out
        scale[:, lanes] = jnp.broadcast_to(one_over, (8, CH))
        joined_t[256:320, lanes] = out.astype(BF16)
        joined[8 * qi : 8 * qi + 8, :, 256:320] = (
            jnp.transpose(out).astype(BF16).reshape(8, SPAN, HEAD)
        )
    out_tree.far_of_mate()

    def put_units(base, at, count):
        @pl.loop(0, count // 2, unroll=True)
        def _(i):
            pair = [unfold(wout_all[base + 2 * i + j].astype(F32)) for j in range(2)]
            rows = pl.ds(pl.multiple_of(at + i * 16, 16), 16)
            wo[rows] = jnp.concatenate(pair, axis=0).astype(BF16)

    late = (me + 12) // 16
    put_units(8 * (1 - late), 0, 32)
    put_units(32 * late, 256, 8)

    def of_chips(ref, chips):
        return jnp.concatenate(
            [ref[span_ref[i % 2, 2 * j + i // 2]] for j in chips for i in range(4)], axis=0
        )

    order = [(mate, 2), (mate, 1), (mate, 3), (me, 2), (me, 3), (me, 1), (mate, 0), (me, 0)]

    class ChipSums:
        def __init__(self, part, buf, sib_buf, land, s_send, s_recv, send, recv):
            self.part, self.buf, self.sib_buf, self.land = part, buf, sib_buf, land
            self.s_send, self.s_recv = s_send, s_recv
            self.tree = SumTree(
                "seq",
                lambda slot, h: buf.at[2 * slot + h],
                land,
                me,
                seq_turn,
                mate,
                send,
                recv,
            )

        def to_sib(self, j):
            return remote(
                self.buf.at[pl.ds(4 * j + 2 - 2 * core, 2)],
                self.sib_buf.at[j],
                self.s_send,
                self.s_recv.at[j],
                {"seq": sib},
            )

        def compute(self, n):
            chips = [seq_turn(*order[m]) // 2 for m in (n, n + 1)]
            value = self.part(chips).astype(BF16).reshape(8, SPAN, D)
            for m, j in enumerate(chips):
                self.buf[pl.ds(4 * j, 4)] = value[4 * m : 4 * m + 4]
                self.to_sib(j).start()

        def pair(self, n):
            j = seq_turn(*order[n]) // 2
            self.to_sib(j).wait_recv()
            mine = pl.ds(4 * j + 2 * core, 2)
            self.buf[mine] = (self.buf[mine].astype(F32) + self.sib_buf[j].astype(F32)).astype(BF16)
            if n == 0:
                self.tree.far_of_mate()
            elif n < 3:
                self.tree.near_of_mate(order[n][1])
            elif n in (4, 5):
                self.tree.near_early(order[n][1])

        def begin(self, between=()):
            for n in range(8):
                if n % 2 == 0:
                    self.compute(n)
                for at, step in between:
                    if at == n:
                        step()
                if n > 2:
                    self.pair(n - 3)
            self.pair(5)

        def of_mate(self):
            self.pair(6)
            self.tree.of_mate()
            self.pair(7)

        def total(self):
            return self.tree.total()

        def sent(self):
            all_sent(self.land, self.tree.send)
            all_sent(self.sib_buf, self.s_send)

    po = ChipSums(
        lambda chips: dot(of_chips(joined, chips), wo[...]),
        xh_all,
        po_sib,
        po_land,
        ps_send.at[0],
        ps_recv,
        p_send.at[0],
        p_recv,
    )
    hg = ChipSums(
        lambda chips: dot_nt(of_chips(mixed, chips), wp[...]),
        cot_all,
        hg_sib,
        hg_land,
        hs_send.at[0],
        hs_recv,
        h_send.at[0],
        h_recv,
    )
    all_sent(xh_all.at[pl.ds(0, 30)], x_send.at[0])
    po.begin(((2, cot_tree.near_of_mate), (4, cot_tree.far_of_mate)))
    all_here(cot_all.at[pl.ds(0, 16)], c_given.at[0])

    @pl.loop(0, 32, unroll=True)
    def _(i):
        cs[pl.ds(SPAN * i, SPAN)] = cot_all[inv_ref[i]]

    def grads_by_owner(dst, base, columns):
        sums = jnp.sum(
            mixed[:, :, base : base + 256].reshape(ROW, 256).astype(F32), axis=0, keepdims=True
        )

        @pl.loop(0, 4, unroll=True)
        def _(i):
            rows = pl.ds(pl.multiple_of(i * 256, 256), 256)
            h = jnp.transpose(dot(mixed_t[base : base + 256], xs[:, rows]))
            raw = wr[rows, base : base + 256].astype(F32)
            vecs = wr[rows, 384:512].astype(F32)
            gain, bias = (vecs[:, columns + 64 + j : columns + 65 + j] for j in range(2))
            grad = gain * h + bias * sums
            lanes = lane_iota((256, 128))
            extra = vg[rows]
            for j, col in enumerate((raw * h, raw * sums)):
                extra = extra + jnp.where(
                    lanes == 64 + columns + j, jnp.sum(col, axis=1, keepdims=True), 0.0
                )
            if base:
                grad = jnp.concatenate([grad[:, :128], grad[:, 128:] + extra], axis=1)
            else:
                vg[rows] = extra
            for j in range(2):
                pair = [
                    grad[128 * j + 64 * t : 128 * j + 64 * t + 64].reshape(8, 8, 256)
                    for t in range(2)
                ]
                dst[:, 2 * i + j] = jnp.concatenate(pair, axis=1).astype(BF16)

    def owner_sums(dst, land, send, recv):
        return ColumnSums(
            "dp",
            lambda slot: dst.at[slot],
            land,
            dm,
            dp_turn,
            dp_mate,
            send.at[0],
            recv,
        )

    gf_sums = owner_sums(gf, gf_land, gf_send, gf_recv)
    gq_sums = owner_sums(gq, gq_land, gq_send, gq_recv)
    go_sums = ColumnSums(
        "dp",
        lambda slot: go_buf.at[pl.ds(5 * slot, 5)],
        go_land,
        dm,
        dp_turn,
        dp_mate,
        go_send.at[0],
        go_recv,
    )
    @pl.loop(0, 2, unroll=True)
    def _(i):
        left = dot(joined_t[...], cs[:, pl.ds(pl.multiple_of(i * 256, 256), 256)])
        right = dot(joined_t[...], cs[:, pl.ds(pl.multiple_of(i * 256 + 512, 256), 256)])
        units = jnp.concatenate([left.reshape(40, 8, 256), right.reshape(40, 8, 256)], axis=1)
        lanes = pl.ds(pl.multiple_of(i * 256, 256), 256)
        go_buf[pl.ds(8 * (1 - late), 32), :, lanes] = units[:32].astype(BF16)
        go_buf[pl.ds(32 * late, 8), :, lanes] = units[32:].astype(BF16)

    go_sums.start()

    @pl.loop(0, NCH, unroll=True)
    def _(i):
        rows = pl.ds(pl.multiple_of(i * CH, CH), CH)
        cot = cs[rows]
        back = dot_nt(cot, wo[...])
        ag = back[:, 256:].astype(BF16).astype(F32)
        ag_t = jnp.transpose(ag)
        dot_n[rows] = ag.astype(BF16)
        dot_t[:, rows] = ag_t.astype(BF16)
        delta[:, rows] = jnp.broadcast_to(
            jnp.sum(ag_t * ot[:, rows], axis=0, keepdims=True), (8, CH)
        )
        pg = back[:, :256] * dact[rows]
        mixed[pl.ds(8 * i, 8), :, 0:256] = pg.astype(BF16).reshape(8, SPAN, 256)
        mixed_t[0:256, rows] = jnp.transpose(pg).astype(BF16)

    lanes_d = lane_iota((D, 128))
    vg[...] = jnp.where((lanes_d == 71) | (lanes_d == 72), vg[...], 0.0)
    lanes_h = lane_iota((64, 128))
    cols_f = jnp.sum(mixed_t[0:256].astype(F32), axis=1, keepdims=True)
    for r in range(4):
        w = hidden_index(me, r)
        rows = pl.ds(pl.multiple_of(lax.rem(w, 16) * 64, 64), 64)
        vg[rows] += jnp.where(lanes_h == 64 + 9 + w // 16, cols_f[64 * r : 64 * r + 64], 0.0)
    grads_by_owner(gf, 0, 2)
    gf_sums.start()
    po.tree.far_of_me()
    po.of_mate()

    for qi in reversed(range(NCH)):
        lanes = slice(qi * CH, (qi + 1) * CH)
        dq = jnp.zeros((64, CH), F32)
        for k0, keys, q0, queries in tiles(qi):
            at, cols = slice(k0, k0 + keys), slice(q0, q0 + queries)
            p = held(k0, keys, q0, queries)[...].astype(F32) * scale[0:1, cols]
            dp = dot(vn[at, 0:64], dot_t[:, cols])
            ds = (p * (dp - delta[0:1, cols])).astype(BF16)
            dv = dot(p.astype(BF16), dot_n[cols])
            dk = dot(ds, qn[cols, 0:64])
            dq = dq + spread(dot(kt[:, at], ds), queries, 0.0)
            if qi == NCH - 1:
                dvn[at] = dv
                dkn[at] = dk
            else:
                dvn[at] += dv
                dkn[at] += dk
        dqt[:, lanes] = dq * 0.125

    @pl.loop(0, NCH, unroll=True)
    def _(i):
        rows = pl.ds(pl.multiple_of(i * CH, CH), CH)
        cosine, sine = cos_ref[:, rows], sin_ref[:, rows]
        dq = rotate_t(dqt[:, rows], cosine, sine, -1.0)
        dk = rotate_t(jnp.transpose(dkn[rows]), cosine, sine, -1.0)
        dv = jnp.transpose(dvn[rows])
        full = jnp.concatenate([dq, dk, dv, zeros_aug], axis=0)
        mixed_t[256:512, rows] = full.astype(BF16)
        mixed[pl.ds(8 * i, 8), :, 256:512] = jnp.transpose(full).astype(BF16).reshape(8, SPAN, 256)

    cols_q = jnp.sum(mixed_t[256:448].astype(F32), axis=1, keepdims=True)
    for i in range(3):
        vg[head_rows] += jnp.where(lanes_h == 68 + i, cols_q[64 * i : 64 * i + 64], 0.0)
    go_sums.middle()
    grads_by_owner(gq, 256, 0)
    gq_sums.start()
    po.tree.near_late()
    gf_sums.middle()

    all_sent(cot_all.at[pl.ds(0, 30)], c_send.at[0])

    def to_owner(part, total, send, recv, k, to, frm):
        return remote(part.at[to], total.at[frm], send.at[0], recv.at[0], {"seq": to})

    def own_sums(part, total, send, recv):
        @pl.loop(1, SEQ)
        def _(k):
            to_owner(part, total, send, recv, k, lax.rem(me + k, SEQ), me).start()

        total[me] = part[me]

    def own_arrived(part, total, send, recv):
        all_here(total.at[pl.ds(0, SEQ - 1)], recv.at[0])

    def squares_of(value):
        return jnp.sum(jnp.sum(value * value, axis=0), axis=0, keepdims=True)

    def fold_rows(value):
        return jnp.concatenate([value[:, :, :128], value[:, :, 128:]], axis=1).astype(BF16)

    f_squares = []

    def hidden_on():
        value = gf_sums.total().reshape(SEQ, 8, 256)
        f_squares.append(squares_of(value))
        f_part[...] = fold_rows(value)


    hg.begin(((6, hidden_on),))
    gq_sums.middle()
    out_total = go_sums.total()
    out_part[...] = out_total

    out_back = Trade(out_part, wout_sum, v_relay, 0, v_send, v_recv)
    out_back.whole = False

    def keep_total(u):
        wout_sum[u] = out_part[u]

    out_back.begin()
    kept(keep_total)
    out_squares = squares_of(out_total)
    squares = f_squares[0] + out_squares[:, :256] + out_squares[:, 256:]

    hg.tree.far_of_me()
    total = gq_sums.total().reshape(SEQ, 8, 256)
    weights = jnp.where(lane_iota(total.shape) < 192, total, 0.0)
    squares = squares + squares_of(weights)
    tile_a[...] = jnp.transpose(total[:, :, 128:].reshape(128, 128))[64:80]
    tile_a[15:16] = squares[:, :128] + squares[:, 128:]

    def ta_copy(k, to, frm):
        return remote(tile_a, got_a.at[frm], ta_send.at[0], ta_recv.at[0], {"seq": to})

    @pl.loop(1, SEQ)
    def _(k):
        ta_copy(k, lax.rem(me + k, SEQ), me).start()

    got_a[me] = tile_a[...]
    q_part[...] = fold_rows(total)
    own_sums(q_part, q_sum, bq_send, bq_recv)
    own_sums(f_part, f_sum, bf_send, bf_recv)
    hg.of_mate()
    hg.tree.near_late()
    out_back.relay_on()
    all_here(got_a.at[pl.ds(0, SEQ - 1)], ta_recv.at[0])
    sums = jnp.sum(got_a[...], axis=0)
    vec_total = jnp.where(lax.broadcasted_iota(jnp.int32, sums.shape, 0) < VEC_ROWS, sums, 0.0)
    row = sums[15:16] + jnp.sum(vec_total * vec_total, axis=0, keepdims=True)
    tile_b[...] = jnp.broadcast_to(jnp.sum(row, axis=1, keepdims=True), (8, 128))

    def tb_copy(k, to, frm):
        return remote(tile_b, got_b.at[frm], tb_send.at[0], tb_recv.at[0], {"dp": to})

    @pl.loop(1, DP)
    def _(k):
        tb_copy(k, lax.rem(dm + k, DP), dm).start()

    got_b[dm] = tile_b[...]
    small[...] = jnp.zeros((128, 128), F32)
    small[0:16] = vec_total
    small[...] = jnp.transpose(small[...])
    vec_grad[...] = small[pl.ds(pl.multiple_of(8 * me, 8), 8)]
    vec_store.start()
    own_arrived(f_part, f_sum, bf_send, bf_recv)
    x_rows, x_hat, inv_std = own_rows()
    cot_own = own_cot()
    block_out[...] = (x_rows + po.total() + (vec_ref[7:8] + vec_ref[8:9])).astype(BF16)
    block_store.start()
    own_arrived(q_part, q_sum, bq_send, bq_recv)
    for s in range(SEQ):
        for j, p in enumerate(PIECES[s]):
            at = 64 * int(p)
            ref, k = (q_sum, j) if j < 3 else (f_sum, j - 3)
            both = ref[s].astype(F32)
            grad_in[:, at : at + 64] = both[8 * (k // 2) : 8 * (k // 2) + 8, 64 * (k % 2) : 64 * (k % 2) + 64]
    in_store.start()
    out_back.end()
    for u in range(5):
        grad_out[8 * u : 8 * u + 8] = unfold(wout_sum[u])
    out_store.start()

    all_here(got_b.at[pl.ds(0, DP - 1)], tb_recv.at[0])
    everything = jnp.sum(got_b[...], axis=0)
    square_ref[...] = jnp.broadcast_to(everything[:, 0:1], (8, 128))
    square_store.start()
    grad = hg.total()
    back = (
        grad
        - jnp.mean(grad, axis=-1, keepdims=True)
        - x_hat * jnp.mean(grad * x_hat, axis=-1, keepdims=True)
    )
    input_grad[...] = (cot_own + inv_std * back).astype(BF16)
    grad_store.start()
    po.sent()
    hg.sent()
    out_trade.sent()
    out_back.sent()
    for sums in (gf_sums, gq_sums, go_sums):
        sums.sent()
    all_sent(win_all.at[pl.ds(0, 7)], l_send.at[0])
    all_sent(wout_all.at[pl.ds(0, 35)], o_send.at[0])
    all_sent(win_own.at[pl.ds(0, SEQ - 1)], a_send.at[0])
    all_sent(got_a.at[pl.ds(0, SEQ - 1)], ta_send.at[0])
    all_sent(got_b.at[pl.ds(0, DP - 1)], tb_send.at[0])
    all_sent(f_part.at[pl.ds(0, SEQ - 1)], bf_send.at[0])
    all_sent(q_part.at[pl.ds(0, SEQ - 1)], bq_send.at[0])
    for store in stores:
        store.wait()


def layer_call(span, length, x, cot, w_in, w_out, vectors):
    freqs = np.float32(THETA_BASE) ** (-2.0 * np.arange(ROT // 2) / ROT)
    angles = np.arange(ROW, dtype=np.float32)[None, :] * freqs.astype(np.float32)[:, None]
    cosine, sine = np.cos(angles).astype(np.float32), np.sin(angles).astype(np.float32)
    smem = pl.BlockSpec(memory_space=pltpu.SMEM)
    anywhere = pl.BlockSpec(memory_space=pl.ANY)
    sds = jax.ShapeDtypeStruct
    dma = pltpu.SemaphoreType.DMA

    def buf(shape, dtype=BF16):
        return pltpu.VMEM(shape, dtype)

    return pl.pallas_call(
        layer_kernel,
        out_shape=(
            sds((TOK, D), BF16),
            sds((TOK, D), BF16),
            sds((8, 7 * D), F32),
            sds((40, D), F32),
            sds((8, 128), F32),
            sds((8, 128), F32),
        ),
        in_specs=[smem] * 2 + [anywhere] * 7,
        out_specs=[anywhere] * 6,
        scratch_shapes=[
            buf((TOK, D)),
            buf((TOK, D)),
            buf((8, 7 * D), F32),
            buf((40, D), F32),
            buf((8, VEC_ROWS), F32),
            buf((8, ROW), F32),
            buf((8, ROW), F32),
            buf((TOK, D)),
            buf((TOK, D)),
            buf((8, 7 * D), F32),
            buf((40, D), F32),
            buf((SEQ, 16, 128)),
            buf((SEQ, 16, 128)),
            buf((5, 16, 512), F32),
            buf((8, 128), F32),
            buf((8, 128), F32),
            dma((7,)),
            dma((6,)),
            pltpu.SMEM((32,), jnp.int32),
            buf((32, SPAN, D)),
            buf((32, SPAN, D)),
            buf((SEQ, 16, 256)),
            buf((DP, SEQ, 16, 256)),
            buf((40, 16, 512)),
            buf((5, 16, 512)),
            buf((2, 5, 16, 512)),
            buf((2, 5, 16, 512), F32),
            buf((128, 128), F32),
            buf((16, D), F32),
            buf((ROW, D)),
            buf((ROW, D)),
            buf((D, 512)),
            buf((D, 512)),
            buf((320, D)),
            buf((128, ROW)),
            buf((ROW, 128)),
            buf((64, ROW)),
            buf((ROW, 128)),
            buf((64, ROW)),
            buf((ROW, 128)),
            buf((64, ROW)),
            buf((ROW, 64)),
            buf((64, ROW), F32),
            buf((8, ROW), F32),
            buf((10, CH, CH)),
            buf((8, ROW), F32),
            buf((32, SPAN, 320)),
            buf((320, ROW)),
            buf((ROW, 256), F32),
            buf((32, SPAN, 512)),
            buf((512, ROW)),
            buf((64, ROW), F32),
            buf((ROW, 64), F32),
            buf((ROW, 64), F32),
            buf((D, 128), F32),
            buf((40, 16, 512)),
            buf((5, 16, 512), F32),
            buf((DP, 8, 16, 256)),
            buf((DP, 8, 16, 256)),
            buf((8, 2, SPAN, D)),
            buf((8, 2, SPAN, D)),
            buf((7, 2, SPAN, D)),
            buf((7, 2, SPAN, D)),
            buf((8, 8, 16, 256)),
            buf((8, 8, 16, 256)),
            buf((8, 5, 16, 512)),
            buf((SEQ, 16, 128)),
            buf((SEQ, 16, 128)),
            buf((16, 128), F32),
            buf((8, 128), F32),
            buf((SEQ, 16, 128), F32),
            buf((DP, 8, 128), F32),
            dma((1,)),
            dma((1,)),
            dma((1,)),
            dma((1,)),
            dma((8, 2)),
            dma((1,)),
            dma((1,)),
            dma((8, 2)),
            dma((1,)),
            dma((1,)),
            dma((DP, 2)),
            dma((1,)),
            dma((DP, 2)),
            dma((2, 5)),
            dma((2, 5)),
            dma((1,)),
            dma((8,)),
            dma((1,)),
            dma((6,)),
            dma((1,)),
            dma((8,)),
            dma((1,)),
            dma((6,)),
            dma((1,)),
            dma((3,)),
            dma((1,)),
            dma((3,)),
            dma((1,)),
            dma((3,)),
            dma((2, 5)),
            dma((2, 5)),
            dma((1,)),
            dma((1,)),
            dma((1,)),
            dma((1,)),
            dma((1,)),
            dma((1,)),
            dma((1,)),
            dma((1,)),
        ],
        compiler_params=pltpu.CompilerParams(
            collective_id=0, has_side_effects=True, vmem_limit_bytes=VMEM_LIMIT
        ),
        name="layer_of_one_row",
    )(span, length, x, cot, w_in, w_out, vectors, jnp.asarray(cosine), jnp.asarray(sine))


def adam(weight, grad, first, second, factor, rate, decay):
    clipped = grad * factor
    first_new = BETA_ONE * first + (1.0 - BETA_ONE) * clipped
    second_new = BETA_TWO * second + (1.0 - BETA_TWO) * clipped * clipped
    first_hat = first_new / (1.0 - BETA_ONE**STEP)
    second_hat = second_new / (1.0 - BETA_TWO**STEP)
    weight_new = weight * (1.0 - rate * decay) - rate * first_hat / (
        jnp.sqrt(second_hat) + ADAM_EPS
    )
    return (weight_new, first_new, second_new, weight_new.astype(BF16))


UPDATE_IN = (
    ("block_out", (TOK, D), BF16),
    ("input_grad", (TOK, D), BF16),
    ("square", (8, 128), F32),
    ("grad_in", (8, 7 * D), F32),
    ("w_in", (8, 7 * D), F32),
    ("in_first", (8, 7 * D), F32),
    ("in_second", (8, 7 * D), F32),
    ("grad_out", (40, D), F32),
    ("w_out", (40, D), F32),
    ("out_first", (40, D), F32),
    ("out_second", (40, D), F32),
    ("vectors", (8, VEC_ROWS), F32),
    ("vec_first", (8, VEC_ROWS), F32),
    ("vec_second", (8, VEC_ROWS), F32),
    ("vec_grad", (8, 128), F32),
)
UPDATE_OUT = (
    ((TOK, D), BF16),
    ((TOK, D), BF16),
    ((8, 7 * D), F32),
    ((40, D), F32),
    ((8, VEC_ROWS), F32),
    ((8, 7 * D), F32),
    ((40, D), F32),
    ((8, VEC_ROWS), F32),
    ((8, 7 * D), F32),
    ((40, D), F32),
    ((8, VEC_ROWS), F32),
    ((8, 7 * D), BF16),
    ((40, D), BF16),
    ((8, VEC_ROWS), BF16),
)


def update_kernel(*refs):
    ins, refs = refs[: len(UPDATE_IN)], refs[len(UPDATE_IN) :]
    norm_ref, refs = refs[0], refs[1:]
    outs, refs = refs[: len(UPDATE_OUT)], refs[len(UPDATE_OUT) :]
    in_bufs, refs = refs[: len(UPDATE_IN)], refs[len(UPDATE_IN) :]
    out_bufs, (in_sem, out_sem) = refs[: len(UPDATE_OUT)], refs[len(UPDATE_OUT) :]
    loads = [
        pltpu.make_async_copy(a, b, in_sem.at[i]) for i, (a, b) in enumerate(zip(ins, in_bufs))
    ]
    stores = [
        pltpu.make_async_copy(in_bufs[i] if i < 2 else b, a, out_sem.at[i])
        for i, (a, b) in enumerate(zip(outs, out_bufs))
    ]
    order = list(range(2, len(loads))) + [0, 1]
    for i in order:
        loads[i].start()
    names = [name for name, _, _ in UPDATE_IN]

    def take(name):
        i = names.index(name)
        loads[i].wait()
        return in_bufs[i]

    def give(i, value):
        out_bufs[i][...] = value
        stores[i].start()

    norm = jnp.sqrt(take("square")[...])
    norm_ref[0, 0] = norm[0, 0]
    factor = jnp.minimum(1.0, CLIP_NORM / norm)[0:1, 0:1]

    for i in range(2):
        loads[i].wait()
        stores[i].start()

    def matrix(at, grad, weight, first, second, rate, decay):
        values = adam(
            take(weight)[...], grad, take(first)[...], take(second)[...], factor, rate, decay
        )
        for k, value in enumerate(values):
            give(at + 3 * k, value)

    matrix(2, take("grad_in")[...], "w_in", "in_first", "in_second", RATE_MATRIX, DECAY_RATE)
    matrix(3, take("grad_out")[...], "w_out", "out_first", "out_second", RATE_MATRIX, DECAY_RATE)
    grad_vec = take("vec_grad")[:, 0:VEC_ROWS]
    matrix(4, grad_vec, "vectors", "vec_first", "vec_second", RATE_VECTOR, 0.0)

    for store in stores:
        store.wait()


def update_call(*args):
    anywhere = pl.BlockSpec(memory_space=pl.ANY)
    dma = pltpu.SemaphoreType.DMA
    sds = jax.ShapeDtypeStruct
    return pl.pallas_call(
        update_kernel,
        out_shape=(sds((1, 1), F32),) + tuple(sds(shape, kind) for shape, kind in UPDATE_OUT),
        in_specs=[anywhere] * len(UPDATE_IN),
        out_specs=[pl.BlockSpec(memory_space=pltpu.SMEM)] + [anywhere] * len(UPDATE_OUT),
        scratch_shapes=[pltpu.VMEM(shape, kind) for _, shape, kind in UPDATE_IN]
        + [pltpu.VMEM(shape, kind) for shape, kind in UPDATE_OUT]
        + [dma((len(UPDATE_IN),)), dma((len(UPDATE_OUT),))],
        compiler_params=pltpu.CompilerParams(vmem_limit_bytes=UPDATE_LIMIT),
        name="clipped_update",
    )(*args)


def body(
    hidden_in,
    out_cot,
    in_weight,
    out_weight,
    vectors,
    in_first,
    in_second,
    out_first,
    out_second,
    vec_first,
    vec_second,
    lengths,
    span_of,
):
    block_out, input_grad, grad_in, grad_out, squares, vec_grad = layer_call(
        span_of.T, lengths, hidden_in[0], out_cot[0], in_weight, out_weight, vectors.T
    )
    norm, block_out, input_grad, *rest = update_call(
        block_out,
        input_grad,
        squares,
        grad_in,
        in_weight,
        in_first,
        in_second,
        grad_out,
        out_weight,
        out_first,
        out_second,
        vectors.T,
        vec_first.T,
        vec_second.T,
        vec_grad,
    )
    rest = [out.T if i % 3 == 2 else out for i, out in enumerate(rest)]
    return (block_out[None], input_grad[None], norm.reshape(()), *rest)


def solution(mesh):
    tokens = P("dp", "seq", None)
    matrix = P(("seq", "dp"), None)
    vector = P(None, ("seq", "dp"))
    return jax.shard_map(
        body,
        mesh=mesh,
        in_specs=(
            tokens,
            tokens,
            matrix,
            matrix,
            vector,
            matrix,
            matrix,
            matrix,
            matrix,
            vector,
            vector,
            P("dp"),
            P(),
        ),
        out_specs=(tokens, tokens, P()) + (matrix, matrix, vector) * 4,
        check_vma=False,
    )
```

```python
import functools
import math

import jax
import jax.numpy as jnp
import numpy as np
from jax import lax
from jax.experimental import pallas as pl
from jax.experimental.pallas import tpu as pltpu
from jax.sharding import PartitionSpec as P

D = 1024
FF = 4096
HEADS = 16
HEAD = 64
ROT = 16
STEP = 5
SEQ = 16
DP = 8
TOK = 128
ROW = 2048
SPAN = 64
VEC_ROWS = 13

NORM_EPS = 1e-05
NEG_FILL = -1e30
CLIP_NORM = 1.0
RATE_MATRIX = 0.02
RATE_VECTOR = 0.2
BETA_ONE = 0.5
BETA_TWO = 0.5
DECAY_RATE = 0.1
ADAM_EPS = 1e-08
THETA_BASE = 10000.0

F32 = jnp.float32
BF16 = jnp.bfloat16
MESH = pl.DeviceIdType.MESH
VMEM_LIMIT = 60 * 1024 * 1024
UPDATE_LIMIT = 60 * 1024 * 1024


def head_of(s):
    if s < 4:
        return 5 * s
    return 5 * ((s - 4) // 4) + 1 + (s - 4) % 4


def hidden_pieces(s):
    if s < 3:
        return [20 * s + 5 * r + 8 for r in range(4)]
    if s == 3:
        return [0, 1, 2, 3]
    return [5 * s - 16 + r for r in range(4)]


def column_pieces():
    rows = []
    for s in range(SEQ):
        h = head_of(s)
        rows.append([h, 16 + h, 32 + h] + [48 + w for w in hidden_pieces(s)])
    return np.array(rows, np.int32)


PIECES = column_pieces()


def head_index(s):
    late = (s + 12) // 16
    return (1 - late) * (5 * s) + late * (5 * ((s - 4) // 4) + 1 + lax.rem(s, 4))


def hidden_index(s, r):
    late, not_few = (s + 12) // 16, (s + 13) // 16
    return (
        (1 - not_few) * (20 * s + 5 * r + 8) + (not_few - late) * r + late * (5 * s - 16 + r)
    )


def remote(src, dst, send, recv, where):
    return pltpu.make_async_remote_copy(
        src_ref=src, dst_ref=dst, send_sem=send, recv_sem=recv, device_id=where, device_id_type=MESH
    )


def greet(me, dm):
    barrier = pltpu.get_barrier_semaphore()

    @pl.loop(1, SEQ)
    def _(k):
        pl.semaphore_signal(
            barrier, inc=1, device_id={"seq": lax.rem(me + k, SEQ)}, device_id_type=MESH
        )

    @pl.loop(1, DP)
    def _(k):
        pl.semaphore_signal(
            barrier, inc=1, device_id={"dp": lax.rem(dm + k, DP)}, device_id_type=MESH
        )


def await_greetings():
    pl.semaphore_wait(pltpu.get_barrier_semaphore(), SEQ + DP - 2)


def all_sent(ref, sem):
    remote(ref, ref, sem, sem, {"seq": 0}).wait_send()


def all_here(ref, sem):
    pltpu.make_async_copy(ref, ref, sem).wait()


class Tree:
    def __init__(self, axis, piece, me, turn, mate, send, recv, over_mate, sib=None, given=None):
        self.axis, self.piece, self.me, self.turn, self.mate = (axis, piece, me, turn, mate)
        self.send, self.recv, self.over_mate = send, recv, over_mate
        self.sib, self.given = sib, given
        self.per = 1 if sib is None else 2

    def put(self, slot, h, to):
        part = self.piece(slot, h)
        remote(part, part, self.send, self.arrival(slot, h), {self.axis: to}).start()

    def hand(self, slot, h):
        if self.sib is not None:
            part = self.piece(slot, h)
            remote(part, part, self.send, self.given, {self.axis: self.sib}).start()

    def arrival(self, slot, h):
        return self.recv.at[slot // self.per, h]

    def got(self, slot, h):
        part = self.piece(slot, h)
        remote(
            part, part, self.send, self.arrival(slot, h), {self.axis: self.mate}
        ).wait_recv()

    def own_to_ring(self):
        for h, k in ((0, 1), (1, 3), (1, 1), (0, 3)):
            self.put(self.me, h, self.turn(self.me, k))

    def own_to_mate(self):
        for h in range(2):
            self.put(self.me, h, self.mate)
        for h in range(2):
            self.hand(self.me, h)

    def of_mate(self, halves=(0, 1)):
        for h in halves:
            self.got(self.mate, h)
            for k in (1, 3):
                self.put(self.mate, h, self.turn(self.me, k))
            self.hand(self.mate, h)

    def near_first(self, base):
        for h, k in ((0, 3), (1, 1)):
            slot = self.turn(base, k)
            self.got(slot, h)
            self.put(slot, h, self.turn(self.me, 4 - k))
            self.hand(slot, h)

    def near_rest(self, base):
        for h, k in ((1, 3), (0, 1)):
            slot = self.turn(base, k)
            self.got(slot, h)
            self.hand(slot, h)

    def near(self, base):
        self.near_first(base)
        self.near_rest(base)

    def near_of_me(self):
        self.near(self.me)

    def far_of_me(self):
        slot = self.turn(self.me, 2)
        for h in range(2):
            self.got(slot, h)
            if self.over_mate:
                self.put(slot, h, self.mate)
            self.hand(slot, h)

    def near_of_mate(self):
        if not self.over_mate:
            return self.near(self.mate)
        for h in range(2):
            for k in (3, 1):
                slot = self.turn(self.mate, k)
                self.got(slot, h)
                self.hand(slot, h)

    def far_of_mate(self):
        slot = self.turn(self.mate, 2)
        for h in range(2):
            self.got(slot, h)
            self.hand(slot, h)


class SumTree:
    def __init__(self, axis, piece, landing, me, turn, mate, send, recv):
        self.axis, self.piece, self.me, self.turn, self.mate = (axis, piece, me, turn, mate)
        self.landing, self.send, self.recv = landing, send, recv

    def land(self, kind, h):
        return self.landing.at[kind, h]

    def arrival(self, kind, h):
        return self.recv.at[(h, 2, 2, 3 + h, 5, 5, 5)[kind]]

    def put(self, slot, kind, h, to):
        copy = remote(
            self.piece(slot, h),
            self.land(kind, h),
            self.send,
            self.arrival(kind, h),
            {self.axis: to},
        )
        copy.start()

    def add(self, slot, h, *kinds):
        part = self.piece(slot, h)
        total = part[...].astype(F32)
        for kind in kinds:
            total = total + self.land(kind, h)[...].astype(F32)
        part[...] = total.astype(BF16)

    def far_of_mate(self):
        for h in range(2):
            self.put(self.turn(self.mate, 2), 0, h, self.mate)

    def near_of_mate(self, k):
        for h in range(2):
            self.put(self.turn(self.mate, k), 2 if k == 1 else 1, h, self.turn(self.me, k))

    def near_early(self, k):
        h = 0 if k == 1 else 1
        self.put(self.turn(self.me, k), 5 if k == 1 else 4, h, self.turn(self.me, k))

    def far_of_me(self):
        slot = self.turn(self.me, 2)
        for h in range(2):
            all_here(self.land(0, h), self.arrival(0, h))
            self.add(slot, h, 0)
            self.put(slot, 3, h, self.turn(self.me, 3 - 2 * h))

    def near_late(self):
        for h in range(2):
            k = 3 - 2 * h
            slot = self.turn(self.me, k)
            all_here(self.land(3, h), self.arrival(3, h))
            self.add(slot, h, 3)
            self.put(slot, 4 + h, h, self.turn(self.me, k))

    def of_mate(self):
        all_here(self.landing.at[pl.ds(1, 2)], self.arrival(1, 0))
        for h in range(2):
            self.add(self.mate, h, 1, 2)
            self.put(self.mate, 6, h, self.mate)

    def begin(self):
        self.far_of_mate()
        for k in (1, 3):
            self.near_of_mate(k)
        for k in (1, 3):
            self.near_early(k)

    def total(self):
        all_here(self.landing.at[pl.ds(4, 3)], self.arrival(4, 0))
        parts = []
        for h in range(2):
            value = self.piece(self.me, h)[...].astype(F32)
            for kind in (4, 5, 6):
                value = value + self.land(kind, h)[...].astype(F32)
            parts.append(value)
        return jnp.concatenate(parts, axis=0)


class ColumnSums:
    def __init__(self, axis, piece, landing, me, turn, mate, send, recv):
        self.axis, self.piece, self.me, self.turn, self.mate = (axis, piece, me, turn, mate)
        self.land = lambda i: landing.at[i]
        self.lands = lambda i, n: landing.at[pl.ds(i, n)]
        self.send, self.recv = send, recv

    def copy(self, k, of_mate):
        to = self.turn(self.me, k)
        return remote(
            self.piece(self.turn(self.mate, k) if of_mate else to),
            self.land(4 * of_mate + 4 - k),
            self.send,
            self.recv.at[1 + of_mate],
            {self.axis: to},
        )

    def last(self):
        return remote(
            self.piece(self.mate),
            self.land(0),
            self.send,
            self.recv.at[0],
            {self.axis: self.mate},
        )

    def start(self):
        for of_mate in (1, 0):
            for k in (1, 3, 2):
                self.copy(k, of_mate).start()

    def summed(self, slot, of_mate):
        total = self.piece(slot)[...].astype(F32)
        all_here(self.lands(4 * of_mate + 1, 3), self.recv.at[1 + of_mate])
        for k in (1, 3, 2):
            total = total + self.land(4 * of_mate + 4 - k)[...].astype(F32)
        return total

    def middle(self):
        self.piece(self.mate)[...] = self.summed(self.mate, 1).astype(BF16)
        self.last().start()

    def total(self):
        value = self.summed(self.me, 0)
        self.last().wait_recv()
        return value + self.land(0)[...].astype(F32)

    def sent(self):
        all_sent(self.lands(0, 7), self.send)


def dot(a, b):
    return jnp.dot(a, b, preferred_element_type=F32)


def dot_nt(a, b):
    return lax.dot_general(a, b, (((1,), (1,)), ((), ())), preferred_element_type=F32)


def lane_iota(shape):
    return lax.broadcasted_iota(jnp.int32, shape, len(shape) - 1)


def fold(u):
    return jnp.concatenate([u[:, : D // 2], u[:, D // 2 :]], axis=0)


def unfold(u):
    return jnp.concatenate([u[:8], u[8:]], axis=1)


CH = 512
NCH = ROW // CH


def layer_kernel(
    span_ref,
    len_ref,
    x_any,
    cot_any,
    w_in_any,
    w_out_any,
    vectors_any,
    cos_any,
    sin_any,
    block_out_any,
    input_grad_any,
    grad_in_any,
    grad_out_any,
    square_any,
    vec_grad_any,
    x_ref,
    cot_ref,
    w_in_ref,
    w_out_ref,
    vectors_ref,
    cos_ref,
    sin_ref,
    block_out,
    input_grad,
    grad_in,
    grad_out,
    f_sum,
    q_sum,
    wout_sum,
    square_ref,
    vec_grad,
    load_sem,
    store_sem,
    inv_ref,
    xh_all,
    cot_all,
    win_own,
    win_all,
    wout_all,
    wout_own,
    w_relay,
    v_relay,
    small,
    vec_ref,
    xs,
    cs,
    wr,
    wp,
    wo,
    qt,
    qn,
    kt,
    kn,
    vt,
    vn,
    dot_t,
    dot_n,
    ot,
    scale,
    exps,
    delta,
    joined,
    joined_t,
    dact,
    mixed,
    mixed_t,
    dqt,
    dkn,
    dvn,
    vg,
    go_buf,
    out_part,
    gf,
    gq,
    po_sib,
    hg_sib,
    po_land,
    hg_land,
    gf_land,
    gq_land,
    go_land,
    f_part,
    q_part,
    tile_a,
    tile_b,
    got_a,
    got_b,
    local_sem,
    a_send,
    a_recv,
    x_send,
    x_recv,
    x_given,
    c_send,
    c_recv,
    c_given,
    l_send,
    l_recv,
    o_send,
    o_recv,
    w_send,
    w_recv,
    ps_send,
    ps_recv,
    p_send,
    p_recv,
    hs_send,
    hs_recv,
    h_send,
    h_recv,
    gf_send,
    gf_recv,
    gq_send,
    gq_recv,
    go_send,
    go_recv,
    v_send,
    v_recv,
    bf_send,
    bf_recv,
    bq_send,
    bq_recv,
    ta_send,
    ta_recv,
    tb_send,
    tb_recv,
):
    me = lax.axis_index("seq")
    dm = lax.axis_index("dp")
    core = lax.rem(me, 2)
    chip = me // 2
    sib = me + 1 - 2 * core
    mate = me + 2 - 4 * lax.rem(chip, 2)
    dp_mate = lax.rem(dm + 4, DP)
    head = head_index(me)
    loads = [
        pltpu.make_async_copy(a, b, load_sem.at[i])
        for i, (a, b) in enumerate(
            (
                (x_any, x_ref),
                (w_in_any, w_in_ref),
                (vectors_any, vectors_ref),
                (cot_any, cot_ref),
                (w_out_any, w_out_ref),
                (cos_any, cos_ref),
                (sin_any, sin_ref),
            )
        )
    ]
    block_store, grad_store, in_store, out_store, square_store, vec_store = stores = [
        pltpu.make_async_copy(a, b, store_sem.at[i])
        for i, (a, b) in enumerate(
            (
                (block_out, block_out_any),
                (input_grad, input_grad_any),
                (grad_in, grad_in_any),
                (grad_out, grad_out_any),
                (square_ref, square_any),
                (vec_grad, vec_grad_any),
            )
        )
    ]
    def units_of(step):
        for u in range(5):
            i = 5 * dm + u

            @pl.when(me < 3)
            def _(u=u, i=i):
                @pl.when(i >= 8)
                def _():
                    step.few(u, i)

            @pl.when(me > 3)
            def _(u=u, i=i):
                r = lax.rem(me, 4)

                @pl.when(i >= 32)
                def _():
                    @pl.when(r < 3)
                    def _():
                        step.many(u, i, 8 + 8 * r + i - 32)

                    @pl.when(r == 3)
                    def _():
                        step.straight(u, i)

                @pl.when((i >= 8 + 8 * r) & (i < 16 + 8 * r) & (r < 3))
                def _():
                    step.between(u, i, 32 + lax.rem(i, 8))

    class Trade:
        def __init__(self, src, dst, relay, base, send, recv):
            self.src, self.dst, self.relay, self.base = src, dst, relay, base
            self.send, self.recv = send, recv

        def place(self, u):
            return self.dst.at[self.base + u]

        def few_out(self, u, i):
            to = 4 * me + 3 + i // 8
            last = i >= 32

            @pl.when(last)
            def _():
                remote(
                    self.src.at[u], self.place(u), self.send.at[0, u], self.recv.at[0, u], {"seq": to}
                ).start()

            @pl.when(jnp.logical_not(last))
            def _():
                remote(
                    self.src.at[u],
                    self.relay.at[0, u],
                    self.send.at[0, u],
                    self.recv.at[0, u],
                    {"seq": to},
                ).start()

        def many_out(self, u, i, far):
            at = lax.rem(far, 5)
            return remote(
                self.src.at[u],
                self.relay.at[1, at],
                self.send.at[0, u],
                self.recv.at[1, at],
                {"dp": far // 5},
            )

        def straight_out(self, u):
            return remote(
                self.src.at[u],
                self.place(u),
                self.send.at[0, u],
                self.recv.at[0, u],
                {"seq": (me - 4) // 4},
            )

        def on_to_few(self, u):
            return remote(
                self.relay.at[1, u],
                self.place(u),
                self.send.at[1, u],
                self.recv.at[0, u],
                {"seq": (me - 4) // 4},
            )

        def on_to_many(self, u, far):
            at = lax.rem(far, 5)
            base = self.base - 5 * dm + far - at if self.whole else self.base
            return remote(
                self.relay.at[0, u],
                self.dst.at[base + at],
                self.send.at[0, u],
                self.recv.at[0, at],
                {"dp": far // 5},
            )

        def arrived(self, ref, sem):
            remote(ref, ref, self.send.at[0, 0], sem, {"seq": sib}).wait_recv()

        def begin(self):
            class Step:
                few = staticmethod(self.few_out)
                many = staticmethod(lambda u, i, far: self.many_out(u, i, far).start())
                straight = staticmethod(lambda u, i: self.straight_out(u).start())
                between = staticmethod(lambda u, i, far: None)

            units_of(Step)

        def relay_on(self):
            def between(u, i, far):
                self.arrived(self.relay.at[0, u], self.recv.at[0, u])
                self.on_to_many(u, far).start()
                self.arrived(self.relay.at[1, u], self.recv.at[1, u])
                self.on_to_few(u).start()

            class Step:
                few = staticmethod(lambda u, i: None)
                many = staticmethod(lambda u, i, far: None)
                straight = staticmethod(lambda u, i: None)

            Step.between = staticmethod(between)
            units_of(Step)

        def end(self):
            class Step:
                few = staticmethod(lambda u, i: self.arrived(self.place(u), self.recv.at[0, u]))
                many = staticmethod(
                    lambda u, i, far: self.arrived(self.place(u), self.recv.at[0, u])
                )
                straight = staticmethod(lambda u, i: self.arrived(self.place(u), self.recv.at[0, u]))
                between = staticmethod(lambda u, i, far: None)

            units_of(Step)

        def sent(self):
            def done(k, u):
                remote(
                    self.src.at[u], self.src.at[u], self.send.at[k, u], self.recv.at[0, u], {"seq": sib}
                ).wait_send()

            def between(u, i, far):
                done(1, u)
                done(0, u)

            class Step:
                few = staticmethod(lambda u, i: done(0, u))
                many = staticmethod(lambda u, i, far: done(0, u))
                straight = staticmethod(lambda u, i: done(0, u))

            Step.between = staticmethod(between)
            units_of(Step)

    def kept(step):
        for u in range(5):
            i = 5 * dm + u

            @pl.when(me < 3)
            def _(u=u, i=i):
                @pl.when(i < 8)
                def _():
                    step(u)

            @pl.when(me == 3)
            def _(u=u):
                step(u)

            @pl.when(me > 3)
            def _(u=u, i=i):
                @pl.when(i < 32)
                def _():
                    step(u)

    greet(me, dm)
    for load in loads:
        load.start()

    row = lax.broadcasted_iota(jnp.int32, (TOK, 1), 0)
    place = jnp.where(row < SPAN, span_ref[0, me] * SPAN + row, span_ref[1, me] * SPAN + row - SPAN)
    def own_rows():
        x_rows = x_ref[...].astype(F32)
        centered = x_rows - jnp.mean(x_rows, axis=-1, keepdims=True)
        inv_std = lax.rsqrt(jnp.mean(centered * centered, axis=-1, keepdims=True) + NORM_EPS)
        return x_rows, centered * inv_std, inv_std

    def own_cot():
        return jnp.where(place < len_ref[0], cot_ref[...].astype(F32), 0.0)

    loads[0].wait()
    xh_all[pl.ds(2 * me, 2)] = own_rows()[1].astype(BF16).reshape(2, SPAN, D)

    loads[1].wait()
    loads[2].wait()
    small[...] = jnp.zeros((128, 128), F32)
    small[0:8, 0:VEC_ROWS] = vectors_ref[...]
    vec_t = small[0:8, 0:64]
    for s in range(SEQ):
        take = [w_in_ref[:, 64 * int(p) : 64 * int(p) + 64] for p in PIECES[s]]
        qkv = jnp.concatenate(take[:3] + [vec_t], axis=1)
        win_own[s] = jnp.concatenate([jnp.concatenate(take[3:], axis=1), qkv], axis=0).astype(BF16)
    loads[4].wait()
    for u in range(5):
        wout_own[u] = fold(w_out_ref[8 * u : 8 * u + 8]).astype(BF16)

    def keep_unit(u):
        wout_all[5 * dm + u] = wout_own[u]

    kept(keep_unit)
    loads[3].wait()
    cot_own = own_cot()
    cot_all[pl.ds(2 * me, 2)] = cot_own.astype(BF16).reshape(2, SPAN, D)
    cot_sum = jnp.sum(cot_own, axis=0, keepdims=True)
    vg[...] = jnp.transpose(jnp.broadcast_to(cot_sum, (128, D)))
    keep = pltpu.make_async_copy(win_own.at[me], win_all.at[dm, me], local_sem.at[0])
    keep.start()

    @pl.loop(0, 32)
    def _(i):
        slot = jnp.int32(0)
        for s in range(SEQ):
            for j in range(2):
                slot = jnp.maximum(slot, jnp.where(span_ref[j, s] == i, 2 * s + j, 0))
        inv_ref[i] = slot

    def seq_turn(s, k):
        return lax.rem(s + 4 * k, SEQ)

    def dp_turn(d, k):
        return d // 4 * 4 + lax.rem(d + k, 4)

    x_tree = Tree(
        "seq",
        lambda slot, h: xh_all.at[2 * slot + h],
        me,
        seq_turn,
        mate,
        x_send.at[0],
        x_recv,
        True,
        sib,
        x_given.at[0],
    )
    cot_tree = Tree(
        "seq",
        lambda slot, h: cot_all.at[2 * slot + h],
        me,
        seq_turn,
        mate,
        c_send.at[0],
        c_recv,
        True,
        sib,
        c_given.at[0],
    )
    in_tree = Tree(
        "dp",
        lambda slot, h: win_all.at[slot, pl.ds(8 * h, 8)],
        dm,
        dp_turn,
        dp_mate,
        l_send.at[0],
        l_recv,
        False,
    )
    out_tree = Tree(
        "dp",
        lambda slot, h: wout_all.at[pl.ds(5 * slot + 2 * h, 2 + h)],
        dm,
        dp_turn,
        dp_mate,
        o_send.at[0],
        o_recv,
        False,
    )

    def a_copy(k, to, frm):
        return remote(
            win_own.at[to], win_all.at[dm, frm], a_send.at[0], a_recv.at[0], {"seq": to}
        )

    await_greetings()

    @pl.loop(1, SEQ)
    def _(k):
        a_copy(k, lax.rem(me + k, SEQ), me).start()

    out_trade = Trade(wout_own, wout_all, w_relay, 5 * dm, w_send, w_recv)
    out_trade.whole = True
    out_trade.begin()
    x_tree.own_to_mate()
    x_tree.own_to_ring()
    keep.wait()

    all_here(win_own.at[pl.ds(0, SEQ - 1)], a_recv.at[0])

    in_tree.own_to_mate()
    in_tree.own_to_ring()
    out_trade.relay_on()
    x_tree.near_first(me)
    x_tree.of_mate((0,))
    in_tree.near_first(dm)
    x_tree.near_rest(me)
    x_tree.of_mate((1,))
    in_tree.near_rest(dm)
    in_tree.of_mate()
    x_tree.far_of_me()
    in_tree.far_of_me()
    cot_tree.own_to_ring()

    def unpack(column):
        def step(sb, carry):
            cq, cf = carry
            tiles = [win_all[4 * column + y, sb].astype(F32) for y in range(4)]
            ff = jnp.concatenate([t[:8] for t in tiles], axis=0)
            qk = jnp.concatenate([t[8:] for t in tiles], axis=0)
            rows = pl.ds(pl.multiple_of(sb * 64 + 32 * column, 32), 32)
            gain_a, bias_a, gain_m, bias_m = (qk[:, 192 + i : 193 + i] for i in range(4))
            wr[rows] = jnp.concatenate([ff, qk], axis=1).astype(BF16)
            folded = jnp.where(lane_iota(qk.shape) < 192, qk * gain_a, 0.0)
            wp[rows] = jnp.concatenate([ff * gain_m, folded], axis=1).astype(BF16)
            return (
                cq + jnp.sum(qk * bias_a, axis=0, keepdims=True),
                cf + jnp.sum(ff * bias_m, axis=0, keepdims=True),
            )

        return step

    zero_row = jnp.zeros((1, 256), F32)
    sums = (zero_row, zero_row)
    for sb in range(SEQ):
        sums = unpack(dm // 4)(sb, sums)
    in_tree.near_of_mate()
    x_tree.near_of_mate()
    out_trade.end()
    out_tree.own_to_mate()
    out_tree.own_to_ring()
    cot_tree.own_to_mate()
    in_tree.far_of_mate()
    x_tree.far_of_mate()
    for sb in range(SEQ):
        sums = unpack(dp_mate // 4)(sb, sums)
    cq, cf = sums

    slab = jnp.transpose(wr[:, 384:512].astype(F32))
    vec_ref[...] = slab[64:80]
    loads[5].wait()
    loads[6].wait()

    hid = []
    for r in range(4):
        w = hidden_index(me, r)
        rows = pl.ds(pl.multiple_of(lax.rem(w, 16) * 64, 64), 64)
        part = wr[rows, 384:512].astype(F32)
        lane = 64 + 9 + w // 16
        hid.append(
            jnp.sum(jnp.where(lane_iota(part.shape) == lane, part, 0.0), axis=1, keepdims=True)
        )
    hid = jnp.concatenate(hid, axis=0)
    cf = cf + jnp.transpose(jnp.broadcast_to(hid, (256, 128)))[0:1]

    head_rows = pl.ds(pl.multiple_of(head * 64, 64), 64)
    head_vecs = wr[head_rows, 384:512].astype(F32)
    bq, bk, bv = (head_vecs[:, 68 + i : 69 + i] for i in range(3))

    all_here(xh_all.at[pl.ds(0, 16)], x_given.at[0])

    aug = jnp.where(lax.broadcasted_iota(jnp.int32, (64, CH), 0) == 0, 1.0, 0.0)
    zeros_aug = jnp.zeros((64, CH), F32)

    def rotate_t(u, cosine, sine, sign):
        first, second = u[0:8], u[8:16]
        return jnp.concatenate(
            [
                first * cosine - sign * (second * sine),
                second * cosine + sign * (first * sine),
                u[16:],
            ],
            axis=0,
        )

    def project(i):
        start = pl.multiple_of(i * CH, CH)
        rows = pl.ds(start, CH)
        xh = jnp.concatenate([xh_all[inv_ref[8 * i + k]] for k in range(8)], axis=0)
        xs[rows] = xh
        first = dot(xh, wp[...])
        qkv = jnp.transpose(first[:, 256:] + cq)
        cosine, sine = cos_ref[:, rows], sin_ref[:, rows]
        q = rotate_t(qkv[0:64] + bq, cosine, sine, 1.0) * 0.125
        k = rotate_t(qkv[64:128] + bk, cosine, sine, 1.0)
        v = qkv[128:192] + bv
        q_full = jnp.concatenate([q, aug], axis=0)
        past = (start + lane_iota((64, CH))) >= len_ref[0]
        k_full = jnp.concatenate([k, jnp.where(past, NEG_FILL, 0.0) * aug], axis=0)
        v_full = jnp.concatenate([v, zeros_aug], axis=0)
        qt[:, rows] = q_full.astype(BF16)
        kt[:, rows] = k.astype(BF16)
        vt[:, rows] = v.astype(BF16)
        qn[rows] = jnp.transpose(q_full).astype(BF16)
        kn[rows] = jnp.transpose(k_full).astype(BF16)
        vn[rows] = jnp.transpose(v_full).astype(BF16)
        pre = first[:, :256] + cf
        cdf = 0.5 * (1.0 + lax.erf(pre * (1.0 / math.sqrt(2.0))))
        pdf = jnp.exp(-0.5 * pre * pre) * (1.0 / math.sqrt(2.0 * math.pi))
        activ = pre * cdf
        joined[pl.ds(8 * i, 8), :, 0:256] = activ.astype(BF16).reshape(8, SPAN, 256)
        joined_t[0:256, rows] = jnp.transpose(activ).astype(BF16)
        dact[rows] = cdf + pre * pdf

    project(0)
    cot_tree.near_of_me()
    out_tree.near_of_me()
    out_tree.of_mate()
    project(1)
    project(2)
    cot_tree.of_mate()
    project(3)
    cot_tree.far_of_me()
    out_tree.near_of_mate()
    out_tree.far_of_me()
    half = CH // 2

    def tiles(qi):
        below = [(kc * CH, CH, qi * CH, CH) for kc in range(qi)]
        return below + [(qi * CH, half, qi * CH, CH), (qi * CH + half, half, qi * CH + half, half)]

    def scores(k0, keys, q0, queries):
        s = dot(kn[k0 : k0 + keys], qt[:, q0 : q0 + queries])
        if k0 >= q0:
            shape = (keys, queries)
            seen = lax.broadcasted_iota(jnp.int32, shape, 0) <= lane_iota(shape)
            s = jnp.where(seen, s, NEG_FILL)
        return s

    def held(k0, keys, q0, queries):
        qi, kc = q0 // CH, k0 // CH
        rows, cols = slice(k0 % CH, k0 % CH + keys), slice(q0 % CH, q0 % CH + queries)
        return exps.at[qi * (qi + 1) // 2 + kc, rows, cols]

    def spread(value, queries, fill):
        if queries == CH:
            return value
        return jnp.concatenate([jnp.full_like(value, fill), value], axis=1)

    for qi in range(NCH):
        lanes = slice(qi * CH, (qi + 1) * CH)
        parts = [(t, scores(*t)) for t in tiles(qi)]
        tops = [spread(jnp.max(s, axis=0, keepdims=True), t[3], NEG_FILL) for t, s in parts]
        top = functools.reduce(jnp.maximum, tops)
        total = jnp.zeros((1, CH), F32)
        out = jnp.zeros((64, CH), F32)
        for (k0, keys, q0, queries), s in parts:
            p = jnp.exp(s - top[:, CH - queries :])
            total = total + spread(jnp.sum(p, axis=0, keepdims=True), queries, 0.0)
            p = p.astype(BF16)
            held(k0, keys, q0, queries)[...] = p
            out = out + spread(dot(vt[:, k0 : k0 + keys], p), queries, 0.0)
        one_over = 1.0 / total
        out = out * one_over
        ot[:, lanes] = out
        scale[:, lanes] = jnp.broadcast_to(one_over, (8, CH))
        joined_t[256:320, lanes] = out.astype(BF16)
        joined[8 * qi : 8 * qi + 8, :, 256:320] = (
            jnp.transpose(out).astype(BF16).reshape(8, SPAN, HEAD)
        )
    out_tree.far_of_mate()

    def put_units(base, at, count):
        @pl.loop(0, count // 2, unroll=True)
        def _(i):
            pair = [unfold(wout_all[base + 2 * i + j].astype(F32)) for j in range(2)]
            rows = pl.ds(pl.multiple_of(at + i * 16, 16), 16)
            wo[rows] = jnp.concatenate(pair, axis=0).astype(BF16)

    late = (me + 12) // 16
    put_units(8 * (1 - late), 0, 32)
    put_units(32 * late, 256, 8)

    def of_chips(ref, chips):
        return jnp.concatenate(
            [ref[span_ref[i % 2, 2 * j + i // 2]] for j in chips for i in range(4)], axis=0
        )

    order = [(mate, 2), (mate, 1), (mate, 3), (me, 2), (me, 3), (me, 1), (mate, 0), (me, 0)]

    class ChipSums:
        def __init__(self, part, buf, sib_buf, land, s_send, s_recv, send, recv):
            self.part, self.buf, self.sib_buf, self.land = part, buf, sib_buf, land
            self.s_send, self.s_recv = s_send, s_recv
            self.tree = SumTree(
                "seq",
                lambda slot, h: buf.at[2 * slot + h],
                land,
                me,
                seq_turn,
                mate,
                send,
                recv,
            )

        def to_sib(self, j):
            return remote(
                self.buf.at[pl.ds(4 * j + 2 - 2 * core, 2)],
                self.sib_buf.at[j],
                self.s_send,
                self.s_recv.at[j],
                {"seq": sib},
            )

        def compute(self, n):
            chips = [seq_turn(*order[m]) // 2 for m in (n, n + 1)]
            value = self.part(chips).astype(BF16).reshape(8, SPAN, D)
            for m, j in enumerate(chips):
                self.buf[pl.ds(4 * j, 4)] = value[4 * m : 4 * m + 4]
                self.to_sib(j).start()

        def pair(self, n):
            j = seq_turn(*order[n]) // 2
            self.to_sib(j).wait_recv()
            mine = pl.ds(4 * j + 2 * core, 2)
            self.buf[mine] = (self.buf[mine].astype(F32) + self.sib_buf[j].astype(F32)).astype(BF16)
            if n == 0:
                self.tree.far_of_mate()
            elif n < 3:
                self.tree.near_of_mate(order[n][1])
            elif n in (4, 5):
                self.tree.near_early(order[n][1])

        def begin(self, between=(), pairs=6):
            for n in range(8):
                if n % 2 == 0:
                    self.compute(n)
                for at, step in between:
                    if at == n:
                        step()
                if 2 < n < pairs + 3:
                    self.pair(n - 3)
            if pairs == 6:
                self.pair(5)

        def pair_rest(self, pairs):
            for n in range(pairs, 6):
                self.pair(n)

        def of_mate(self):
            self.pair(6)
            self.tree.of_mate()
            self.pair(7)

        def total(self):
            return self.tree.total()

        def sent(self):
            all_sent(self.land, self.tree.send)
            all_sent(self.sib_buf, self.s_send)

    po = ChipSums(
        lambda chips: dot(of_chips(joined, chips), wo[...]),
        xh_all,
        po_sib,
        po_land,
        ps_send.at[0],
        ps_recv,
        p_send.at[0],
        p_recv,
    )
    hg = ChipSums(
        lambda chips: dot_nt(of_chips(mixed, chips), wp[...]),
        cot_all,
        hg_sib,
        hg_land,
        hs_send.at[0],
        hs_recv,
        h_send.at[0],
        h_recv,
    )
    all_sent(xh_all.at[pl.ds(0, 30)], x_send.at[0])
    po.begin(((2, cot_tree.near_of_mate), (3, cot_tree.far_of_mate)), 3)
    all_here(cot_all.at[pl.ds(0, 16)], c_given.at[0])

    @pl.loop(0, 32, unroll=True)
    def _(i):
        cs[pl.ds(SPAN * i, SPAN)] = cot_all[inv_ref[i]]

    def grads_by_owner(dst, base, columns):
        sums = jnp.sum(
            mixed[:, :, base : base + 256].reshape(ROW, 256).astype(F32), axis=0, keepdims=True
        )

        @pl.loop(0, 4, unroll=True)
        def _(i):
            rows = pl.ds(pl.multiple_of(i * 256, 256), 256)
            h = jnp.transpose(dot(mixed_t[base : base + 256], xs[:, rows]))
            raw = wr[rows, base : base + 256].astype(F32)
            vecs = wr[rows, 384:512].astype(F32)
            gain, bias = (vecs[:, columns + 64 + j : columns + 65 + j] for j in range(2))
            grad = gain * h + bias * sums
            lanes = lane_iota((256, 128))
            extra = vg[rows]
            for j, col in enumerate((raw * h, raw * sums)):
                extra = extra + jnp.where(
                    lanes == 64 + columns + j, jnp.sum(col, axis=1, keepdims=True), 0.0
                )
            if base:
                grad = jnp.concatenate([grad[:, :128], grad[:, 128:] + extra], axis=1)
            else:
                vg[rows] = extra
            for j in range(2):
                pair = [
                    grad[128 * j + 64 * t : 128 * j + 64 * t + 64].reshape(8, 8, 256)
                    for t in range(2)
                ]
                dst[:, 2 * i + j] = jnp.concatenate(pair, axis=1).astype(BF16)

    def owner_sums(dst, land, send, recv):
        return ColumnSums(
            "dp",
            lambda slot: dst.at[slot],
            land,
            dm,
            dp_turn,
            dp_mate,
            send.at[0],
            recv,
        )

    gf_sums = owner_sums(gf, gf_land, gf_send, gf_recv)
    gq_sums = owner_sums(gq, gq_land, gq_send, gq_recv)
    go_sums = ColumnSums(
        "dp",
        lambda slot: go_buf.at[pl.ds(5 * slot, 5)],
        go_land,
        dm,
        dp_turn,
        dp_mate,
        go_send.at[0],
        go_recv,
    )
    @pl.loop(0, 2, unroll=True)
    def _(i):
        left = dot(joined_t[...], cs[:, pl.ds(pl.multiple_of(i * 256, 256), 256)])
        right = dot(joined_t[...], cs[:, pl.ds(pl.multiple_of(i * 256 + 512, 256), 256)])
        units = jnp.concatenate([left.reshape(40, 8, 256), right.reshape(40, 8, 256)], axis=1)
        lanes = pl.ds(pl.multiple_of(i * 256, 256), 256)
        go_buf[pl.ds(8 * (1 - late), 32), :, lanes] = units[:32].astype(BF16)
        go_buf[pl.ds(32 * late, 8), :, lanes] = units[32:].astype(BF16)

    go_sums.start()
    po.pair_rest(3)

    @pl.loop(0, NCH, unroll=True)
    def _(i):
        rows = pl.ds(pl.multiple_of(i * CH, CH), CH)
        cot = cs[rows]
        back = dot_nt(cot, wo[...])
        ag = back[:, 256:].astype(BF16).astype(F32)
        ag_t = jnp.transpose(ag)
        dot_n[rows] = ag.astype(BF16)
        dot_t[:, rows] = ag_t.astype(BF16)
        delta[:, rows] = jnp.broadcast_to(
            jnp.sum(ag_t * ot[:, rows], axis=0, keepdims=True), (8, CH)
        )
        pg = back[:, :256] * dact[rows]
        mixed[pl.ds(8 * i, 8), :, 0:256] = pg.astype(BF16).reshape(8, SPAN, 256)
        mixed_t[0:256, rows] = jnp.transpose(pg).astype(BF16)

    lanes_d = lane_iota((D, 128))
    vg[...] = jnp.where((lanes_d == 71) | (lanes_d == 72), vg[...], 0.0)
    lanes_h = lane_iota((64, 128))
    cols_f = jnp.sum(mixed_t[0:256].astype(F32), axis=1, keepdims=True)
    for r in range(4):
        w = hidden_index(me, r)
        rows = pl.ds(pl.multiple_of(lax.rem(w, 16) * 64, 64), 64)
        vg[rows] += jnp.where(lanes_h == 64 + 9 + w // 16, cols_f[64 * r : 64 * r + 64], 0.0)
    grads_by_owner(gf, 0, 2)
    gf_sums.start()
    po.tree.far_of_me()
    po.of_mate()

    for qi in reversed(range(NCH)):
        lanes = slice(qi * CH, (qi + 1) * CH)
        dq = jnp.zeros((64, CH), F32)
        for k0, keys, q0, queries in tiles(qi):
            at, cols = slice(k0, k0 + keys), slice(q0, q0 + queries)
            p = held(k0, keys, q0, queries)[...].astype(F32) * scale[0:1, cols]
            dp = dot(vn[at, 0:64], dot_t[:, cols])
            ds = (p * (dp - delta[0:1, cols])).astype(BF16)
            dv = dot(p.astype(BF16), dot_n[cols])
            dk = dot(ds, qn[cols, 0:64])
            dq = dq + spread(dot(kt[:, at], ds), queries, 0.0)
            if qi == NCH - 1:
                dvn[at] = dv
                dkn[at] = dk
            else:
                dvn[at] += dv
                dkn[at] += dk
        dqt[:, lanes] = dq * 0.125

    @pl.loop(0, NCH, unroll=True)
    def _(i):
        rows = pl.ds(pl.multiple_of(i * CH, CH), CH)
        cosine, sine = cos_ref[:, rows], sin_ref[:, rows]
        dq = rotate_t(dqt[:, rows], cosine, sine, -1.0)
        dk = rotate_t(jnp.transpose(dkn[rows]), cosine, sine, -1.0)
        dv = jnp.transpose(dvn[rows])
        full = jnp.concatenate([dq, dk, dv, zeros_aug], axis=0)
        mixed_t[256:512, rows] = full.astype(BF16)
        mixed[pl.ds(8 * i, 8), :, 256:512] = jnp.transpose(full).astype(BF16).reshape(8, SPAN, 256)

    cols_q = jnp.sum(mixed_t[256:448].astype(F32), axis=1, keepdims=True)
    for i in range(3):
        vg[head_rows] += jnp.where(lanes_h == 68 + i, cols_q[64 * i : 64 * i + 64], 0.0)
    go_sums.middle()
    grads_by_owner(gq, 256, 0)
    gq_sums.start()
    po.tree.near_late()
    gf_sums.middle()

    all_sent(cot_all.at[pl.ds(0, 30)], c_send.at[0])

    def to_owner(part, total, send, recv, k, to, frm):
        return remote(part.at[to], total.at[frm], send.at[0], recv.at[0], {"seq": to})

    def own_sums(part, total, send, recv):
        @pl.loop(1, SEQ)
        def _(k):
            to_owner(part, total, send, recv, k, lax.rem(me + k, SEQ), me).start()

        total[me] = part[me]

    def own_arrived(part, total, send, recv):
        all_here(total.at[pl.ds(0, SEQ - 1)], recv.at[0])

    def squares_of(value):
        return jnp.sum(jnp.sum(value * value, axis=0), axis=0, keepdims=True)

    def fold_rows(value):
        return jnp.concatenate([value[:, :, :128], value[:, :, 128:]], axis=1).astype(BF16)

    f_squares = []

    def hidden_on():
        value = gf_sums.total().reshape(SEQ, 8, 256)
        f_squares.append(squares_of(value))
        f_part[...] = fold_rows(value)


    hg.begin(((6, hidden_on),))
    gq_sums.middle()
    out_total = go_sums.total()
    out_part[...] = out_total

    out_back = Trade(out_part, wout_sum, v_relay, 0, v_send, v_recv)
    out_back.whole = False

    def keep_total(u):
        wout_sum[u] = out_part[u]

    out_back.begin()
    kept(keep_total)
    out_squares = squares_of(out_total)
    squares = f_squares[0] + out_squares[:, :256] + out_squares[:, 256:]

    total = gq_sums.total().reshape(SEQ, 8, 256)
    weights = jnp.where(lane_iota(total.shape) < 192, total, 0.0)
    squares = squares + squares_of(weights)
    tile_a[...] = jnp.transpose(total[:, :, 128:].reshape(128, 128))[64:80]
    tile_a[15:16] = squares[:, :128] + squares[:, 128:]

    def ta_copy(k, to, frm):
        return remote(tile_a, got_a.at[frm], ta_send.at[0], ta_recv.at[0], {"seq": to})

    @pl.loop(1, SEQ)
    def _(k):
        ta_copy(k, lax.rem(me + k, SEQ), me).start()

    got_a[me] = tile_a[...]
    hg.tree.far_of_me()
    q_part[...] = fold_rows(total)
    own_sums(q_part, q_sum, bq_send, bq_recv)
    own_sums(f_part, f_sum, bf_send, bf_recv)
    hg.of_mate()
    out_back.relay_on()
    all_here(got_a.at[pl.ds(0, SEQ - 1)], ta_recv.at[0])
    sums = jnp.sum(got_a[...], axis=0)
    vec_total = jnp.where(lax.broadcasted_iota(jnp.int32, sums.shape, 0) < VEC_ROWS, sums, 0.0)
    row = sums[15:16] + jnp.sum(vec_total * vec_total, axis=0, keepdims=True)
    tile_b[...] = jnp.broadcast_to(jnp.sum(row, axis=1, keepdims=True), (8, 128))

    def tb_copy(k, to, frm):
        return remote(tile_b, got_b.at[frm], tb_send.at[0], tb_recv.at[0], {"dp": to})

    @pl.loop(1, DP)
    def _(k):
        tb_copy(k, lax.rem(dm + k, DP), dm).start()

    hg.tree.near_late()
    got_b[dm] = tile_b[...]
    small[...] = jnp.zeros((128, 128), F32)
    small[0:16] = vec_total
    small[...] = jnp.transpose(small[...])
    vec_grad[...] = small[pl.ds(pl.multiple_of(8 * me, 8), 8)]
    vec_store.start()
    own_arrived(f_part, f_sum, bf_send, bf_recv)
    x_rows, x_hat, inv_std = own_rows()
    cot_own = own_cot()
    block_out[...] = (x_rows + po.total() + (vec_ref[7:8] + vec_ref[8:9])).astype(BF16)
    block_store.start()
    own_arrived(q_part, q_sum, bq_send, bq_recv)
    for s in range(SEQ):
        for j, p in enumerate(PIECES[s]):
            at = 64 * int(p)
            ref, k = (q_sum, j) if j < 3 else (f_sum, j - 3)
            both = ref[s].astype(F32)
            grad_in[:, at : at + 64] = both[8 * (k // 2) : 8 * (k // 2) + 8, 64 * (k % 2) : 64 * (k % 2) + 64]
    in_store.start()
    out_back.end()
    for u in range(5):
        grad_out[8 * u : 8 * u + 8] = unfold(wout_sum[u])
    out_store.start()

    all_here(got_b.at[pl.ds(0, DP - 1)], tb_recv.at[0])
    everything = jnp.sum(got_b[...], axis=0)
    square_ref[...] = jnp.broadcast_to(everything[:, 0:1], (8, 128))
    square_store.start()
    grad = hg.total()
    back = (
        grad
        - jnp.mean(grad, axis=-1, keepdims=True)
        - x_hat * jnp.mean(grad * x_hat, axis=-1, keepdims=True)
    )
    input_grad[...] = (cot_own + inv_std * back).astype(BF16)
    grad_store.start()
    po.sent()
    hg.sent()
    out_trade.sent()
    out_back.sent()
    for sums in (gf_sums, gq_sums, go_sums):
        sums.sent()
    all_sent(win_all.at[pl.ds(0, 7)], l_send.at[0])
    all_sent(wout_all.at[pl.ds(0, 35)], o_send.at[0])
    all_sent(win_own.at[pl.ds(0, SEQ - 1)], a_send.at[0])
    all_sent(got_a.at[pl.ds(0, SEQ - 1)], ta_send.at[0])
    all_sent(got_b.at[pl.ds(0, DP - 1)], tb_send.at[0])
    all_sent(f_part.at[pl.ds(0, SEQ - 1)], bf_send.at[0])
    all_sent(q_part.at[pl.ds(0, SEQ - 1)], bq_send.at[0])
    for store in stores:
        store.wait()


def layer_call(span, length, x, cot, w_in, w_out, vectors):
    freqs = np.float32(THETA_BASE) ** (-2.0 * np.arange(ROT // 2) / ROT)
    angles = np.arange(ROW, dtype=np.float32)[None, :] * freqs.astype(np.float32)[:, None]
    cosine, sine = np.cos(angles).astype(np.float32), np.sin(angles).astype(np.float32)
    smem = pl.BlockSpec(memory_space=pltpu.SMEM)
    anywhere = pl.BlockSpec(memory_space=pl.ANY)
    sds = jax.ShapeDtypeStruct
    dma = pltpu.SemaphoreType.DMA

    def buf(shape, dtype=BF16):
        return pltpu.VMEM(shape, dtype)

    return pl.pallas_call(
        layer_kernel,
        out_shape=(
            sds((TOK, D), BF16),
            sds((TOK, D), BF16),
            sds((8, 7 * D), F32),
            sds((40, D), F32),
            sds((8, 128), F32),
            sds((8, 128), F32),
        ),
        in_specs=[smem] * 2 + [anywhere] * 7,
        out_specs=[anywhere] * 6,
        scratch_shapes=[
            buf((TOK, D)),
            buf((TOK, D)),
            buf((8, 7 * D), F32),
            buf((40, D), F32),
            buf((8, VEC_ROWS), F32),
            buf((8, ROW), F32),
            buf((8, ROW), F32),
            buf((TOK, D)),
            buf((TOK, D)),
            buf((8, 7 * D), F32),
            buf((40, D), F32),
            buf((SEQ, 16, 128)),
            buf((SEQ, 16, 128)),
            buf((5, 16, 512), F32),
            buf((8, 128), F32),
            buf((8, 128), F32),
            dma((7,)),
            dma((6,)),
            pltpu.SMEM((32,), jnp.int32),
            buf((32, SPAN, D)),
            buf((32, SPAN, D)),
            buf((SEQ, 16, 256)),
            buf((DP, SEQ, 16, 256)),
            buf((40, 16, 512)),
            buf((5, 16, 512)),
            buf((2, 5, 16, 512)),
            buf((2, 5, 16, 512), F32),
            buf((128, 128), F32),
            buf((16, D), F32),
            buf((ROW, D)),
            buf((ROW, D)),
            buf((D, 512)),
            buf((D, 512)),
            buf((320, D)),
            buf((128, ROW)),
            buf((ROW, 128)),
            buf((64, ROW)),
            buf((ROW, 128)),
            buf((64, ROW)),
            buf((ROW, 128)),
            buf((64, ROW)),
            buf((ROW, 64)),
            buf((64, ROW), F32),
            buf((8, ROW), F32),
            buf((10, CH, CH)),
            buf((8, ROW), F32),
            buf((32, SPAN, 320)),
            buf((320, ROW)),
            buf((ROW, 256), F32),
            buf((32, SPAN, 512)),
            buf((512, ROW)),
            buf((64, ROW), F32),
            buf((ROW, 64), F32),
            buf((ROW, 64), F32),
            buf((D, 128), F32),
            buf((40, 16, 512)),
            buf((5, 16, 512), F32),
            buf((DP, 8, 16, 256)),
            buf((DP, 8, 16, 256)),
            buf((8, 2, SPAN, D)),
            buf((8, 2, SPAN, D)),
            buf((7, 2, SPAN, D)),
            buf((7, 2, SPAN, D)),
            buf((8, 8, 16, 256)),
            buf((8, 8, 16, 256)),
            buf((8, 5, 16, 512)),
            buf((SEQ, 16, 128)),
            buf((SEQ, 16, 128)),
            buf((16, 128), F32),
            buf((8, 128), F32),
            buf((SEQ, 16, 128), F32),
            buf((DP, 8, 128), F32),
            dma((1,)),
            dma((1,)),
            dma((1,)),
            dma((1,)),
            dma((8, 2)),
            dma((1,)),
            dma((1,)),
            dma((8, 2)),
            dma((1,)),
            dma((1,)),
            dma((DP, 2)),
            dma((1,)),
            dma((DP, 2)),
            dma((2, 5)),
            dma((2, 5)),
            dma((1,)),
            dma((8,)),
            dma((1,)),
            dma((6,)),
            dma((1,)),
            dma((8,)),
            dma((1,)),
            dma((6,)),
            dma((1,)),
            dma((3,)),
            dma((1,)),
            dma((3,)),
            dma((1,)),
            dma((3,)),
            dma((2, 5)),
            dma((2, 5)),
            dma((1,)),
            dma((1,)),
            dma((1,)),
            dma((1,)),
            dma((1,)),
            dma((1,)),
            dma((1,)),
            dma((1,)),
        ],
        compiler_params=pltpu.CompilerParams(
            collective_id=0, has_side_effects=True, vmem_limit_bytes=VMEM_LIMIT
        ),
        name="layer_of_one_row",
    )(span, length, x, cot, w_in, w_out, vectors, jnp.asarray(cosine), jnp.asarray(sine))


def adam(weight, grad, first, second, factor, rate, decay):
    clipped = grad * factor
    first_new = BETA_ONE * first + (1.0 - BETA_ONE) * clipped
    second_new = BETA_TWO * second + (1.0 - BETA_TWO) * clipped * clipped
    first_hat = first_new / (1.0 - BETA_ONE**STEP)
    second_hat = second_new / (1.0 - BETA_TWO**STEP)
    weight_new = weight * (1.0 - rate * decay) - rate * first_hat / (
        jnp.sqrt(second_hat) + ADAM_EPS
    )
    return (weight_new, first_new, second_new, weight_new.astype(BF16))


UPDATE_IN = (
    ("block_out", (TOK, D), BF16),
    ("input_grad", (TOK, D), BF16),
    ("square", (8, 128), F32),
    ("grad_in", (8, 7 * D), F32),
    ("w_in", (8, 7 * D), F32),
    ("in_first", (8, 7 * D), F32),
    ("in_second", (8, 7 * D), F32),
    ("grad_out", (40, D), F32),
    ("w_out", (40, D), F32),
    ("out_first", (40, D), F32),
    ("out_second", (40, D), F32),
    ("vectors", (8, VEC_ROWS), F32),
    ("vec_first", (8, VEC_ROWS), F32),
    ("vec_second", (8, VEC_ROWS), F32),
    ("vec_grad", (8, 128), F32),
)
UPDATE_OUT = (
    ((TOK, D), BF16),
    ((TOK, D), BF16),
    ((8, 7 * D), F32),
    ((40, D), F32),
    ((8, VEC_ROWS), F32),
    ((8, 7 * D), F32),
    ((40, D), F32),
    ((8, VEC_ROWS), F32),
    ((8, 7 * D), F32),
    ((40, D), F32),
    ((8, VEC_ROWS), F32),
    ((8, 7 * D), BF16),
    ((40, D), BF16),
    ((8, VEC_ROWS), BF16),
)


def update_kernel(*refs):
    ins, refs = refs[: len(UPDATE_IN)], refs[len(UPDATE_IN) :]
    norm_ref, refs = refs[0], refs[1:]
    outs, refs = refs[: len(UPDATE_OUT)], refs[len(UPDATE_OUT) :]
    in_bufs, refs = refs[: len(UPDATE_IN)], refs[len(UPDATE_IN) :]
    out_bufs, (in_sem, out_sem) = refs[: len(UPDATE_OUT)], refs[len(UPDATE_OUT) :]
    loads = [
        pltpu.make_async_copy(a, b, in_sem.at[i]) for i, (a, b) in enumerate(zip(ins, in_bufs))
    ]
    stores = [
        pltpu.make_async_copy(in_bufs[i] if i < 2 else b, a, out_sem.at[i])
        for i, (a, b) in enumerate(zip(outs, out_bufs))
    ]
    order = list(range(2, len(loads))) + [0, 1]
    for i in order:
        loads[i].start()
    names = [name for name, _, _ in UPDATE_IN]

    def take(name):
        i = names.index(name)
        loads[i].wait()
        return in_bufs[i]

    def give(i, value):
        out_bufs[i][...] = value
        stores[i].start()

    norm = jnp.sqrt(take("square")[...])
    norm_ref[0, 0] = norm[0, 0]
    factor = jnp.minimum(1.0, CLIP_NORM / norm)[0:1, 0:1]

    for i in range(2):
        loads[i].wait()
        stores[i].start()

    def matrix(at, grad, weight, first, second, rate, decay):
        values = adam(
            take(weight)[...], grad, take(first)[...], take(second)[...], factor, rate, decay
        )
        for k, value in enumerate(values):
            give(at + 3 * k, value)

    matrix(2, take("grad_in")[...], "w_in", "in_first", "in_second", RATE_MATRIX, DECAY_RATE)
    matrix(3, take("grad_out")[...], "w_out", "out_first", "out_second", RATE_MATRIX, DECAY_RATE)
    grad_vec = take("vec_grad")[:, 0:VEC_ROWS]
    matrix(4, grad_vec, "vectors", "vec_first", "vec_second", RATE_VECTOR, 0.0)

    for store in stores:
        store.wait()


def update_call(*args):
    anywhere = pl.BlockSpec(memory_space=pl.ANY)
    dma = pltpu.SemaphoreType.DMA
    sds = jax.ShapeDtypeStruct
    return pl.pallas_call(
        update_kernel,
        out_shape=(sds((1, 1), F32),) + tuple(sds(shape, kind) for shape, kind in UPDATE_OUT),
        in_specs=[anywhere] * len(UPDATE_IN),
        out_specs=[pl.BlockSpec(memory_space=pltpu.SMEM)] + [anywhere] * len(UPDATE_OUT),
        scratch_shapes=[pltpu.VMEM(shape, kind) for _, shape, kind in UPDATE_IN]
        + [pltpu.VMEM(shape, kind) for shape, kind in UPDATE_OUT]
        + [dma((len(UPDATE_IN),)), dma((len(UPDATE_OUT),))],
        compiler_params=pltpu.CompilerParams(vmem_limit_bytes=UPDATE_LIMIT),
        name="clipped_update",
    )(*args)


def body(
    hidden_in,
    out_cot,
    in_weight,
    out_weight,
    vectors,
    in_first,
    in_second,
    out_first,
    out_second,
    vec_first,
    vec_second,
    lengths,
    span_of,
):
    block_out, input_grad, grad_in, grad_out, squares, vec_grad = layer_call(
        span_of.T, lengths, hidden_in[0], out_cot[0], in_weight, out_weight, vectors.T
    )
    norm, block_out, input_grad, *rest = update_call(
        block_out,
        input_grad,
        squares,
        grad_in,
        in_weight,
        in_first,
        in_second,
        grad_out,
        out_weight,
        out_first,
        out_second,
        vectors.T,
        vec_first.T,
        vec_second.T,
        vec_grad,
    )
    rest = [out.T if i % 3 == 2 else out for i, out in enumerate(rest)]
    return (block_out[None], input_grad[None], norm.reshape(()), *rest)


def solution(mesh):
    tokens = P("dp", "seq", None)
    matrix = P(("seq", "dp"), None)
    vector = P(None, ("seq", "dp"))
    return jax.shard_map(
        body,
        mesh=mesh,
        in_specs=(
            tokens,
            tokens,
            matrix,
            matrix,
            vector,
            matrix,
            matrix,
            matrix,
            matrix,
            vector,
            vector,
            P("dp"),
            P(),
        ),
        out_specs=(tokens, tokens, P()) + (matrix, matrix, vector) * 4,
        check_vma=False,
    )
```

```python
import functools
import math

import jax
import jax.numpy as jnp
import numpy as np
from jax import lax
from jax.experimental import pallas as pl
from jax.experimental.pallas import tpu as pltpu
from jax.sharding import PartitionSpec as P

D = 1024
FF = 4096
HEADS = 16
HEAD = 64
ROT = 16
STEP = 5
SEQ = 16
DP = 8
TOK = 128
ROW = 2048
SPAN = 64
VEC_ROWS = 13

NORM_EPS = 1e-05
NEG_FILL = -1e30
CLIP_NORM = 1.0
RATE_MATRIX = 0.02
RATE_VECTOR = 0.2
BETA_ONE = 0.5
BETA_TWO = 0.5
DECAY_RATE = 0.1
ADAM_EPS = 1e-08
THETA_BASE = 10000.0

F32 = jnp.float32
BF16 = jnp.bfloat16
MESH = pl.DeviceIdType.MESH
VMEM_LIMIT = 60 * 1024 * 1024
UPDATE_LIMIT = 60 * 1024 * 1024


def head_of(s):
    if s < 4:
        return 5 * s
    return 5 * ((s - 4) // 4) + 1 + (s - 4) % 4


def hidden_pieces(s):
    if s < 3:
        return [20 * s + 5 * r + 8 for r in range(4)]
    if s == 3:
        return [0, 1, 2, 3]
    return [5 * s - 16 + r for r in range(4)]


def column_pieces():
    rows = []
    for s in range(SEQ):
        h = head_of(s)
        rows.append([h, 16 + h, 32 + h] + [48 + w for w in hidden_pieces(s)])
    return np.array(rows, np.int32)


PIECES = column_pieces()


def head_index(s):
    late = (s + 12) // 16
    return (1 - late) * (5 * s) + late * (5 * ((s - 4) // 4) + 1 + lax.rem(s, 4))


def hidden_index(s, r):
    late, not_few = (s + 12) // 16, (s + 13) // 16
    return (
        (1 - not_few) * (20 * s + 5 * r + 8) + (not_few - late) * r + late * (5 * s - 16 + r)
    )


def remote(src, dst, send, recv, where):
    return pltpu.make_async_remote_copy(
        src_ref=src, dst_ref=dst, send_sem=send, recv_sem=recv, device_id=where, device_id_type=MESH
    )


def greet(me, dm):
    barrier = pltpu.get_barrier_semaphore()

    @pl.loop(1, SEQ)
    def _(k):
        pl.semaphore_signal(
            barrier, inc=1, device_id={"seq": lax.rem(me + k, SEQ)}, device_id_type=MESH
        )

    @pl.loop(1, DP)
    def _(k):
        pl.semaphore_signal(
            barrier, inc=1, device_id={"dp": lax.rem(dm + k, DP)}, device_id_type=MESH
        )


def await_greetings():
    pl.semaphore_wait(pltpu.get_barrier_semaphore(), SEQ + DP - 2)


def all_sent(ref, sem):
    remote(ref, ref, sem, sem, {"seq": 0}).wait_send()


def all_here(ref, sem):
    pltpu.make_async_copy(ref, ref, sem).wait()


class Tree:
    def __init__(self, axis, piece, me, turn, mate, send, recv, over_mate, sib=None, given=None):
        self.axis, self.piece, self.me, self.turn, self.mate = (axis, piece, me, turn, mate)
        self.send, self.recv, self.over_mate = send, recv, over_mate
        self.sib, self.given = sib, given
        self.per = 1 if sib is None else 2

    def put(self, slot, h, to):
        part = self.piece(slot, h)
        remote(part, part, self.send, self.arrival(slot, h), {self.axis: to}).start()

    def hand(self, slot, h):
        if self.sib is not None:
            part = self.piece(slot, h)
            remote(part, part, self.send, self.given, {self.axis: self.sib}).start()

    def arrival(self, slot, h):
        return self.recv.at[slot // self.per, h]

    def got(self, slot, h):
        part = self.piece(slot, h)
        remote(
            part, part, self.send, self.arrival(slot, h), {self.axis: self.mate}
        ).wait_recv()

    def own_to_ring(self):
        for h, k in ((0, 1), (1, 3), (1, 1), (0, 3)):
            self.put(self.me, h, self.turn(self.me, k))

    def own_to_mate(self):
        for h in range(2):
            self.put(self.me, h, self.mate)
        for h in range(2):
            self.hand(self.me, h)

    def of_mate(self, halves=(0, 1)):
        for h in halves:
            self.got(self.mate, h)
            for k in (1, 3):
                self.put(self.mate, h, self.turn(self.me, k))
            self.hand(self.mate, h)

    def near_first(self, base):
        for h, k in ((0, 3), (1, 1)):
            slot = self.turn(base, k)
            self.got(slot, h)
            self.put(slot, h, self.turn(self.me, 4 - k))
            self.hand(slot, h)

    def near_rest(self, base):
        for h, k in ((1, 3), (0, 1)):
            slot = self.turn(base, k)
            self.got(slot, h)
            self.hand(slot, h)

    def near(self, base):
        self.near_first(base)
        self.near_rest(base)

    def near_of_me(self):
        self.near(self.me)

    def far_of_me(self):
        slot = self.turn(self.me, 2)
        for h in range(2):
            self.got(slot, h)
            if self.over_mate:
                self.put(slot, h, self.mate)
            self.hand(slot, h)

    def near_of_mate(self):
        if not self.over_mate:
            return self.near(self.mate)
        for h in range(2):
            for k in (3, 1):
                slot = self.turn(self.mate, k)
                self.got(slot, h)
                self.hand(slot, h)

    def far_of_mate(self):
        slot = self.turn(self.mate, 2)
        for h in range(2):
            self.got(slot, h)
            self.hand(slot, h)


class SumTree:
    def __init__(self, axis, piece, landing, me, turn, mate, send, recv):
        self.axis, self.piece, self.me, self.turn, self.mate = (axis, piece, me, turn, mate)
        self.landing, self.send, self.recv = landing, send, recv

    def land(self, kind, h):
        return self.landing.at[kind, h]

    def arrival(self, kind, h):
        return self.recv.at[(h, 2, 2, 3 + h, 5, 5, 5)[kind]]

    def put(self, slot, kind, h, to):
        copy = remote(
            self.piece(slot, h),
            self.land(kind, h),
            self.send,
            self.arrival(kind, h),
            {self.axis: to},
        )
        copy.start()

    def add(self, slot, h, *kinds):
        part = self.piece(slot, h)
        total = part[...].astype(F32)
        for kind in kinds:
            total = total + self.land(kind, h)[...].astype(F32)
        part[...] = total.astype(BF16)

    def far_of_mate(self):
        for h in range(2):
            self.put(self.turn(self.mate, 2), 0, h, self.mate)

    def near_of_mate(self, k):
        for h in range(2):
            self.put(self.turn(self.mate, k), 2 if k == 1 else 1, h, self.turn(self.me, k))

    def near_early(self, k):
        h = 0 if k == 1 else 1
        self.put(self.turn(self.me, k), 5 if k == 1 else 4, h, self.turn(self.me, k))

    def far_of_me(self):
        slot = self.turn(self.me, 2)
        for h in range(2):
            all_here(self.land(0, h), self.arrival(0, h))
            self.add(slot, h, 0)
            self.put(slot, 3, h, self.turn(self.me, 3 - 2 * h))

    def near_late(self):
        for h in range(2):
            k = 3 - 2 * h
            slot = self.turn(self.me, k)
            all_here(self.land(3, h), self.arrival(3, h))
            self.add(slot, h, 3)
            self.put(slot, 4 + h, h, self.turn(self.me, k))

    def of_mate(self):
        all_here(self.landing.at[pl.ds(1, 2)], self.arrival(1, 0))
        for h in range(2):
            self.add(self.mate, h, 1, 2)
            self.put(self.mate, 6, h, self.mate)

    def begin(self):
        self.far_of_mate()
        for k in (1, 3):
            self.near_of_mate(k)
        for k in (1, 3):
            self.near_early(k)

    def total(self):
        all_here(self.landing.at[pl.ds(4, 3)], self.arrival(4, 0))
        parts = []
        for h in range(2):
            value = self.piece(self.me, h)[...].astype(F32)
            for kind in (4, 5, 6):
                value = value + self.land(kind, h)[...].astype(F32)
            parts.append(value)
        return jnp.concatenate(parts, axis=0)


class ColumnSums:
    def __init__(self, axis, piece, landing, me, turn, mate, send, recv):
        self.axis, self.piece, self.me, self.turn, self.mate = (axis, piece, me, turn, mate)
        self.land = lambda i: landing.at[i]
        self.lands = lambda i, n: landing.at[pl.ds(i, n)]
        self.send, self.recv = send, recv

    def copy(self, k, of_mate):
        to = self.turn(self.me, k)
        return remote(
            self.piece(self.turn(self.mate, k) if of_mate else to),
            self.land(4 * of_mate + 4 - k),
            self.send,
            self.recv.at[1 + of_mate],
            {self.axis: to},
        )

    def last(self):
        return remote(
            self.piece(self.mate),
            self.land(0),
            self.send,
            self.recv.at[0],
            {self.axis: self.mate},
        )

    def start(self):
        for of_mate in (1, 0):
            for k in (1, 3, 2):
                self.copy(k, of_mate).start()

    def summed(self, slot, of_mate):
        total = self.piece(slot)[...].astype(F32)
        all_here(self.lands(4 * of_mate + 1, 3), self.recv.at[1 + of_mate])
        for k in (1, 3, 2):
            total = total + self.land(4 * of_mate + 4 - k)[...].astype(F32)
        return total

    def middle(self):
        self.piece(self.mate)[...] = self.summed(self.mate, 1).astype(BF16)
        self.last().start()

    def total(self):
        value = self.summed(self.me, 0)
        self.last().wait_recv()
        return value + self.land(0)[...].astype(F32)

    def sent(self):
        all_sent(self.lands(0, 7), self.send)


def dot(a, b):
    return jnp.dot(a, b, preferred_element_type=F32)


def dot_nt(a, b):
    return lax.dot_general(a, b, (((1,), (1,)), ((), ())), preferred_element_type=F32)


def lane_iota(shape):
    return lax.broadcasted_iota(jnp.int32, shape, len(shape) - 1)


def fold(u):
    return jnp.concatenate([u[:, : D // 2], u[:, D // 2 :]], axis=0)


def unfold(u):
    return jnp.concatenate([u[:8], u[8:]], axis=1)


CH = 512
NCH = ROW // CH


def layer_kernel(
    span_ref,
    len_ref,
    x_any,
    cot_any,
    w_in_any,
    w_out_any,
    vectors_any,
    cos_any,
    sin_any,
    block_out_any,
    input_grad_any,
    grad_in_any,
    grad_out_any,
    square_any,
    vec_grad_any,
    x_ref,
    cot_ref,
    w_in_ref,
    w_out_ref,
    vectors_ref,
    cos_ref,
    sin_ref,
    block_out,
    input_grad,
    grad_in,
    grad_out,
    f_sum,
    q_sum,
    wout_sum,
    square_ref,
    vec_grad,
    load_sem,
    store_sem,
    inv_ref,
    xh_all,
    cot_all,
    win_own,
    win_all,
    wout_all,
    wout_own,
    w_relay,
    v_relay,
    small,
    vec_ref,
    xs,
    cs,
    wr,
    wp,
    wo,
    qt,
    qn,
    kt,
    kn,
    vt,
    vn,
    dot_t,
    dot_n,
    ot,
    scale,
    exps,
    delta,
    joined,
    joined_t,
    dact,
    mixed,
    mixed_t,
    dqt,
    dkn,
    dvn,
    vg,
    go_buf,
    out_part,
    gf,
    gq,
    po_sib,
    hg_sib,
    po_land,
    hg_land,
    gf_land,
    gq_land,
    go_land,
    f_part,
    q_part,
    tile_a,
    tile_b,
    got_a,
    got_b,
    local_sem,
    a_send,
    a_recv,
    x_send,
    x_recv,
    x_given,
    c_send,
    c_recv,
    c_given,
    l_send,
    l_recv,
    o_send,
    o_recv,
    w_send,
    w_recv,
    ps_send,
    ps_recv,
    p_send,
    p_recv,
    hs_send,
    hs_recv,
    h_send,
    h_recv,
    gf_send,
    gf_recv,
    gq_send,
    gq_recv,
    go_send,
    go_recv,
    v_send,
    v_recv,
    bf_send,
    bf_recv,
    bq_send,
    bq_recv,
    ta_send,
    ta_recv,
    tb_send,
    tb_recv,
):
    me = lax.axis_index("seq")
    dm = lax.axis_index("dp")
    core = lax.rem(me, 2)
    chip = me // 2
    sib = me + 1 - 2 * core
    mate = me + 2 - 4 * lax.rem(chip, 2)
    dp_mate = lax.rem(dm + 4, DP)
    head = head_index(me)
    loads = [
        pltpu.make_async_copy(a, b, load_sem.at[i])
        for i, (a, b) in enumerate(
            (
                (x_any, x_ref),
                (w_in_any, w_in_ref),
                (vectors_any, vectors_ref),
                (cot_any, cot_ref),
                (w_out_any, w_out_ref),
                (cos_any, cos_ref),
                (sin_any, sin_ref),
            )
        )
    ]
    block_store, grad_store, in_store, out_store, square_store, vec_store = stores = [
        pltpu.make_async_copy(a, b, store_sem.at[i])
        for i, (a, b) in enumerate(
            (
                (block_out, block_out_any),
                (input_grad, input_grad_any),
                (grad_in, grad_in_any),
                (grad_out, grad_out_any),
                (square_ref, square_any),
                (vec_grad, vec_grad_any),
            )
        )
    ]
    def units_of(step):
        for u in range(5):
            i = 5 * dm + u

            @pl.when(me < 3)
            def _(u=u, i=i):
                @pl.when(i >= 8)
                def _():
                    step.few(u, i)

            @pl.when(me > 3)
            def _(u=u, i=i):
                r = lax.rem(me, 4)

                @pl.when(i >= 32)
                def _():
                    @pl.when(r < 3)
                    def _():
                        step.many(u, i, 8 + 8 * r + i - 32)

                    @pl.when(r == 3)
                    def _():
                        step.straight(u, i)

                @pl.when((i >= 8 + 8 * r) & (i < 16 + 8 * r) & (r < 3))
                def _():
                    step.between(u, i, 32 + lax.rem(i, 8))

    class Trade:
        def __init__(self, src, dst, relay, base, send, recv):
            self.src, self.dst, self.relay, self.base = src, dst, relay, base
            self.send, self.recv = send, recv

        def place(self, u):
            return self.dst.at[self.base + u]

        def few_out(self, u, i):
            to = 4 * me + 3 + i // 8
            last = i >= 32

            @pl.when(last)
            def _():
                remote(
                    self.src.at[u], self.place(u), self.send.at[0, u], self.recv.at[0, u], {"seq": to}
                ).start()

            @pl.when(jnp.logical_not(last))
            def _():
                remote(
                    self.src.at[u],
                    self.relay.at[0, u],
                    self.send.at[0, u],
                    self.recv.at[0, u],
                    {"seq": to},
                ).start()

        def many_out(self, u, i, far):
            at = lax.rem(far, 5)
            return remote(
                self.src.at[u],
                self.relay.at[1, at],
                self.send.at[0, u],
                self.recv.at[1, at],
                {"dp": far // 5},
            )

        def straight_out(self, u):
            return remote(
                self.src.at[u],
                self.place(u),
                self.send.at[0, u],
                self.recv.at[0, u],
                {"seq": (me - 4) // 4},
            )

        def on_to_few(self, u):
            return remote(
                self.relay.at[1, u],
                self.place(u),
                self.send.at[1, u],
                self.recv.at[0, u],
                {"seq": (me - 4) // 4},
            )

        def on_to_many(self, u, far):
            at = lax.rem(far, 5)
            base = self.base - 5 * dm + far - at if self.whole else self.base
            return remote(
                self.relay.at[0, u],
                self.dst.at[base + at],
                self.send.at[0, u],
                self.recv.at[0, at],
                {"dp": far // 5},
            )

        def arrived(self, ref, sem):
            remote(ref, ref, self.send.at[0, 0], sem, {"seq": sib}).wait_recv()

        def begin(self):
            class Step:
                few = staticmethod(self.few_out)
                many = staticmethod(lambda u, i, far: self.many_out(u, i, far).start())
                straight = staticmethod(lambda u, i: self.straight_out(u).start())
                between = staticmethod(lambda u, i, far: None)

            units_of(Step)

        def relay_on(self):
            def between(u, i, far):
                self.arrived(self.relay.at[0, u], self.recv.at[0, u])
                self.on_to_many(u, far).start()
                self.arrived(self.relay.at[1, u], self.recv.at[1, u])
                self.on_to_few(u).start()

            class Step:
                few = staticmethod(lambda u, i: None)
                many = staticmethod(lambda u, i, far: None)
                straight = staticmethod(lambda u, i: None)

            Step.between = staticmethod(between)
            units_of(Step)

        def end(self):
            class Step:
                few = staticmethod(lambda u, i: self.arrived(self.place(u), self.recv.at[0, u]))
                many = staticmethod(
                    lambda u, i, far: self.arrived(self.place(u), self.recv.at[0, u])
                )
                straight = staticmethod(lambda u, i: self.arrived(self.place(u), self.recv.at[0, u]))
                between = staticmethod(lambda u, i, far: None)

            units_of(Step)

        def sent(self):
            def done(k, u):
                remote(
                    self.src.at[u], self.src.at[u], self.send.at[k, u], self.recv.at[0, u], {"seq": sib}
                ).wait_send()

            def between(u, i, far):
                done(1, u)
                done(0, u)

            class Step:
                few = staticmethod(lambda u, i: done(0, u))
                many = staticmethod(lambda u, i, far: done(0, u))
                straight = staticmethod(lambda u, i: done(0, u))

            Step.between = staticmethod(between)
            units_of(Step)

    def kept(step):
        for u in range(5):
            i = 5 * dm + u

            @pl.when(me < 3)
            def _(u=u, i=i):
                @pl.when(i < 8)
                def _():
                    step(u)

            @pl.when(me == 3)
            def _(u=u):
                step(u)

            @pl.when(me > 3)
            def _(u=u, i=i):
                @pl.when(i < 32)
                def _():
                    step(u)

    greet(me, dm)
    for load in loads:
        load.start()

    row = lax.broadcasted_iota(jnp.int32, (TOK, 1), 0)
    place = jnp.where(row < SPAN, span_ref[0, me] * SPAN + row, span_ref[1, me] * SPAN + row - SPAN)
    def own_rows():
        x_rows = x_ref[...].astype(F32)
        centered = x_rows - jnp.mean(x_rows, axis=-1, keepdims=True)
        inv_std = lax.rsqrt(jnp.mean(centered * centered, axis=-1, keepdims=True) + NORM_EPS)
        return x_rows, centered * inv_std, inv_std

    def own_cot():
        return jnp.where(place < len_ref[0], cot_ref[...].astype(F32), 0.0)

    loads[0].wait()
    xh_all[pl.ds(2 * me, 2)] = own_rows()[1].astype(BF16).reshape(2, SPAN, D)

    loads[1].wait()
    loads[2].wait()
    small[...] = jnp.zeros((128, 128), F32)
    small[0:8, 0:VEC_ROWS] = vectors_ref[...]
    vec_t = small[0:8, 0:64]
    for s in range(SEQ):
        take = [w_in_ref[:, 64 * int(p) : 64 * int(p) + 64] for p in PIECES[s]]
        qkv = jnp.concatenate(take[:3] + [vec_t], axis=1)
        win_own[s] = jnp.concatenate([jnp.concatenate(take[3:], axis=1), qkv], axis=0).astype(BF16)
    loads[4].wait()
    for u in range(5):
        wout_own[u] = fold(w_out_ref[8 * u : 8 * u + 8]).astype(BF16)

    def keep_unit(u):
        wout_all[5 * dm + u] = wout_own[u]

    kept(keep_unit)
    loads[3].wait()
    cot_own = own_cot()
    cot_all[pl.ds(2 * me, 2)] = cot_own.astype(BF16).reshape(2, SPAN, D)
    cot_sum = jnp.sum(cot_own, axis=0, keepdims=True)
    vg[...] = jnp.transpose(jnp.broadcast_to(cot_sum, (128, D)))
    keep = pltpu.make_async_copy(win_own.at[me], win_all.at[dm, me], local_sem.at[0])
    keep.start()

    @pl.loop(0, 32)
    def _(i):
        slot = jnp.int32(0)
        for s in range(SEQ):
            for j in range(2):
                slot = jnp.maximum(slot, jnp.where(span_ref[j, s] == i, 2 * s + j, 0))
        inv_ref[i] = slot

    def seq_turn(s, k):
        return lax.rem(s + 4 * k, SEQ)

    def dp_turn(d, k):
        return d // 4 * 4 + lax.rem(d + k, 4)

    x_tree = Tree(
        "seq",
        lambda slot, h: xh_all.at[2 * slot + h],
        me,
        seq_turn,
        mate,
        x_send.at[0],
        x_recv,
        True,
        sib,
        x_given.at[0],
    )
    cot_tree = Tree(
        "seq",
        lambda slot, h: cot_all.at[2 * slot + h],
        me,
        seq_turn,
        mate,
        c_send.at[0],
        c_recv,
        True,
        sib,
        c_given.at[0],
    )
    in_tree = Tree(
        "dp",
        lambda slot, h: win_all.at[slot, pl.ds(8 * h, 8)],
        dm,
        dp_turn,
        dp_mate,
        l_send.at[0],
        l_recv,
        False,
    )
    out_tree = Tree(
        "dp",
        lambda slot, h: wout_all.at[pl.ds(5 * slot + 2 * h, 2 + h)],
        dm,
        dp_turn,
        dp_mate,
        o_send.at[0],
        o_recv,
        False,
    )

    def a_copy(k, to, frm):
        return remote(
            win_own.at[to], win_all.at[dm, frm], a_send.at[0], a_recv.at[0], {"seq": to}
        )

    await_greetings()

    @pl.loop(1, SEQ)
    def _(k):
        a_copy(k, lax.rem(me + k, SEQ), me).start()

    out_trade = Trade(wout_own, wout_all, w_relay, 5 * dm, w_send, w_recv)
    out_trade.whole = True
    out_trade.begin()
    x_tree.own_to_mate()
    x_tree.own_to_ring()
    keep.wait()

    all_here(win_own.at[pl.ds(0, SEQ - 1)], a_recv.at[0])

    in_tree.own_to_mate()
    in_tree.own_to_ring()
    out_trade.relay_on()
    x_tree.near_first(me)
    x_tree.of_mate((0,))
    in_tree.near_first(dm)
    x_tree.near_rest(me)
    x_tree.of_mate((1,))
    in_tree.near_rest(dm)
    in_tree.of_mate()
    x_tree.far_of_me()
    in_tree.far_of_me()
    cot_tree.own_to_ring()

    def unpack(column):
        def step(sb, carry):
            cq, cf = carry
            tiles = [win_all[4 * column + y, sb].astype(F32) for y in range(4)]
            ff = jnp.concatenate([t[:8] for t in tiles], axis=0)
            qk = jnp.concatenate([t[8:] for t in tiles], axis=0)
            rows = pl.ds(pl.multiple_of(sb * 64 + 32 * column, 32), 32)
            gain_a, bias_a, gain_m, bias_m = (qk[:, 192 + i : 193 + i] for i in range(4))
            wr[rows] = jnp.concatenate([ff, qk], axis=1).astype(BF16)
            folded = jnp.where(lane_iota(qk.shape) < 192, qk * gain_a, 0.0)
            wp[rows] = jnp.concatenate([ff * gain_m, folded], axis=1).astype(BF16)
            return (
                cq + jnp.sum(qk * bias_a, axis=0, keepdims=True),
                cf + jnp.sum(ff * bias_m, axis=0, keepdims=True),
            )

        return step

    zero_row = jnp.zeros((1, 256), F32)
    sums = (zero_row, zero_row)
    for sb in range(SEQ):
        sums = unpack(dm // 4)(sb, sums)
    in_tree.near_of_mate()
    x_tree.near_of_mate()
    out_trade.end()
    out_tree.own_to_mate()
    out_tree.own_to_ring()
    cot_tree.own_to_mate()
    in_tree.far_of_mate()
    x_tree.far_of_mate()
    for sb in range(SEQ):
        sums = unpack(dp_mate // 4)(sb, sums)
    cq, cf = sums

    slab = jnp.transpose(wr[:, 384:512].astype(F32))
    vec_ref[...] = slab[64:80]
    loads[5].wait()
    loads[6].wait()

    hid = []
    for r in range(4):
        w = hidden_index(me, r)
        rows = pl.ds(pl.multiple_of(lax.rem(w, 16) * 64, 64), 64)
        part = wr[rows, 384:512].astype(F32)
        lane = 64 + 9 + w // 16
        hid.append(
            jnp.sum(jnp.where(lane_iota(part.shape) == lane, part, 0.0), axis=1, keepdims=True)
        )
    hid = jnp.concatenate(hid, axis=0)
    cf = cf + jnp.transpose(jnp.broadcast_to(hid, (256, 128)))[0:1]

    head_rows = pl.ds(pl.multiple_of(head * 64, 64), 64)
    head_vecs = wr[head_rows, 384:512].astype(F32)
    bq, bk, bv = (head_vecs[:, 68 + i : 69 + i] for i in range(3))

    all_here(xh_all.at[pl.ds(0, 16)], x_given.at[0])

    aug = jnp.where(lax.broadcasted_iota(jnp.int32, (64, CH), 0) == 0, 1.0, 0.0)
    zeros_aug = jnp.zeros((64, CH), F32)

    def rotate_t(u, cosine, sine, sign):
        first, second = u[0:8], u[8:16]
        return jnp.concatenate(
            [
                first * cosine - sign * (second * sine),
                second * cosine + sign * (first * sine),
                u[16:],
            ],
            axis=0,
        )

    def project(i):
        start = pl.multiple_of(i * CH, CH)
        rows = pl.ds(start, CH)
        xh = jnp.concatenate([xh_all[inv_ref[8 * i + k]] for k in range(8)], axis=0)
        xs[rows] = xh
        first = dot(xh, wp[...])
        qkv = jnp.transpose(first[:, 256:] + cq)
        cosine, sine = cos_ref[:, rows], sin_ref[:, rows]
        q = rotate_t(qkv[0:64] + bq, cosine, sine, 1.0) * 0.125
        k = rotate_t(qkv[64:128] + bk, cosine, sine, 1.0)
        v = qkv[128:192] + bv
        q_full = jnp.concatenate([q, aug], axis=0)
        past = (start + lane_iota((64, CH))) >= len_ref[0]
        k_full = jnp.concatenate([k, jnp.where(past, NEG_FILL, 0.0) * aug], axis=0)
        v_full = jnp.concatenate([v, zeros_aug], axis=0)
        qt[:, rows] = q_full.astype(BF16)
        kt[:, rows] = k.astype(BF16)
        vt[:, rows] = v.astype(BF16)
        qn[rows] = jnp.transpose(q_full).astype(BF16)
        kn[rows] = jnp.transpose(k_full).astype(BF16)
        vn[rows] = jnp.transpose(v_full).astype(BF16)
        pre = first[:, :256] + cf
        cdf = 0.5 * (1.0 + lax.erf(pre * (1.0 / math.sqrt(2.0))))
        pdf = jnp.exp(-0.5 * pre * pre) * (1.0 / math.sqrt(2.0 * math.pi))
        activ = pre * cdf
        joined[pl.ds(8 * i, 8), :, 0:256] = activ.astype(BF16).reshape(8, SPAN, 256)
        joined_t[0:256, rows] = jnp.transpose(activ).astype(BF16)
        dact[rows] = cdf + pre * pdf

    project(0)
    cot_tree.near_of_me()
    out_tree.near_of_me()
    out_tree.of_mate()
    project(1)
    project(2)
    cot_tree.of_mate()
    project(3)
    cot_tree.far_of_me()
    out_tree.near_of_mate()
    out_tree.far_of_me()
    half = CH // 2

    def tiles(qi):
        below = [(kc * CH, CH, qi * CH, CH) for kc in range(qi)]
        return below + [(qi * CH, half, qi * CH, CH), (qi * CH + half, half, qi * CH + half, half)]

    def scores(k0, keys, q0, queries):
        s = dot(kn[k0 : k0 + keys], qt[:, q0 : q0 + queries])
        if k0 >= q0:
            shape = (keys, queries)
            seen = lax.broadcasted_iota(jnp.int32, shape, 0) <= lane_iota(shape)
            s = jnp.where(seen, s, NEG_FILL)
        return s

    def held(k0, keys, q0, queries):
        qi, kc = q0 // CH, k0 // CH
        rows, cols = slice(k0 % CH, k0 % CH + keys), slice(q0 % CH, q0 % CH + queries)
        return exps.at[qi * (qi + 1) // 2 + kc, rows, cols]

    def spread(value, queries, fill):
        if queries == CH:
            return value
        return jnp.concatenate([jnp.full_like(value, fill), value], axis=1)

    for qi in range(NCH):
        lanes = slice(qi * CH, (qi + 1) * CH)
        parts = [(t, scores(*t)) for t in tiles(qi)]
        tops = [spread(jnp.max(s, axis=0, keepdims=True), t[3], NEG_FILL) for t, s in parts]
        top = functools.reduce(jnp.maximum, tops)
        total = jnp.zeros((1, CH), F32)
        out = jnp.zeros((64, CH), F32)
        for (k0, keys, q0, queries), s in parts:
            p = jnp.exp(s - top[:, CH - queries :])
            total = total + spread(jnp.sum(p, axis=0, keepdims=True), queries, 0.0)
            p = p.astype(BF16)
            held(k0, keys, q0, queries)[...] = p
            out = out + spread(dot(vt[:, k0 : k0 + keys], p), queries, 0.0)
        one_over = 1.0 / total
        out = out * one_over
        ot[:, lanes] = out
        scale[:, lanes] = jnp.broadcast_to(one_over, (8, CH))
        joined_t[256:320, lanes] = out.astype(BF16)
        joined[8 * qi : 8 * qi + 8, :, 256:320] = (
            jnp.transpose(out).astype(BF16).reshape(8, SPAN, HEAD)
        )
    out_tree.far_of_mate()

    def put_units(base, at, count):
        @pl.loop(0, count // 2, unroll=True)
        def _(i):
            pair = [unfold(wout_all[base + 2 * i + j].astype(F32)) for j in range(2)]
            rows = pl.ds(pl.multiple_of(at + i * 16, 16), 16)
            wo[rows] = jnp.concatenate(pair, axis=0).astype(BF16)

    late = (me + 12) // 16
    put_units(8 * (1 - late), 0, 32)
    put_units(32 * late, 256, 8)

    def of_chips(ref, chips):
        return jnp.concatenate(
            [ref[span_ref[i % 2, 2 * j + i // 2]] for j in chips for i in range(4)], axis=0
        )

    order = [(mate, 2), (mate, 1), (mate, 3), (me, 2), (me, 3), (me, 1), (mate, 0), (me, 0)]

    class ChipSums:
        def __init__(self, part, buf, sib_buf, land, s_send, s_recv, send, recv):
            self.part, self.buf, self.sib_buf, self.land = part, buf, sib_buf, land
            self.s_send, self.s_recv = s_send, s_recv
            self.tree = SumTree(
                "seq",
                lambda slot, h: buf.at[2 * slot + h],
                land,
                me,
                seq_turn,
                mate,
                send,
                recv,
            )

        def to_sib(self, j):
            return remote(
                self.buf.at[pl.ds(4 * j + 2 - 2 * core, 2)],
                self.sib_buf.at[j],
                self.s_send,
                self.s_recv.at[j],
                {"seq": sib},
            )

        def compute(self, n):
            chips = [seq_turn(*order[m]) // 2 for m in range(n, min(n + (2 if n else 1), 8))]
            value = self.part(chips).astype(BF16).reshape(4 * len(chips), SPAN, D)
            for m, j in enumerate(chips):
                self.buf[pl.ds(4 * j, 4)] = value[4 * m : 4 * m + 4]
                self.to_sib(j).start()

        def pair(self, n):
            j = seq_turn(*order[n]) // 2
            self.to_sib(j).wait_recv()
            mine = pl.ds(4 * j + 2 * core, 2)
            self.buf[mine] = (self.buf[mine].astype(F32) + self.sib_buf[j].astype(F32)).astype(BF16)
            if n == 0:
                self.tree.far_of_mate()
            elif n < 3:
                self.tree.near_of_mate(order[n][1])
            elif n in (4, 5):
                self.tree.near_early(order[n][1])

        def begin(self, between=(), pairs=6):
            for n in range(8):
                if n == 0 or n % 2 == 1:
                    self.compute(n)
                for at, step in between:
                    if at == n:
                        step()
                if 1 < n < pairs + 2:
                    self.pair(n - 2)

        def pair_rest(self, pairs):
            for n in range(pairs, 6):
                self.pair(n)

        def of_mate(self):
            self.pair(6)
            self.tree.of_mate()
            self.pair(7)

        def total(self):
            return self.tree.total()

        def sent(self):
            all_sent(self.land, self.tree.send)
            all_sent(self.sib_buf, self.s_send)

    po = ChipSums(
        lambda chips: dot(of_chips(joined, chips), wo[...]),
        xh_all,
        po_sib,
        po_land,
        ps_send.at[0],
        ps_recv,
        p_send.at[0],
        p_recv,
    )
    hg = ChipSums(
        lambda chips: dot_nt(of_chips(mixed, chips), wp[...]),
        cot_all,
        hg_sib,
        hg_land,
        hs_send.at[0],
        hs_recv,
        h_send.at[0],
        h_recv,
    )
    all_sent(xh_all.at[pl.ds(0, 30)], x_send.at[0])
    po.begin(((2, cot_tree.near_of_mate), (3, cot_tree.far_of_mate)), 3)
    all_here(cot_all.at[pl.ds(0, 16)], c_given.at[0])

    @pl.loop(0, 32, unroll=True)
    def _(i):
        cs[pl.ds(SPAN * i, SPAN)] = cot_all[inv_ref[i]]

    def grads_by_owner(dst, base, columns):
        sums = jnp.sum(
            mixed[:, :, base : base + 256].reshape(ROW, 256).astype(F32), axis=0, keepdims=True
        )

        @pl.loop(0, 4, unroll=True)
        def _(i):
            rows = pl.ds(pl.multiple_of(i * 256, 256), 256)
            h = jnp.transpose(dot(mixed_t[base : base + 256], xs[:, rows]))
            raw = wr[rows, base : base + 256].astype(F32)
            vecs = wr[rows, 384:512].astype(F32)
            gain, bias = (vecs[:, columns + 64 + j : columns + 65 + j] for j in range(2))
            grad = gain * h + bias * sums
            lanes = lane_iota((256, 128))
            extra = vg[rows]
            for j, col in enumerate((raw * h, raw * sums)):
                extra = extra + jnp.where(
                    lanes == 64 + columns + j, jnp.sum(col, axis=1, keepdims=True), 0.0
                )
            if base:
                grad = jnp.concatenate([grad[:, :128], grad[:, 128:] + extra], axis=1)
            else:
                vg[rows] = extra
            for j in range(2):
                pair = [
                    grad[128 * j + 64 * t : 128 * j + 64 * t + 64].reshape(8, 8, 256)
                    for t in range(2)
                ]
                dst[:, 2 * i + j] = jnp.concatenate(pair, axis=1).astype(BF16)

    def owner_sums(dst, land, send, recv):
        return ColumnSums(
            "dp",
            lambda slot: dst.at[slot],
            land,
            dm,
            dp_turn,
            dp_mate,
            send.at[0],
            recv,
        )

    gf_sums = owner_sums(gf, gf_land, gf_send, gf_recv)
    gq_sums = owner_sums(gq, gq_land, gq_send, gq_recv)
    go_sums = ColumnSums(
        "dp",
        lambda slot: go_buf.at[pl.ds(5 * slot, 5)],
        go_land,
        dm,
        dp_turn,
        dp_mate,
        go_send.at[0],
        go_recv,
    )
    @pl.loop(0, 2, unroll=True)
    def _(i):
        left = dot(joined_t[...], cs[:, pl.ds(pl.multiple_of(i * 256, 256), 256)])
        right = dot(joined_t[...], cs[:, pl.ds(pl.multiple_of(i * 256 + 512, 256), 256)])
        units = jnp.concatenate([left.reshape(40, 8, 256), right.reshape(40, 8, 256)], axis=1)
        lanes = pl.ds(pl.multiple_of(i * 256, 256), 256)
        go_buf[pl.ds(8 * (1 - late), 32), :, lanes] = units[:32].astype(BF16)
        go_buf[pl.ds(32 * late, 8), :, lanes] = units[32:].astype(BF16)

    go_sums.start()
    po.pair_rest(3)

    @pl.loop(0, NCH, unroll=True)
    def _(i):
        rows = pl.ds(pl.multiple_of(i * CH, CH), CH)
        cot = cs[rows]
        back = dot_nt(cot, wo[...])
        ag = back[:, 256:].astype(BF16).astype(F32)
        ag_t = jnp.transpose(ag)
        dot_n[rows] = ag.astype(BF16)
        dot_t[:, rows] = ag_t.astype(BF16)
        delta[:, rows] = jnp.broadcast_to(
            jnp.sum(ag_t * ot[:, rows], axis=0, keepdims=True), (8, CH)
        )
        pg = back[:, :256] * dact[rows]
        mixed[pl.ds(8 * i, 8), :, 0:256] = pg.astype(BF16).reshape(8, SPAN, 256)
        mixed_t[0:256, rows] = jnp.transpose(pg).astype(BF16)

    lanes_d = lane_iota((D, 128))
    vg[...] = jnp.where((lanes_d == 71) | (lanes_d == 72), vg[...], 0.0)
    lanes_h = lane_iota((64, 128))
    cols_f = jnp.sum(mixed_t[0:256].astype(F32), axis=1, keepdims=True)
    for r in range(4):
        w = hidden_index(me, r)
        rows = pl.ds(pl.multiple_of(lax.rem(w, 16) * 64, 64), 64)
        vg[rows] += jnp.where(lanes_h == 64 + 9 + w // 16, cols_f[64 * r : 64 * r + 64], 0.0)
    grads_by_owner(gf, 0, 2)
    gf_sums.start()
    po.tree.far_of_me()
    po.of_mate()

    for qi in reversed(range(NCH)):
        lanes = slice(qi * CH, (qi + 1) * CH)
        dq = jnp.zeros((64, CH), F32)
        for k0, keys, q0, queries in tiles(qi):
            at, cols = slice(k0, k0 + keys), slice(q0, q0 + queries)
            p = held(k0, keys, q0, queries)[...].astype(F32) * scale[0:1, cols]
            dp = dot(vn[at, 0:64], dot_t[:, cols])
            ds = (p * (dp - delta[0:1, cols])).astype(BF16)
            dv = dot(p.astype(BF16), dot_n[cols])
            dk = dot(ds, qn[cols, 0:64])
            dq = dq + spread(dot(kt[:, at], ds), queries, 0.0)
            if qi == NCH - 1:
                dvn[at] = dv
                dkn[at] = dk
            else:
                dvn[at] += dv
                dkn[at] += dk
        dqt[:, lanes] = dq * 0.125

    @pl.loop(0, NCH, unroll=True)
    def _(i):
        rows = pl.ds(pl.multiple_of(i * CH, CH), CH)
        cosine, sine = cos_ref[:, rows], sin_ref[:, rows]
        dq = rotate_t(dqt[:, rows], cosine, sine, -1.0)
        dk = rotate_t(jnp.transpose(dkn[rows]), cosine, sine, -1.0)
        dv = jnp.transpose(dvn[rows])
        full = jnp.concatenate([dq, dk, dv, zeros_aug], axis=0)
        mixed_t[256:512, rows] = full.astype(BF16)
        mixed[pl.ds(8 * i, 8), :, 256:512] = jnp.transpose(full).astype(BF16).reshape(8, SPAN, 256)

    cols_q = jnp.sum(mixed_t[256:448].astype(F32), axis=1, keepdims=True)
    for i in range(3):
        vg[head_rows] += jnp.where(lanes_h == 68 + i, cols_q[64 * i : 64 * i + 64], 0.0)
    go_sums.middle()
    grads_by_owner(gq, 256, 0)
    gq_sums.start()
    po.tree.near_late()
    gf_sums.middle()

    all_sent(cot_all.at[pl.ds(0, 30)], c_send.at[0])

    def to_owner(part, total, send, recv, k, to, frm):
        return remote(part.at[to], total.at[frm], send.at[0], recv.at[0], {"seq": to})

    def own_sums(part, total, send, recv):
        @pl.loop(1, SEQ)
        def _(k):
            to_owner(part, total, send, recv, k, lax.rem(me + k, SEQ), me).start()

        total[me] = part[me]

    def own_arrived(part, total, send, recv):
        all_here(total.at[pl.ds(0, SEQ - 1)], recv.at[0])

    def squares_of(value):
        return jnp.sum(jnp.sum(value * value, axis=0), axis=0, keepdims=True)

    def fold_rows(value):
        return jnp.concatenate([value[:, :, :128], value[:, :, 128:]], axis=1).astype(BF16)

    f_squares = []

    def hidden_on():
        value = gf_sums.total().reshape(SEQ, 8, 256)
        f_squares.append(squares_of(value))
        f_part[...] = fold_rows(value)


    hg.begin(((6, hidden_on),))
    gq_sums.middle()
    out_total = go_sums.total()
    out_part[...] = out_total

    out_back = Trade(out_part, wout_sum, v_relay, 0, v_send, v_recv)
    out_back.whole = False

    def keep_total(u):
        wout_sum[u] = out_part[u]

    out_back.begin()
    kept(keep_total)
    out_squares = squares_of(out_total)
    squares = f_squares[0] + out_squares[:, :256] + out_squares[:, 256:]

    total = gq_sums.total().reshape(SEQ, 8, 256)
    weights = jnp.where(lane_iota(total.shape) < 192, total, 0.0)
    squares = squares + squares_of(weights)
    vec_rows = jnp.transpose(total[:, :, 128:].reshape(128, 128))[64:80]
    row_of = lax.broadcasted_iota(jnp.int32, vec_rows.shape, 0)
    tile_a[...] = jnp.where(row_of == 15, squares[:, :128] + squares[:, 128:], vec_rows).astype(BF16)

    def ta_copy(k, to, frm):
        return remote(tile_a, got_a.at[frm], ta_send.at[0], ta_recv.at[0], {"seq": to})

    @pl.loop(1, SEQ)
    def _(k):
        ta_copy(k, lax.rem(me + k, SEQ), me).start()

    got_a[me] = tile_a[...]
    hg.tree.far_of_me()
    q_part[...] = fold_rows(total)
    own_sums(q_part, q_sum, bq_send, bq_recv)
    own_sums(f_part, f_sum, bf_send, bf_recv)
    hg.of_mate()
    out_back.relay_on()
    all_here(got_a.at[pl.ds(0, SEQ - 1)], ta_recv.at[0])
    sums = jnp.sum(got_a[...].astype(F32), axis=0)
    vec_total = jnp.where(lax.broadcasted_iota(jnp.int32, sums.shape, 0) < VEC_ROWS, sums, 0.0)
    row = sums[15:16] + jnp.sum(vec_total * vec_total, axis=0, keepdims=True)
    tile_b[...] = jnp.broadcast_to(jnp.sum(row, axis=1, keepdims=True), (8, 128))

    def tb_copy(k, to, frm):
        return remote(tile_b, got_b.at[frm], tb_send.at[0], tb_recv.at[0], {"dp": to})

    @pl.loop(1, DP)
    def _(k):
        tb_copy(k, lax.rem(dm + k, DP), dm).start()

    hg.tree.near_late()
    got_b[dm] = tile_b[...]
    small[...] = jnp.zeros((128, 128), F32)
    small[0:16] = vec_total
    small[...] = jnp.transpose(small[...])
    vec_grad[...] = small[pl.ds(pl.multiple_of(8 * me, 8), 8)]
    vec_store.start()
    own_arrived(f_part, f_sum, bf_send, bf_recv)
    x_rows, x_hat, inv_std = own_rows()
    cot_own = own_cot()
    block_out[...] = (x_rows + po.total() + (vec_ref[7:8] + vec_ref[8:9])).astype(BF16)
    block_store.start()
    own_arrived(q_part, q_sum, bq_send, bq_recv)
    for s in range(SEQ):
        for j, p in enumerate(PIECES[s]):
            at = 64 * int(p)
            ref, k = (q_sum, j) if j < 3 else (f_sum, j - 3)
            both = ref[s].astype(F32)
            grad_in[:, at : at + 64] = both[8 * (k // 2) : 8 * (k // 2) + 8, 64 * (k % 2) : 64 * (k % 2) + 64]
    in_store.start()
    out_back.end()
    for u in range(5):
        grad_out[8 * u : 8 * u + 8] = unfold(wout_sum[u])
    out_store.start()

    all_here(got_b.at[pl.ds(0, DP - 1)], tb_recv.at[0])
    everything = jnp.sum(got_b[...], axis=0)
    square_ref[...] = jnp.broadcast_to(everything[:, 0:1], (8, 128))
    square_store.start()
    grad = hg.total()
    back = (
        grad
        - jnp.mean(grad, axis=-1, keepdims=True)
        - x_hat * jnp.mean(grad * x_hat, axis=-1, keepdims=True)
    )
    input_grad[...] = (cot_own + inv_std * back).astype(BF16)
    grad_store.start()
    po.sent()
    hg.sent()
    out_trade.sent()
    out_back.sent()
    for sums in (gf_sums, gq_sums, go_sums):
        sums.sent()
    all_sent(win_all.at[pl.ds(0, 7)], l_send.at[0])
    all_sent(wout_all.at[pl.ds(0, 35)], o_send.at[0])
    all_sent(win_own.at[pl.ds(0, SEQ - 1)], a_send.at[0])
    all_sent(got_a.at[pl.ds(0, SEQ - 1)], ta_send.at[0])
    all_sent(got_b.at[pl.ds(0, DP - 1)], tb_send.at[0])
    all_sent(f_part.at[pl.ds(0, SEQ - 1)], bf_send.at[0])
    all_sent(q_part.at[pl.ds(0, SEQ - 1)], bq_send.at[0])
    for store in stores:
        store.wait()


def layer_call(span, length, x, cot, w_in, w_out, vectors):
    freqs = np.float32(THETA_BASE) ** (-2.0 * np.arange(ROT // 2) / ROT)
    angles = np.arange(ROW, dtype=np.float32)[None, :] * freqs.astype(np.float32)[:, None]
    cosine, sine = np.cos(angles).astype(np.float32), np.sin(angles).astype(np.float32)
    smem = pl.BlockSpec(memory_space=pltpu.SMEM)
    anywhere = pl.BlockSpec(memory_space=pl.ANY)
    sds = jax.ShapeDtypeStruct
    dma = pltpu.SemaphoreType.DMA

    def buf(shape, dtype=BF16):
        return pltpu.VMEM(shape, dtype)

    return pl.pallas_call(
        layer_kernel,
        out_shape=(
            sds((TOK, D), BF16),
            sds((TOK, D), BF16),
            sds((8, 7 * D), F32),
            sds((40, D), F32),
            sds((8, 128), F32),
            sds((8, 128), F32),
        ),
        in_specs=[smem] * 2 + [anywhere] * 7,
        out_specs=[anywhere] * 6,
        scratch_shapes=[
            buf((TOK, D)),
            buf((TOK, D)),
            buf((8, 7 * D), F32),
            buf((40, D), F32),
            buf((8, VEC_ROWS), F32),
            buf((8, ROW), F32),
            buf((8, ROW), F32),
            buf((TOK, D)),
            buf((TOK, D)),
            buf((8, 7 * D), F32),
            buf((40, D), F32),
            buf((SEQ, 16, 128)),
            buf((SEQ, 16, 128)),
            buf((5, 16, 512), F32),
            buf((8, 128), F32),
            buf((8, 128), F32),
            dma((7,)),
            dma((6,)),
            pltpu.SMEM((32,), jnp.int32),
            buf((32, SPAN, D)),
            buf((32, SPAN, D)),
            buf((SEQ, 16, 256)),
            buf((DP, SEQ, 16, 256)),
            buf((40, 16, 512)),
            buf((5, 16, 512)),
            buf((2, 5, 16, 512)),
            buf((2, 5, 16, 512), F32),
            buf((128, 128), F32),
            buf((16, D), F32),
            buf((ROW, D)),
            buf((ROW, D)),
            buf((D, 512)),
            buf((D, 512)),
            buf((320, D)),
            buf((128, ROW)),
            buf((ROW, 128)),
            buf((64, ROW)),
            buf((ROW, 128)),
            buf((64, ROW)),
            buf((ROW, 128)),
            buf((64, ROW)),
            buf((ROW, 64)),
            buf((64, ROW), F32),
            buf((8, ROW), F32),
            buf((10, CH, CH)),
            buf((8, ROW), F32),
            buf((32, SPAN, 320)),
            buf((320, ROW)),
            buf((ROW, 256), F32),
            buf((32, SPAN, 512)),
            buf((512, ROW)),
            buf((64, ROW), F32),
            buf((ROW, 64), F32),
            buf((ROW, 64), F32),
            buf((D, 128), F32),
            buf((40, 16, 512)),
            buf((5, 16, 512), F32),
            buf((DP, 8, 16, 256)),
            buf((DP, 8, 16, 256)),
            buf((8, 2, SPAN, D)),
            buf((8, 2, SPAN, D)),
            buf((7, 2, SPAN, D)),
            buf((7, 2, SPAN, D)),
            buf((8, 8, 16, 256)),
            buf((8, 8, 16, 256)),
            buf((8, 5, 16, 512)),
            buf((SEQ, 16, 128)),
            buf((SEQ, 16, 128)),
            buf((16, 128)),
            buf((8, 128), F32),
            buf((SEQ, 16, 128)),
            buf((DP, 8, 128), F32),
            dma((1,)),
            dma((1,)),
            dma((1,)),
            dma((1,)),
            dma((8, 2)),
            dma((1,)),
            dma((1,)),
            dma((8, 2)),
            dma((1,)),
            dma((1,)),
            dma((DP, 2)),
            dma((1,)),
            dma((DP, 2)),
            dma((2, 5)),
            dma((2, 5)),
            dma((1,)),
            dma((8,)),
            dma((1,)),
            dma((6,)),
            dma((1,)),
            dma((8,)),
            dma((1,)),
            dma((6,)),
            dma((1,)),
            dma((3,)),
            dma((1,)),
            dma((3,)),
            dma((1,)),
            dma((3,)),
            dma((2, 5)),
            dma((2, 5)),
            dma((1,)),
            dma((1,)),
            dma((1,)),
            dma((1,)),
            dma((1,)),
            dma((1,)),
            dma((1,)),
            dma((1,)),
        ],
        compiler_params=pltpu.CompilerParams(
            collective_id=0, has_side_effects=True, vmem_limit_bytes=VMEM_LIMIT
        ),
        name="layer_of_one_row",
    )(span, length, x, cot, w_in, w_out, vectors, jnp.asarray(cosine), jnp.asarray(sine))


def adam(weight, grad, first, second, factor, rate, decay):
    clipped = grad * factor
    first_new = BETA_ONE * first + (1.0 - BETA_ONE) * clipped
    second_new = BETA_TWO * second + (1.0 - BETA_TWO) * clipped * clipped
    first_hat = first_new / (1.0 - BETA_ONE**STEP)
    second_hat = second_new / (1.0 - BETA_TWO**STEP)
    weight_new = weight * (1.0 - rate * decay) - rate * first_hat / (
        jnp.sqrt(second_hat) + ADAM_EPS
    )
    return (weight_new, first_new, second_new, weight_new.astype(BF16))


UPDATE_IN = (
    ("block_out", (TOK, D), BF16),
    ("input_grad", (TOK, D), BF16),
    ("square", (8, 128), F32),
    ("grad_in", (8, 7 * D), F32),
    ("w_in", (8, 7 * D), F32),
    ("in_first", (8, 7 * D), F32),
    ("in_second", (8, 7 * D), F32),
    ("grad_out", (40, D), F32),
    ("w_out", (40, D), F32),
    ("out_first", (40, D), F32),
    ("out_second", (40, D), F32),
    ("vectors", (8, VEC_ROWS), F32),
    ("vec_first", (8, VEC_ROWS), F32),
    ("vec_second", (8, VEC_ROWS), F32),
    ("vec_grad", (8, 128), F32),
)
UPDATE_OUT = (
    ((TOK, D), BF16),
    ((TOK, D), BF16),
    ((8, 7 * D), F32),
    ((40, D), F32),
    ((8, VEC_ROWS), F32),
    ((8, 7 * D), F32),
    ((40, D), F32),
    ((8, VEC_ROWS), F32),
    ((8, 7 * D), F32),
    ((40, D), F32),
    ((8, VEC_ROWS), F32),
    ((8, 7 * D), BF16),
    ((40, D), BF16),
    ((8, VEC_ROWS), BF16),
)


def update_kernel(*refs):
    ins, refs = refs[: len(UPDATE_IN)], refs[len(UPDATE_IN) :]
    norm_ref, refs = refs[0], refs[1:]
    outs, refs = refs[: len(UPDATE_OUT)], refs[len(UPDATE_OUT) :]
    in_bufs, refs = refs[: len(UPDATE_IN)], refs[len(UPDATE_IN) :]
    out_bufs, (in_sem, out_sem) = refs[: len(UPDATE_OUT)], refs[len(UPDATE_OUT) :]
    loads = [
        pltpu.make_async_copy(a, b, in_sem.at[i]) for i, (a, b) in enumerate(zip(ins, in_bufs))
    ]
    stores = [
        pltpu.make_async_copy(in_bufs[i] if i < 2 else b, a, out_sem.at[i])
        for i, (a, b) in enumerate(zip(outs, out_bufs))
    ]
    order = list(range(2, len(loads))) + [0, 1]
    for i in order:
        loads[i].start()
    names = [name for name, _, _ in UPDATE_IN]

    def take(name):
        i = names.index(name)
        loads[i].wait()
        return in_bufs[i]

    def give(i, value):
        out_bufs[i][...] = value
        stores[i].start()

    norm = jnp.sqrt(take("square")[...])
    norm_ref[0, 0] = norm[0, 0]
    factor = jnp.minimum(1.0, CLIP_NORM / norm)[0:1, 0:1]

    for i in range(2):
        loads[i].wait()
        stores[i].start()

    def matrix(at, grad, weight, first, second, rate, decay):
        values = adam(
            take(weight)[...], grad, take(first)[...], take(second)[...], factor, rate, decay
        )
        for k, value in enumerate(values):
            give(at + 3 * k, value)

    matrix(2, take("grad_in")[...], "w_in", "in_first", "in_second", RATE_MATRIX, DECAY_RATE)
    matrix(3, take("grad_out")[...], "w_out", "out_first", "out_second", RATE_MATRIX, DECAY_RATE)
    grad_vec = take("vec_grad")[:, 0:VEC_ROWS]
    matrix(4, grad_vec, "vectors", "vec_first", "vec_second", RATE_VECTOR, 0.0)

    for store in stores:
        store.wait()


def update_call(*args):
    anywhere = pl.BlockSpec(memory_space=pl.ANY)
    dma = pltpu.SemaphoreType.DMA
    sds = jax.ShapeDtypeStruct
    return pl.pallas_call(
        update_kernel,
        out_shape=(sds((1, 1), F32),) + tuple(sds(shape, kind) for shape, kind in UPDATE_OUT),
        in_specs=[anywhere] * len(UPDATE_IN),
        out_specs=[pl.BlockSpec(memory_space=pltpu.SMEM)] + [anywhere] * len(UPDATE_OUT),
        scratch_shapes=[pltpu.VMEM(shape, kind) for _, shape, kind in UPDATE_IN]
        + [pltpu.VMEM(shape, kind) for shape, kind in UPDATE_OUT]
        + [dma((len(UPDATE_IN),)), dma((len(UPDATE_OUT),))],
        compiler_params=pltpu.CompilerParams(vmem_limit_bytes=UPDATE_LIMIT),
        name="clipped_update",
    )(*args)


def body(
    hidden_in,
    out_cot,
    in_weight,
    out_weight,
    vectors,
    in_first,
    in_second,
    out_first,
    out_second,
    vec_first,
    vec_second,
    lengths,
    span_of,
):
    block_out, input_grad, grad_in, grad_out, squares, vec_grad = layer_call(
        span_of.T, lengths, hidden_in[0], out_cot[0], in_weight, out_weight, vectors.T
    )
    norm, block_out, input_grad, *rest = update_call(
        block_out,
        input_grad,
        squares,
        grad_in,
        in_weight,
        in_first,
        in_second,
        grad_out,
        out_weight,
        out_first,
        out_second,
        vectors.T,
        vec_first.T,
        vec_second.T,
        vec_grad,
    )
    rest = [out.T if i % 3 == 2 else out for i, out in enumerate(rest)]
    return (block_out[None], input_grad[None], norm.reshape(()), *rest)


def solution(mesh):
    tokens = P("dp", "seq", None)
    matrix = P(("seq", "dp"), None)
    vector = P(None, ("seq", "dp"))
    return jax.shard_map(
        body,
        mesh=mesh,
        in_specs=(
            tokens,
            tokens,
            matrix,
            matrix,
            vector,
            matrix,
            matrix,
            matrix,
            matrix,
            vector,
            vector,
            P("dp"),
            P(),
        ),
        out_specs=(tokens, tokens, P()) + (matrix, matrix, vector) * 4,
        check_vma=False,
    )
```
